32 devices in a mesh: group: 2 (over y), dom: 4 (over z), dp: 4 (over x, core).
Axes of the slice: x: 2, y: 2, z: 4, core: 2. Of those that a mesh axis runs over, the one named last changes fastest.
Arguments:
- node_latents: bfloat16 [8, 512, 512], P(('group', 'dp'), 'dom'), parts along dimension 0, may hold values from -6 to 6
- edge_latents: bfloat16 [8, 3072, 512], P(('group', 'dp'), 'dom'), parts along dimension 0, may hold values from -6 to 6
- agg_cotangent: bfloat16 [8, 512, 512], P(('group', 'dp'), 'dom'), parts along dimension 0, may hold values from -6 to 6
- weight_in: bfloat16 [1536, 512], replicated, may hold values from -0.15625 to 0.15625
- weight_out: bfloat16 [512, 512], replicated, may hold values from -0.25 to 0.25
- boundary: int32 [8, 4], P(('group', 'dom')), parts along dimension 0, may hold values from 0 to 1
- tile_src: int32 [96], P(('group', 'dom')), parts along dimension 0, may hold values from 0 to 5, as said below
- tile_dst: int32 [96], P(('group', 'dom')), parts along dimension 0, may hold values from 0 to 1
- edge_slot: int32 [96, 64], P(('group', 'dom')), parts along dimension 0, may hold values from 0 to 63
- tile_count: int32 [8], P(('group', 'dom')), parts along dimension 0, may hold values from 4 to 12, as said below
Outputs:
- aggregate: bfloat16 [8, 512, 512], P(('group', 'dp'), 'dom'), parts along dimension 0
- edge_grad: bfloat16 [8, 3072, 512], P(('group', 'dp'), 'dom'), parts along dimension 0
- node_grad: bfloat16 [8, 512, 512], P(('group', 'dp'), 'dom'), parts along dimension 0
- w_in_grad: float32 [3072, 512], P(('group', 'dp')), parts along dimension 0
- w_out_grad: float32 [1024, 512], P(('group', 'dp')), parts along dimension 0
The draws below stay inside these ranges and needn't reach their ends.
There are 2 independent parts, one for each index of `group`. The reference program is written for one: setup_inputs(seed, part) draws one part's arguments, and reference() takes and returns one part's arrays. A program takes and returns all parts, laid end to end along the dimension named above; an argument that names none is the same for every part. Nothing has to cross between parts.
Inputs may be any that keep to these rules, and one draw needn't show every extreme that they name: `boundary`: block a partition sends to its partner at offset o_q, o = (1, -1, 2, -2), that is to partition d + o_q. `tile_src`: values below 2 name a block of the tile's own partition d; 2 + q names block boundary[d - o_q, q] of partition d - o_q, and only for partitions that exist. Tile j < 4 of a partition names 2 + j whenever partition d - o_j exists. The first tile_count[d] tiles of partition d are live; some partition has exactly 12 and some exactly 4.
All inputs are finite; a program needn't handle non-finite values.
Results may differ from the reference program's by a relative error of at most 0.0046.
Values may be sent and summed in bfloat16 or wider, within the bound.
No kernel may reach another device: no remote copies, remote signals or barrier semaphores. Data moves between devices by JAX's collectives and lax.ppermute only.
A program may use at most 64 MiB of HBM per device.

```python
import jax
import jax.numpy as jnp
from jax import lax

LATENT = 512
BLOCK = 64
BLOCKS_DEV = 2
TILES_DEV = 12
SAMPLES = 4
NODES = 512
EDGES = 3072
N_DOM = 4


def draw_tile_src(key, part):
    key = jax.random.fold_in(key, 11)
    cand_key, local_key = jax.random.split(key)
    owner_index = jnp.arange(N_DOM, dtype=jnp.int32)[:, None]
    offsets = jnp.array([1, -1, 2, -2], jnp.int32)
    candidate = jax.random.randint(cand_key, (N_DOM, TILES_DEV), 0, BLOCKS_DEV + 4)
    fallback = jax.random.randint(local_key, (N_DOM, TILES_DEV), 0, BLOCKS_DEV)
    partner = owner_index - offsets[jnp.clip(candidate - BLOCKS_DEV, 0, 3)]
    usable = (candidate < BLOCKS_DEV) | (partner >= 0) & (partner < N_DOM)
    chosen = jnp.where(usable, candidate, fallback)
    slot_index = jnp.arange(TILES_DEV, dtype=jnp.int32)[None, :]
    forced_partner = owner_index - offsets[jnp.clip(slot_index, 0, 3)]
    forced_valid = (slot_index < 4) & (forced_partner >= 0) & (forced_partner < N_DOM)
    chosen = jnp.where(forced_valid, BLOCKS_DEV + slot_index, chosen)
    return chosen.reshape(N_DOM * TILES_DEV).astype(jnp.int32)


def draw_tile_count(key, part):
    key = jax.random.fold_in(key, 23)
    first_key, second_key, third_key, pick_key = jax.random.split(key, 4)
    extent = (N_DOM,)
    counts = jax.random.randint(first_key, extent, 4, TILES_DEV + 1)
    counts = jnp.minimum(counts, jax.random.randint(second_key, extent, 4, TILES_DEV + 1))
    counts = jnp.minimum(counts, jax.random.randint(third_key, extent, 4, TILES_DEV + 1))
    places = jax.random.permutation(pick_key, N_DOM)
    positions = jnp.arange(N_DOM)
    counts = jnp.where(positions == places[0], TILES_DEV, counts)
    counts = jnp.where(positions == places[1], 4, counts)
    return counts.astype(jnp.int32)


def place_ends(drawn, rng, least, largest):
    longest = drawn.shape.index(max(drawn.shape))
    spots = []
    for shift in (0, 1):
        where = [jax.random.randint(jax.random.fold_in(rng, axis), (), 0, length) for axis, length in enumerate(drawn.shape)]
        where[longest] = (where[longest] + shift) % drawn.shape[longest]
        spots.append(tuple(where))
    return drawn.at[spots[0]].set(least).at[spots[1]].set(largest)


def block_scale(key, shape, shards, smallest, largest):
    def one(dim, shards_of):
        draws = jax.random.uniform(jax.random.fold_in(jax.random.fold_in(key, 6), dim), (shards_of,), jnp.float32, smallest / len(shards), largest / len(shards))
        return jnp.repeat(jnp.exp(draws), shape[dim] // shards_of).reshape((-1,) + (1,) * (len(shape) - dim - 1))

    loudness = one(*shards[0])
    for cut in shards[1:]:
        loudness = loudness * one(*cut)
    return loudness


def noise(key, shape, scale, most, cuts=(), kind=jnp.bfloat16):
    values = scale * jax.random.normal(key, shape, jnp.float32)
    if cuts:
        values = values * block_scale(key, shape, cuts, -0.22, 0.18)
    return jnp.clip(values, -most, most).astype(kind)


def setup_inputs(seed: int = 0, part: int = 0) -> dict:
    key_list = jax.random.split(jax.random.key(seed), 11)
    own_keys = jax.random.split(jax.random.fold_in(key_list[10], part), 11)
    return {
        "node_latents": noise(own_keys[0], (SAMPLES, NODES, LATENT), 1.0, 6.0, ((0, 4), (1, 4))),
        "edge_latents": noise(own_keys[1], (SAMPLES, EDGES, LATENT), 1.0, 6.0, ((0, 4), (1, 4))),
        "agg_cotangent": noise(own_keys[2], (SAMPLES, NODES, LATENT), 1.0, 6.0, ((0, 4), (1, 4))),
        "weight_in": noise(key_list[3], (3 * LATENT, LATENT), (3 * LATENT) ** -0.5, 0.15625),
        "weight_out": noise(key_list[4], (LATENT, LATENT), LATENT ** -0.5, 0.25),
        "boundary": place_ends(jax.random.randint(own_keys[5], (N_DOM, 4), 0, BLOCKS_DEV), jax.random.fold_in(own_keys[5], 1), 0, BLOCKS_DEV - 1).astype(jnp.int32),
        "tile_src": draw_tile_src(jax.random.fold_in(jax.random.fold_in(key_list[10], part), 71), part),
        "tile_dst": place_ends(jax.random.randint(own_keys[7], (N_DOM * TILES_DEV,), 0, BLOCKS_DEV), jax.random.fold_in(own_keys[7], 1), 0, BLOCKS_DEV - 1).astype(jnp.int32),
        "edge_slot": place_ends(jax.random.randint(own_keys[8], (N_DOM * TILES_DEV, BLOCK), 0, BLOCK), jax.random.fold_in(own_keys[8], 1), 0, BLOCK - 1).astype(jnp.int32),
        "tile_count": draw_tile_count(jax.random.fold_in(jax.random.fold_in(key_list[10], part), 71), part),
    }


OFFSET_LIST = (1, -1, 2, -2)
EPSILON = 1e-05

def build_tables(boundary, tile_src, tile_dst, edge_slot, tile_count):
    total_tiles = N_DOM * TILES_DEV
    tile_index = jnp.arange(total_tiles, dtype=jnp.int32)
    owner_part = tile_index // TILES_DEV
    within_part = tile_index % TILES_DEV
    tile_live = (within_part < tile_count[owner_part]).astype(jnp.float32)
    offsets = jnp.array(OFFSET_LIST, jnp.int32)
    partner_slot = jnp.clip(tile_src - BLOCKS_DEV, 0, 3)
    partner = owner_part - offsets[partner_slot]
    exists = (partner >= 0) & (partner < N_DOM)
    safe_partner = jnp.clip(partner, 0, N_DOM - 1)
    remote_block = safe_partner * BLOCKS_DEV + boundary[safe_partner, partner_slot]
    is_local = tile_src < BLOCKS_DEV
    local_block = owner_part * BLOCKS_DEV + jnp.clip(tile_src, 0, BLOCKS_DEV - 1)
    send_block = jnp.where(is_local, local_block, remote_block)
    tile_present = (is_local | exists).astype(jnp.float32)
    recv_block = owner_part * BLOCKS_DEV + tile_dst
    send_ids = (send_block[:, None] * BLOCK + edge_slot).reshape(-1).astype(jnp.int32)
    recv_ids = (recv_block[:, None] * BLOCK + jnp.arange(BLOCK, dtype=jnp.int32)[None, :]).reshape(-1).astype(jnp.int32)
    return (tile_live, tile_present, send_ids, recv_ids)

def reference(node_latents, edge_latents, agg_cotangent, weight_in, weight_out, boundary, tile_src, tile_dst, edge_slot, tile_count):
    tile_live, tile_present, send_ids, recv_ids = build_tables(boundary, tile_src, tile_dst, edge_slot, tile_count)
    row_live = jnp.repeat(tile_live, BLOCK)[:, None]
    row_present = jnp.repeat(tile_present, BLOCK)[:, None]

    def one_sample(totals, sample):
        node_rows, edge_rows, cot_rows = sample
        senders = (node_rows[send_ids].astype(jnp.float32) * row_present).astype(jnp.bfloat16)
        receivers = node_rows[recv_ids]
        joined = jnp.concatenate([edge_rows, senders, receivers], axis=1)
        preact = jnp.dot(joined, weight_in, preferred_element_type=jnp.float32)
        sigmoid_pre = jax.nn.sigmoid(preact)
        activated = (preact * sigmoid_pre).astype(jnp.bfloat16)
        projected = jnp.dot(activated, weight_out, preferred_element_type=jnp.float32)
        centered = projected - lax.optimization_barrier(jnp.mean(projected, axis=1, keepdims=True))
        inv_scale = lax.rsqrt(lax.optimization_barrier(jnp.mean(centered * centered, axis=1, keepdims=True)) + EPSILON)
        message = centered * inv_scale
        updated = (edge_rows.astype(jnp.float32) + message) * row_live
        aggregate = jax.ops.segment_sum(updated, recv_ids, num_segments=NODES).astype(jnp.bfloat16)
        upstream = cot_rows[recv_ids].astype(jnp.float32) * row_live
        grad_project = inv_scale * (upstream - lax.optimization_barrier(jnp.mean(upstream, axis=1, keepdims=True)) - message * lax.optimization_barrier(jnp.mean(upstream * message, axis=1, keepdims=True)))
        grad_project = grad_project.astype(jnp.bfloat16)
        grad_out = jnp.dot(activated.T, grad_project, preferred_element_type=jnp.float32)
        grad_act = jnp.dot(grad_project, weight_out.T, preferred_element_type=jnp.float32)
        grad_pre = (grad_act * sigmoid_pre * (1.0 + preact * (1.0 - sigmoid_pre))).astype(jnp.bfloat16)
        grad_in = jnp.dot(joined.T, grad_pre, preferred_element_type=jnp.float32)
        grad_edge = jnp.dot(grad_pre, weight_in[:LATENT].T, preferred_element_type=jnp.float32)
        grad_send = jnp.dot(grad_pre, weight_in[LATENT:2 * LATENT].T, preferred_element_type=jnp.float32)
        grad_recv = jnp.dot(grad_pre, weight_in[2 * LATENT:].T, preferred_element_type=jnp.float32)
        edge_grad = (upstream + grad_edge).astype(jnp.bfloat16)
        node_grad = jax.ops.segment_sum(grad_send * row_present, send_ids, num_segments=NODES)
        node_grad = node_grad + jax.ops.segment_sum(grad_recv, recv_ids, num_segments=NODES)
        return ((totals[0] + grad_in, totals[1] + grad_out), (aggregate, edge_grad, node_grad.astype(jnp.bfloat16)))
    zeros_in = jnp.zeros((3 * LATENT, LATENT), jnp.float32)
    zeros_out = jnp.zeros((LATENT, LATENT), jnp.float32)
    totals, outputs = lax.scan(one_sample, (zeros_in, zeros_out), (node_latents, edge_latents, agg_cotangent))
    return (outputs[0], outputs[1], outputs[2], totals[0], totals[1])
```

```python
import jax
import jax.numpy as jnp
from jax import lax
from jax.sharding import PartitionSpec as P

OFFSET_LIST = (1, -1, 2, -2)
EPSILON = 1e-05


def from_behind(array, axis, by):
    devices = lax.axis_size(axis)
    pairs = [(i, i + by) for i in range(devices) if 0 <= i + by < devices]
    return lax.ppermute(array, axis, pairs)


def pair_dot(left, right):
    return lax.dot_general(
        left, right, (((1,), (1,)), ((), ())), preferred_element_type=jnp.float32
    )


def outer_dot(left, right):
    return lax.dot_general(
        left, right, (((0,), (0,)), ((), ())), preferred_element_type=jnp.float32
    )


def send_blocks(outgoing):
    arrived = [from_behind(outgoing[which], "dom", OFFSET_LIST[which]) for which in range(4)]
    return jnp.stack(arrived)


def return_blocks(partial_grads):
    arrived = [
        from_behind(partial_grads[which].astype(jnp.bfloat16), "dom", -OFFSET_LIST[which]).astype(
            jnp.float32
        )
        for which in range(4)
    ]
    return jnp.stack(arrived)


def edge_pass(
    ext_nodes,
    edge_rows,
    cot_blocks,
    sources,
    targets,
    slot_table,
    live_tiles,
    weight_in,
    weight_out,
):
    tile_number = sources.shape[0]
    block_size = slot_table.shape[1]
    latent = edge_rows.shape[1]
    extent = ext_nodes.shape[0]
    owned_blocks = cot_blocks.shape[0]
    edge_total = tile_number * block_size
    pick_src = (sources[:, None] == jnp.arange(extent)[None, :]).astype(jnp.bfloat16)
    pick_dst = (targets[:, None] == jnp.arange(owned_blocks)[None, :]).astype(jnp.bfloat16)
    slot_hot = (slot_table[:, :, None] == jnp.arange(block_size)[None, None, :]).astype(
        jnp.bfloat16
    )
    src_blocks = jnp.einsum(
        "tb,bkl->tkl", pick_src, ext_nodes, preferred_element_type=jnp.float32
    ).astype(jnp.bfloat16)
    senders = jnp.einsum(
        "tks,tsl->tkl", slot_hot, src_blocks, preferred_element_type=jnp.float32
    ).astype(jnp.bfloat16)
    receivers = jnp.einsum(
        "tb,bkl->tkl", pick_dst, ext_nodes[:owned_blocks], preferred_element_type=jnp.float32
    ).astype(jnp.bfloat16)
    joined = jnp.concatenate(
        [edge_rows, senders.reshape(edge_total, latent), receivers.reshape(edge_total, latent)],
        axis=1,
    )
    preact = jnp.dot(joined, weight_in, preferred_element_type=jnp.float32)
    sigmoid_pre = jax.nn.sigmoid(preact)
    activated = (preact * sigmoid_pre).astype(jnp.bfloat16)
    projected = jnp.dot(activated, weight_out, preferred_element_type=jnp.float32)
    centered = projected - jnp.mean(projected, axis=1, keepdims=True)
    inv_scale = lax.rsqrt(jnp.mean(centered * centered, axis=1, keepdims=True) + EPSILON)
    message = centered * inv_scale
    row_live = jnp.repeat(live_tiles, block_size)[:, None]
    updated = (edge_rows.astype(jnp.float32) + message) * row_live
    hot_dst = pick_dst.astype(jnp.float32)
    aggregate = jnp.einsum(
        "tb,tkl->bkl",
        hot_dst,
        updated.reshape(tile_number, block_size, latent),
        precision=lax.Precision.HIGHEST,
    )
    upstream = (
        jnp.einsum("tb,bkl->tkl", pick_dst, cot_blocks, preferred_element_type=jnp.float32).reshape(
            edge_total, latent
        )
        * row_live
    )
    grad_project = inv_scale * (
        upstream
        - jnp.mean(upstream, axis=1, keepdims=True)
        - message * jnp.mean(upstream * message, axis=1, keepdims=True)
    )
    grad_project = grad_project.astype(jnp.bfloat16)
    grad_out = outer_dot(activated, grad_project)
    grad_act = pair_dot(grad_project, weight_out)
    grad_pre = (grad_act * sigmoid_pre * (1.0 + preact * (1.0 - sigmoid_pre))).astype(jnp.bfloat16)
    grad_in = outer_dot(joined, grad_pre)
    grad_edge = pair_dot(grad_pre, weight_in[:latent])
    grad_send = pair_dot(grad_pre, weight_in[latent : 2 * latent])
    grad_recv = pair_dot(grad_pre, weight_in[2 * latent :])
    edge_grad = (upstream + grad_edge).astype(jnp.bfloat16)
    slot_sums = jnp.einsum(
        "tks,tkl->tsl",
        slot_hot.astype(jnp.float32),
        grad_send.reshape(tile_number, block_size, latent),
        precision=lax.Precision.HIGHEST,
    )
    ext_grad = jnp.einsum(
        "tb,tsl->bsl", pick_src.astype(jnp.float32), slot_sums, precision=lax.Precision.HIGHEST
    )
    recv_grad = jnp.einsum(
        "tb,tkl->bkl",
        hot_dst,
        grad_recv.reshape(tile_number, block_size, latent),
        precision=lax.Precision.HIGHEST,
    )
    return (aggregate, edge_grad, ext_grad, recv_grad, grad_in, grad_out)


def halve_over_dp(stacked):
    devices = lax.axis_size("dp")
    if devices & (devices - 1):
        return lax.psum_scatter(stacked, "dp", scatter_dimension=0, tiled=True)[0]
    index = lax.axis_index("dp")
    bit = 1
    while bit < devices:
        pairs = [(i, i ^ bit) for i in range(devices)]
        mine = (index // bit) % 2
        split = stacked.reshape((-1, 2) + stacked.shape[1:])
        away = lax.dynamic_index_in_dim(split, 1 - mine, 1, keepdims=False).astype(jnp.bfloat16)
        kept = lax.dynamic_index_in_dim(split, mine, 1, keepdims=False)
        stacked = kept + lax.ppermute(away, "dp", pairs).astype(jnp.float32)
        bit *= 2
    return stacked[0]


def sum_over_dom(rows):
    devices = lax.axis_size("dom")
    if devices > 4:
        piece = lax.psum_scatter(rows, "dom", scatter_dimension=0, tiled=True)
        return lax.all_gather(piece, "dom", axis=0, tiled=True)
    index = lax.axis_index("dom")
    pieces = rows.reshape((devices, -1) + rows.shape[1:])
    narrow = pieces.astype(jnp.bfloat16)
    total = lax.dynamic_index_in_dim(pieces, index, 0, keepdims=False)
    for shift in range(1, devices):
        pairs = [(i, (i + shift) % devices) for i in range(devices)]
        away = lax.dynamic_index_in_dim(narrow, (index + shift) % devices, 0, keepdims=False)
        total = total + lax.ppermute(away, "dom", pairs).astype(jnp.float32)
    total = total.astype(jnp.bfloat16)
    whole = jnp.zeros(pieces.shape, jnp.float32)
    whole = lax.dynamic_update_index_in_dim(whole, total.astype(jnp.float32), index, 0)
    for shift in range(1, devices):
        pairs = [(i, (i + shift) % devices) for i in range(devices)]
        came = lax.ppermute(total, "dom", pairs).astype(jnp.float32)
        whole = lax.dynamic_update_index_in_dim(whole, came, (index - shift) % devices, 0)
    return whole.reshape(rows.shape)


def body(
    node_latents,
    edge_latents,
    agg_cotangent,
    weight_in,
    weight_out,
    boundary,
    tile_src,
    tile_dst,
    edge_slot,
    tile_count,
):
    latent = node_latents.shape[2]
    block_size = edge_slot.shape[1]
    owned_blocks = node_latents.shape[1] // block_size
    tiles_here = tile_src.shape[0]
    node_blocks = node_latents[0].reshape(owned_blocks, block_size, latent)
    cot_blocks = agg_cotangent[0].reshape(owned_blocks, block_size, latent)
    chosen = boundary[0]
    outgoing = node_blocks[chosen]
    incoming = send_blocks(outgoing)
    ext_nodes = jnp.concatenate([node_blocks, incoming], axis=0)
    edge_rows = edge_latents[0]
    live_limit = tile_count[0]
    live_tiles = (jnp.arange(tiles_here) < live_limit).astype(jnp.float32)
    agg_sum, edge_grad, ext_grad, recv_grad, grad_in, grad_out = edge_pass(
        ext_nodes,
        edge_rows,
        cot_blocks,
        tile_src,
        tile_dst,
        edge_slot,
        live_tiles,
        weight_in,
        weight_out,
    )
    returned = return_blocks(ext_grad[owned_blocks:])
    node_grad = ext_grad[:owned_blocks] + recv_grad
    node_grad = node_grad.at[chosen].add(returned)
    dp_count = lax.axis_size("dp")
    stacked = jnp.concatenate(
        [grad_in.reshape(dp_count, -1, latent), grad_out.reshape(dp_count, -1, latent)], axis=1
    )
    in_rows = grad_in.shape[0] // dp_count
    mine = sum_over_dom(halve_over_dp(stacked))
    aggregate = agg_sum.reshape(1, owned_blocks * block_size, latent).astype(jnp.bfloat16)
    node_out = node_grad.reshape(1, owned_blocks * block_size, latent).astype(jnp.bfloat16)
    return (aggregate, edge_grad[None], node_out, mine[:in_rows], mine[in_rows:])


def solution(mesh):
    in_specs = (
        P(("group", "dp"), "dom", None),
        P(("group", "dp"), "dom", None),
        P(("group", "dp"), "dom", None),
        P(),
        P(),
        P(("group", "dom"), None),
        P(("group", "dom")),
        P(("group", "dom")),
        P(("group", "dom"), None),
        P(("group", "dom")),
    )
    out_specs = (
        P(("group", "dp"), "dom", None),
        P(("group", "dp"), "dom", None),
        P(("group", "dp"), "dom", None),
        P(("group", "dp"), None),
        P(("group", "dp"), None),
    )
    return jax.shard_map(body, mesh=mesh, in_specs=in_specs, out_specs=out_specs, check_vma=False)
```

```python
import functools

import jax
import jax.numpy as jnp
from jax import lax
from jax.experimental import pallas as pl
from jax.experimental.pallas import tpu as pltpu
from jax.sharding import PartitionSpec as P

OFFSET_LIST = (1, -1, 2, -2)
EPSILON = 1e-05
VMEM = pl.BlockSpec(memory_space=pltpu.VMEM)
SMEM = pl.BlockSpec(memory_space=pltpu.SMEM)
F32 = jnp.float32
BF16 = jnp.bfloat16


def dot(left, right):
    return jnp.dot(left, right, preferred_element_type=F32)


def dot_t(left, right):
    return lax.dot_general(left, right, (((1,), (1,)), ((), ())), preferred_element_type=F32)


def t_dot(left, right):
    return lax.dot_general(left, right, (((0,), (0,)), ((), ())), preferred_element_type=F32)


def row_mean(array):
    return jnp.sum(array, axis=1, keepdims=True) * (1.0 / array.shape[1])


def rows_of(ref, block, size):
    return ref[pl.ds(pl.multiple_of(block * size, size), size), :]


def edge_kernel(
    parts,
    ways,
    arrivals,
    src_ref,
    dst_ref,
    count_ref,
    slot_ref,
    node_ref,
    *refs,
):
    arrived = refs[:arrivals]
    edge_ref, cot_ref, win_ref, wout_ref = refs[arrivals : arrivals + 4]
    (
        agg_out,
        gpre_ref,
        own_sums,
        back_sums,
        recv_sums,
        away_a,
        kept_a,
        away_b,
        kept_b,
    ) = refs[arrivals + 4 : arrivals + 13]
    ext_ref, send_ref, act_ref, proj_ref, pre_recv, cot_mid, agg_ref, sums_ref = refs[
        arrivals + 13 :
    ]
    tiles, block = slot_ref.shape
    latent = node_ref.shape[1]
    owned = node_ref.shape[0] // block
    part = lax.axis_index("dom")
    bit = lax.axis_index("dp") % 2
    live_count = count_ref[0]

    ext_ref[: owned * block, :] = node_ref[...]
    for which in range(arrivals):
        at = (owned + which) * block
        ext_ref[at : at + block, :] = arrived[which][...]
    pre_recv[...] = dot(node_ref[...], win_ref[2 * latent :, :])
    cot = cot_ref[...].astype(F32)
    cot_mid[...] = cot - row_mean(cot)
    agg_ref[...] = jnp.zeros_like(agg_ref)
    sums_ref[...] = jnp.zeros_like(sums_ref)
    recv_sums[...] = jnp.zeros_like(recv_sums)

    def hot(tile):
        source = src_ref[tile]
        which = source - owned
        reach = jnp.where(which >= 2, 2, 1)
        partner = part - jnp.where(which % 2 == 1, -reach, reach)
        exists = (source < owned) | ((partner >= 0) & (partner < parts))
        place = jnp.minimum(source, owned + arrivals - 1)
        there = jnp.where(exists, 1.0, 0.0)
        index = lax.broadcasted_iota(jnp.int32, (block, block), 0)
        return jnp.where(index == slot_ref[tile : tile + 1, :], there, 0.0).astype(BF16), place

    group = 4 if tiles % 4 == 0 else 1
    span = group * block
    for first in range(0, tiles, group):
        rows = slice(first * block, first * block + span)
        members = range(first, first + group)
        for tile in members:
            chosen, place = hot(tile)
            at = tile * block
            send_ref[at : at + block, :] = t_dot(chosen, rows_of(ext_ref, place, block)).astype(
                BF16
            )
        edges = edge_ref[rows, :]
        received = jnp.concatenate([rows_of(pre_recv, dst_ref[t], block) for t in members], axis=0)
        preact = (
            dot(edges, win_ref[:latent, :])
            + dot(send_ref[rows, :], win_ref[latent : 2 * latent, :])
            + received
        )
        gate = 0.5 * jnp.tanh(0.5 * preact) + 0.5
        activated = preact * gate
        slope = gate + activated * (1.0 - gate)
        activated = activated.astype(BF16)
        act_ref[rows, :] = activated
        projected = dot(activated, wout_ref[...])
        centered = projected - row_mean(projected)
        inv_scale = lax.rsqrt(row_mean(centered * centered) + EPSILON)
        message = centered * inv_scale
        updated = edges.astype(F32) + message
        upstream = []
        for number, tile in enumerate(members):
            live = jnp.where(tile < live_count, 1.0, 0.0)
            target = pl.ds(pl.multiple_of(dst_ref[tile] * block, block), block)
            agg_ref[target, :] += updated[number * block : (number + 1) * block] * live
            upstream.append(cot_mid[target, :] * live)
        upstream = jnp.concatenate(upstream, axis=0)
        grad_project = inv_scale * (upstream - message * row_mean(upstream * message))
        grad_project = grad_project.astype(BF16)
        proj_ref[rows, :] = grad_project
        grad_pre = (dot_t(grad_project, wout_ref[...]) * slope).astype(BF16)
        gpre_ref[rows, :] = grad_pre
        for number, tile in enumerate(members):
            chosen, place = hot(tile)
            mine = grad_pre[number * block : (number + 1) * block]
            target = pl.ds(pl.multiple_of(dst_ref[tile] * block, block), block)
            recv_sums[target, :] += mine.astype(F32)
            spot = pl.ds(pl.multiple_of(place * block, block), block)
            sums_ref[spot, :] += dot(chosen, mine)

    agg_out[...] = agg_ref[...].astype(BF16)
    own_sums[...] = sums_ref[: owned * block, :]
    for which in range(arrivals):
        at = (owned + which) * block
        back_sums[which] = sums_ref[at : at + block, :].astype(BF16)

    unit = latent // ways

    def put(owner, spot, value):
        away, kept = (away_a, kept_a) if spot < 2 else (away_b, kept_b)
        where = slice((spot % 2) * unit, (spot % 2 + 1) * unit)

        @pl.when(bit == owner % 2)
        def _():
            kept[owner // 2, where, :] = value

        @pl.when(bit != owner % 2)
        def _():
            away[owner // 2, where, :] = value.astype(BF16)

    step = 256
    for start in range(0, latent, step):
        value = t_dot(act_ref[:, start : start + step], proj_ref[...])
        for at in range(0, step, unit):
            put((start + at) // unit, 0, value[at : at + unit])
    sections = (
        (edge_ref, gpre_ref),
        (ext_ref, sums_ref),
        (node_ref, recv_sums),
    )
    for number, (left, right) in enumerate(sections):
        for start in range(0, latent, step):
            value = t_dot(left[:, start : start + step], right[...].astype(BF16))
            for at in range(0, step, unit):
                spot = (number * latent + start + at) // unit
                put(spot // 3, 1 + spot % 3, value[at : at + unit])


def edge_grad_kernel(block, dst_ref, count_ref, gpre_ref, cot_ref, win_ref, out_ref):
    latent = cot_ref.shape[1]
    tiles = gpre_ref.shape[0] // block
    group = 4 if tiles % 4 == 0 else 1
    for first in range(0, tiles, group):
        rows = slice(first * block, (first + group) * block)
        upstream = jnp.concatenate(
            [
                rows_of(cot_ref, dst_ref[t], block).astype(F32)
                * jnp.where(t < count_ref[0], 1.0, 0.0)
                for t in range(first, first + group)
            ],
            axis=0,
        )
        out_ref[rows, :] = (dot_t(gpre_ref[rows, :], win_ref[:latent, :]) + upstream).astype(BF16)


def node_grad_kernel(arrivals, chosen_ref, own_ref, recv_ref, win_ref, *refs):
    returned = refs[:arrivals]
    out_ref, total_ref = refs[arrivals:]
    latent = own_ref.shape[1]
    block = returned[0].shape[0]
    total_ref[...] = own_ref[...]
    for which in range(arrivals):
        spot = pl.ds(pl.multiple_of(chosen_ref[which] * block, block), block)
        total_ref[spot, :] += returned[which][...].astype(F32)

    def wide_dot(value, weight):
        high = value.astype(BF16)
        low = (value - high.astype(F32)).astype(BF16)
        return dot_t(high, weight) + dot_t(low, weight)

    out_ref[...] = (
        wide_dot(total_ref[...], win_ref[latent : 2 * latent, :])
        + wide_dot(recv_ref[...], win_ref[2 * latent :, :])
    ).astype(BF16)


def swap(array, axis, partner):
    devices = lax.axis_size(axis)
    return lax.ppermute(array, axis, [(i, partner(i)) for i in range(devices)])


def from_behind(array, axis, by):
    devices = lax.axis_size(axis)
    pairs = [(i, i + by) for i in range(devices) if 0 <= i + by < devices]
    return lax.ppermute(array, axis, pairs)


def partners_of_four(which):
    return ((1, 0, 3, 2), (0, 2, 1, 3), (2, 3, 0, 1))[which]


def exchange_of_four(first, second, third):
    return [
        swap(array, "dom", lambda i, which=which: partners_of_four(which)[i])
        for which, array in enumerate((first, second, third))
    ]


def sum_over_dp(away, kept):
    devices = lax.axis_size("dp")
    index = lax.axis_index("dp")
    total = kept + swap(away, "dp", lambda i: i ^ 1).astype(F32)
    bit = 2
    while bit < devices:
        mine = (index // bit) % 2
        split = total.reshape((-1, 2) + total.shape[1:])
        away = lax.dynamic_index_in_dim(split, 1 - mine, 1, keepdims=False).astype(BF16)
        kept = lax.dynamic_index_in_dim(split, mine, 1, keepdims=False)
        total = kept + swap(away, "dp", lambda i, bit=bit: i ^ bit).astype(F32)
        bit *= 2
    return total[0]


def sum_over_dom(rows):
    devices = lax.axis_size("dom")
    if devices != 4:
        piece = lax.psum_scatter(rows, "dom", scatter_dimension=0, tiled=True)
        return lax.all_gather(piece, "dom", axis=0, tiled=True)
    index = lax.axis_index("dom")
    inner = (index == 1) | (index == 2)
    low, high = jnp.split(rows, 2, axis=0)
    away = jnp.where(inner, high, low).astype(BF16)
    kept = jnp.where(inner, low, high)
    kept = (kept + swap(away, "dom", lambda i: i ^ 1).astype(F32)).astype(BF16)
    kept = (kept.astype(F32) + swap(kept, "dom", lambda i: 3 - i).astype(F32)).astype(BF16)
    other = swap(kept, "dom", lambda i: i ^ 1)
    low = jnp.where(inner, kept, other)
    high = jnp.where(inner, other, kept)
    return jnp.concatenate([low, high], axis=0).astype(F32)


def body(
    node_latents,
    edge_latents,
    agg_cotangent,
    weight_in,
    weight_out,
    boundary,
    tile_src,
    tile_dst,
    edge_slot,
    tile_count,
):
    tiles, block = edge_slot.shape
    edges, latent = edge_latents.shape[1:]
    nodes = node_latents.shape[1]
    parts = lax.axis_size("dom")
    ways = lax.axis_size("dp")
    part = lax.axis_index("dom")
    four = parts == 4
    node_rows = node_latents[0]
    chosen = boundary[0]

    def pick(which):
        return lax.dynamic_slice(node_rows, (chosen[which] * block, 0), (block, latent))

    if four:
        even = part % 2 == 0
        low = part < 2
        index = [
            jnp.where(even, chosen[0], chosen[1]),
            jnp.where(even, chosen[1], chosen[0]),
            jnp.where(low, chosen[2], chosen[3]),
        ]
        sent = [lax.dynamic_slice(node_rows, (i * block, 0), (block, latent)) for i in index]
        one, two, three = exchange_of_four(*sent)
        came = [jnp.where(even, two, one), jnp.where(even, one, two), three]
    else:
        came = [from_behind(pick(which), "dom", OFFSET_LIST[which]) for which in range(4)]
    arrivals = len(came)
    unit = latent // ways
    half = ways // 2

    agg, grad_pre, own_sums, back_sums, recv_sums, away_a, kept_a, away_b, kept_b = pl.pallas_call(
        functools.partial(edge_kernel, parts, ways, arrivals),
        out_shape=(
            jax.ShapeDtypeStruct((nodes, latent), BF16),
            jax.ShapeDtypeStruct((edges, latent), BF16),
            jax.ShapeDtypeStruct((nodes, latent), F32),
            jax.ShapeDtypeStruct((arrivals, block, latent), BF16),
            jax.ShapeDtypeStruct((nodes, latent), F32),
            jax.ShapeDtypeStruct((half, 2 * unit, latent), BF16),
            jax.ShapeDtypeStruct((half, 2 * unit, latent), F32),
            jax.ShapeDtypeStruct((half, 2 * unit, latent), BF16),
            jax.ShapeDtypeStruct((half, 2 * unit, latent), F32),
        ),
        in_specs=[SMEM] * 3 + [VMEM] * (6 + arrivals),
        out_specs=(VMEM,) * 9,
        scratch_shapes=[
            pltpu.VMEM((nodes + arrivals * block, latent), BF16),
            pltpu.VMEM((edges, latent), BF16),
            pltpu.VMEM((edges, latent), BF16),
            pltpu.VMEM((edges, latent), BF16),
            pltpu.VMEM((nodes, latent), F32),
            pltpu.VMEM((nodes, latent), F32),
            pltpu.VMEM((nodes, latent), F32),
            pltpu.VMEM((nodes + arrivals * block, latent), F32),
        ],
        compiler_params=pltpu.CompilerParams(vmem_limit_bytes=32 * 1024 * 1024),
        cost_estimate=pl.CostEstimate(
            flops=14 * edges * latent * latent,
            bytes_accessed=12_000_000,
            transcendentals=edges * latent,
        ),
        name="edge_block",
    )(
        tile_src,
        tile_dst,
        tile_count,
        edge_slot,
        node_rows,
        *came,
        edge_latents[0],
        agg_cotangent[0],
        weight_in,
        weight_out,
    )
    if four:
        first = jnp.where(even, back_sums[1], back_sums[0])
        second = jnp.where(even, back_sums[0], back_sums[1])
        returned = exchange_of_four(first, second, back_sums[2])
        spots = jnp.stack(index)
    else:
        returned = [
            from_behind(back_sums[which], "dom", -OFFSET_LIST[which]) for which in range(4)
        ]
        spots = chosen
    edge_grad = pl.pallas_call(
        functools.partial(edge_grad_kernel, block),
        out_shape=jax.ShapeDtypeStruct((edges, latent), BF16),
        in_specs=[SMEM] * 2 + [VMEM] * 3,
        out_specs=VMEM,
        compiler_params=pltpu.CompilerParams(vmem_limit_bytes=16 * 1024 * 1024),
        cost_estimate=pl.CostEstimate(
            flops=2 * edges * latent * latent, bytes_accessed=3_000_000, transcendentals=0
        ),
        name="edge_grads",
    )(tile_dst, tile_count, grad_pre, agg_cotangent[0], weight_in)
    node_out = pl.pallas_call(
        functools.partial(node_grad_kernel, arrivals),
        out_shape=jax.ShapeDtypeStruct((nodes, latent), BF16),
        in_specs=[SMEM] + [VMEM] * (3 + arrivals),
        out_specs=VMEM,
        scratch_shapes=[pltpu.VMEM((nodes, latent), F32)],
        compiler_params=pltpu.CompilerParams(vmem_limit_bytes=16 * 1024 * 1024),
        cost_estimate=pl.CostEstimate(
            flops=8 * nodes * latent * latent, bytes_accessed=2_000_000, transcendentals=0
        ),
        name="node_grads",
    )(spots, own_sums, recv_sums, weight_in, *returned)
    sum_a = sum_over_dom(sum_over_dp(away_a, kept_a))
    sum_b = sum_over_dom(sum_over_dp(away_b, kept_b))
    w_in_grad = jnp.concatenate([sum_a[unit:], sum_b], axis=0)
    return (agg[None], edge_grad[None], node_out[None], w_in_grad, sum_a[:unit])


def solution(mesh):
    in_specs = (
        P(("group", "dp"), "dom", None),
        P(("group", "dp"), "dom", None),
        P(("group", "dp"), "dom", None),
        P(),
        P(),
        P(("group", "dom"), None),
        P(("group", "dom")),
        P(("group", "dom")),
        P(("group", "dom"), None),
        P(("group", "dom")),
    )
    out_specs = (
        P(("group", "dp"), "dom", None),
        P(("group", "dp"), "dom", None),
        P(("group", "dp"), "dom", None),
        P(("group", "dp"), None),
        P(("group", "dp"), None),
    )
    return jax.shard_map(body, mesh=mesh, in_specs=in_specs, out_specs=out_specs, check_vma=False)
```

```python
import functools

import jax
import jax.numpy as jnp
from jax import lax
from jax.experimental import pallas as pl
from jax.experimental.pallas import tpu as pltpu
from jax.sharding import PartitionSpec as P

OFFSET_LIST = (1, -1, 2, -2)
EPSILON = 1e-05
VMEM = pl.BlockSpec(memory_space=pltpu.VMEM)
HBM = pl.BlockSpec(memory_space=pltpu.HBM)
SMEM = pl.BlockSpec(memory_space=pltpu.SMEM)
ANY = pl.BlockSpec(memory_space=pl.ANY)
F32 = jnp.float32
BF16 = jnp.bfloat16


def dot(left, right):
    return jnp.dot(left, right, preferred_element_type=F32)


def dot_t(left, right):
    return lax.dot_general(left, right, (((1,), (1,)), ((), ())), preferred_element_type=F32)


def t_dot(left, right):
    return lax.dot_general(left, right, (((0,), (0,)), ((), ())), preferred_element_type=F32)


def row_mean(array):
    return jnp.sum(array, axis=1, keepdims=True) * (1.0 / array.shape[1])


def rows_of(ref, block, size):
    return ref[pl.ds(pl.multiple_of(block * size, size), size), :]


def load_small(source, target, sem):
    copy = pltpu.make_async_copy(source, target, sem)
    copy.start()
    return copy


def boundary_places(boundary_ref, part, four):
    taken = [boundary_ref[0, which] for which in range(4)]
    if not four:
        return taken
    even = part % 2 == 0
    return [
        jnp.where(even, taken[0], taken[1]),
        jnp.where(even, taken[1], taken[0]),
        jnp.where(part < 2, taken[2], taken[3]),
    ]


def arrival_places(part, four, arrivals):
    if not four:
        return list(range(arrivals))
    even = part % 2 == 0
    return [jnp.where(even, 1, 0), jnp.where(even, 0, 1), 2]


def pick_kernel(four, block, boundary_hbm, node_hbm, *refs):
    count = 3 if four else 4
    outs = refs[:count]
    boundary_ref, small_sem, sems = refs[count:]
    load_small(boundary_hbm, boundary_ref, small_sem).wait()
    copies = []
    for which, place in enumerate(boundary_places(boundary_ref, lax.axis_index("dom"), four)):
        spot = pl.ds(pl.multiple_of(place * block, block), block)
        copies.append(pltpu.make_async_copy(node_hbm.at[spot, :], outs[which], sems.at[which]))
        copies[-1].start()
    for copy in copies:
        copy.wait()


def prep_kernel(
    parts,
    arrivals,
    src_hbm,
    dst_hbm,
    slot_hbm,
    node_hbm,
    edge_hbm,
    cot_hbm,
    win_hbm,
    wout_hbm,
    node_ref,
    edge_ref,
    cot_ref,
    win_ref,
    wout_ref,
    pre_ref,
    mid_ref,
    hot_ref,
    hot_turned,
    src_ref,
    dst_ref,
    slot_ref,
    recv_ref,
    sems,
):
    tiles, block = slot_ref.shape
    nodes, latent = node_ref.shape
    owned = nodes // block
    extent = hot_turned.shape[0]
    pairs = (
        (src_hbm, src_ref),
        (dst_hbm, dst_ref),
        (slot_hbm, slot_ref),
        (node_hbm, node_ref),
        (win_hbm.at[2 * latent :, :], win_ref.at[2 * latent :, :]),
        (win_hbm.at[:latent, :], win_ref.at[:latent, :]),
        (edge_hbm, edge_ref),
        (cot_hbm, cot_ref),
        (win_hbm.at[latent : 2 * latent, :], win_ref.at[latent : 2 * latent, :]),
        (wout_hbm, wout_ref),
    )
    copies = [load_small(*pair, sems.at[number]) for number, pair in enumerate(pairs)]
    part = lax.axis_index("dom")
    for copy in copies[:3]:
        copy.wait()
    index = lax.broadcasted_iota(jnp.int32, (extent, 2 * block), 0)
    first = lax.broadcasted_iota(jnp.int32, (1, 2 * block), 1) < block
    for tile in range(0, tiles, 2):
        wanted = []
        for member in (tile, tile + 1):
            source = src_ref[member]
            which = source - owned
            reach = jnp.where(which >= 2, 2, 1)
            partner = part - jnp.where(which % 2 == 1, -reach, reach)
            exists = (source < owned) | ((partner >= 0) & (partner < parts))
            place = jnp.minimum(source, owned + arrivals - 1)
            wanted.append(jnp.where(exists, place * block, -2 * extent))
        slots = jnp.concatenate(
            [slot_ref[tile : tile + 1, :], slot_ref[tile + 1 : tile + 2, :]], axis=1
        )
        row = slots + jnp.where(first, wanted[0], wanted[1])
        hot = jnp.where(index == row, 1.0, 0.0)
        at = slice(tile * block, (tile + 2) * block)
        hot_turned[:, at] = hot.astype(BF16)
        hot_ref[at, :] = hot.T.astype(BF16)
    copies[3].wait()
    copies[4].wait()
    recv_ref[...] = dot(node_ref[...], win_ref[2 * latent :, :])
    copies[5].wait()
    copies[6].wait()
    group = 4 if tiles % 4 == 0 else 2
    for tile in range(0, tiles, group):
        rows = slice(tile * block, (tile + group) * block)
        received = jnp.concatenate(
            [rows_of(recv_ref, dst_ref[t], block) for t in range(tile, tile + group)], axis=0
        )
        pre_ref[rows, :] = dot(edge_ref[rows, :], win_ref[:latent, :]) + received
    copies[7].wait()
    cot = cot_ref[...].astype(F32)
    mid_ref[...] = cot - row_mean(cot)
    copies[8].wait()
    copies[9].wait()


def edge_kernel(
    ways,
    arrivals,
    four,
    block,
    dst_hbm,
    count_ref,
    *refs,
):
    arrived = refs[:arrivals]
    (
        node_ref,
        edge_ref,
        win_ref,
        wout_ref,
        pre_ref,
        mid_ref,
        hot_ref,
        hot_turned,
        agg_hbm,
        gpre_ref,
        own_sums,
        recv_sums,
    ) = refs[arrivals : arrivals + 12]
    back_sums = refs[arrivals + 12 : 2 * arrivals + 12]
    away_a, kept_a, away_b, kept_b = refs[2 * arrivals + 12 : 2 * arrivals + 16]
    (
        dst_ref,
        ext_ref,
        act_ref,
        proj_ref,
        agg_ref,
        agg_bf16,
        sums_ref,
        sems,
    ) = refs[2 * arrivals + 16 :]
    nodes, latent = node_ref.shape
    edges = edge_ref.shape[0]
    tiles = edges // block
    owned = nodes // block
    part = lax.axis_index("dom")
    bit = lax.axis_index("dp") % 2
    dst_copy = load_small(dst_hbm, dst_ref, sems.at[0])
    places = arrival_places(part, four, arrivals)

    ext_ref[:nodes, :] = node_ref[...]
    for which in range(arrivals):
        at = pl.multiple_of((owned + places[which]) * block, block)
        ext_ref[pl.ds(at, block), :] = arrived[which][...]
    filled = nodes + arrivals * block
    if filled < ext_ref.shape[0]:
        ext_ref[filled:, :] = jnp.zeros((ext_ref.shape[0] - filled, latent), BF16)
    agg_ref[...] = jnp.zeros_like(agg_ref)
    recv_sums[...] = jnp.zeros_like(recv_sums)

    group = 4 if tiles % 4 == 0 else 1
    span = group * block
    for first in range(0, tiles, group):
        rows = slice(first * block, first * block + span)
        members = range(first, first + group)
        edge_rows = edge_ref[rows, :]
        senders = dot(hot_ref[rows, :], ext_ref[...]).astype(BF16)
        preact = pre_ref[rows, :] + dot(senders, win_ref[latent : 2 * latent, :])
        gate = 0.5 * jnp.tanh(0.5 * preact) + 0.5
        activated = preact * gate
        slope = gate + activated * (1.0 - gate)
        activated = activated.astype(BF16)
        act_ref[rows, :] = activated
        projected = dot(activated, wout_ref[...])
        centered = projected - row_mean(projected)
        inv_scale = lax.rsqrt(row_mean(centered * centered) + EPSILON)
        message = centered * inv_scale
        updated = edge_rows.astype(F32) + message
        if first == 0:
            dst_copy.wait()
        upstream = []
        for number, tile in enumerate(members):
            live = jnp.where(tile < count_ref[0], 1.0, 0.0)
            target = pl.ds(pl.multiple_of(dst_ref[tile] * block, block), block)
            agg_ref[target, :] += updated[number * block : (number + 1) * block] * live
            upstream.append(mid_ref[target, :] * live)
        upstream = jnp.concatenate(upstream, axis=0)
        grad_project = inv_scale * (upstream - message * row_mean(upstream * message))
        grad_project = grad_project.astype(BF16)
        proj_ref[rows, :] = grad_project
        grad_pre = (dot_t(grad_project, wout_ref[...]) * slope).astype(BF16)
        gpre_ref[rows, :] = grad_pre
        for number, tile in enumerate(members):
            mine = grad_pre[number * block : (number + 1) * block]
            target = pl.ds(pl.multiple_of(dst_ref[tile] * block, block), block)
            recv_sums[target, :] += mine.astype(F32)

    agg_bf16[...] = agg_ref[...].astype(BF16)
    agg_copy = load_small(agg_bf16, agg_hbm, sems.at[1])
    sums_ref[...] = dot(hot_turned[...], gpre_ref[...])
    own_sums[...] = sums_ref[:nodes, :]
    for which in range(arrivals):
        at = pl.multiple_of((owned + places[which]) * block, block)
        back_sums[which][...] = sums_ref[pl.ds(at, block), :].astype(BF16)

    unit = latent // ways

    def put(owner, spot, value):
        away, kept = (away_a, kept_a) if spot < 2 else (away_b, kept_b)
        where = slice((spot % 2) * unit, (spot % 2 + 1) * unit)

        @pl.when(bit == owner % 2)
        def _():
            kept[owner // 2, where, :] = value

        @pl.when(bit != owner % 2)
        def _():
            away[owner // 2, where, :] = value.astype(BF16)

    step = 256
    for start in range(0, latent, step):
        value = t_dot(act_ref[:, start : start + step], proj_ref[...])
        for at in range(0, step, unit):
            put((start + at) // unit, 0, value[at : at + unit])
    sections = (
        (edge_ref, gpre_ref),
        (ext_ref, sums_ref),
        (node_ref, recv_sums),
    )
    for number, (left, right) in enumerate(sections):
        for start in range(0, latent, step):
            value = t_dot(left[:, start : start + step], right[...].astype(BF16))
            for at in range(0, step, unit):
                spot = (number * latent + start + at) // unit
                put(spot // 3, 1 + spot % 3, value[at : at + unit])
    agg_copy.wait()


def edge_grad_kernel(
    block, dst_hbm, count_ref, after, gpre_ref, cot_ref, win_ref, out_ref, dst_ref, sem
):
    latent = cot_ref.shape[1]
    tiles = gpre_ref.shape[0] // block
    group = 4 if tiles % 4 == 0 else 1
    load_small(dst_hbm, dst_ref, sem).wait()
    for first in range(0, tiles, group):
        rows = slice(first * block, (first + group) * block)
        upstream = jnp.concatenate(
            [
                rows_of(cot_ref, dst_ref[t], block).astype(F32)
                * jnp.where(t < count_ref[0], 1.0, 0.0)
                for t in range(first, first + group)
            ],
            axis=0,
        )
        out_ref[rows, :] = (dot_t(gpre_ref[rows, :], win_ref[:latent, :]) + upstream).astype(BF16)


def node_grad_kernel(arrivals, four, boundary_hbm, after, own_ref, recv_ref, win_ref, *refs):
    returned = refs[:arrivals]
    out_ref, total_ref, boundary_ref, sem = refs[arrivals:]
    latent = own_ref.shape[1]
    block = returned[0].shape[0]
    copy = load_small(boundary_hbm, boundary_ref, sem)
    total_ref[...] = own_ref[...]
    copy.wait()
    for which, place in enumerate(boundary_places(boundary_ref, lax.axis_index("dom"), four)):
        spot = pl.ds(pl.multiple_of(place * block, block), block)
        total_ref[spot, :] += returned[which][...].astype(F32)

    def wide_dot(value, weight):
        high = value.astype(BF16)
        low = (value - high.astype(F32)).astype(BF16)
        return dot_t(high, weight) + dot_t(low, weight)

    out_ref[...] = (
        wide_dot(total_ref[...], win_ref[latent : 2 * latent, :])
        + wide_dot(recv_ref[...], win_ref[2 * latent :, :])
    ).astype(BF16)


def last_kernel(own_a, other_a, own_b, other_b, in_ref, out_ref):
    unit = out_ref.shape[0]
    part = lax.axis_index("dom")
    inner = (part == 1) | (part == 2)

    def write(low_a, high_a, low_b, high_b):
        out_ref[...] = low_a[...].astype(F32)
        in_ref[:unit, :] = high_a[...].astype(F32)
        in_ref[unit : 2 * unit, :] = low_b[...].astype(F32)
        in_ref[2 * unit :, :] = high_b[...].astype(F32)

    @pl.when(inner)
    def _():
        write(own_a, other_a, own_b, other_b)

    @pl.when(jnp.logical_not(inner))
    def _():
        write(other_a, own_a, other_b, own_b)


def swap(array, axis, partner):
    devices = lax.axis_size(axis)
    return lax.ppermute(array, axis, [(i, partner(i)) for i in range(devices)])


def from_behind(array, axis, by):
    devices = lax.axis_size(axis)
    pairs = [(i, i + by) for i in range(devices) if 0 <= i + by < devices]
    return lax.ppermute(array, axis, pairs)


def partners_of_four(which):
    return ((1, 0, 3, 2), (0, 2, 1, 3), (2, 3, 0, 1))[which]


def exchange_of_four(first, second, third):
    return [
        swap(array, "dom", lambda i, which=which: partners_of_four(which)[i])
        for which, array in enumerate((first, second, third))
    ]


def sum_over_dp(away, kept):
    devices = lax.axis_size("dp")
    index = lax.axis_index("dp")
    bit = 1
    while True:
        came = swap(away, "dp", lambda i, bit=bit: i ^ bit)
        bit *= 2
        if bit >= devices:
            return kept[0] + came[0].astype(F32), away
        mine = (index // bit) % 2

        def half(array, side):
            split = array.reshape((-1, 2) + array.shape[1:])
            return lax.dynamic_index_in_dim(split, side, 1, keepdims=False)

        away = (half(kept, 1 - mine) + half(came, 1 - mine).astype(F32)).astype(BF16)
        kept = half(kept, mine) + half(came, mine).astype(F32)


def sum_over_four(rows):
    index = lax.axis_index("dom")
    inner = (index == 1) | (index == 2)
    low, high = jnp.split(rows, 2, axis=0)
    away = jnp.where(inner, high, low).astype(BF16)
    kept = jnp.where(inner, low, high)
    kept = (kept + swap(away, "dom", lambda i: i ^ 1).astype(F32)).astype(BF16)
    kept = (kept.astype(F32) + swap(kept, "dom", lambda i: 3 - i).astype(F32)).astype(BF16)
    return kept, swap(kept, "dom", lambda i: i ^ 1)


def sum_over_dom(rows):
    piece = lax.psum_scatter(rows, "dom", scatter_dimension=0, tiled=True)
    return lax.all_gather(piece, "dom", axis=0, tiled=True)


def in_vmem(array):
    return pltpu.with_memory_space_constraint(array, pltpu.VMEM)


def in_hbm(array):
    return pltpu.with_memory_space_constraint(array, pltpu.HBM)


def body(
    node_latents,
    edge_latents,
    agg_cotangent,
    weight_in,
    weight_out,
    boundary,
    tile_src,
    tile_dst,
    edge_slot,
    tile_count,
):
    tiles, block = edge_slot.shape
    edges, latent = edge_latents.shape[1:]
    nodes = node_latents.shape[1]
    parts = lax.axis_size("dom")
    ways = lax.axis_size("dp")
    four = parts == 4
    arrivals = 3 if four else 4
    boundary = in_hbm(boundary)
    tile_dst = in_hbm(tile_dst)
    node_rows = in_hbm(node_latents[0])
    block_shape = pltpu.VMEM((block, latent), BF16)
    small = pltpu.CompilerParams(vmem_limit_bytes=8 * 1024 * 1024)

    sent = pl.pallas_call(
        functools.partial(pick_kernel, four, block),
        out_shape=(block_shape,) * arrivals,
        in_specs=[HBM] * 2,
        out_specs=(VMEM,) * arrivals,
        scratch_shapes=[
            pltpu.SMEM(boundary.shape, jnp.int32),
            pltpu.SemaphoreType.DMA,
            pltpu.SemaphoreType.DMA((arrivals,)),
        ],
        compiler_params=small,
        cost_estimate=pl.CostEstimate(flops=0, bytes_accessed=400_000, transcendentals=0),
        name="pick_blocks",
    )(boundary, node_rows)
    if four:
        came = exchange_of_four(*sent)
    else:
        came = [from_behind(sent[which], "dom", OFFSET_LIST[which]) for which in range(4)]
    unit = latent // ways
    half = ways // 2
    extent = -(-(nodes + arrivals * block) // 128) * 128

    node_v, edge_v, cot_v, win_v, wout_v, pre, mid, hot, turned = pl.pallas_call(
        functools.partial(prep_kernel, parts, arrivals),
        out_shape=(
            pltpu.VMEM((nodes, latent), BF16),
            pltpu.VMEM((edges, latent), BF16),
            pltpu.VMEM((nodes, latent), BF16),
            pltpu.VMEM(weight_in.shape, BF16),
            pltpu.VMEM(weight_out.shape, BF16),
            pltpu.VMEM((edges, latent), F32),
            pltpu.VMEM((nodes, latent), F32),
            pltpu.VMEM((edges, extent), BF16),
            pltpu.VMEM((extent, edges), BF16),
        ),
        in_specs=[HBM] * 8,
        out_specs=(VMEM,) * 9,
        scratch_shapes=[
            pltpu.SMEM((tiles,), jnp.int32),
            pltpu.SMEM((tiles,), jnp.int32),
            pltpu.VMEM((tiles, block), jnp.int32),
            pltpu.VMEM((nodes, latent), F32),
            pltpu.SemaphoreType.DMA((10,)),
        ],
        compiler_params=small,
        cost_estimate=pl.CostEstimate(
            flops=2 * edges * latent * latent, bytes_accessed=8_000_000, transcendentals=0
        ),
        name="prepare",
    )(
        in_hbm(tile_src),
        tile_dst,
        in_hbm(edge_slot),
        node_rows,
        in_hbm(edge_latents[0]),
        in_hbm(agg_cotangent[0]),
        in_hbm(weight_in),
        in_hbm(weight_out),
    )
    outs = pl.pallas_call(
        functools.partial(edge_kernel, ways, arrivals, four, block),
        out_shape=(
            jax.ShapeDtypeStruct((nodes, latent), BF16),
            pltpu.VMEM((edges, latent), BF16),
            pltpu.VMEM((nodes, latent), F32),
            pltpu.VMEM((nodes, latent), F32),
            *[block_shape] * arrivals,
            pltpu.VMEM((half, 2 * unit, latent), BF16),
            pltpu.VMEM((half, 2 * unit, latent), F32),
            pltpu.VMEM((half, 2 * unit, latent), BF16),
            pltpu.VMEM((half, 2 * unit, latent), F32),
        ),
        in_specs=[HBM, SMEM] + [VMEM] * (8 + arrivals),
        out_specs=(HBM,) + (VMEM,) * (7 + arrivals),
        scratch_shapes=[
            pltpu.SMEM((tiles,), jnp.int32),
            pltpu.VMEM((extent, latent), BF16),
            pltpu.VMEM((edges, latent), BF16),
            pltpu.VMEM((edges, latent), BF16),
            pltpu.VMEM((nodes, latent), F32),
            pltpu.VMEM((nodes, latent), BF16),
            pltpu.VMEM((extent, latent), F32),
            pltpu.SemaphoreType.DMA((2,)),
        ],
        compiler_params=pltpu.CompilerParams(vmem_limit_bytes=16 * 1024 * 1024),
        cost_estimate=pl.CostEstimate(
            flops=14 * edges * latent * latent,
            bytes_accessed=12_000_000,
            transcendentals=edges * latent,
        ),
        name="edge_block",
    )(
        tile_dst,
        tile_count,
        *[
            in_vmem(array)
            for array in (*came, node_v, edge_v, win_v, wout_v, pre, mid, hot, turned)
        ],
    )
    agg, grad_pre, own_sums, recv_sums = outs[:4]
    back_sums = outs[4 : 4 + arrivals]
    away_a, kept_a, away_b, kept_b = outs[4 + arrivals :]
    rows_a, sent_a = sum_over_dp(away_a, kept_a)
    rows_b, _ = sum_over_dp(away_b, kept_b)
    if four:
        returned = exchange_of_four(*back_sums)
    else:
        returned = [
            from_behind(back_sums[which], "dom", -OFFSET_LIST[which]) for which in range(4)
        ]
    edge_grad = pl.pallas_call(
        functools.partial(edge_grad_kernel, block),
        out_shape=jax.ShapeDtypeStruct((edges, latent), BF16),
        in_specs=[HBM, SMEM, ANY] + [VMEM] * 3,
        out_specs=VMEM,
        scratch_shapes=[
            pltpu.SMEM((tiles,), jnp.int32),
            pltpu.SemaphoreType.DMA,
        ],
        compiler_params=small,
        cost_estimate=pl.CostEstimate(
            flops=2 * edges * latent * latent, bytes_accessed=3_000_000, transcendentals=0
        ),
        name="edge_grads",
    )(tile_dst, tile_count, sent_a, in_vmem(grad_pre), in_vmem(cot_v), in_vmem(win_v))
    node_out = pl.pallas_call(
        functools.partial(node_grad_kernel, arrivals, four),
        out_shape=jax.ShapeDtypeStruct((nodes, latent), BF16),
        in_specs=[HBM, ANY] + [VMEM] * (3 + arrivals),
        out_specs=VMEM,
        scratch_shapes=[
            pltpu.VMEM((nodes, latent), F32),
            pltpu.SMEM(boundary.shape, jnp.int32),
            pltpu.SemaphoreType.DMA,
        ],
        compiler_params=small,
        cost_estimate=pl.CostEstimate(
            flops=8 * nodes * latent * latent, bytes_accessed=2_000_000, transcendentals=0
        ),
        name="node_grads",
    )(
        boundary,
        sent_a,
        *[in_vmem(array) for array in (own_sums, recv_sums, win_v, *returned)],
    )
    if four:
        w_in_grad, w_out_grad = pl.pallas_call(
            last_kernel,
            out_shape=(
                jax.ShapeDtypeStruct((3 * unit, latent), F32),
                jax.ShapeDtypeStruct((unit, latent), F32),
            ),
            in_specs=[VMEM] * 4,
            out_specs=(VMEM,) * 2,
            compiler_params=small,
            cost_estimate=pl.CostEstimate(flops=0, bytes_accessed=1_500_000, transcendentals=0),
            name="widen",
        )(*sum_over_four(rows_a), *sum_over_four(rows_b))
    else:
        sum_a, sum_b = sum_over_dom(rows_a), sum_over_dom(rows_b)
        w_in_grad = jnp.concatenate([sum_a[unit:], sum_b], axis=0)
        w_out_grad = sum_a[:unit]
    return (agg[None], edge_grad[None], node_out[None], w_in_grad, w_out_grad)


def solution(mesh):
    in_specs = (
        P(("group", "dp"), "dom", None),
        P(("group", "dp"), "dom", None),
        P(("group", "dp"), "dom", None),
        P(),
        P(),
        P(("group", "dom"), None),
        P(("group", "dom")),
        P(("group", "dom")),
        P(("group", "dom"), None),
        P(("group", "dom")),
    )
    out_specs = (
        P(("group", "dp"), "dom", None),
        P(("group", "dp"), "dom", None),
        P(("group", "dp"), "dom", None),
        P(("group", "dp"), None),
        P(("group", "dp"), None),
    )
    return jax.shard_map(body, mesh=mesh, in_specs=in_specs, out_specs=out_specs, check_vma=False)
```

```python
import functools

import jax
import jax.numpy as jnp
from jax import lax
from jax.experimental import pallas as pl
from jax.experimental.pallas import tpu as pltpu
from jax.sharding import PartitionSpec as P

OFFSET_LIST = (1, -1, 2, -2)
EPSILON = 1e-05
VMEM = pl.BlockSpec(memory_space=pltpu.VMEM)
HBM = pl.BlockSpec(memory_space=pltpu.HBM)
SMEM = pl.BlockSpec(memory_space=pltpu.SMEM)
ANY = pl.BlockSpec(memory_space=pl.ANY)
F32 = jnp.float32
BF16 = jnp.bfloat16


def dot(left, right):
    return jnp.dot(left, right, preferred_element_type=F32)


def dot_t(left, right):
    return lax.dot_general(left, right, (((1,), (1,)), ((), ())), preferred_element_type=F32)


def t_dot(left, right):
    return lax.dot_general(left, right, (((0,), (0,)), ((), ())), preferred_element_type=F32)


def row_mean(array):
    return jnp.sum(array, axis=1, keepdims=True) * (1.0 / array.shape[1])


def rows_of(ref, block, size):
    return ref[pl.ds(pl.multiple_of(block * size, size), size), :]


def load_small(source, target, sem):
    copy = pltpu.make_async_copy(source, target, sem)
    copy.start()
    return copy


def boundary_places(boundary_ref, part, four):
    taken = [boundary_ref[0, which] for which in range(4)]
    if not four:
        return taken
    even = part % 2 == 0
    return [
        jnp.where(even, taken[0], taken[1]),
        jnp.where(even, taken[1], taken[0]),
        jnp.where(part < 2, taken[2], taken[3]),
    ]


def arrival_places(part, four, arrivals):
    if not four:
        return list(range(arrivals))
    even = part % 2 == 0
    return [jnp.where(even, 1, 0), jnp.where(even, 0, 1), 2]


def pick_kernel(four, block, boundary_hbm, node_hbm, *refs):
    count = 3 if four else 4
    outs = refs[:count]
    boundary_ref, small_sem, sems = refs[count:]
    load_small(boundary_hbm, boundary_ref, small_sem).wait()
    copies = []
    for which, place in enumerate(boundary_places(boundary_ref, lax.axis_index("dom"), four)):
        spot = pl.ds(pl.multiple_of(place * block, block), block)
        copies.append(pltpu.make_async_copy(node_hbm.at[spot, :], outs[which], sems.at[which]))
        copies[-1].start()
    for copy in copies:
        copy.wait()


def prep_kernel(
    parts,
    arrivals,
    src_hbm,
    dst_hbm,
    slot_hbm,
    node_hbm,
    edge_hbm,
    cot_hbm,
    win_hbm,
    wout_hbm,
    node_ref,
    edge_ref,
    cot_ref,
    win_ref,
    wout_ref,
    pre_ref,
    mid_ref,
    hot_ref,
    hot_turned,
    src_ref,
    dst_ref,
    slot_ref,
    recv_ref,
    sems,
):
    tiles, block = slot_ref.shape
    nodes, latent = node_ref.shape
    owned = nodes // block
    extent = hot_turned.shape[0]
    pairs = (
        (src_hbm, src_ref),
        (dst_hbm, dst_ref),
        (slot_hbm, slot_ref),
        (node_hbm, node_ref),
        (win_hbm.at[2 * latent :, :], win_ref.at[2 * latent :, :]),
        (win_hbm.at[:latent, :], win_ref.at[:latent, :]),
        (edge_hbm, edge_ref),
        (cot_hbm, cot_ref),
        (win_hbm.at[latent : 2 * latent, :], win_ref.at[latent : 2 * latent, :]),
        (wout_hbm, wout_ref),
    )
    copies = [load_small(*pair, sems.at[number]) for number, pair in enumerate(pairs)]
    part = lax.axis_index("dom")
    for copy in copies[:3]:
        copy.wait()
    index = lax.broadcasted_iota(jnp.int32, (extent, 2 * block), 0)
    first = lax.broadcasted_iota(jnp.int32, (1, 2 * block), 1) < block
    for tile in range(0, tiles, 2):
        wanted = []
        for member in (tile, tile + 1):
            source = src_ref[member]
            which = source - owned
            reach = jnp.where(which >= 2, 2, 1)
            partner = part - jnp.where(which % 2 == 1, -reach, reach)
            exists = (source < owned) | ((partner >= 0) & (partner < parts))
            place = jnp.minimum(source, owned + arrivals - 1)
            wanted.append(jnp.where(exists, place * block, -2 * extent))
        slots = jnp.concatenate(
            [slot_ref[tile : tile + 1, :], slot_ref[tile + 1 : tile + 2, :]], axis=1
        )
        row = slots + jnp.where(first, wanted[0], wanted[1])
        hot = jnp.where(index == row, 1.0, 0.0)
        at = slice(tile * block, (tile + 2) * block)
        hot_turned[:, at] = hot.astype(BF16)
        hot_ref[at, :] = hot.T.astype(BF16)
    copies[3].wait()
    copies[4].wait()
    recv_ref[...] = dot(node_ref[...], win_ref[2 * latent :, :])
    copies[5].wait()
    copies[6].wait()
    group = 4 if tiles % 4 == 0 else 2
    for tile in range(0, tiles, group):
        rows = slice(tile * block, (tile + group) * block)
        received = jnp.concatenate(
            [rows_of(recv_ref, dst_ref[t], block) for t in range(tile, tile + group)], axis=0
        )
        pre_ref[rows, :] = dot(edge_ref[rows, :], win_ref[:latent, :]) + received
    copies[7].wait()
    cot = cot_ref[...].astype(F32)
    mid_ref[...] = cot - row_mean(cot)
    copies[8].wait()
    copies[9].wait()


def edge_kernel(
    ways,
    arrivals,
    four,
    block,
    dst_hbm,
    count_ref,
    *refs,
):
    arrived = refs[:arrivals]
    (
        node_ref,
        edge_ref,
        win_ref,
        wout_ref,
        pre_ref,
        mid_ref,
        hot_ref,
        hot_turned,
        agg_hbm,
        gpre_ref,
        sums_ref,
        recv_sums,
        away_a,
        kept_a,
        away_b,
        kept_b,
        dst_ref,
        ext_ref,
        act_ref,
        proj_ref,
        agg_ref,
        agg_bf16,
        sems,
    ) = refs[arrivals:]
    nodes, latent = node_ref.shape
    edges = edge_ref.shape[0]
    tiles = edges // block
    owned = nodes // block
    part = lax.axis_index("dom")
    bit = lax.axis_index("dp") % 2
    dst_copy = load_small(dst_hbm, dst_ref, sems.at[0])
    places = arrival_places(part, four, arrivals)

    ext_ref[:nodes, :] = node_ref[...]
    for which in range(arrivals):
        at = pl.multiple_of((owned + places[which]) * block, block)
        ext_ref[pl.ds(at, block), :] = arrived[which][...]
    filled = nodes + arrivals * block
    if filled < ext_ref.shape[0]:
        ext_ref[filled:, :] = jnp.zeros((ext_ref.shape[0] - filled, latent), BF16)
    agg_ref[...] = jnp.zeros_like(agg_ref)
    recv_sums[...] = jnp.zeros_like(recv_sums)

    group = 4 if tiles % 4 == 0 else 1
    span = group * block
    for first in range(0, tiles, group):
        rows = slice(first * block, first * block + span)
        members = range(first, first + group)
        edge_rows = edge_ref[rows, :]
        senders = dot(hot_ref[rows, :], ext_ref[...]).astype(BF16)
        preact = pre_ref[rows, :] + dot(senders, win_ref[latent : 2 * latent, :])
        gate = 0.5 * jnp.tanh(0.5 * preact) + 0.5
        activated = preact * gate
        slope = gate + activated * (1.0 - gate)
        activated = activated.astype(BF16)
        act_ref[rows, :] = activated
        projected = dot(activated, wout_ref[...])
        centered = projected - row_mean(projected)
        inv_scale = lax.rsqrt(row_mean(centered * centered) + EPSILON)
        message = centered * inv_scale
        updated = edge_rows.astype(F32) + message
        if first == 0:
            dst_copy.wait()
        upstream = []
        for number, tile in enumerate(members):
            live = jnp.where(tile < count_ref[0], 1.0, 0.0)
            target = pl.ds(pl.multiple_of(dst_ref[tile] * block, block), block)
            agg_ref[target, :] += updated[number * block : (number + 1) * block] * live
            upstream.append(mid_ref[target, :] * live)
        upstream = jnp.concatenate(upstream, axis=0)
        grad_project = inv_scale * (upstream - message * row_mean(upstream * message))
        grad_project = grad_project.astype(BF16)
        proj_ref[rows, :] = grad_project
        grad_pre = (dot_t(grad_project, wout_ref[...]) * slope).astype(BF16)
        gpre_ref[rows, :] = grad_pre
        for number, tile in enumerate(members):
            mine = grad_pre[number * block : (number + 1) * block]
            target = pl.ds(pl.multiple_of(dst_ref[tile] * block, block), block)
            recv_sums[target, :] += mine.astype(F32)

    agg_bf16[...] = agg_ref[...].astype(BF16)
    agg_copy = load_small(agg_bf16, agg_hbm, sems.at[1])
    sums_ref[...] = dot(hot_turned[...], gpre_ref[...])

    unit = latent // ways

    def put(owner, spot, value):
        away, kept = (away_a, kept_a) if spot < 2 else (away_b, kept_b)
        where = slice((spot % 2) * unit, (spot % 2 + 1) * unit)

        @pl.when(bit == owner % 2)
        def _():
            kept[owner // 2, where, :] = value

        @pl.when(bit != owner % 2)
        def _():
            away[owner // 2, where, :] = value.astype(BF16)

    step = 256
    for start in range(0, latent, step):
        value = t_dot(act_ref[:, start : start + step], proj_ref[...])
        for at in range(0, step, unit):
            put((start + at) // unit, 0, value[at : at + unit])
    sections = (
        (edge_ref, gpre_ref),
        (ext_ref, sums_ref),
        (node_ref, recv_sums),
    )
    for number, (left, right) in enumerate(sections):
        for start in range(0, latent, step):
            value = t_dot(left[:, start : start + step], right[...].astype(BF16))
            for at in range(0, step, unit):
                spot = (number * latent + start + at) // unit
                put(spot // 3, 1 + spot % 3, value[at : at + unit])
    agg_copy.wait()


def edge_grad_kernel(
    block,
    arrivals,
    four,
    dst_hbm,
    count_ref,
    after,
    gpre_ref,
    sums_ref,
    cot_ref,
    win_ref,
    out_ref,
    *refs,
):
    back_sums = refs[:arrivals]
    dst_ref, sem = refs[arrivals:]
    copy = load_small(dst_hbm, dst_ref, sem)
    nodes, latent = cot_ref.shape
    tiles = gpre_ref.shape[0] // block
    group = 4 if tiles % 4 == 0 else 1
    places = arrival_places(lax.axis_index("dom"), four, arrivals)
    for which in range(arrivals):
        at = pl.multiple_of(nodes + places[which] * block, block)
        back_sums[which][...] = sums_ref[pl.ds(at, block), :].astype(BF16)
    copy.wait()
    for first in range(0, tiles, group):
        rows = slice(first * block, (first + group) * block)
        upstream = jnp.concatenate(
            [
                rows_of(cot_ref, dst_ref[t], block).astype(F32)
                * jnp.where(t < count_ref[0], 1.0, 0.0)
                for t in range(first, first + group)
            ],
            axis=0,
        )
        out_ref[rows, :] = (dot_t(gpre_ref[rows, :], win_ref[:latent, :]) + upstream).astype(BF16)


def halve_kernel(bit, came_ref, kept_ref, after, away_ref, left_ref):
    mine = (lax.axis_index("dp") // bit) % 2
    for slot in range(left_ref.shape[0]):
        there, here = 2 * slot + 1 - mine, 2 * slot + mine
        away_ref[slot] = (kept_ref[there] + came_ref[there].astype(F32)).astype(BF16)
        left_ref[slot] = kept_ref[here] + came_ref[here].astype(F32)


def split_kernel(came_ref, kept_ref, after, away_ref, left_ref):
    part = lax.axis_index("dom")
    inner = (part == 1) | (part == 2)
    rows = left_ref.shape[0]
    here = pl.ds(pl.multiple_of(jnp.where(inner, 0, rows), rows), rows)
    there = pl.ds(pl.multiple_of(jnp.where(inner, rows, 0), rows), rows)
    away_ref[...] = (kept_ref[0, there, :] + came_ref[0, there, :].astype(F32)).astype(BF16)
    left_ref[...] = kept_ref[0, here, :] + came_ref[0, here, :].astype(F32)


def node_grad_kernel(arrivals, four, boundary_hbm, sums_ref, recv_ref, win_ref, *refs):
    returned = refs[:arrivals]
    out_ref, total_ref, boundary_ref, sem = refs[arrivals:]
    nodes, latent = recv_ref.shape
    block = returned[0].shape[0]
    copy = load_small(boundary_hbm, boundary_ref, sem)
    total_ref[...] = sums_ref[:nodes, :]
    copy.wait()
    for which, place in enumerate(boundary_places(boundary_ref, lax.axis_index("dom"), four)):
        spot = pl.ds(pl.multiple_of(place * block, block), block)
        total_ref[spot, :] += returned[which][...].astype(F32)

    def wide_dot(value, weight):
        high = value.astype(BF16)
        low = (value - high.astype(F32)).astype(BF16)
        return dot_t(high, weight) + dot_t(low, weight)

    out_ref[...] = (
        wide_dot(total_ref[...], win_ref[latent : 2 * latent, :])
        + wide_dot(recv_ref[...], win_ref[2 * latent :, :])
    ).astype(BF16)


def last_kernel(own_a, other_a, own_b, other_b, in_ref, out_ref):
    unit = out_ref.shape[0]
    part = lax.axis_index("dom")
    inner = (part == 1) | (part == 2)

    def write(low_a, high_a, low_b, high_b):
        out_ref[...] = low_a[...].astype(F32)
        in_ref[:unit, :] = high_a[...].astype(F32)
        in_ref[unit : 2 * unit, :] = low_b[...].astype(F32)
        in_ref[2 * unit :, :] = high_b[...].astype(F32)

    @pl.when(inner)
    def _():
        write(own_a, other_a, own_b, other_b)

    @pl.when(jnp.logical_not(inner))
    def _():
        write(other_a, own_a, other_b, own_b)


def swap(array, axis, partner):
    devices = lax.axis_size(axis)
    return lax.ppermute(array, axis, [(i, partner(i)) for i in range(devices)])


def from_behind(array, axis, by):
    devices = lax.axis_size(axis)
    pairs = [(i, i + by) for i in range(devices) if 0 <= i + by < devices]
    return lax.ppermute(array, axis, pairs)


def partners_of_four(which):
    return ((1, 0, 3, 2), (0, 2, 1, 3), (2, 3, 0, 1))[which]


def exchange_of_four(first, second, third):
    return [
        swap(array, "dom", lambda i, which=which: partners_of_four(which)[i])
        for which, array in enumerate((first, second, third))
    ]


def halve(bit, came, kept, after):
    slots, rows, latent = kept.shape
    return pl.pallas_call(
        functools.partial(halve_kernel, bit),
        out_shape=(
            pltpu.VMEM((slots // 2, rows, latent), BF16),
            pltpu.VMEM((slots // 2, rows, latent), F32),
        ),
        in_specs=[VMEM] * 3,
        out_specs=(VMEM,) * 2,
        cost_estimate=pl.CostEstimate(flops=0, bytes_accessed=500_000, transcendentals=0),
        name="halve",
    )(in_vmem(came), in_vmem(kept), in_vmem(after))


def sum_over_dp(away, kept, after):
    devices = lax.axis_size("dp")
    bit = 1
    while True:
        came = swap(away, "dp", lambda i, bit=bit: i ^ bit)
        bit *= 2
        if bit >= devices:
            return came, kept, away
        away, kept = halve(bit, came, kept, after)


def sum_over_four(came, kept, after):
    rows, latent = kept.shape[1:]
    away, kept = pl.pallas_call(
        split_kernel,
        out_shape=(
            pltpu.VMEM((rows // 2, latent), BF16),
            pltpu.VMEM((rows // 2, latent), F32),
        ),
        in_specs=[VMEM] * 2 + [HBM],
        out_specs=(VMEM,) * 2,
        cost_estimate=pl.CostEstimate(flops=0, bytes_accessed=500_000, transcendentals=0),
        name="split",
    )(in_vmem(came), in_vmem(kept), in_hbm(after))
    kept = (kept + swap(away, "dom", lambda i: i ^ 1).astype(F32)).astype(BF16)
    kept = (kept.astype(F32) + swap(kept, "dom", lambda i: 3 - i).astype(F32)).astype(BF16)
    return kept, swap(kept, "dom", lambda i: i ^ 1)


def sum_over_dom(rows):
    piece = lax.psum_scatter(rows, "dom", scatter_dimension=0, tiled=True)
    return lax.all_gather(piece, "dom", axis=0, tiled=True)


def in_vmem(array):
    return pltpu.with_memory_space_constraint(array, pltpu.VMEM)


def in_hbm(array):
    return pltpu.with_memory_space_constraint(array, pltpu.HBM)


def body(
    node_latents,
    edge_latents,
    agg_cotangent,
    weight_in,
    weight_out,
    boundary,
    tile_src,
    tile_dst,
    edge_slot,
    tile_count,
):
    tiles, block = edge_slot.shape
    edges, latent = edge_latents.shape[1:]
    nodes = node_latents.shape[1]
    parts = lax.axis_size("dom")
    ways = lax.axis_size("dp")
    four = parts == 4
    arrivals = 3 if four else 4
    boundary = in_hbm(boundary)
    tile_dst = in_hbm(tile_dst)
    node_rows = in_hbm(node_latents[0])
    block_shape = pltpu.VMEM((block, latent), BF16)
    small = pltpu.CompilerParams(vmem_limit_bytes=8 * 1024 * 1024)

    sent = pl.pallas_call(
        functools.partial(pick_kernel, four, block),
        out_shape=(block_shape,) * arrivals,
        in_specs=[HBM] * 2,
        out_specs=(VMEM,) * arrivals,
        scratch_shapes=[
            pltpu.SMEM(boundary.shape, jnp.int32),
            pltpu.SemaphoreType.DMA,
            pltpu.SemaphoreType.DMA((arrivals,)),
        ],
        compiler_params=small,
        cost_estimate=pl.CostEstimate(flops=0, bytes_accessed=400_000, transcendentals=0),
        name="pick_blocks",
    )(boundary, node_rows)
    if four:
        came = exchange_of_four(*sent)
    else:
        came = [from_behind(sent[which], "dom", OFFSET_LIST[which]) for which in range(4)]
    unit = latent // ways
    half = ways // 2
    extent = -(-(nodes + arrivals * block) // 128) * 128

    node_v, edge_v, cot_v, win_v, wout_v, pre, mid, hot, turned = pl.pallas_call(
        functools.partial(prep_kernel, parts, arrivals),
        out_shape=(
            pltpu.VMEM((nodes, latent), BF16),
            pltpu.VMEM((edges, latent), BF16),
            pltpu.VMEM((nodes, latent), BF16),
            pltpu.VMEM(weight_in.shape, BF16),
            pltpu.VMEM(weight_out.shape, BF16),
            pltpu.VMEM((edges, latent), F32),
            pltpu.VMEM((nodes, latent), F32),
            pltpu.VMEM((edges, extent), BF16),
            pltpu.VMEM((extent, edges), BF16),
        ),
        in_specs=[HBM] * 8,
        out_specs=(VMEM,) * 9,
        scratch_shapes=[
            pltpu.SMEM((tiles,), jnp.int32),
            pltpu.SMEM((tiles,), jnp.int32),
            pltpu.VMEM((tiles, block), jnp.int32),
            pltpu.VMEM((nodes, latent), F32),
            pltpu.SemaphoreType.DMA((10,)),
        ],
        compiler_params=small,
        cost_estimate=pl.CostEstimate(
            flops=2 * edges * latent * latent, bytes_accessed=8_000_000, transcendentals=0
        ),
        name="prepare",
    )(
        in_hbm(tile_src),
        tile_dst,
        in_hbm(edge_slot),
        node_rows,
        in_hbm(edge_latents[0]),
        in_hbm(agg_cotangent[0]),
        in_hbm(weight_in),
        in_hbm(weight_out),
    )
    outs = pl.pallas_call(
        functools.partial(edge_kernel, ways, arrivals, four, block),
        out_shape=(
            jax.ShapeDtypeStruct((nodes, latent), BF16),
            pltpu.VMEM((edges, latent), BF16),
            pltpu.VMEM((extent, latent), F32),
            pltpu.VMEM((nodes, latent), F32),
            pltpu.VMEM((half, 2 * unit, latent), BF16),
            pltpu.VMEM((half, 2 * unit, latent), F32),
            pltpu.VMEM((half, 2 * unit, latent), BF16),
            pltpu.VMEM((half, 2 * unit, latent), F32),
        ),
        in_specs=[HBM, SMEM] + [VMEM] * (8 + arrivals),
        out_specs=(HBM,) + (VMEM,) * 7,
        scratch_shapes=[
            pltpu.SMEM((tiles,), jnp.int32),
            pltpu.VMEM((extent, latent), BF16),
            pltpu.VMEM((edges, latent), BF16),
            pltpu.VMEM((edges, latent), BF16),
            pltpu.VMEM((nodes, latent), F32),
            pltpu.VMEM((nodes, latent), BF16),
            pltpu.SemaphoreType.DMA((2,)),
        ],
        compiler_params=pltpu.CompilerParams(vmem_limit_bytes=16 * 1024 * 1024),
        cost_estimate=pl.CostEstimate(
            flops=14 * edges * latent * latent,
            bytes_accessed=12_000_000,
            transcendentals=edges * latent,
        ),
        name="edge_block",
    )(
        tile_dst,
        tile_count,
        *[
            in_vmem(array)
            for array in (*came, node_v, edge_v, win_v, wout_v, pre, mid, hot, turned)
        ],
    )
    agg, grad_pre, sums, recv_sums, away_a, kept_a, away_b, kept_b = outs
    came_a, kept_a, sent_a = sum_over_dp(away_a, kept_a, cot_v)
    edge_grad, *back_sums = pl.pallas_call(
        functools.partial(edge_grad_kernel, block, arrivals, four),
        out_shape=(jax.ShapeDtypeStruct((edges, latent), BF16),) + (block_shape,) * arrivals,
        in_specs=[HBM, SMEM] + [VMEM] * 5,
        out_specs=(VMEM,) * (1 + arrivals),
        scratch_shapes=[
            pltpu.SMEM((tiles,), jnp.int32),
            pltpu.SemaphoreType.DMA,
        ],
        compiler_params=small,
        cost_estimate=pl.CostEstimate(
            flops=2 * edges * latent * latent, bytes_accessed=3_000_000, transcendentals=0
        ),
        name="edge_grads",
    )(
        tile_dst,
        tile_count,
        *[in_vmem(array) for array in (sent_a, grad_pre, sums, cot_v, win_v)],
    )
    came_b, kept_b, _ = sum_over_dp(away_b, kept_b, back_sums[0])
    if four:
        returned = exchange_of_four(*back_sums)
    else:
        returned = [
            from_behind(back_sums[which], "dom", -OFFSET_LIST[which]) for which in range(4)
        ]
    node_out = pl.pallas_call(
        functools.partial(node_grad_kernel, arrivals, four),
        out_shape=jax.ShapeDtypeStruct((nodes, latent), BF16),
        in_specs=[HBM] + [VMEM] * (3 + arrivals),
        out_specs=VMEM,
        scratch_shapes=[
            pltpu.VMEM((nodes, latent), F32),
            pltpu.SMEM(boundary.shape, jnp.int32),
            pltpu.SemaphoreType.DMA,
        ],
        compiler_params=small,
        cost_estimate=pl.CostEstimate(
            flops=8 * nodes * latent * latent, bytes_accessed=2_000_000, transcendentals=0
        ),
        name="node_grads",
    )(boundary, *[in_vmem(array) for array in (sums, recv_sums, win_v, *returned)])
    if four:
        w_in_grad, w_out_grad = pl.pallas_call(
            last_kernel,
            out_shape=(
                jax.ShapeDtypeStruct((3 * unit, latent), F32),
                jax.ShapeDtypeStruct((unit, latent), F32),
            ),
            in_specs=[VMEM] * 4,
            out_specs=(VMEM,) * 2,
            compiler_params=small,
            cost_estimate=pl.CostEstimate(flops=0, bytes_accessed=1_500_000, transcendentals=0),
            name="widen",
        )(*sum_over_four(came_a, kept_a, edge_grad), *sum_over_four(came_b, kept_b, node_out))
    else:
        sum_a = sum_over_dom(kept_a[0] + came_a[0].astype(F32))
        sum_b = sum_over_dom(kept_b[0] + came_b[0].astype(F32))
        w_in_grad = jnp.concatenate([sum_a[unit:], sum_b], axis=0)
        w_out_grad = sum_a[:unit]
    return (agg[None], edge_grad[None], node_out[None], w_in_grad, w_out_grad)


def solution(mesh):
    in_specs = (
        P(("group", "dp"), "dom", None),
        P(("group", "dp"), "dom", None),
        P(("group", "dp"), "dom", None),
        P(),
        P(),
        P(("group", "dom"), None),
        P(("group", "dom")),
        P(("group", "dom")),
        P(("group", "dom"), None),
        P(("group", "dom")),
    )
    out_specs = (
        P(("group", "dp"), "dom", None),
        P(("group", "dp"), "dom", None),
        P(("group", "dp"), "dom", None),
        P(("group", "dp"), None),
        P(("group", "dp"), None),
    )
    return jax.shard_map(body, mesh=mesh, in_specs=in_specs, out_specs=out_specs, check_vma=False)
```

```python
import functools

import jax
import jax.numpy as jnp
from jax import lax
from jax.experimental import pallas as pl
from jax.experimental.pallas import tpu as pltpu
from jax.sharding import PartitionSpec as P

OFFSET_LIST = (1, -1, 2, -2)
EPSILON = 1e-05
VMEM = pl.BlockSpec(memory_space=pltpu.VMEM)
HBM = pl.BlockSpec(memory_space=pltpu.HBM)
SMEM = pl.BlockSpec(memory_space=pltpu.SMEM)
ANY = pl.BlockSpec(memory_space=pl.ANY)
F32 = jnp.float32
BF16 = jnp.bfloat16


def dot(left, right):
    return jnp.dot(left, right, preferred_element_type=F32)


def dot_t(left, right):
    return lax.dot_general(left, right, (((1,), (1,)), ((), ())), preferred_element_type=F32)


def t_dot(left, right):
    return lax.dot_general(left, right, (((0,), (0,)), ((), ())), preferred_element_type=F32)


def row_mean(array):
    return jnp.sum(array, axis=1, keepdims=True) * (1.0 / array.shape[1])


def rows_of(ref, block, size):
    return ref[pl.ds(pl.multiple_of(block * size, size), size), :]


def load_small(source, target, sem):
    copy = pltpu.make_async_copy(source, target, sem)
    copy.start()
    return copy


def boundary_places(boundary_ref, part, four):
    taken = [boundary_ref[0, which] for which in range(4)]
    if not four:
        return taken
    even = part % 2 == 0
    return [
        jnp.where(even, taken[0], taken[1]),
        jnp.where(even, taken[1], taken[0]),
        jnp.where(part < 2, taken[2], taken[3]),
    ]


def arrival_places(part, four, arrivals):
    if not four:
        return list(range(arrivals))
    even = part % 2 == 0
    return [jnp.where(even, 1, 0), jnp.where(even, 0, 1), 2]


def pick_kernel(four, block, boundary_hbm, node_hbm, *refs):
    count = 3 if four else 4
    outs = refs[:count]
    boundary_ref, small_sem, sems = refs[count:]
    load_small(boundary_hbm, boundary_ref, small_sem).wait()
    copies = []
    for which, place in enumerate(boundary_places(boundary_ref, lax.axis_index("dom"), four)):
        spot = pl.ds(pl.multiple_of(place * block, block), block)
        copies.append(pltpu.make_async_copy(node_hbm.at[spot, :], outs[which], sems.at[which]))
        copies[-1].start()
    for copy in copies:
        copy.wait()


def prep_kernel(
    parts,
    arrivals,
    src_hbm,
    dst_hbm,
    slot_hbm,
    node_hbm,
    edge_hbm,
    cot_hbm,
    win_hbm,
    wout_hbm,
    node_ref,
    edge_ref,
    cot_ref,
    win_ref,
    wout_ref,
    pre_ref,
    mid_ref,
    hot_ref,
    hot_turned,
    src_ref,
    dst_ref,
    slot_ref,
    recv_ref,
    sems,
):
    tiles, block = slot_ref.shape
    nodes, latent = node_ref.shape
    owned = nodes // block
    extent = hot_turned.shape[0]
    pairs = (
        (src_hbm, src_ref),
        (dst_hbm, dst_ref),
        (slot_hbm, slot_ref),
        (node_hbm, node_ref),
        (win_hbm.at[2 * latent :, :], win_ref.at[2 * latent :, :]),
        (win_hbm.at[:latent, :], win_ref.at[:latent, :]),
        (edge_hbm, edge_ref),
        (cot_hbm, cot_ref),
        (win_hbm.at[latent : 2 * latent, :], win_ref.at[latent : 2 * latent, :]),
        (wout_hbm, wout_ref),
    )
    copies = [load_small(*pair, sems.at[number]) for number, pair in enumerate(pairs)]
    part = lax.axis_index("dom")
    for copy in copies[:3]:
        copy.wait()
    index = lax.broadcasted_iota(jnp.int32, (extent, 2 * block), 0)
    first = lax.broadcasted_iota(jnp.int32, (1, 2 * block), 1) < block
    for tile in range(0, tiles, 2):
        wanted = []
        for member in (tile, tile + 1):
            source = src_ref[member]
            which = source - owned
            reach = jnp.where(which >= 2, 2, 1)
            partner = part - jnp.where(which % 2 == 1, -reach, reach)
            exists = (source < owned) | ((partner >= 0) & (partner < parts))
            place = jnp.minimum(source, owned + arrivals - 1)
            wanted.append(jnp.where(exists, place * block, -2 * extent))
        slots = jnp.concatenate(
            [slot_ref[tile : tile + 1, :], slot_ref[tile + 1 : tile + 2, :]], axis=1
        )
        row = slots + jnp.where(first, wanted[0], wanted[1])
        hot = jnp.where(index == row, 1.0, 0.0)
        at = slice(tile * block, (tile + 2) * block)
        hot_turned[:, at] = hot.astype(BF16)
        hot_ref[at, :] = hot.T.astype(BF16)
    copies[3].wait()
    copies[4].wait()
    recv_ref[...] = dot(node_ref[...], win_ref[2 * latent :, :])
    copies[5].wait()
    copies[6].wait()
    group = 4 if tiles % 4 == 0 else 2
    for tile in range(0, tiles, group):
        rows = slice(tile * block, (tile + group) * block)
        received = jnp.concatenate(
            [rows_of(recv_ref, dst_ref[t], block) for t in range(tile, tile + group)], axis=0
        )
        pre_ref[rows, :] = dot(edge_ref[rows, :], win_ref[:latent, :]) + received
    copies[7].wait()
    cot = cot_ref[...].astype(F32)
    mid_ref[...] = cot - row_mean(cot)
    copies[8].wait()
    copies[9].wait()


def edge_kernel(
    ways,
    arrivals,
    four,
    block,
    dst_hbm,
    count_ref,
    *refs,
):
    arrived = refs[:arrivals]
    (
        node_ref,
        edge_ref,
        win_ref,
        wout_ref,
        pre_ref,
        mid_ref,
        hot_ref,
        hot_turned,
        agg_hbm,
        gpre_ref,
        sums_ref,
        recv_sums,
        away_a,
        kept_a,
        away_b,
        kept_b,
        dst_ref,
        ext_ref,
        act_ref,
        proj_ref,
        agg_ref,
        agg_bf16,
        sems,
    ) = refs[arrivals:]
    nodes, latent = node_ref.shape
    edges = edge_ref.shape[0]
    tiles = edges // block
    owned = nodes // block
    part = lax.axis_index("dom")
    bit = lax.axis_index("dp") % 2
    dst_copy = load_small(dst_hbm, dst_ref, sems.at[0])
    places = arrival_places(part, four, arrivals)

    ext_ref[:nodes, :] = node_ref[...]
    for which in range(arrivals):
        at = pl.multiple_of((owned + places[which]) * block, block)
        ext_ref[pl.ds(at, block), :] = arrived[which][...]
    filled = nodes + arrivals * block
    if filled < ext_ref.shape[0]:
        ext_ref[filled:, :] = jnp.zeros((ext_ref.shape[0] - filled, latent), BF16)
    agg_ref[...] = jnp.zeros_like(agg_ref)
    recv_sums[...] = jnp.zeros_like(recv_sums)

    group = 4 if tiles % 4 == 0 else 1
    span = group * block
    for first in range(0, tiles, group):
        rows = slice(first * block, first * block + span)
        members = range(first, first + group)
        edge_rows = edge_ref[rows, :]
        senders = dot(hot_ref[rows, :], ext_ref[...]).astype(BF16)
        preact = pre_ref[rows, :] + dot(senders, win_ref[latent : 2 * latent, :])
        gate = 0.5 * jnp.tanh(0.5 * preact) + 0.5
        activated = preact * gate
        slope = gate + activated * (1.0 - gate)
        activated = activated.astype(BF16)
        act_ref[rows, :] = activated
        projected = dot(activated, wout_ref[...])
        centered = projected - row_mean(projected)
        inv_scale = lax.rsqrt(row_mean(centered * centered) + EPSILON)
        message = centered * inv_scale
        updated = edge_rows.astype(F32) + message
        if first == 0:
            dst_copy.wait()
        upstream = []
        for number, tile in enumerate(members):
            live = jnp.where(tile < count_ref[0], 1.0, 0.0)
            target = pl.ds(pl.multiple_of(dst_ref[tile] * block, block), block)
            agg_ref[target, :] += updated[number * block : (number + 1) * block] * live
            upstream.append(mid_ref[target, :] * live)
        upstream = jnp.concatenate(upstream, axis=0)
        grad_project = inv_scale * (upstream - message * row_mean(upstream * message))
        grad_project = grad_project.astype(BF16)
        proj_ref[rows, :] = grad_project
        grad_pre = (dot_t(grad_project, wout_ref[...]) * slope).astype(BF16)
        gpre_ref[rows, :] = grad_pre
        for number, tile in enumerate(members):
            mine = grad_pre[number * block : (number + 1) * block]
            target = pl.ds(pl.multiple_of(dst_ref[tile] * block, block), block)
            recv_sums[target, :] += mine.astype(F32)

    agg_bf16[...] = agg_ref[...].astype(BF16)
    agg_copy = load_small(agg_bf16, agg_hbm, sems.at[1])
    sums_ref[...] = dot(hot_turned[...], gpre_ref[...])

    unit = latent // ways

    def put(owner, spot, value):
        away, kept = (away_a, kept_a) if spot < 2 else (away_b, kept_b)
        where = slice((spot % 2) * unit, (spot % 2 + 1) * unit)

        @pl.when(bit == owner % 2)
        def _():
            kept[owner // 2, where, :] = value

        @pl.when(bit != owner % 2)
        def _():
            away[owner // 2, where, :] = value.astype(BF16)

    step = 256
    for start in range(0, latent, step):
        value = t_dot(act_ref[:, start : start + step], proj_ref[...])
        for at in range(0, step, unit):
            put((start + at) // unit, 0, value[at : at + unit])
    sections = (
        (edge_ref, gpre_ref),
        (ext_ref, sums_ref),
        (node_ref, recv_sums),
    )
    for number, (left, right) in enumerate(sections):
        for start in range(0, latent, step):
            value = t_dot(left[:, start : start + step], right[...].astype(BF16))
            for at in range(0, step, unit):
                spot = (number * latent + start + at) // unit
                put(spot // 3, 1 + spot % 3, value[at : at + unit])
    agg_copy.wait()


def edge_grad_kernel(
    block,
    arrivals,
    four,
    dst_hbm,
    count_ref,
    after,
    gpre_ref,
    sums_ref,
    cot_ref,
    win_ref,
    out_ref,
    *refs,
):
    back_sums = refs[:arrivals]
    dst_ref, sem = refs[arrivals:]
    copy = load_small(dst_hbm, dst_ref, sem)
    nodes, latent = cot_ref.shape
    tiles = gpre_ref.shape[0] // block
    group = 4 if tiles % 4 == 0 else 1
    places = arrival_places(lax.axis_index("dom"), four, arrivals)
    for which in range(arrivals):
        at = pl.multiple_of(nodes + places[which] * block, block)
        back_sums[which][...] = sums_ref[pl.ds(at, block), :].astype(BF16)
    copy.wait()
    for first in range(0, tiles, group):
        rows = slice(first * block, (first + group) * block)
        upstream = jnp.concatenate(
            [
                rows_of(cot_ref, dst_ref[t], block).astype(F32)
                * jnp.where(t < count_ref[0], 1.0, 0.0)
                for t in range(first, first + group)
            ],
            axis=0,
        )
        out_ref[rows, :] = (dot_t(gpre_ref[rows, :], win_ref[:latent, :]) + upstream).astype(BF16)


def halve_kernel(bit, came_ref, kept_ref, after, away_ref, left_ref):
    mine = (lax.axis_index("dp") // bit) % 2
    for slot in range(left_ref.shape[0]):
        there, here = 2 * slot + 1 - mine, 2 * slot + mine
        away_ref[slot] = (kept_ref[there] + came_ref[there].astype(F32)).astype(BF16)
        left_ref[slot] = kept_ref[here] + came_ref[here].astype(F32)


def split_kernel(came_ref, kept_ref, *refs):
    away_ref, left_ref = refs[-2:]
    part = lax.axis_index("dom")
    inner = (part == 1) | (part == 2)
    rows = left_ref.shape[0]
    here = pl.ds(pl.multiple_of(jnp.where(inner, 0, rows), rows), rows)
    there = pl.ds(pl.multiple_of(jnp.where(inner, rows, 0), rows), rows)
    away_ref[...] = (kept_ref[0, there, :] + came_ref[0, there, :].astype(F32)).astype(BF16)
    left_ref[...] = kept_ref[0, here, :] + came_ref[0, here, :].astype(F32)


def node_grad_kernel(arrivals, four, boundary_hbm, after, sums_ref, recv_ref, win_ref, *refs):
    returned = refs[:arrivals]
    out_ref, total_ref, boundary_ref, sem = refs[arrivals:]
    nodes, latent = recv_ref.shape
    block = returned[0].shape[0]
    copy = load_small(boundary_hbm, boundary_ref, sem)
    total_ref[...] = sums_ref[:nodes, :]
    copy.wait()
    for which, place in enumerate(boundary_places(boundary_ref, lax.axis_index("dom"), four)):
        spot = pl.ds(pl.multiple_of(place * block, block), block)
        total_ref[spot, :] += returned[which][...].astype(F32)

    def wide_dot(value, weight):
        high = value.astype(BF16)
        low = (value - high.astype(F32)).astype(BF16)
        return dot_t(high, weight) + dot_t(low, weight)

    out_ref[...] = (
        wide_dot(total_ref[...], win_ref[latent : 2 * latent, :])
        + wide_dot(recv_ref[...], win_ref[2 * latent :, :])
    ).astype(BF16)


def last_kernel(after, own_a, other_a, own_b, other_b, in_ref, out_ref):
    unit = out_ref.shape[0]
    part = lax.axis_index("dom")
    inner = (part == 1) | (part == 2)

    def write(low_a, high_a, low_b, high_b):
        out_ref[...] = low_a[...].astype(F32)
        in_ref[:unit, :] = high_a[...].astype(F32)
        in_ref[unit : 2 * unit, :] = low_b[...].astype(F32)
        in_ref[2 * unit :, :] = high_b[...].astype(F32)

    @pl.when(inner)
    def _():
        write(own_a, other_a, own_b, other_b)

    @pl.when(jnp.logical_not(inner))
    def _():
        write(other_a, own_a, other_b, own_b)


def swap(array, axis, partner):
    devices = lax.axis_size(axis)
    return lax.ppermute(array, axis, [(i, partner(i)) for i in range(devices)])


def from_behind(array, axis, by):
    devices = lax.axis_size(axis)
    pairs = [(i, i + by) for i in range(devices) if 0 <= i + by < devices]
    return lax.ppermute(array, axis, pairs)


def partners_of_four(which):
    return ((1, 0, 3, 2), (0, 2, 1, 3), (2, 3, 0, 1))[which]


def exchange_of_four(first, second, third):
    return [
        swap(array, "dom", lambda i, which=which: partners_of_four(which)[i])
        for which, array in enumerate((first, second, third))
    ]


def halve(bit, came, kept, after):
    slots, rows, latent = kept.shape
    return pl.pallas_call(
        functools.partial(halve_kernel, bit),
        out_shape=(
            pltpu.VMEM((slots // 2, rows, latent), BF16),
            pltpu.VMEM((slots // 2, rows, latent), F32),
        ),
        in_specs=[VMEM] * 3,
        out_specs=(VMEM,) * 2,
        compiler_params=pltpu.CompilerParams(vmem_limit_bytes=4 * 1024 * 1024),
        cost_estimate=pl.CostEstimate(flops=0, bytes_accessed=500_000, transcendentals=0),
        name="halve",
    )(in_vmem(came), in_vmem(kept), in_vmem(after))


def sum_over_dp(away, kept, after):
    devices = lax.axis_size("dp")
    bit = 1
    while True:
        came = swap(away, "dp", lambda i, bit=bit: i ^ bit)
        bit *= 2
        if bit >= devices:
            return came, kept, away
        away, kept = halve(bit, came, kept, after)


def split(came, kept, after):
    rows, latent = kept.shape[1:]
    return pl.pallas_call(
        split_kernel,
        out_shape=(
            pltpu.VMEM((rows // 2, latent), BF16),
            pltpu.VMEM((rows // 2, latent), F32),
        ),
        in_specs=[VMEM] * (2 + len(after)),
        out_specs=(VMEM,) * 2,
        compiler_params=pltpu.CompilerParams(vmem_limit_bytes=4 * 1024 * 1024),
        cost_estimate=pl.CostEstimate(flops=0, bytes_accessed=500_000, transcendentals=0),
        name="split",
    )(in_vmem(came), in_vmem(kept), *[in_vmem(array) for array in after])


def sum_of_pair(away, kept):
    return (kept + swap(away, "dom", lambda i: i ^ 1).astype(F32)).astype(BF16)


def sum_of_four(kept):
    kept = (kept.astype(F32) + swap(kept, "dom", lambda i: 3 - i).astype(F32)).astype(BF16)
    return kept, swap(kept, "dom", lambda i: i ^ 1)


def sum_over_dom(rows):
    piece = lax.psum_scatter(rows, "dom", scatter_dimension=0, tiled=True)
    return lax.all_gather(piece, "dom", axis=0, tiled=True)


def in_vmem(array):
    return pltpu.with_memory_space_constraint(array, pltpu.VMEM)


def in_hbm(array):
    return pltpu.with_memory_space_constraint(array, pltpu.HBM)


def body(
    node_latents,
    edge_latents,
    agg_cotangent,
    weight_in,
    weight_out,
    boundary,
    tile_src,
    tile_dst,
    edge_slot,
    tile_count,
):
    tiles, block = edge_slot.shape
    edges, latent = edge_latents.shape[1:]
    nodes = node_latents.shape[1]
    parts = lax.axis_size("dom")
    ways = lax.axis_size("dp")
    four = parts == 4
    arrivals = 3 if four else 4
    boundary = in_hbm(boundary)
    tile_dst = in_hbm(tile_dst)
    node_rows = in_hbm(node_latents[0])
    block_shape = pltpu.VMEM((block, latent), BF16)
    small = pltpu.CompilerParams(vmem_limit_bytes=8 * 1024 * 1024)

    sent = pl.pallas_call(
        functools.partial(pick_kernel, four, block),
        out_shape=(block_shape,) * arrivals,
        in_specs=[HBM] * 2,
        out_specs=(VMEM,) * arrivals,
        scratch_shapes=[
            pltpu.SMEM(boundary.shape, jnp.int32),
            pltpu.SemaphoreType.DMA,
            pltpu.SemaphoreType.DMA((arrivals,)),
        ],
        compiler_params=small,
        cost_estimate=pl.CostEstimate(flops=0, bytes_accessed=400_000, transcendentals=0),
        name="pick_blocks",
    )(boundary, node_rows)
    if four:
        came = exchange_of_four(*sent)
    else:
        came = [from_behind(sent[which], "dom", OFFSET_LIST[which]) for which in range(4)]
    unit = latent // ways
    half = ways // 2
    extent = -(-(nodes + arrivals * block) // 128) * 128

    node_v, edge_v, cot_v, win_v, wout_v, pre, mid, hot, turned = pl.pallas_call(
        functools.partial(prep_kernel, parts, arrivals),
        out_shape=(
            pltpu.VMEM((nodes, latent), BF16),
            pltpu.VMEM((edges, latent), BF16),
            pltpu.VMEM((nodes, latent), BF16),
            pltpu.VMEM(weight_in.shape, BF16),
            pltpu.VMEM(weight_out.shape, BF16),
            pltpu.VMEM((edges, latent), F32),
            pltpu.VMEM((nodes, latent), F32),
            pltpu.VMEM((edges, extent), BF16),
            pltpu.VMEM((extent, edges), BF16),
        ),
        in_specs=[HBM] * 8,
        out_specs=(VMEM,) * 9,
        scratch_shapes=[
            pltpu.SMEM((tiles,), jnp.int32),
            pltpu.SMEM((tiles,), jnp.int32),
            pltpu.VMEM((tiles, block), jnp.int32),
            pltpu.VMEM((nodes, latent), F32),
            pltpu.SemaphoreType.DMA((10,)),
        ],
        compiler_params=small,
        cost_estimate=pl.CostEstimate(
            flops=2 * edges * latent * latent, bytes_accessed=8_000_000, transcendentals=0
        ),
        name="prepare",
    )(
        in_hbm(tile_src),
        tile_dst,
        in_hbm(edge_slot),
        node_rows,
        in_hbm(edge_latents[0]),
        in_hbm(agg_cotangent[0]),
        in_hbm(weight_in),
        in_hbm(weight_out),
    )
    outs = pl.pallas_call(
        functools.partial(edge_kernel, ways, arrivals, four, block),
        out_shape=(
            jax.ShapeDtypeStruct((nodes, latent), BF16),
            pltpu.VMEM((edges, latent), BF16),
            pltpu.VMEM((extent, latent), F32),
            pltpu.VMEM((nodes, latent), F32),
            pltpu.VMEM((half, 2 * unit, latent), BF16),
            pltpu.VMEM((half, 2 * unit, latent), F32),
            pltpu.VMEM((half, 2 * unit, latent), BF16),
            pltpu.VMEM((half, 2 * unit, latent), F32),
        ),
        in_specs=[HBM, SMEM] + [VMEM] * (8 + arrivals),
        out_specs=(HBM,) + (VMEM,) * 7,
        scratch_shapes=[
            pltpu.SMEM((tiles,), jnp.int32),
            pltpu.VMEM((extent, latent), BF16),
            pltpu.VMEM((edges, latent), BF16),
            pltpu.VMEM((edges, latent), BF16),
            pltpu.VMEM((nodes, latent), F32),
            pltpu.VMEM((nodes, latent), BF16),
            pltpu.SemaphoreType.DMA((2,)),
        ],
        compiler_params=pltpu.CompilerParams(vmem_limit_bytes=16 * 1024 * 1024),
        cost_estimate=pl.CostEstimate(
            flops=14 * edges * latent * latent,
            bytes_accessed=12_000_000,
            transcendentals=edges * latent,
        ),
        name="edge_block",
    )(
        tile_dst,
        tile_count,
        *[
            in_vmem(array)
            for array in (*came, node_v, edge_v, win_v, wout_v, pre, mid, hot, turned)
        ],
    )
    agg, grad_pre, sums, recv_sums, away_a, kept_a, away_b, kept_b = outs
    came_a, kept_a, sent_a = sum_over_dp(away_a, kept_a, cot_v)
    edge_grad, *back_sums = pl.pallas_call(
        functools.partial(edge_grad_kernel, block, arrivals, four),
        out_shape=(jax.ShapeDtypeStruct((edges, latent), BF16),) + (block_shape,) * arrivals,
        in_specs=[HBM, SMEM] + [VMEM] * 5,
        out_specs=(VMEM,) * (1 + arrivals),
        scratch_shapes=[
            pltpu.SMEM((tiles,), jnp.int32),
            pltpu.SemaphoreType.DMA,
        ],
        compiler_params=small,
        cost_estimate=pl.CostEstimate(
            flops=2 * edges * latent * latent, bytes_accessed=3_000_000, transcendentals=0
        ),
        name="edge_grads",
    )(
        tile_dst,
        tile_count,
        *[in_vmem(array) for array in (sent_a, grad_pre, sums, cot_v, win_v)],
    )
    came_b, kept_b, _ = sum_over_dp(away_b, kept_b, back_sums[0])
    if four:
        returned = exchange_of_four(*back_sums)
    else:
        returned = [
            from_behind(back_sums[which], "dom", -OFFSET_LIST[which]) for which in range(4)
        ]
    if four:
        pair_a = sum_of_pair(*split(came_a, kept_a, returned))
        pair_b = sum_of_pair(*split(came_b, kept_b, ()))
        late = pair_b
    else:
        late = sent_a
    node_out = pl.pallas_call(
        functools.partial(node_grad_kernel, arrivals, four),
        out_shape=jax.ShapeDtypeStruct((nodes, latent), BF16),
        in_specs=[HBM] + [VMEM] * (4 + arrivals),
        out_specs=VMEM,
        scratch_shapes=[
            pltpu.VMEM((nodes, latent), F32),
            pltpu.SMEM(boundary.shape, jnp.int32),
            pltpu.SemaphoreType.DMA,
        ],
        compiler_params=small,
        cost_estimate=pl.CostEstimate(
            flops=8 * nodes * latent * latent, bytes_accessed=2_000_000, transcendentals=0
        ),
        name="node_grads",
    )(boundary, *[in_vmem(array) for array in (late, sums, recv_sums, win_v, *returned)])
    if four:
        w_in_grad, w_out_grad = pl.pallas_call(
            last_kernel,
            out_shape=(
                jax.ShapeDtypeStruct((3 * unit, latent), F32),
                jax.ShapeDtypeStruct((unit, latent), F32),
            ),
            in_specs=[HBM] + [VMEM] * 4,
            out_specs=(VMEM,) * 2,
            compiler_params=small,
            cost_estimate=pl.CostEstimate(flops=0, bytes_accessed=1_500_000, transcendentals=0),
            name="widen",
        )(in_hbm(node_out), *sum_of_four(pair_a), *sum_of_four(pair_b))
    else:
        sum_a = sum_over_dom(kept_a[0] + came_a[0].astype(F32))
        sum_b = sum_over_dom(kept_b[0] + came_b[0].astype(F32))
        w_in_grad = jnp.concatenate([sum_a[unit:], sum_b], axis=0)
        w_out_grad = sum_a[:unit]
    return (agg[None], edge_grad[None], node_out[None], w_in_grad, w_out_grad)


def solution(mesh):
    in_specs = (
        P(("group", "dp"), "dom", None),
        P(("group", "dp"), "dom", None),
        P(("group", "dp"), "dom", None),
        P(),
        P(),
        P(("group", "dom"), None),
        P(("group", "dom")),
        P(("group", "dom")),
        P(("group", "dom"), None),
        P(("group", "dom")),
    )
    out_specs = (
        P(("group", "dp"), "dom", None),
        P(("group", "dp"), "dom", None),
        P(("group", "dp"), "dom", None),
        P(("group", "dp"), None),
        P(("group", "dp"), None),
    )
    return jax.shard_map(body, mesh=mesh, in_specs=in_specs, out_specs=out_specs, check_vma=False)
```

```python
import functools

import jax
import jax.numpy as jnp
from jax import lax
from jax.experimental import pallas as pl
from jax.experimental.pallas import tpu as pltpu
from jax.sharding import PartitionSpec as P

OFFSET_LIST = (1, -1, 2, -2)
EPSILON = 1e-05
VMEM = pl.BlockSpec(memory_space=pltpu.VMEM)
HBM = pl.BlockSpec(memory_space=pltpu.HBM)
SMEM = pl.BlockSpec(memory_space=pltpu.SMEM)
ANY = pl.BlockSpec(memory_space=pl.ANY)
F32 = jnp.float32
BF16 = jnp.bfloat16


def dot(left, right):
    return jnp.dot(left, right, preferred_element_type=F32)


def dot_t(left, right):
    return lax.dot_general(left, right, (((1,), (1,)), ((), ())), preferred_element_type=F32)


def t_dot(left, right):
    return lax.dot_general(left, right, (((0,), (0,)), ((), ())), preferred_element_type=F32)


def row_mean(array):
    return jnp.sum(array, axis=1, keepdims=True) * (1.0 / array.shape[1])


def rows_of(ref, block, size):
    return ref[pl.ds(pl.multiple_of(block * size, size), size), :]


def load_small(source, target, sem):
    copy = pltpu.make_async_copy(source, target, sem)
    copy.start()
    return copy


def boundary_places(boundary_ref, part, four):
    taken = [boundary_ref[0, which] for which in range(4)]
    if not four:
        return taken
    even = part % 2 == 0
    return [
        jnp.where(even, taken[0], taken[1]),
        jnp.where(even, taken[1], taken[0]),
        jnp.where(part < 2, taken[2], taken[3]),
    ]


def arrival_places(part, four, arrivals):
    if not four:
        return list(range(arrivals))
    even = part % 2 == 0
    return [jnp.where(even, 1, 0), jnp.where(even, 0, 1), 2]


def pick_kernel(four, block, boundary_hbm, node_hbm, *refs):
    count = 3 if four else 4
    outs = refs[:count]
    boundary_ref, small_sem, sems = refs[count:]
    load_small(boundary_hbm, boundary_ref, small_sem).wait()
    copies = []
    for which, place in enumerate(boundary_places(boundary_ref, lax.axis_index("dom"), four)):
        spot = pl.ds(pl.multiple_of(place * block, block), block)
        copies.append(pltpu.make_async_copy(node_hbm.at[spot, :], outs[which], sems.at[which]))
        copies[-1].start()
    for copy in copies:
        copy.wait()


def prep_kernel(
    parts,
    arrivals,
    count_ref,
    src_hbm,
    dst_hbm,
    slot_hbm,
    node_hbm,
    edge_hbm,
    cot_hbm,
    win_hbm,
    wout_hbm,
    node_ref,
    edge_ref,
    cot_ref,
    win_ref,
    wout_ref,
    pre_ref,
    up_ref,
    hot_ref,
    hot_turned,
    src_ref,
    dst_ref,
    slot_ref,
    recv_ref,
    mid_ref,
    sems,
):
    tiles, block = slot_ref.shape
    nodes, latent = node_ref.shape
    owned = nodes // block
    extent = hot_ref.shape[1]
    pairs = (
        (src_hbm, src_ref),
        (dst_hbm, dst_ref),
        (slot_hbm, slot_ref),
        (node_hbm, node_ref),
        (win_hbm.at[2 * latent :, :], win_ref.at[2 * latent :, :]),
        (win_hbm.at[:latent, :], win_ref.at[:latent, :]),
        (edge_hbm, edge_ref),
        (cot_hbm, cot_ref),
        (win_hbm.at[latent : 2 * latent, :], win_ref.at[latent : 2 * latent, :]),
        (wout_hbm, wout_ref),
    )
    copies = [load_small(*pair, sems.at[number]) for number, pair in enumerate(pairs)]
    part = lax.axis_index("dom")
    for copy in copies[:3]:
        copy.wait()
    index = lax.broadcasted_iota(jnp.int32, (extent, 2 * block), 0)
    lane = lax.broadcasted_iota(jnp.int32, (1, 2 * block), 1)
    first = lane < block
    within = jnp.where(first, lane, lane - block)
    node_index = lax.broadcasted_iota(jnp.int32, (nodes, 2 * block), 0)
    for tile in range(0, tiles, 2):
        wanted = []
        for member in (tile, tile + 1):
            source = src_ref[member]
            which = source - owned
            reach = jnp.where(which >= 2, 2, 1)
            partner = part - jnp.where(which % 2 == 1, -reach, reach)
            exists = (source < owned) | ((partner >= 0) & (partner < parts))
            place = jnp.minimum(source, owned + arrivals - 1)
            wanted.append(jnp.where(exists, place * block, -2 * extent))
        slots = jnp.concatenate(
            [slot_ref[tile : tile + 1, :], slot_ref[tile + 1 : tile + 2, :]], axis=1
        )
        row = slots + jnp.where(first, wanted[0], wanted[1])
        hot = jnp.where(index == row, 1.0, 0.0)
        at = slice(tile * block, (tile + 2) * block)
        hot_turned[:extent, at] = hot.astype(BF16)
        target = within + jnp.where(first, dst_ref[tile] * block, dst_ref[tile + 1] * block)
        hot_turned[extent:, at] = jnp.where(node_index == target, 1.0, 0.0).astype(BF16)
        hot_ref[at, :] = hot.T.astype(BF16)
    copies[3].wait()
    copies[4].wait()
    recv_ref[...] = dot(node_ref[...], win_ref[2 * latent :, :])
    copies[5].wait()
    copies[6].wait()
    group = 4 if tiles % 4 == 0 else 2
    for tile in range(0, tiles, group):
        rows = slice(tile * block, (tile + group) * block)
        received = jnp.concatenate(
            [rows_of(recv_ref, dst_ref[t], block) for t in range(tile, tile + group)], axis=0
        )
        pre_ref[rows, :] = dot(edge_ref[rows, :], win_ref[:latent, :]) + received
    copies[7].wait()
    cot = cot_ref[...].astype(F32)
    mid_ref[...] = cot - row_mean(cot)
    for tile in range(tiles):
        live = jnp.where(tile < count_ref[0], 1.0, 0.0)
        up_ref[tile * block : (tile + 1) * block, :] = rows_of(mid_ref, dst_ref[tile], block) * live
    copies[8].wait()
    copies[9].wait()


def put_units(chunk, ways, bit, away, kept, sections):
    latent = sections[0][0].shape[1]
    unit = latent // ways
    step = 128

    def wanted(number, start):
        if number == 0:
            return [(start + at) // unit for at in range(0, step, unit)] if chunk == 0 else []
        found = []
        for at in range(0, step, unit):
            spot = ((number - 1) * latent + start + at) // unit
            if (1 + spot % 3) // 2 == chunk:
                found.append(spot)
        return found

    for number, (left, right) in enumerate(sections):
        value_right = right()
        start = 0
        while start < latent:
            size = step
            if start + 2 * step <= latent and wanted(number, start + step):
                size = 2 * step
            if wanted(number, start):
                value = t_dot(left[:, start : start + size], value_right)
                for at in range(0, size, unit):
                    if number == 0:
                        owner, spot = (start + at) // unit, 0
                    else:
                        place = ((number - 1) * latent + start + at) // unit
                        owner, spot = place // 3, 1 + place % 3
                    if spot // 2 != chunk:
                        continue
                    part = value[at : at + unit]
                    where = slice((spot % 2) * unit, (spot % 2 + 1) * unit)

                    @pl.when(bit == owner % 2)
                    def _(owner=owner, where=where, part=part):
                        kept[owner // 2, where, :] = part

                    @pl.when(bit != owner % 2)
                    def _(owner=owner, where=where, part=part):
                        away[owner // 2, where, :] = part.astype(BF16)

                start += size
            else:
                start += step


def edge_kernel(ways, arrivals, four, block, *refs):
    arrived = refs[:arrivals]
    (
        node_ref,
        edge_ref,
        win_ref,
        wout_ref,
        pre_ref,
        up_ref,
        hot_ref,
        hot_turned,
        gpre_ref,
        message_ref,
        sums_ref,
        ext_ref,
        away_ref,
        kept_ref,
        act_ref,
        proj_ref,
    ) = refs[arrivals:]
    nodes, latent = node_ref.shape
    edges = edge_ref.shape[0]
    extent = ext_ref.shape[0]
    places = arrival_places(lax.axis_index("dom"), four, arrivals)

    ext_ref[:nodes, :] = node_ref[...]
    for which in range(arrivals):
        at = pl.multiple_of(nodes + places[which] * block, block)
        ext_ref[pl.ds(at, block), :] = arrived[which][...]
    filled = nodes + arrivals * block
    if filled < extent:
        ext_ref[filled:, :] = jnp.zeros((extent - filled, latent), BF16)

    span = 256 if edges % 256 == 0 else block
    for start in range(0, edges, span):
        rows = slice(start, start + span)
        senders = dot(hot_ref[rows, :], ext_ref[...]).astype(BF16)
        preact = pre_ref[rows, :] + dot(senders, win_ref[latent : 2 * latent, :])
        gate = 0.5 * jnp.tanh(0.5 * preact) + 0.5
        activated = preact * gate
        slope = gate + activated * (1.0 - gate)
        activated = activated.astype(BF16)
        act_ref[rows, :] = activated
        projected = dot(activated, wout_ref[...])
        centered = projected - row_mean(projected)
        inv_scale = lax.rsqrt(row_mean(centered * centered) + EPSILON)
        message = centered * inv_scale
        message_ref[rows, :] = message
        upstream = up_ref[rows, :]
        grad_project = inv_scale * (upstream - message * row_mean(upstream * message))
        grad_project = grad_project.astype(BF16)
        proj_ref[rows, :] = grad_project
        gpre_ref[rows, :] = (dot_t(grad_project, wout_ref[...]) * slope).astype(BF16)

    sums_ref[...] = dot(hot_turned[...], gpre_ref[...])
    sections = (
        (act_ref, lambda: proj_ref[...]),
        (edge_ref, lambda: gpre_ref[...]),
        (ext_ref, lambda: sums_ref[:extent, :].astype(BF16)),
        (node_ref, lambda: sums_ref[extent:, :].astype(BF16)),
    )
    put_units(0, ways, lax.axis_index("dp") % 2, away_ref, kept_ref, sections)


def rest_kernel(ways, node_ref, edge_ref, ext_ref, gpre_ref, sums_ref, away_ref, kept_ref):
    extent = ext_ref.shape[0]
    sections = (
        (edge_ref, lambda: None),
        (edge_ref, lambda: gpre_ref[...]),
        (ext_ref, lambda: sums_ref[:extent, :].astype(BF16)),
        (node_ref, lambda: sums_ref[extent:, :].astype(BF16)),
    )
    put_units(1, ways, lax.axis_index("dp") % 2, away_ref, kept_ref, sections)


def edge_grad_kernel(
    block,
    arrivals,
    four,
    dst_hbm,
    count_ref,
    after,
    gpre_ref,
    sums_ref,
    cot_ref,
    win_ref,
    edge_ref,
    message_ref,
    out_ref,
    agg_out,
    *refs,
):
    back_sums = refs[:arrivals]
    dst_ref, agg_ref, sem = refs[arrivals:]
    copy = load_small(dst_hbm, dst_ref, sem)
    nodes, latent = cot_ref.shape
    tiles = gpre_ref.shape[0] // block
    group = 4 if tiles % 4 == 0 else 1
    places = arrival_places(lax.axis_index("dom"), four, arrivals)
    for which in range(arrivals):
        at = pl.multiple_of(nodes + places[which] * block, block)
        back_sums[which][...] = sums_ref[pl.ds(at, block), :].astype(BF16)
    agg_ref[...] = jnp.zeros_like(agg_ref)
    copy.wait()
    for first in range(0, tiles, group):
        rows = slice(first * block, (first + group) * block)
        upstream = jnp.concatenate(
            [
                rows_of(cot_ref, dst_ref[t], block).astype(F32)
                * jnp.where(t < count_ref[0], 1.0, 0.0)
                for t in range(first, first + group)
            ],
            axis=0,
        )
        out_ref[rows, :] = (dot_t(gpre_ref[rows, :], win_ref[:latent, :]) + upstream).astype(BF16)
        for t in range(first, first + group):
            live = jnp.where(t < count_ref[0], 1.0, 0.0)
            mine = slice(t * block, (t + 1) * block)
            updated = edge_ref[mine, :].astype(F32) + message_ref[mine, :]
            target = pl.ds(pl.multiple_of(dst_ref[t] * block, block), block)
            agg_ref[target, :] += updated * live
    agg_out[...] = agg_ref[...].astype(BF16)


def halve_kernel(bit, came_ref, kept_ref, after, away_ref, left_ref):
    mine = (lax.axis_index("dp") // bit) % 2
    for slot in range(left_ref.shape[0]):
        there, here = 2 * slot + 1 - mine, 2 * slot + mine
        away_ref[slot] = (kept_ref[there] + came_ref[there].astype(F32)).astype(BF16)
        left_ref[slot] = kept_ref[here] + came_ref[here].astype(F32)


def quarter_kernel(came_ref, kept_ref, after, cross_ref, over_ref, beside_ref, left_ref):
    part = lax.axis_index("dom")
    mine = lax.axis_index("dp") // 2
    inner = (part == 1) | (part == 2)
    rows = left_ref.shape[0]
    here = pl.ds(pl.multiple_of(jnp.where(inner, 0, rows), rows), rows)
    there = pl.ds(pl.multiple_of(jnp.where(inner, rows, 0), rows), rows)

    def total(slot, where):
        return kept_ref[slot, where, :] + came_ref[slot, where, :].astype(F32)

    cross_ref[...] = total(1 - mine, there).astype(BF16)
    over_ref[...] = total(1 - mine, here).astype(BF16)
    beside_ref[...] = total(mine, there).astype(BF16)
    left_ref[...] = total(mine, here)


def add_kernel(left_ref, cross_ref, over_ref, beside_ref, *refs):
    out_ref = refs[-1]
    terms = [ref[...].astype(F32) for ref in (cross_ref, over_ref, beside_ref)]
    out_ref[...] = ((left_ref[...] + terms[1]) + (terms[0] + terms[2])).astype(BF16)


def node_grad_kernel(arrivals, four, boundary_hbm, after, sums_ref, win_ref, *refs):
    returned = refs[:arrivals]
    out_ref, total_ref, boundary_ref, sem = refs[arrivals:]
    nodes, latent = out_ref.shape
    extent = sums_ref.shape[0] - nodes
    block = returned[0].shape[0]
    copy = load_small(boundary_hbm, boundary_ref, sem)
    total_ref[...] = sums_ref[:nodes, :]
    copy.wait()
    for which, place in enumerate(boundary_places(boundary_ref, lax.axis_index("dom"), four)):
        spot = pl.ds(pl.multiple_of(place * block, block), block)
        total_ref[spot, :] += returned[which][...].astype(F32)

    def wide_dot(value, weight):
        high = value.astype(BF16)
        low = (value - high.astype(F32)).astype(BF16)
        return dot_t(high, weight) + dot_t(low, weight)

    out_ref[...] = (
        wide_dot(total_ref[...], win_ref[latent : 2 * latent, :])
        + wide_dot(sums_ref[extent:, :], win_ref[2 * latent :, :])
    ).astype(BF16)


def last_kernel(after, own_a, other_a, own_b, other_b, in_ref, out_ref):
    unit = out_ref.shape[0]
    part = lax.axis_index("dom")
    inner = (part == 1) | (part == 2)

    def write(low_a, high_a, low_b, high_b):
        out_ref[...] = low_a[...].astype(F32)
        in_ref[:unit, :] = high_a[...].astype(F32)
        in_ref[unit : 2 * unit, :] = low_b[...].astype(F32)
        in_ref[2 * unit :, :] = high_b[...].astype(F32)

    @pl.when(inner)
    def _():
        write(own_a, other_a, own_b, other_b)

    @pl.when(jnp.logical_not(inner))
    def _():
        write(other_a, own_a, other_b, own_b)


def swap(array, axis, partner):
    devices = lax.axis_size(axis)
    return lax.ppermute(array, axis, [(i, partner(i)) for i in range(devices)])


def from_behind(array, axis, by):
    devices = lax.axis_size(axis)
    pairs = [(i, i + by) for i in range(devices) if 0 <= i + by < devices]
    return lax.ppermute(array, axis, pairs)


def partners_of_four(which):
    return ((1, 0, 3, 2), (0, 2, 1, 3), (2, 3, 0, 1))[which]


def exchange_of_four(first, second, third):
    third = swap(third, "dom", lambda i: partners_of_four(2)[i])
    second = swap(second, "dom", lambda i: partners_of_four(1)[i])
    first = swap(first, "dom", lambda i: partners_of_four(0)[i])
    return [first, second, third]


def halve(bit, came, kept, after):
    slots, rows, latent = kept.shape
    return pl.pallas_call(
        functools.partial(halve_kernel, bit),
        out_shape=(
            pltpu.VMEM((slots // 2, rows, latent), BF16),
            pltpu.VMEM((slots // 2, rows, latent), F32),
        ),
        in_specs=[VMEM] * 3,
        out_specs=(VMEM,) * 2,
        compiler_params=pltpu.CompilerParams(vmem_limit_bytes=4 * 1024 * 1024),
        cost_estimate=pl.CostEstimate(flops=0, bytes_accessed=500_000, transcendentals=0),
        name="halve",
    )(in_vmem(came), in_vmem(kept), in_vmem(after))


def sum_over_dp(away, kept, after):
    devices = lax.axis_size("dp")
    bit = 1
    while True:
        came = swap(away, "dp", lambda i, bit=bit: i ^ bit)
        bit *= 2
        if bit >= devices:
            return came, kept, away
        away, kept = halve(bit, came, kept, after)


def sum_of_square(away, kept, after):
    slots, rows, latent = kept.shape
    came = swap(away, "dp", lambda i: i ^ 1)
    piece = pltpu.VMEM((rows // 2, latent), BF16)
    limit = pltpu.CompilerParams(vmem_limit_bytes=4 * 1024 * 1024)
    cost = pl.CostEstimate(flops=0, bytes_accessed=500_000, transcendentals=0)
    cross, over, beside, left = pl.pallas_call(
        quarter_kernel,
        out_shape=(piece, piece, piece, pltpu.VMEM((rows // 2, latent), F32)),
        in_specs=[VMEM] * 3,
        out_specs=(VMEM,) * 4,
        compiler_params=limit,
        cost_estimate=cost,
        name="quarter",
    )(in_vmem(came), in_vmem(kept), in_vmem(after))
    ways = lax.axis_size("dp")
    parts = lax.axis_size("dom")
    diagonal = [
        (d * ways + p, (d ^ 1) * ways + (p ^ 2)) for d in range(parts) for p in range(ways)
    ]
    arrived = [
        lax.ppermute(cross, ("dom", "dp"), diagonal),
        swap(over, "dp", lambda i: i ^ 2),
        swap(beside, "dom", lambda i: i ^ 1),
    ]

    def finish(*late):
        return pl.pallas_call(
            add_kernel,
            out_shape=piece,
            in_specs=[VMEM] * (4 + len(late)),
            out_specs=VMEM,
            compiler_params=limit,
            cost_estimate=cost,
            name="add_terms",
        )(*[in_vmem(array) for array in (left, *arrived, *late)])

    return cross, finish


def sum_of_four(kept):
    kept = (kept.astype(F32) + swap(kept, "dom", lambda i: 3 - i).astype(F32)).astype(BF16)
    return kept, swap(kept, "dom", lambda i: i ^ 1)


def sum_over_dom(rows):
    piece = lax.psum_scatter(rows, "dom", scatter_dimension=0, tiled=True)
    return lax.all_gather(piece, "dom", axis=0, tiled=True)


def in_vmem(array):
    return pltpu.with_memory_space_constraint(array, pltpu.VMEM)


def in_hbm(array):
    return pltpu.with_memory_space_constraint(array, pltpu.HBM)


def body(
    node_latents,
    edge_latents,
    agg_cotangent,
    weight_in,
    weight_out,
    boundary,
    tile_src,
    tile_dst,
    edge_slot,
    tile_count,
):
    tiles, block = edge_slot.shape
    edges, latent = edge_latents.shape[1:]
    nodes = node_latents.shape[1]
    parts = lax.axis_size("dom")
    ways = lax.axis_size("dp")
    four = parts == 4 and ways == 4
    arrivals = 3 if four else 4
    boundary = in_hbm(boundary)
    tile_dst = in_hbm(tile_dst)
    node_rows = in_hbm(node_latents[0])
    block_shape = pltpu.VMEM((block, latent), BF16)
    small = pltpu.CompilerParams(vmem_limit_bytes=8 * 1024 * 1024)

    sent = pl.pallas_call(
        functools.partial(pick_kernel, four, block),
        out_shape=(block_shape,) * arrivals,
        in_specs=[HBM] * 2,
        out_specs=(VMEM,) * arrivals,
        scratch_shapes=[
            pltpu.SMEM(boundary.shape, jnp.int32),
            pltpu.SemaphoreType.DMA,
            pltpu.SemaphoreType.DMA((arrivals,)),
        ],
        compiler_params=small,
        cost_estimate=pl.CostEstimate(flops=0, bytes_accessed=400_000, transcendentals=0),
        name="pick_blocks",
    )(boundary, node_rows)
    if four:
        came = exchange_of_four(*sent)
    else:
        came = [from_behind(sent[which], "dom", OFFSET_LIST[which]) for which in range(4)]
    unit = latent // ways
    half = ways // 2
    extent = -(-(nodes + arrivals * block) // 128) * 128

    node_v, edge_v, cot_v, win_v, wout_v, pre, up, hot, turned = pl.pallas_call(
        functools.partial(prep_kernel, parts, arrivals),
        out_shape=(
            pltpu.VMEM((nodes, latent), BF16),
            pltpu.VMEM((edges, latent), BF16),
            pltpu.VMEM((nodes, latent), BF16),
            pltpu.VMEM(weight_in.shape, BF16),
            pltpu.VMEM(weight_out.shape, BF16),
            pltpu.VMEM((edges, latent), F32),
            pltpu.VMEM((edges, latent), F32),
            pltpu.VMEM((edges, extent), BF16),
            pltpu.VMEM((extent + nodes, edges), BF16),
        ),
        in_specs=[SMEM] + [HBM] * 8,
        out_specs=(VMEM,) * 9,
        scratch_shapes=[
            pltpu.SMEM((tiles,), jnp.int32),
            pltpu.SMEM((tiles,), jnp.int32),
            pltpu.VMEM((tiles, block), jnp.int32),
            pltpu.VMEM((nodes, latent), F32),
            pltpu.VMEM((nodes, latent), F32),
            pltpu.SemaphoreType.DMA((10,)),
        ],
        compiler_params=small,
        cost_estimate=pl.CostEstimate(
            flops=2 * edges * latent * latent, bytes_accessed=8_000_000, transcendentals=0
        ),
        name="prepare",
    )(
        tile_count,
        in_hbm(tile_src),
        tile_dst,
        in_hbm(edge_slot),
        node_rows,
        in_hbm(edge_latents[0]),
        in_hbm(agg_cotangent[0]),
        in_hbm(weight_in),
        in_hbm(weight_out),
    )
    sent_shape = pltpu.VMEM((half, 2 * unit, latent), BF16)
    kept_shape = pltpu.VMEM((half, 2 * unit, latent), F32)
    grad_pre, message, sums, ext, away_a, kept_a = pl.pallas_call(
        functools.partial(edge_kernel, ways, arrivals, four, block),
        out_shape=(
            pltpu.VMEM((edges, latent), BF16),
            pltpu.VMEM((edges, latent), F32),
            pltpu.VMEM((extent + nodes, latent), F32),
            pltpu.VMEM((extent, latent), BF16),
            sent_shape,
            kept_shape,
        ),
        in_specs=[VMEM] * (8 + arrivals),
        out_specs=(VMEM,) * 6,
        scratch_shapes=[
            pltpu.VMEM((edges, latent), BF16),
            pltpu.VMEM((edges, latent), BF16),
        ],
        compiler_params=pltpu.CompilerParams(vmem_limit_bytes=16 * 1024 * 1024),
        cost_estimate=pl.CostEstimate(
            flops=12 * edges * latent * latent,
            bytes_accessed=12_000_000,
            transcendentals=edges * latent,
        ),
        name="edge_block",
    )(
        *[
            in_vmem(array)
            for array in (*came, node_v, edge_v, win_v, wout_v, pre, up, hot, turned)
        ],
    )
    away_b, kept_b = pl.pallas_call(
        functools.partial(rest_kernel, ways),
        out_shape=(sent_shape, kept_shape),
        in_specs=[VMEM] * 5,
        out_specs=(VMEM,) * 2,
        compiler_params=small,
        cost_estimate=pl.CostEstimate(
            flops=2 * edges * latent * latent, bytes_accessed=4_000_000, transcendentals=0
        ),
        name="rest_weights",
    )(*[in_vmem(array) for array in (node_v, edge_v, ext, grad_pre, sums)])
    if four:
        sent_a, finish_a = sum_of_square(away_a, kept_a, cot_v)
    else:
        came_a, kept_a, sent_a = sum_over_dp(away_a, kept_a, cot_v)
    edge_grad, agg, *back_sums = pl.pallas_call(
        functools.partial(edge_grad_kernel, block, arrivals, four),
        out_shape=(
            jax.ShapeDtypeStruct((edges, latent), BF16),
            jax.ShapeDtypeStruct((nodes, latent), BF16),
        )
        + (block_shape,) * arrivals,
        in_specs=[HBM, SMEM] + [VMEM] * 7,
        out_specs=(VMEM,) * (2 + arrivals),
        scratch_shapes=[
            pltpu.SMEM((tiles,), jnp.int32),
            pltpu.VMEM((nodes, latent), F32),
            pltpu.SemaphoreType.DMA,
        ],
        compiler_params=small,
        cost_estimate=pl.CostEstimate(
            flops=2 * edges * latent * latent, bytes_accessed=3_000_000, transcendentals=0
        ),
        name="edge_grads",
    )(
        tile_dst,
        tile_count,
        *[in_vmem(array) for array in (sent_a, grad_pre, sums, cot_v, win_v, edge_v, message)],
    )
    if four:
        returned = exchange_of_four(*back_sums)
        _, finish_b = sum_of_square(away_b, kept_b, back_sums[0])
        pair_a = finish_a()
        pair_b = finish_b(*returned)
        late = pair_b
    else:
        returned = [
            from_behind(back_sums[which], "dom", -OFFSET_LIST[which]) for which in range(4)
        ]
        came_b, kept_b, _ = sum_over_dp(away_b, kept_b, back_sums[0])
        late = sent_a
    node_out = pl.pallas_call(
        functools.partial(node_grad_kernel, arrivals, four),
        out_shape=jax.ShapeDtypeStruct((nodes, latent), BF16),
        in_specs=[HBM] + [VMEM] * (3 + arrivals),
        out_specs=VMEM,
        scratch_shapes=[
            pltpu.VMEM((nodes, latent), F32),
            pltpu.SMEM(boundary.shape, jnp.int32),
            pltpu.SemaphoreType.DMA,
        ],
        compiler_params=small,
        cost_estimate=pl.CostEstimate(
            flops=8 * nodes * latent * latent, bytes_accessed=2_000_000, transcendentals=0
        ),
        name="node_grads",
    )(boundary, *[in_vmem(array) for array in (late, sums, win_v, *returned)])
    if four:
        w_in_grad, w_out_grad = pl.pallas_call(
            last_kernel,
            out_shape=(
                jax.ShapeDtypeStruct((3 * unit, latent), F32),
                jax.ShapeDtypeStruct((unit, latent), F32),
            ),
            in_specs=[HBM] + [VMEM] * 4,
            out_specs=(VMEM,) * 2,
            compiler_params=small,
            cost_estimate=pl.CostEstimate(flops=0, bytes_accessed=1_500_000, transcendentals=0),
            name="widen",
        )(in_hbm(node_out), *sum_of_four(pair_a), *sum_of_four(pair_b))
    else:
        sum_a = sum_over_dom(kept_a[0] + came_a[0].astype(F32))
        sum_b = sum_over_dom(kept_b[0] + came_b[0].astype(F32))
        w_in_grad = jnp.concatenate([sum_a[unit:], sum_b], axis=0)
        w_out_grad = sum_a[:unit]
    return (agg[None], edge_grad[None], node_out[None], w_in_grad, w_out_grad)


def solution(mesh):
    in_specs = (
        P(("group", "dp"), "dom", None),
        P(("group", "dp"), "dom", None),
        P(("group", "dp"), "dom", None),
        P(),
        P(),
        P(("group", "dom"), None),
        P(("group", "dom")),
        P(("group", "dom")),
        P(("group", "dom"), None),
        P(("group", "dom")),
    )
    out_specs = (
        P(("group", "dp"), "dom", None),
        P(("group", "dp"), "dom", None),
        P(("group", "dp"), "dom", None),
        P(("group", "dp"), None),
        P(("group", "dp"), None),
    )
    return jax.shard_map(body, mesh=mesh, in_specs=in_specs, out_specs=out_specs, check_vma=False)
```

```python
import functools

import jax
import jax.numpy as jnp
from jax import lax
from jax.experimental import pallas as pl
from jax.experimental.pallas import tpu as pltpu
from jax.sharding import PartitionSpec as P

OFFSET_LIST = (1, -1, 2, -2)
EPSILON = 1e-05
VMEM = pl.BlockSpec(memory_space=pltpu.VMEM)
HBM = pl.BlockSpec(memory_space=pltpu.HBM)
SMEM = pl.BlockSpec(memory_space=pltpu.SMEM)
ANY = pl.BlockSpec(memory_space=pl.ANY)
F32 = jnp.float32
BF16 = jnp.bfloat16


def dot(left, right):
    return jnp.dot(left, right, preferred_element_type=F32)


def dot_t(left, right):
    return lax.dot_general(left, right, (((1,), (1,)), ((), ())), preferred_element_type=F32)


def t_dot(left, right):
    return lax.dot_general(left, right, (((0,), (0,)), ((), ())), preferred_element_type=F32)


def row_mean(array):
    return jnp.sum(array, axis=1, keepdims=True) * (1.0 / array.shape[1])


def rows_of(ref, block, size):
    return ref[pl.ds(pl.multiple_of(block * size, size), size), :]


def load_small(source, target, sem):
    copy = pltpu.make_async_copy(source, target, sem)
    copy.start()
    return copy


def boundary_places(boundary_ref, part, four):
    taken = [boundary_ref[0, which] for which in range(4)]
    if not four:
        return taken
    even = part % 2 == 0
    return [
        jnp.where(even, taken[0], taken[1]),
        jnp.where(even, taken[1], taken[0]),
        jnp.where(part < 2, taken[2], taken[3]),
    ]


def arrival_places(part, four, arrivals):
    if not four:
        return list(range(arrivals))
    even = part % 2 == 0
    return [jnp.where(even, 1, 0), jnp.where(even, 0, 1), 2]


def pick_kernel(four, block, boundary_hbm, node_hbm, *refs):
    count = 3 if four else 4
    outs = refs[:count]
    boundary_ref, small_sem, sems = refs[count:]
    load_small(boundary_hbm, boundary_ref, small_sem).wait()
    copies = []
    for which, place in enumerate(boundary_places(boundary_ref, lax.axis_index("dom"), four)):
        spot = pl.ds(pl.multiple_of(place * block, block), block)
        copies.append(pltpu.make_async_copy(node_hbm.at[spot, :], outs[which], sems.at[which]))
        copies[-1].start()
    for copy in copies:
        copy.wait()


def prep_kernel(
    parts,
    arrivals,
    count_ref,
    src_hbm,
    dst_hbm,
    slot_hbm,
    node_hbm,
    edge_hbm,
    cot_hbm,
    win_hbm,
    wout_hbm,
    node_ref,
    edge_ref,
    cot_ref,
    win_ref,
    wout_ref,
    pre_ref,
    up_ref,
    hot_ref,
    hot_turned,
    src_ref,
    dst_ref,
    slot_ref,
    recv_ref,
    mid_ref,
    sems,
):
    tiles, block = slot_ref.shape
    nodes, latent = node_ref.shape
    owned = nodes // block
    extent = hot_ref.shape[1]
    pairs = (
        (src_hbm, src_ref),
        (dst_hbm, dst_ref),
        (slot_hbm, slot_ref),
        (node_hbm, node_ref),
        (win_hbm.at[2 * latent :, :], win_ref.at[2 * latent :, :]),
        (win_hbm.at[:latent, :], win_ref.at[:latent, :]),
        (edge_hbm, edge_ref),
        (cot_hbm, cot_ref),
        (win_hbm.at[latent : 2 * latent, :], win_ref.at[latent : 2 * latent, :]),
        (wout_hbm, wout_ref),
    )
    copies = [load_small(*pair, sems.at[number]) for number, pair in enumerate(pairs)]
    part = lax.axis_index("dom")
    for copy in copies[:3]:
        copy.wait()
    index = lax.broadcasted_iota(jnp.int32, (extent, 2 * block), 0)
    lane = lax.broadcasted_iota(jnp.int32, (1, 2 * block), 1)
    first = lane < block
    within = jnp.where(first, lane, lane - block)
    node_index = lax.broadcasted_iota(jnp.int32, (nodes, 2 * block), 0)
    for tile in range(0, tiles, 2):
        wanted = []
        for member in (tile, tile + 1):
            source = src_ref[member]
            which = source - owned
            reach = jnp.where(which >= 2, 2, 1)
            partner = part - jnp.where(which % 2 == 1, -reach, reach)
            exists = (source < owned) | ((partner >= 0) & (partner < parts))
            place = jnp.minimum(source, owned + arrivals - 1)
            wanted.append(jnp.where(exists, place * block, -2 * extent))
        slots = jnp.concatenate(
            [slot_ref[tile : tile + 1, :], slot_ref[tile + 1 : tile + 2, :]], axis=1
        )
        row = slots + jnp.where(first, wanted[0], wanted[1])
        hot = jnp.where(index == row, 1.0, 0.0)
        at = slice(tile * block, (tile + 2) * block)
        hot_turned[:extent, at] = hot.astype(BF16)
        target = within + jnp.where(first, dst_ref[tile] * block, dst_ref[tile + 1] * block)
        hot_turned[extent:, at] = jnp.where(node_index == target, 1.0, 0.0).astype(BF16)
        hot_ref[at, :] = hot.T.astype(BF16)
    copies[3].wait()
    copies[4].wait()
    recv_ref[...] = dot(node_ref[...], win_ref[2 * latent :, :])
    copies[5].wait()
    copies[6].wait()
    group = 4 if tiles % 4 == 0 else 2
    for tile in range(0, tiles, group):
        rows = slice(tile * block, (tile + group) * block)
        received = jnp.concatenate(
            [rows_of(recv_ref, dst_ref[t], block) for t in range(tile, tile + group)], axis=0
        )
        pre_ref[rows, :] = dot(edge_ref[rows, :], win_ref[:latent, :]) + received
    copies[7].wait()
    cot = cot_ref[...].astype(F32)
    mid_ref[...] = cot - row_mean(cot)
    for tile in range(tiles):
        live = jnp.where(tile < count_ref[0], 1.0, 0.0)
        up_ref[tile * block : (tile + 1) * block, :] = rows_of(mid_ref, dst_ref[tile], block) * live
    copies[8].wait()
    copies[9].wait()


def put_units(chunk, ways, bit, away, kept, sections):
    latent = sections[0][0].shape[1]
    unit = latent // ways
    step = 128

    def wanted(number, start):
        if number == 0:
            return [(start + at) // unit for at in range(0, step, unit)] if chunk == 0 else []
        found = []
        for at in range(0, step, unit):
            spot = ((number - 1) * latent + start + at) // unit
            if (1 + spot % 3) // 2 == chunk:
                found.append(spot)
        return found

    for number, (left, right) in enumerate(sections):
        value_right = right()
        start = 0
        while start < latent:
            size = step
            if start + 2 * step <= latent and wanted(number, start + step):
                size = 2 * step
            if wanted(number, start):
                value = t_dot(left[:, start : start + size], value_right)
                for at in range(0, size, unit):
                    if number == 0:
                        owner, spot = (start + at) // unit, 0
                    else:
                        place = ((number - 1) * latent + start + at) // unit
                        owner, spot = place // 3, 1 + place % 3
                    if spot // 2 != chunk:
                        continue
                    part = value[at : at + unit]
                    where = slice((spot % 2) * unit, (spot % 2 + 1) * unit)

                    @pl.when(bit == owner % 2)
                    def _(owner=owner, where=where, part=part):
                        kept[owner // 2, where, :] = part

                    @pl.when(bit != owner % 2)
                    def _(owner=owner, where=where, part=part):
                        away[owner // 2, where, :] = part.astype(BF16)

                start += size
            else:
                start += step


def edge_kernel(ways, arrivals, four, block, *refs):
    arrived = refs[:arrivals]
    (
        node_ref,
        edge_ref,
        win_ref,
        wout_ref,
        pre_ref,
        up_ref,
        hot_ref,
        hot_turned,
        gpre_ref,
        message_ref,
        sums_ref,
        ext_ref,
        away_ref,
        kept_ref,
        act_ref,
        proj_ref,
    ) = refs[arrivals:]
    nodes, latent = node_ref.shape
    edges = edge_ref.shape[0]
    extent = ext_ref.shape[0]
    places = arrival_places(lax.axis_index("dom"), four, arrivals)

    ext_ref[:nodes, :] = node_ref[...]
    for which in range(arrivals):
        at = pl.multiple_of(nodes + places[which] * block, block)
        ext_ref[pl.ds(at, block), :] = arrived[which][...]
    filled = nodes + arrivals * block
    if filled < extent:
        ext_ref[filled:, :] = jnp.zeros((extent - filled, latent), BF16)

    span = 256 if edges % 256 == 0 else block
    for start in range(0, edges, span):
        rows = slice(start, start + span)
        senders = dot(hot_ref[rows, :], ext_ref[...]).astype(BF16)
        preact = pre_ref[rows, :] + dot(senders, win_ref[latent : 2 * latent, :])
        gate = 0.5 * jnp.tanh(0.5 * preact) + 0.5
        activated = preact * gate
        slope = gate + activated * (1.0 - gate)
        activated = activated.astype(BF16)
        act_ref[rows, :] = activated
        projected = dot(activated, wout_ref[...])
        centered = projected - row_mean(projected)
        inv_scale = lax.rsqrt(row_mean(centered * centered) + EPSILON)
        message = centered * inv_scale
        message_ref[rows, :] = message
        upstream = up_ref[rows, :]
        grad_project = inv_scale * (upstream - message * row_mean(upstream * message))
        grad_project = grad_project.astype(BF16)
        proj_ref[rows, :] = grad_project
        gpre_ref[rows, :] = (dot_t(grad_project, wout_ref[...]) * slope).astype(BF16)

    sums_ref[...] = dot(hot_turned[...], gpre_ref[...])
    sections = (
        (act_ref, lambda: proj_ref[...]),
        (edge_ref, lambda: gpre_ref[...]),
        (ext_ref, lambda: sums_ref[:extent, :].astype(BF16)),
        (node_ref, lambda: sums_ref[extent:, :].astype(BF16)),
    )
    put_units(0, ways, lax.axis_index("dp") % 2, away_ref, kept_ref, sections)


def rest_kernel(ways, node_ref, edge_ref, ext_ref, gpre_ref, sums_ref, away_ref, kept_ref):
    extent = ext_ref.shape[0]
    sections = (
        (edge_ref, lambda: None),
        (edge_ref, lambda: gpre_ref[...]),
        (ext_ref, lambda: sums_ref[:extent, :].astype(BF16)),
        (node_ref, lambda: sums_ref[extent:, :].astype(BF16)),
    )
    put_units(1, ways, lax.axis_index("dp") % 2, away_ref, kept_ref, sections)


def edge_grad_kernel(
    block,
    arrivals,
    four,
    dst_hbm,
    count_ref,
    after,
    gpre_ref,
    sums_ref,
    cot_ref,
    win_ref,
    edge_ref,
    message_ref,
    out_ref,
    agg_out,
    *refs,
):
    back_sums = refs[:-3]
    dst_ref, agg_ref, sem = refs[-3:]
    copy = load_small(dst_hbm, dst_ref, sem)
    nodes, latent = cot_ref.shape
    tiles = gpre_ref.shape[0] // block
    group = 4 if tiles % 4 == 0 else 1
    places = arrival_places(lax.axis_index("dom"), four, arrivals)[-len(back_sums) :]
    for place, back_ref in zip(places, back_sums):
        at = pl.multiple_of(nodes + place * block, block)
        back_ref[...] = sums_ref[pl.ds(at, block), :].astype(BF16)
    agg_ref[...] = jnp.zeros_like(agg_ref)
    copy.wait()
    for first in range(0, tiles, group):
        rows = slice(first * block, (first + group) * block)
        upstream = jnp.concatenate(
            [
                rows_of(cot_ref, dst_ref[t], block).astype(F32)
                * jnp.where(t < count_ref[0], 1.0, 0.0)
                for t in range(first, first + group)
            ],
            axis=0,
        )
        out_ref[rows, :] = (dot_t(gpre_ref[rows, :], win_ref[:latent, :]) + upstream).astype(BF16)
        for t in range(first, first + group):
            live = jnp.where(t < count_ref[0], 1.0, 0.0)
            mine = slice(t * block, (t + 1) * block)
            updated = edge_ref[mine, :].astype(F32) + message_ref[mine, :]
            target = pl.ds(pl.multiple_of(dst_ref[t] * block, block), block)
            agg_ref[target, :] += updated * live
    agg_out[...] = agg_ref[...].astype(BF16)


def halve_kernel(bit, came_ref, kept_ref, after, away_ref, left_ref):
    mine = (lax.axis_index("dp") // bit) % 2
    for slot in range(left_ref.shape[0]):
        there, here = 2 * slot + 1 - mine, 2 * slot + mine
        away_ref[slot] = (kept_ref[there] + came_ref[there].astype(F32)).astype(BF16)
        left_ref[slot] = kept_ref[here] + came_ref[here].astype(F32)


def quarter_kernel(
    nodes,
    block,
    came_a,
    kept_a,
    came_b,
    kept_b,
    sums_ref,
    cross_ref,
    over_ref,
    beside_ref,
    left_ref,
):
    part = lax.axis_index("dom")
    mine = lax.axis_index("dp") // 2
    inner = (part == 1) | (part == 2)
    rows = left_ref.shape[0] // 2
    here = pl.ds(pl.multiple_of(jnp.where(inner, 0, rows), rows), rows)
    there = pl.ds(pl.multiple_of(jnp.where(inner, rows, 0), rows), rows)
    for number, (came_ref, kept_ref) in enumerate(((came_a, kept_a), (came_b, kept_b))):
        spot = slice(number * rows, (number + 1) * rows)

        def total(slot, where, came_ref=came_ref, kept_ref=kept_ref):
            return kept_ref[slot, where, :] + came_ref[slot, where, :].astype(F32)

        cross_ref[spot, :] = total(1 - mine, there).astype(BF16)
        over_ref[spot, :] = total(1 - mine, here).astype(BF16)
        beside_ref[spot, :] = total(mine, there).astype(BF16)
        left_ref[spot, :] = total(mine, here)
    place = arrival_places(part, True, 3)[0]
    back = pl.ds(pl.multiple_of(nodes + place * block, block), block)
    beside_ref[2 * rows :, :] = sums_ref[back, :].astype(BF16)


def add_kernel(left_ref, cross_ref, over_ref, beside_ref, *refs):
    out_refs = refs[-2:]
    rows = out_refs[0].shape[0]
    for number, out_ref in enumerate(out_refs):
        spot = slice(number * rows, (number + 1) * rows)
        terms = [ref[spot, :].astype(F32) for ref in (cross_ref, over_ref, beside_ref)]
        out_ref[...] = ((left_ref[spot, :] + terms[1]) + (terms[0] + terms[2])).astype(BF16)


def node_grad_kernel(arrivals, four, boundary_hbm, after, sums_ref, win_ref, *refs):
    returned = refs[:arrivals]
    out_ref, total_ref, boundary_ref, sem = refs[arrivals:]
    nodes, latent = out_ref.shape
    extent = sums_ref.shape[0] - nodes
    block = returned[-1].shape[0]
    copy = load_small(boundary_hbm, boundary_ref, sem)
    total_ref[...] = sums_ref[:nodes, :]
    copy.wait()
    for which, place in enumerate(boundary_places(boundary_ref, lax.axis_index("dom"), four)):
        spot = pl.ds(pl.multiple_of(place * block, block), block)
        total_ref[spot, :] += returned[which][-block:, :].astype(F32)

    def wide_dot(value, weight):
        high = value.astype(BF16)
        low = (value - high.astype(F32)).astype(BF16)
        return dot_t(high, weight) + dot_t(low, weight)

    out_ref[...] = (
        wide_dot(total_ref[...], win_ref[latent : 2 * latent, :])
        + wide_dot(sums_ref[extent:, :], win_ref[2 * latent :, :])
    ).astype(BF16)


def last_kernel(after, own_a, other_a, own_b, other_b, in_ref, out_ref):
    unit = out_ref.shape[0]
    part = lax.axis_index("dom")
    inner = (part == 1) | (part == 2)

    def write(low_a, high_a, low_b, high_b):
        out_ref[...] = low_a[...].astype(F32)
        in_ref[:unit, :] = high_a[...].astype(F32)
        in_ref[unit : 2 * unit, :] = low_b[...].astype(F32)
        in_ref[2 * unit :, :] = high_b[...].astype(F32)

    @pl.when(inner)
    def _():
        write(own_a, other_a, own_b, other_b)

    @pl.when(jnp.logical_not(inner))
    def _():
        write(other_a, own_a, other_b, own_b)


def swap(array, axis, partner):
    devices = lax.axis_size(axis)
    return lax.ppermute(array, axis, [(i, partner(i)) for i in range(devices)])


def from_behind(array, axis, by):
    devices = lax.axis_size(axis)
    pairs = [(i, i + by) for i in range(devices) if 0 <= i + by < devices]
    return lax.ppermute(array, axis, pairs)


def partners_of_four(which):
    return ((1, 0, 3, 2), (0, 2, 1, 3), (2, 3, 0, 1))[which]


def exchange_of_four(first, second, third):
    third = swap(third, "dom", lambda i: partners_of_four(2)[i])
    second = swap(second, "dom", lambda i: partners_of_four(1)[i])
    first = swap(first, "dom", lambda i: partners_of_four(0)[i])
    return [first, second, third]


def halve(bit, came, kept, after):
    slots, rows, latent = kept.shape
    return pl.pallas_call(
        functools.partial(halve_kernel, bit),
        out_shape=(
            pltpu.VMEM((slots // 2, rows, latent), BF16),
            pltpu.VMEM((slots // 2, rows, latent), F32),
        ),
        in_specs=[VMEM] * 3,
        out_specs=(VMEM,) * 2,
        compiler_params=pltpu.CompilerParams(vmem_limit_bytes=4 * 1024 * 1024),
        cost_estimate=pl.CostEstimate(flops=0, bytes_accessed=500_000, transcendentals=0),
        name="halve",
    )(in_vmem(came), in_vmem(kept), in_vmem(after))


def sum_over_dp(away, kept, after):
    devices = lax.axis_size("dp")
    bit = 1
    while True:
        came = swap(away, "dp", lambda i, bit=bit: i ^ bit)
        bit *= 2
        if bit >= devices:
            return came, kept, away
        away, kept = halve(bit, came, kept, after)


def sum_of_square(nodes, block, chunks, sums):
    slots, rows, latent = chunks[0][1].shape
    operands = []
    for away, kept in chunks:
        operands += [swap(away, "dp", lambda i: i ^ 1), kept]
    limit = pltpu.CompilerParams(vmem_limit_bytes=4 * 1024 * 1024)
    cost = pl.CostEstimate(flops=0, bytes_accessed=500_000, transcendentals=0)
    cross, over, beside, left = pl.pallas_call(
        functools.partial(quarter_kernel, nodes, block),
        out_shape=(
            pltpu.VMEM((rows, latent), BF16),
            pltpu.VMEM((rows, latent), BF16),
            pltpu.VMEM((rows + block, latent), BF16),
            pltpu.VMEM((rows, latent), F32),
        ),
        in_specs=[VMEM] * 5,
        out_specs=(VMEM,) * 4,
        compiler_params=limit,
        cost_estimate=cost,
        name="quarter",
    )(*[in_vmem(array) for array in (*operands, sums)])
    ways = lax.axis_size("dp")
    parts = lax.axis_size("dom")
    diagonal = [
        (d * ways + p, (d ^ 1) * ways + (p ^ 2)) for d in range(parts) for p in range(ways)
    ]
    arrived = [
        lax.ppermute(cross, ("dom", "dp"), diagonal),
        swap(over, "dp", lambda i: i ^ 2),
        swap(beside, "dom", lambda i: i ^ 1),
    ]

    def finish(*late):
        return pl.pallas_call(
            add_kernel,
            out_shape=(pltpu.VMEM((rows // 2, latent), BF16),) * 2,
            in_specs=[VMEM] * (4 + len(late)),
            out_specs=(VMEM,) * 2,
            compiler_params=limit,
            cost_estimate=cost,
            name="add_terms",
        )(*[in_vmem(array) for array in (left, *arrived, *late)])

    return cross, arrived[2], finish


def sum_of_four(kept):
    kept = (kept.astype(F32) + swap(kept, "dom", lambda i: 3 - i).astype(F32)).astype(BF16)
    return kept, swap(kept, "dom", lambda i: i ^ 1)


def sum_over_dom(rows):
    piece = lax.psum_scatter(rows, "dom", scatter_dimension=0, tiled=True)
    return lax.all_gather(piece, "dom", axis=0, tiled=True)


def in_vmem(array):
    return pltpu.with_memory_space_constraint(array, pltpu.VMEM)


def in_hbm(array):
    return pltpu.with_memory_space_constraint(array, pltpu.HBM)


def body(
    node_latents,
    edge_latents,
    agg_cotangent,
    weight_in,
    weight_out,
    boundary,
    tile_src,
    tile_dst,
    edge_slot,
    tile_count,
):
    tiles, block = edge_slot.shape
    edges, latent = edge_latents.shape[1:]
    nodes = node_latents.shape[1]
    parts = lax.axis_size("dom")
    ways = lax.axis_size("dp")
    four = parts == 4 and ways == 4
    arrivals = 3 if four else 4
    boundary = in_hbm(boundary)
    tile_dst = in_hbm(tile_dst)
    node_rows = in_hbm(node_latents[0])
    block_shape = pltpu.VMEM((block, latent), BF16)
    small = pltpu.CompilerParams(vmem_limit_bytes=8 * 1024 * 1024)

    sent = pl.pallas_call(
        functools.partial(pick_kernel, four, block),
        out_shape=(block_shape,) * arrivals,
        in_specs=[HBM] * 2,
        out_specs=(VMEM,) * arrivals,
        scratch_shapes=[
            pltpu.SMEM(boundary.shape, jnp.int32),
            pltpu.SemaphoreType.DMA,
            pltpu.SemaphoreType.DMA((arrivals,)),
        ],
        compiler_params=small,
        cost_estimate=pl.CostEstimate(flops=0, bytes_accessed=400_000, transcendentals=0),
        name="pick_blocks",
    )(boundary, node_rows)
    if four:
        came = exchange_of_four(*sent)
    else:
        came = [from_behind(sent[which], "dom", OFFSET_LIST[which]) for which in range(4)]
    unit = latent // ways
    half = ways // 2
    extent = -(-(nodes + arrivals * block) // 128) * 128

    node_v, edge_v, cot_v, win_v, wout_v, pre, up, hot, turned = pl.pallas_call(
        functools.partial(prep_kernel, parts, arrivals),
        out_shape=(
            pltpu.VMEM((nodes, latent), BF16),
            pltpu.VMEM((edges, latent), BF16),
            pltpu.VMEM((nodes, latent), BF16),
            pltpu.VMEM(weight_in.shape, BF16),
            pltpu.VMEM(weight_out.shape, BF16),
            pltpu.VMEM((edges, latent), F32),
            pltpu.VMEM((edges, latent), F32),
            pltpu.VMEM((edges, extent), BF16),
            pltpu.VMEM((extent + nodes, edges), BF16),
        ),
        in_specs=[SMEM] + [HBM] * 8,
        out_specs=(VMEM,) * 9,
        scratch_shapes=[
            pltpu.SMEM((tiles,), jnp.int32),
            pltpu.SMEM((tiles,), jnp.int32),
            pltpu.VMEM((tiles, block), jnp.int32),
            pltpu.VMEM((nodes, latent), F32),
            pltpu.VMEM((nodes, latent), F32),
            pltpu.SemaphoreType.DMA((10,)),
        ],
        compiler_params=small,
        cost_estimate=pl.CostEstimate(
            flops=2 * edges * latent * latent, bytes_accessed=8_000_000, transcendentals=0
        ),
        name="prepare",
    )(
        tile_count,
        in_hbm(tile_src),
        tile_dst,
        in_hbm(edge_slot),
        node_rows,
        in_hbm(edge_latents[0]),
        in_hbm(agg_cotangent[0]),
        in_hbm(weight_in),
        in_hbm(weight_out),
    )
    sent_shape = pltpu.VMEM((half, 2 * unit, latent), BF16)
    kept_shape = pltpu.VMEM((half, 2 * unit, latent), F32)
    grad_pre, message, sums, ext, away_a, kept_a = pl.pallas_call(
        functools.partial(edge_kernel, ways, arrivals, four, block),
        out_shape=(
            pltpu.VMEM((edges, latent), BF16),
            pltpu.VMEM((edges, latent), F32),
            pltpu.VMEM((extent + nodes, latent), F32),
            pltpu.VMEM((extent, latent), BF16),
            sent_shape,
            kept_shape,
        ),
        in_specs=[VMEM] * (8 + arrivals),
        out_specs=(VMEM,) * 6,
        scratch_shapes=[
            pltpu.VMEM((edges, latent), BF16),
            pltpu.VMEM((edges, latent), BF16),
        ],
        compiler_params=pltpu.CompilerParams(vmem_limit_bytes=16 * 1024 * 1024),
        cost_estimate=pl.CostEstimate(
            flops=12 * edges * latent * latent,
            bytes_accessed=12_000_000,
            transcendentals=edges * latent,
        ),
        name="edge_block",
    )(
        *[
            in_vmem(array)
            for array in (*came, node_v, edge_v, win_v, wout_v, pre, up, hot, turned)
        ],
    )
    away_b, kept_b = pl.pallas_call(
        functools.partial(rest_kernel, ways),
        out_shape=(sent_shape, kept_shape),
        in_specs=[VMEM] * 5,
        out_specs=(VMEM,) * 2,
        compiler_params=small,
        cost_estimate=pl.CostEstimate(
            flops=2 * edges * latent * latent, bytes_accessed=4_000_000, transcendentals=0
        ),
        name="rest_weights",
    )(*[in_vmem(array) for array in (node_v, edge_v, ext, grad_pre, sums)])
    backs = arrivals
    if four:
        sent_a, beside, finish = sum_of_square(
            nodes, block, ((away_a, kept_a), (away_b, kept_b)), sums
        )
        backs = 2
    else:
        came_a, kept_a, sent_a = sum_over_dp(away_a, kept_a, cot_v)
    edge_grad, agg, *back_sums = pl.pallas_call(
        functools.partial(edge_grad_kernel, block, arrivals, four),
        out_shape=(
            jax.ShapeDtypeStruct((edges, latent), BF16),
            jax.ShapeDtypeStruct((nodes, latent), BF16),
        )
        + (block_shape,) * backs,
        in_specs=[HBM, SMEM] + [VMEM] * 7,
        out_specs=(VMEM,) * (2 + backs),
        scratch_shapes=[
            pltpu.SMEM((tiles,), jnp.int32),
            pltpu.VMEM((nodes, latent), F32),
            pltpu.SemaphoreType.DMA,
        ],
        compiler_params=small,
        cost_estimate=pl.CostEstimate(
            flops=2 * edges * latent * latent, bytes_accessed=3_000_000, transcendentals=0
        ),
        name="edge_grads",
    )(
        tile_dst,
        tile_count,
        *[in_vmem(array) for array in (sent_a, grad_pre, sums, cot_v, win_v, edge_v, message)],
    )
    if four:
        far = swap(back_sums[1], "dom", lambda i: partners_of_four(2)[i])
        near = swap(back_sums[0], "dom", lambda i: partners_of_four(1)[i])
        pair_a, pair_b = finish(near, far)
        returned = [beside, near, far]
        late = pair_b
    else:
        returned = [
            from_behind(back_sums[which], "dom", -OFFSET_LIST[which]) for which in range(4)
        ]
        came_b, kept_b, _ = sum_over_dp(away_b, kept_b, back_sums[0])
        late = sent_a
    node_out = pl.pallas_call(
        functools.partial(node_grad_kernel, arrivals, four),
        out_shape=jax.ShapeDtypeStruct((nodes, latent), BF16),
        in_specs=[HBM] + [VMEM] * (3 + arrivals),
        out_specs=VMEM,
        scratch_shapes=[
            pltpu.VMEM((nodes, latent), F32),
            pltpu.SMEM(boundary.shape, jnp.int32),
            pltpu.SemaphoreType.DMA,
        ],
        compiler_params=small,
        cost_estimate=pl.CostEstimate(
            flops=8 * nodes * latent * latent, bytes_accessed=2_000_000, transcendentals=0
        ),
        name="node_grads",
    )(boundary, *[in_vmem(array) for array in (late, sums, win_v, *returned)])
    if four:
        w_in_grad, w_out_grad = pl.pallas_call(
            last_kernel,
            out_shape=(
                jax.ShapeDtypeStruct((3 * unit, latent), F32),
                jax.ShapeDtypeStruct((unit, latent), F32),
            ),
            in_specs=[HBM] + [VMEM] * 4,
            out_specs=(VMEM,) * 2,
            compiler_params=small,
            cost_estimate=pl.CostEstimate(flops=0, bytes_accessed=1_500_000, transcendentals=0),
            name="widen",
        )(in_hbm(node_out), *sum_of_four(pair_a), *sum_of_four(pair_b))
    else:
        sum_a = sum_over_dom(kept_a[0] + came_a[0].astype(F32))
        sum_b = sum_over_dom(kept_b[0] + came_b[0].astype(F32))
        w_in_grad = jnp.concatenate([sum_a[unit:], sum_b], axis=0)
        w_out_grad = sum_a[:unit]
    return (agg[None], edge_grad[None], node_out[None], w_in_grad, w_out_grad)


def solution(mesh):
    in_specs = (
        P(("group", "dp"), "dom", None),
        P(("group", "dp"), "dom", None),
        P(("group", "dp"), "dom", None),
        P(),
        P(),
        P(("group", "dom"), None),
        P(("group", "dom")),
        P(("group", "dom")),
        P(("group", "dom"), None),
        P(("group", "dom")),
    )
    out_specs = (
        P(("group", "dp"), "dom", None),
        P(("group", "dp"), "dom", None),
        P(("group", "dp"), "dom", None),
        P(("group", "dp"), None),
        P(("group", "dp"), None),
    )
    return jax.shard_map(body, mesh=mesh, in_specs=in_specs, out_specs=out_specs, check_vma=False)
```

```python
import functools

import jax
import jax.numpy as jnp
from jax import lax
from jax.experimental import pallas as pl
from jax.experimental.pallas import tpu as pltpu
from jax.sharding import PartitionSpec as P

OFFSET_LIST = (1, -1, 2, -2)
EPSILON = 1e-05
VMEM = pl.BlockSpec(memory_space=pltpu.VMEM)
HBM = pl.BlockSpec(memory_space=pltpu.HBM)
SMEM = pl.BlockSpec(memory_space=pltpu.SMEM)
ANY = pl.BlockSpec(memory_space=pl.ANY)
F32 = jnp.float32
BF16 = jnp.bfloat16


def dot(left, right):
    return jnp.dot(left, right, preferred_element_type=F32)


def dot_t(left, right):
    return lax.dot_general(left, right, (((1,), (1,)), ((), ())), preferred_element_type=F32)


def t_dot(left, right):
    return lax.dot_general(left, right, (((0,), (0,)), ((), ())), preferred_element_type=F32)


def row_mean(array):
    return jnp.sum(array, axis=1, keepdims=True) * (1.0 / array.shape[1])


def rows_of(ref, block, size):
    return ref[pl.ds(pl.multiple_of(block * size, size), size), :]


def load_small(source, target, sem):
    copy = pltpu.make_async_copy(source, target, sem)
    copy.start()
    return copy


def boundary_places(boundary_ref, part, four):
    taken = [boundary_ref[0, which] for which in range(4)]
    if not four:
        return taken
    even = part % 2 == 0
    return [
        jnp.where(even, taken[0], taken[1]),
        jnp.where(even, taken[1], taken[0]),
        jnp.where(part < 2, taken[2], taken[3]),
    ]


def arrival_places(part, four, arrivals):
    if not four:
        return list(range(arrivals))
    even = part % 2 == 0
    return [jnp.where(even, 1, 0), jnp.where(even, 0, 1), 2]


def pick_kernel(four, block, boundary_hbm, node_hbm, *refs):
    count = 3 if four else 4
    outs = refs[:count]
    boundary_ref, small_sem, sems = refs[count:]
    load_small(boundary_hbm, boundary_ref, small_sem).wait()
    copies = []
    for which, place in enumerate(boundary_places(boundary_ref, lax.axis_index("dom"), four)):
        spot = pl.ds(pl.multiple_of(place * block, block), block)
        copies.append(pltpu.make_async_copy(node_hbm.at[spot, :], outs[which], sems.at[which]))
        copies[-1].start()
    for copy in copies:
        copy.wait()


def prep_kernel(
    parts,
    arrivals,
    count_ref,
    src_hbm,
    dst_hbm,
    slot_hbm,
    node_hbm,
    edge_hbm,
    cot_hbm,
    win_hbm,
    wout_hbm,
    node_ref,
    edge_ref,
    cot_ref,
    win_ref,
    wout_ref,
    pre_ref,
    up_ref,
    hot_ref,
    hot_turned,
    src_ref,
    dst_ref,
    slot_ref,
    recv_ref,
    mid_ref,
    sems,
):
    tiles, block = slot_ref.shape
    nodes, latent = node_ref.shape
    owned = nodes // block
    extent = hot_ref.shape[1]
    pairs = (
        (src_hbm, src_ref),
        (dst_hbm, dst_ref),
        (slot_hbm, slot_ref),
        (node_hbm, node_ref),
        (win_hbm.at[2 * latent :, :], win_ref.at[2 * latent :, :]),
        (win_hbm.at[:latent, :], win_ref.at[:latent, :]),
        (edge_hbm, edge_ref),
        (cot_hbm, cot_ref),
        (win_hbm.at[latent : 2 * latent, :], win_ref.at[latent : 2 * latent, :]),
        (wout_hbm, wout_ref),
    )
    copies = [load_small(*pair, sems.at[number]) for number, pair in enumerate(pairs)]
    part = lax.axis_index("dom")
    for copy in copies[:3]:
        copy.wait()
    index = lax.broadcasted_iota(jnp.int32, (extent, 2 * block), 0)
    lane = lax.broadcasted_iota(jnp.int32, (1, 2 * block), 1)
    first = lane < block
    within = jnp.where(first, lane, lane - block)
    node_index = lax.broadcasted_iota(jnp.int32, (nodes, 2 * block), 0)
    for tile in range(0, tiles, 2):
        wanted = []
        for member in (tile, tile + 1):
            source = src_ref[member]
            which = source - owned
            reach = jnp.where(which >= 2, 2, 1)
            partner = part - jnp.where(which % 2 == 1, -reach, reach)
            exists = (source < owned) | ((partner >= 0) & (partner < parts))
            place = jnp.minimum(source, owned + arrivals - 1)
            wanted.append(jnp.where(exists, place * block, -2 * extent))
        slots = jnp.concatenate(
            [slot_ref[tile : tile + 1, :], slot_ref[tile + 1 : tile + 2, :]], axis=1
        )
        row = slots + jnp.where(first, wanted[0], wanted[1])
        hot = jnp.where(index == row, 1.0, 0.0)
        at = slice(tile * block, (tile + 2) * block)
        hot_turned[:extent, at] = hot.astype(BF16)
        target = within + jnp.where(first, dst_ref[tile] * block, dst_ref[tile + 1] * block)
        hot_turned[extent:, at] = jnp.where(node_index == target, 1.0, 0.0).astype(BF16)
        hot_ref[at, :] = hot.T.astype(BF16)
    copies[3].wait()
    copies[4].wait()
    recv_ref[...] = dot(node_ref[...], win_ref[2 * latent :, :])
    copies[5].wait()
    copies[6].wait()
    group = 4 if tiles % 4 == 0 else 2
    for tile in range(0, tiles, group):
        rows = slice(tile * block, (tile + group) * block)
        received = jnp.concatenate(
            [rows_of(recv_ref, dst_ref[t], block) for t in range(tile, tile + group)], axis=0
        )
        pre_ref[rows, :] = dot(edge_ref[rows, :], win_ref[:latent, :]) + received
    copies[7].wait()
    cot = cot_ref[...].astype(F32)
    mid_ref[...] = cot - row_mean(cot)
    for tile in range(tiles):
        live = jnp.where(tile < count_ref[0], 1.0, 0.0)
        up_ref[tile * block : (tile + 1) * block, :] = rows_of(mid_ref, dst_ref[tile], block) * live
    copies[8].wait()
    copies[9].wait()


def put_units(chunk, ways, bit, away, kept, sections):
    latent = sections[0][0].shape[1]
    unit = latent // ways
    step = 128

    def wanted(number, start):
        if number == 0:
            return [(start + at) // unit for at in range(0, step, unit)] if chunk == 0 else []
        found = []
        for at in range(0, step, unit):
            spot = ((number - 1) * latent + start + at) // unit
            if (1 + spot % 3) // 2 == chunk:
                found.append(spot)
        return found

    for number, (left, right) in enumerate(sections):
        value_right = right()
        start = 0
        while start < latent:
            size = step
            if start + 2 * step <= latent and wanted(number, start + step):
                size = 2 * step
            if wanted(number, start):
                value = t_dot(left[:, start : start + size], value_right)
                for at in range(0, size, unit):
                    if number == 0:
                        owner, spot = (start + at) // unit, 0
                    else:
                        place = ((number - 1) * latent + start + at) // unit
                        owner, spot = place // 3, 1 + place % 3
                    if spot // 2 != chunk:
                        continue
                    part = value[at : at + unit]
                    where = slice((spot % 2) * unit, (spot % 2 + 1) * unit)

                    @pl.when(bit == owner % 2)
                    def _(owner=owner, where=where, part=part):
                        kept[owner // 2, where, :] = part

                    @pl.when(bit != owner % 2)
                    def _(owner=owner, where=where, part=part):
                        away[owner // 2, where, :] = part.astype(BF16)

                start += size
            else:
                start += step


def edge_kernel(ways, arrivals, four, block, *refs):
    arrived = refs[:arrivals]
    (
        node_ref,
        edge_ref,
        win_ref,
        wout_ref,
        pre_ref,
        up_ref,
        hot_ref,
        hot_turned,
        gpre_ref,
        message_ref,
        sums_ref,
        ext_ref,
        away_ref,
        kept_ref,
        act_ref,
        proj_ref,
    ) = refs[arrivals:]
    nodes, latent = node_ref.shape
    edges = edge_ref.shape[0]
    extent = ext_ref.shape[0]
    places = arrival_places(lax.axis_index("dom"), four, arrivals)

    ext_ref[:nodes, :] = node_ref[...]
    for which in range(arrivals):
        at = pl.multiple_of(nodes + places[which] * block, block)
        ext_ref[pl.ds(at, block), :] = arrived[which][...]
    filled = nodes + arrivals * block
    if filled < extent:
        ext_ref[filled:, :] = jnp.zeros((extent - filled, latent), BF16)

    span = 256 if edges % 256 == 0 else block
    for start in range(0, edges, span):
        rows = slice(start, start + span)
        senders = dot(hot_ref[rows, :], ext_ref[...]).astype(BF16)
        preact = pre_ref[rows, :] + dot(senders, win_ref[latent : 2 * latent, :])
        gate = 0.5 * jnp.tanh(0.5 * preact) + 0.5
        activated = preact * gate
        slope = gate + activated * (1.0 - gate)
        activated = activated.astype(BF16)
        act_ref[rows, :] = activated
        projected = dot(activated, wout_ref[...])
        centered = projected - row_mean(projected)
        inv_scale = lax.rsqrt(row_mean(centered * centered) + EPSILON)
        message = centered * inv_scale
        message_ref[rows, :] = message
        upstream = up_ref[rows, :]
        grad_project = inv_scale * (upstream - message * row_mean(upstream * message))
        grad_project = grad_project.astype(BF16)
        proj_ref[rows, :] = grad_project
        gpre_ref[rows, :] = (dot_t(grad_project, wout_ref[...]) * slope).astype(BF16)

    sums_ref[...] = dot(hot_turned[...], gpre_ref[...])
    sections = (
        (act_ref, lambda: proj_ref[...]),
        (edge_ref, lambda: gpre_ref[...]),
        (ext_ref, lambda: sums_ref[:extent, :].astype(BF16)),
        (node_ref, lambda: sums_ref[extent:, :].astype(BF16)),
    )
    put_units(0, ways, lax.axis_index("dp") % 2, away_ref, kept_ref, sections)


def rest_kernel(ways, node_ref, edge_ref, ext_ref, gpre_ref, sums_ref, away_ref, kept_ref):
    extent = ext_ref.shape[0]
    sections = (
        (edge_ref, lambda: None),
        (edge_ref, lambda: gpre_ref[...]),
        (ext_ref, lambda: sums_ref[:extent, :].astype(BF16)),
        (node_ref, lambda: sums_ref[extent:, :].astype(BF16)),
    )
    put_units(1, ways, lax.axis_index("dp") % 2, away_ref, kept_ref, sections)


def edge_grad_kernel(
    block,
    arrivals,
    four,
    dst_hbm,
    count_ref,
    after,
    gpre_ref,
    sums_ref,
    cot_ref,
    win_ref,
    edge_ref,
    message_ref,
    out_ref,
    agg_out,
    *refs,
):
    back_sums = refs[:-3]
    dst_ref, agg_ref, sem = refs[-3:]
    copy = load_small(dst_hbm, dst_ref, sem)
    nodes, latent = cot_ref.shape
    tiles = gpre_ref.shape[0] // block
    group = 4 if tiles % 4 == 0 else 1
    places = arrival_places(lax.axis_index("dom"), four, arrivals)
    for place, back_ref in zip(places, back_sums):
        at = pl.multiple_of(nodes + place * block, block)
        back_ref[...] = sums_ref[pl.ds(at, block), :].astype(BF16)
    agg_ref[...] = jnp.zeros_like(agg_ref)
    copy.wait()
    for first in range(0, tiles, group):
        rows = slice(first * block, (first + group) * block)
        upstream = jnp.concatenate(
            [
                rows_of(cot_ref, dst_ref[t], block).astype(F32)
                * jnp.where(t < count_ref[0], 1.0, 0.0)
                for t in range(first, first + group)
            ],
            axis=0,
        )
        out_ref[rows, :] = (dot_t(gpre_ref[rows, :], win_ref[:latent, :]) + upstream).astype(BF16)
        for t in range(first, first + group):
            live = jnp.where(t < count_ref[0], 1.0, 0.0)
            mine = slice(t * block, (t + 1) * block)
            updated = edge_ref[mine, :].astype(F32) + message_ref[mine, :]
            target = pl.ds(pl.multiple_of(dst_ref[t] * block, block), block)
            agg_ref[target, :] += updated * live
    agg_out[...] = agg_ref[...].astype(BF16)


def halve_kernel(bit, came_ref, kept_ref, after, away_ref, left_ref):
    mine = (lax.axis_index("dp") // bit) % 2
    for slot in range(left_ref.shape[0]):
        there, here = 2 * slot + 1 - mine, 2 * slot + mine
        away_ref[slot] = (kept_ref[there] + came_ref[there].astype(F32)).astype(BF16)
        left_ref[slot] = kept_ref[here] + came_ref[here].astype(F32)


def send_back_kernel(nodes, block, came_ref, kept_ref, sums_ref, away_ref, left_ref, *back_refs):
    halve_kernel(2, came_ref, kept_ref, None, away_ref, left_ref)
    for place, back_ref in zip(arrival_places(lax.axis_index("dom"), True, 3)[1:], back_refs):
        at = pl.multiple_of(nodes + place * block, block)
        back_ref[...] = sums_ref[pl.ds(at, block), :].astype(BF16)


def split_kernel(nodes, block, came_ref, kept_ref, *refs):
    away_ref, left_ref = refs[-2:]
    part = lax.axis_index("dom")
    inner = (part == 1) | (part == 2)
    rows = left_ref.shape[0]
    here = pl.ds(pl.multiple_of(jnp.where(inner, 0, rows), rows), rows)
    there = pl.ds(pl.multiple_of(jnp.where(inner, rows, 0), rows), rows)
    away_ref[:rows, :] = (kept_ref[0, there, :] + came_ref[0, there, :].astype(F32)).astype(BF16)
    left_ref[...] = kept_ref[0, here, :] + came_ref[0, here, :].astype(F32)
    if away_ref.shape[0] > rows:
        sums_ref = refs[0]
        place = arrival_places(part, True, 3)[0]
        at = pl.multiple_of(nodes + place * block, block)
        away_ref[rows:, :] = sums_ref[pl.ds(at, block), :].astype(BF16)


def add_kernel(left_ref, came_ref, *refs):
    out_ref = refs[-1]
    rows = out_ref.shape[0]
    out_ref[...] = (left_ref[...] + came_ref[:rows, :].astype(F32)).astype(BF16)


def node_grad_kernel(arrivals, four, boundary_hbm, after, sums_ref, win_ref, *refs):
    returned = refs[:arrivals]
    out_ref, total_ref, boundary_ref, sem = refs[arrivals:]
    nodes, latent = out_ref.shape
    extent = sums_ref.shape[0] - nodes
    block = returned[-1].shape[0]
    copy = load_small(boundary_hbm, boundary_ref, sem)
    total_ref[...] = sums_ref[:nodes, :]
    copy.wait()
    for which, place in enumerate(boundary_places(boundary_ref, lax.axis_index("dom"), four)):
        spot = pl.ds(pl.multiple_of(place * block, block), block)
        total_ref[spot, :] += returned[which][-block:, :].astype(F32)

    def wide_dot(value, weight):
        high = value.astype(BF16)
        low = (value - high.astype(F32)).astype(BF16)
        return dot_t(high, weight) + dot_t(low, weight)

    out_ref[...] = (
        wide_dot(total_ref[...], win_ref[latent : 2 * latent, :])
        + wide_dot(sums_ref[extent:, :], win_ref[2 * latent :, :])
    ).astype(BF16)


def last_kernel(after, own_a, other_a, own_b, other_b, in_ref, out_ref):
    unit = out_ref.shape[0]
    part = lax.axis_index("dom")
    inner = (part == 1) | (part == 2)

    def write(low_a, high_a, low_b, high_b):
        out_ref[...] = low_a[...].astype(F32)
        in_ref[:unit, :] = high_a[...].astype(F32)
        in_ref[unit : 2 * unit, :] = low_b[...].astype(F32)
        in_ref[2 * unit :, :] = high_b[...].astype(F32)

    @pl.when(inner)
    def _():
        write(own_a, other_a, own_b, other_b)

    @pl.when(jnp.logical_not(inner))
    def _():
        write(other_a, own_a, other_b, own_b)


def swap(array, axis, partner):
    devices = lax.axis_size(axis)
    return lax.ppermute(array, axis, [(i, partner(i)) for i in range(devices)])


def from_behind(array, axis, by):
    devices = lax.axis_size(axis)
    pairs = [(i, i + by) for i in range(devices) if 0 <= i + by < devices]
    return lax.ppermute(array, axis, pairs)


def partners_of_four(which):
    return ((1, 0, 3, 2), (0, 2, 1, 3), (2, 3, 0, 1))[which]


def exchange_of_four(first, second, third):
    third = swap(third, "dom", lambda i: partners_of_four(2)[i])
    second = swap(second, "dom", lambda i: partners_of_four(1)[i])
    first = swap(first, "dom", lambda i: partners_of_four(0)[i])
    return [first, second, third]


def halve(bit, came, kept, after):
    slots, rows, latent = kept.shape
    return pl.pallas_call(
        functools.partial(halve_kernel, bit),
        out_shape=(
            pltpu.VMEM((slots // 2, rows, latent), BF16),
            pltpu.VMEM((slots // 2, rows, latent), F32),
        ),
        in_specs=[VMEM] * 3,
        out_specs=(VMEM,) * 2,
        compiler_params=pltpu.CompilerParams(vmem_limit_bytes=4 * 1024 * 1024),
        cost_estimate=pl.CostEstimate(flops=0, bytes_accessed=500_000, transcendentals=0),
        name="halve",
    )(in_vmem(came), in_vmem(kept), in_vmem(after))


def sum_over_dp(away, kept, after):
    devices = lax.axis_size("dp")
    bit = 1
    while True:
        came = swap(away, "dp", lambda i, bit=bit: i ^ bit)
        bit *= 2
        if bit >= devices:
            return came, kept, away
        away, kept = halve(bit, came, kept, after)


def small_call(kernel, name, out_shape, *operands):
    many = isinstance(out_shape, tuple)
    return pl.pallas_call(
        kernel,
        out_shape=out_shape,
        in_specs=[VMEM] * len(operands),
        out_specs=(VMEM,) * len(out_shape) if many else VMEM,
        compiler_params=pltpu.CompilerParams(vmem_limit_bytes=4 * 1024 * 1024),
        cost_estimate=pl.CostEstimate(flops=0, bytes_accessed=500_000, transcendentals=0),
        name=name,
    )(*[in_vmem(array) for array in operands])


def sum_of_pair(nodes, block, came, kept, sums, after, last):
    rows, latent = kept.shape[1:]
    half = rows // 2
    sent = half if sums is None else half + block
    extra = after if sums is None else (sums, *after)
    away, left = small_call(
        functools.partial(split_kernel, nodes, block),
        "split",
        (pltpu.VMEM((sent, latent), BF16), pltpu.VMEM((half, latent), F32)),
        came,
        kept,
        *extra,
    )
    came = swap(away, "dom", lambda i: i ^ 1)
    return small_call(add_kernel, "add_terms", pltpu.VMEM((half, latent), BF16), left, came, *last), came


def sum_of_four(kept):
    return (kept.astype(F32) + swap(kept, "dom", lambda i: 3 - i).astype(F32)).astype(BF16)


def with_other_half(kept):
    return kept, swap(kept, "dom", lambda i: i ^ 1)


def sum_over_dom(rows):
    piece = lax.psum_scatter(rows, "dom", scatter_dimension=0, tiled=True)
    return lax.all_gather(piece, "dom", axis=0, tiled=True)


def in_vmem(array):
    return pltpu.with_memory_space_constraint(array, pltpu.VMEM)


def in_hbm(array):
    return pltpu.with_memory_space_constraint(array, pltpu.HBM)


def body(
    node_latents,
    edge_latents,
    agg_cotangent,
    weight_in,
    weight_out,
    boundary,
    tile_src,
    tile_dst,
    edge_slot,
    tile_count,
):
    tiles, block = edge_slot.shape
    edges, latent = edge_latents.shape[1:]
    nodes = node_latents.shape[1]
    parts = lax.axis_size("dom")
    ways = lax.axis_size("dp")
    four = parts == 4 and ways == 4
    arrivals = 3 if four else 4
    boundary = in_hbm(boundary)
    tile_dst = in_hbm(tile_dst)
    node_rows = in_hbm(node_latents[0])
    block_shape = pltpu.VMEM((block, latent), BF16)
    small = pltpu.CompilerParams(vmem_limit_bytes=8 * 1024 * 1024)

    sent = pl.pallas_call(
        functools.partial(pick_kernel, four, block),
        out_shape=(block_shape,) * arrivals,
        in_specs=[HBM] * 2,
        out_specs=(VMEM,) * arrivals,
        scratch_shapes=[
            pltpu.SMEM(boundary.shape, jnp.int32),
            pltpu.SemaphoreType.DMA,
            pltpu.SemaphoreType.DMA((arrivals,)),
        ],
        compiler_params=small,
        cost_estimate=pl.CostEstimate(flops=0, bytes_accessed=400_000, transcendentals=0),
        name="pick_blocks",
    )(boundary, node_rows)
    if four:
        came = exchange_of_four(*sent)
    else:
        came = [from_behind(sent[which], "dom", OFFSET_LIST[which]) for which in range(4)]
    unit = latent // ways
    half = ways // 2
    extent = -(-(nodes + arrivals * block) // 128) * 128

    node_v, edge_v, cot_v, win_v, wout_v, pre, up, hot, turned = pl.pallas_call(
        functools.partial(prep_kernel, parts, arrivals),
        out_shape=(
            pltpu.VMEM((nodes, latent), BF16),
            pltpu.VMEM((edges, latent), BF16),
            pltpu.VMEM((nodes, latent), BF16),
            pltpu.VMEM(weight_in.shape, BF16),
            pltpu.VMEM(weight_out.shape, BF16),
            pltpu.VMEM((edges, latent), F32),
            pltpu.VMEM((edges, latent), F32),
            pltpu.VMEM((edges, extent), BF16),
            pltpu.VMEM((extent + nodes, edges), BF16),
        ),
        in_specs=[SMEM] + [HBM] * 8,
        out_specs=(VMEM,) * 9,
        scratch_shapes=[
            pltpu.SMEM((tiles,), jnp.int32),
            pltpu.SMEM((tiles,), jnp.int32),
            pltpu.VMEM((tiles, block), jnp.int32),
            pltpu.VMEM((nodes, latent), F32),
            pltpu.VMEM((nodes, latent), F32),
            pltpu.SemaphoreType.DMA((10,)),
        ],
        compiler_params=small,
        cost_estimate=pl.CostEstimate(
            flops=2 * edges * latent * latent, bytes_accessed=8_000_000, transcendentals=0
        ),
        name="prepare",
    )(
        tile_count,
        in_hbm(tile_src),
        tile_dst,
        in_hbm(edge_slot),
        node_rows,
        in_hbm(edge_latents[0]),
        in_hbm(agg_cotangent[0]),
        in_hbm(weight_in),
        in_hbm(weight_out),
    )
    sent_shape = pltpu.VMEM((half, 2 * unit, latent), BF16)
    kept_shape = pltpu.VMEM((half, 2 * unit, latent), F32)
    grad_pre, message, sums, ext, away_a, kept_a = pl.pallas_call(
        functools.partial(edge_kernel, ways, arrivals, four, block),
        out_shape=(
            pltpu.VMEM((edges, latent), BF16),
            pltpu.VMEM((edges, latent), F32),
            pltpu.VMEM((extent + nodes, latent), F32),
            pltpu.VMEM((extent, latent), BF16),
            sent_shape,
            kept_shape,
        ),
        in_specs=[VMEM] * (8 + arrivals),
        out_specs=(VMEM,) * 6,
        scratch_shapes=[
            pltpu.VMEM((edges, latent), BF16),
            pltpu.VMEM((edges, latent), BF16),
        ],
        compiler_params=pltpu.CompilerParams(vmem_limit_bytes=16 * 1024 * 1024),
        cost_estimate=pl.CostEstimate(
            flops=12 * edges * latent * latent,
            bytes_accessed=12_000_000,
            transcendentals=edges * latent,
        ),
        name="edge_block",
    )(
        *[
            in_vmem(array)
            for array in (*came, node_v, edge_v, win_v, wout_v, pre, up, hot, turned)
        ],
    )
    away_b, kept_b = pl.pallas_call(
        functools.partial(rest_kernel, ways),
        out_shape=(sent_shape, kept_shape),
        in_specs=[VMEM] * 5,
        out_specs=(VMEM,) * 2,
        compiler_params=small,
        cost_estimate=pl.CostEstimate(
            flops=2 * edges * latent * latent, bytes_accessed=4_000_000, transcendentals=0
        ),
        name="rest_weights",
    )(*[in_vmem(array) for array in (node_v, edge_v, ext, grad_pre, sums)])
    if four:
        came_a = swap(away_a, "dp", lambda i: i ^ 1)
        away_a, kept_a, near, far = small_call(
            functools.partial(send_back_kernel, nodes, block),
            "halve",
            (
                pltpu.VMEM((1, 2 * unit, latent), BF16),
                pltpu.VMEM((1, 2 * unit, latent), F32),
                block_shape,
                block_shape,
            ),
            came_a,
            kept_a,
            sums,
        )
        came_a = swap(away_a, "dp", lambda i: i ^ 2)
        far = swap(far, "dom", lambda i: partners_of_four(2)[i])
        near = swap(near, "dom", lambda i: partners_of_four(1)[i])
        pair_a, beside = sum_of_pair(nodes, block, came_a, kept_a, sums, (), ())
        four_a = sum_of_four(pair_a)
        came_b = swap(away_b, "dp", lambda i: i ^ 1)
        away_b, kept_b = halve(2, came_b, kept_b, near)
        came_b = swap(away_b, "dp", lambda i: i ^ 2)
        pair_b, _ = sum_of_pair(nodes, block, came_b, kept_b, None, (pair_a, far), (four_a,))
        returned = [beside, near, far]
        late, later, backs = pair_a, pair_b, 0
    else:
        came_a, kept_a, late = sum_over_dp(away_a, kept_a, cot_v)
        came_b, kept_b, later = sum_over_dp(away_b, kept_b, cot_v)
        backs = arrivals
    edge_grad, agg, *back_sums = pl.pallas_call(
        functools.partial(edge_grad_kernel, block, arrivals, four),
        out_shape=(
            jax.ShapeDtypeStruct((edges, latent), BF16),
            jax.ShapeDtypeStruct((nodes, latent), BF16),
        )
        + (block_shape,) * backs,
        in_specs=[HBM, SMEM] + [VMEM] * 7,
        out_specs=(VMEM,) * (2 + backs),
        scratch_shapes=[
            pltpu.SMEM((tiles,), jnp.int32),
            pltpu.VMEM((nodes, latent), F32),
            pltpu.SemaphoreType.DMA,
        ],
        compiler_params=small,
        cost_estimate=pl.CostEstimate(
            flops=2 * edges * latent * latent, bytes_accessed=3_000_000, transcendentals=0
        ),
        name="edge_grads",
    )(
        tile_dst,
        tile_count,
        *[in_vmem(array) for array in (late, grad_pre, sums, cot_v, win_v, edge_v, message)],
    )
    if not four:
        returned = [
            from_behind(back_sums[which], "dom", -OFFSET_LIST[which]) for which in range(4)
        ]
    node_out = pl.pallas_call(
        functools.partial(node_grad_kernel, arrivals, four),
        out_shape=jax.ShapeDtypeStruct((nodes, latent), BF16),
        in_specs=[HBM] + [VMEM] * (3 + arrivals),
        out_specs=VMEM,
        scratch_shapes=[
            pltpu.VMEM((nodes, latent), F32),
            pltpu.SMEM(boundary.shape, jnp.int32),
            pltpu.SemaphoreType.DMA,
        ],
        compiler_params=small,
        cost_estimate=pl.CostEstimate(
            flops=8 * nodes * latent * latent, bytes_accessed=2_000_000, transcendentals=0
        ),
        name="node_grads",
    )(boundary, *[in_vmem(array) for array in (later, sums, win_v, *returned)])
    if four:
        w_in_grad, w_out_grad = pl.pallas_call(
            last_kernel,
            out_shape=(
                jax.ShapeDtypeStruct((3 * unit, latent), F32),
                jax.ShapeDtypeStruct((unit, latent), F32),
            ),
            in_specs=[HBM] + [VMEM] * 4,
            out_specs=(VMEM,) * 2,
            compiler_params=small,
            cost_estimate=pl.CostEstimate(flops=0, bytes_accessed=1_500_000, transcendentals=0),
            name="widen",
        )(in_hbm(node_out), *with_other_half(four_a), *with_other_half(sum_of_four(pair_b)))
    else:
        sum_a = sum_over_dom(kept_a[0] + came_a[0].astype(F32))
        sum_b = sum_over_dom(kept_b[0] + came_b[0].astype(F32))
        w_in_grad = jnp.concatenate([sum_a[unit:], sum_b], axis=0)
        w_out_grad = sum_a[:unit]
    return (agg[None], edge_grad[None], node_out[None], w_in_grad, w_out_grad)


def solution(mesh):
    in_specs = (
        P(("group", "dp"), "dom", None),
        P(("group", "dp"), "dom", None),
        P(("group", "dp"), "dom", None),
        P(),
        P(),
        P(("group", "dom"), None),
        P(("group", "dom")),
        P(("group", "dom")),
        P(("group", "dom"), None),
        P(("group", "dom")),
    )
    out_specs = (
        P(("group", "dp"), "dom", None),
        P(("group", "dp"), "dom", None),
        P(("group", "dp"), "dom", None),
        P(("group", "dp"), None),
        P(("group", "dp"), None),
    )
    return jax.shard_map(body, mesh=mesh, in_specs=in_specs, out_specs=out_specs, check_vma=False)
```

```python
import functools

import jax
import jax.numpy as jnp
from jax import lax
from jax.experimental import pallas as pl
from jax.experimental.pallas import tpu as pltpu
from jax.sharding import PartitionSpec as P

OFFSET_LIST = (1, -1, 2, -2)
EPSILON = 1e-05
VMEM = pl.BlockSpec(memory_space=pltpu.VMEM)
HBM = pl.BlockSpec(memory_space=pltpu.HBM)
SMEM = pl.BlockSpec(memory_space=pltpu.SMEM)
ANY = pl.BlockSpec(memory_space=pl.ANY)
F32 = jnp.float32
BF16 = jnp.bfloat16


def dot(left, right):
    return jnp.dot(left, right, preferred_element_type=F32)


def dot_t(left, right):
    return lax.dot_general(left, right, (((1,), (1,)), ((), ())), preferred_element_type=F32)


def t_dot(left, right):
    return lax.dot_general(left, right, (((0,), (0,)), ((), ())), preferred_element_type=F32)


def row_mean(array):
    return jnp.sum(array, axis=1, keepdims=True) * (1.0 / array.shape[1])


def rows_of(ref, block, size):
    return ref[pl.ds(pl.multiple_of(block * size, size), size), :]


def load_small(source, target, sem):
    copy = pltpu.make_async_copy(source, target, sem)
    copy.start()
    return copy


def boundary_places(boundary_ref, part, four):
    taken = [boundary_ref[0, which] for which in range(4)]
    if not four:
        return taken
    even = part % 2 == 0
    return [
        jnp.where(even, taken[0], taken[1]),
        jnp.where(even, taken[1], taken[0]),
        jnp.where(part < 2, taken[2], taken[3]),
    ]


def arrival_places(part, four, arrivals):
    if not four:
        return list(range(arrivals))
    even = part % 2 == 0
    return [jnp.where(even, 1, 0), jnp.where(even, 0, 1), 2]


def pick_kernel(four, block, boundary_hbm, node_hbm, *refs):
    count = 3 if four else 4
    outs = refs[:count]
    boundary_ref, small_sem, sems = refs[count:]
    load_small(boundary_hbm, boundary_ref, small_sem).wait()
    copies = []
    for which, place in enumerate(boundary_places(boundary_ref, lax.axis_index("dom"), four)):
        spot = pl.ds(pl.multiple_of(place * block, block), block)
        copies.append(pltpu.make_async_copy(node_hbm.at[spot, :], outs[which], sems.at[which]))
        copies[-1].start()
    for copy in copies:
        copy.wait()


def prep_kernel(
    parts,
    arrivals,
    count_ref,
    src_hbm,
    dst_hbm,
    slot_hbm,
    node_hbm,
    edge_hbm,
    cot_hbm,
    win_hbm,
    wout_hbm,
    node_ref,
    edge_ref,
    cot_ref,
    win_ref,
    wout_ref,
    pre_ref,
    up_ref,
    hot_ref,
    hot_turned,
    src_ref,
    dst_ref,
    slot_ref,
    recv_ref,
    mid_ref,
    sems,
):
    tiles, block = slot_ref.shape
    nodes, latent = node_ref.shape
    owned = nodes // block
    extent = hot_ref.shape[1]
    pairs = (
        (src_hbm, src_ref),
        (dst_hbm, dst_ref),
        (slot_hbm, slot_ref),
        (node_hbm, node_ref),
        (win_hbm.at[2 * latent :, :], win_ref.at[2 * latent :, :]),
        (win_hbm.at[:latent, :], win_ref.at[:latent, :]),
        (edge_hbm, edge_ref),
        (cot_hbm, cot_ref),
        (win_hbm.at[latent : 2 * latent, :], win_ref.at[latent : 2 * latent, :]),
        (wout_hbm, wout_ref),
    )
    copies = [load_small(*pair, sems.at[number]) for number, pair in enumerate(pairs)]
    part = lax.axis_index("dom")
    for copy in copies[:3]:
        copy.wait()
    index = lax.broadcasted_iota(jnp.int32, (extent, 2 * block), 0)
    lane = lax.broadcasted_iota(jnp.int32, (1, 2 * block), 1)
    first = lane < block
    within = jnp.where(first, lane, lane - block)
    node_index = lax.broadcasted_iota(jnp.int32, (nodes, 2 * block), 0)
    for tile in range(0, tiles, 2):
        wanted = []
        for member in (tile, tile + 1):
            source = src_ref[member]
            which = source - owned
            reach = jnp.where(which >= 2, 2, 1)
            partner = part - jnp.where(which % 2 == 1, -reach, reach)
            exists = (source < owned) | ((partner >= 0) & (partner < parts))
            place = jnp.minimum(source, owned + arrivals - 1)
            wanted.append(jnp.where(exists, place * block, -2 * extent))
        slots = jnp.concatenate(
            [slot_ref[tile : tile + 1, :], slot_ref[tile + 1 : tile + 2, :]], axis=1
        )
        row = slots + jnp.where(first, wanted[0], wanted[1])
        hot = jnp.where(index == row, 1.0, 0.0)
        at = slice(tile * block, (tile + 2) * block)
        hot_turned[:extent, at] = hot.astype(BF16)
        target = within + jnp.where(first, dst_ref[tile] * block, dst_ref[tile + 1] * block)
        hot_turned[extent:, at] = jnp.where(node_index == target, 1.0, 0.0).astype(BF16)
        hot_ref[at, :] = hot.T.astype(BF16)
    copies[3].wait()
    copies[4].wait()
    recv_ref[...] = dot(node_ref[...], win_ref[2 * latent :, :])
    copies[5].wait()
    copies[6].wait()
    group = 4 if tiles % 4 == 0 else 2
    for tile in range(0, tiles, group):
        rows = slice(tile * block, (tile + group) * block)
        received = jnp.concatenate(
            [rows_of(recv_ref, dst_ref[t], block) for t in range(tile, tile + group)], axis=0
        )
        pre_ref[rows, :] = dot(edge_ref[rows, :], win_ref[:latent, :]) + received
    copies[7].wait()
    cot = cot_ref[...].astype(F32)
    mid_ref[...] = cot - row_mean(cot)
    for tile in range(tiles):
        live = jnp.where(tile < count_ref[0], 1.0, 0.0)
        up_ref[tile * block : (tile + 1) * block, :] = rows_of(mid_ref, dst_ref[tile], block) * live
    copies[8].wait()
    copies[9].wait()


def put_units(chunk, ways, bit, away, kept, sections):
    latent = sections[0][0].shape[1]
    unit = latent // ways
    step = 128

    def wanted(number, start):
        if number == 0:
            return [(start + at) // unit for at in range(0, step, unit)] if chunk == 0 else []
        found = []
        for at in range(0, step, unit):
            spot = ((number - 1) * latent + start + at) // unit
            if (1 + spot % 3) // 2 == chunk:
                found.append(spot)
        return found

    for number, (left, right) in enumerate(sections):
        value_right = right()
        start = 0
        while start < latent:
            size = step
            if start + 2 * step <= latent and wanted(number, start + step):
                size = 2 * step
            if wanted(number, start):
                value = t_dot(left[:, start : start + size], value_right)
                for at in range(0, size, unit):
                    if number == 0:
                        owner, spot = (start + at) // unit, 0
                    else:
                        place = ((number - 1) * latent + start + at) // unit
                        owner, spot = place // 3, 1 + place % 3
                    if spot // 2 != chunk:
                        continue
                    part = value[at : at + unit]
                    where = slice((spot % 2) * unit, (spot % 2 + 1) * unit)

                    @pl.when(bit == owner % 2)
                    def _(owner=owner, where=where, part=part):
                        kept[owner // 2, where, :] = part

                    @pl.when(bit != owner % 2)
                    def _(owner=owner, where=where, part=part):
                        away[owner // 2, where, :] = part.astype(BF16)

                start += size
            else:
                start += step


def edge_kernel(ways, arrivals, four, block, *refs):
    arrived = refs[:arrivals]
    (
        node_ref,
        edge_ref,
        win_ref,
        wout_ref,
        pre_ref,
        up_ref,
        hot_ref,
        hot_turned,
        gpre_ref,
        message_ref,
        sums_ref,
        ext_ref,
        away_ref,
        kept_ref,
        act_ref,
        proj_ref,
    ) = refs[arrivals:]
    nodes, latent = node_ref.shape
    edges = edge_ref.shape[0]
    extent = ext_ref.shape[0]
    places = arrival_places(lax.axis_index("dom"), four, arrivals)

    ext_ref[:nodes, :] = node_ref[...]
    for which in range(arrivals):
        at = pl.multiple_of(nodes + places[which] * block, block)
        ext_ref[pl.ds(at, block), :] = arrived[which][...]
    filled = nodes + arrivals * block
    if filled < extent:
        ext_ref[filled:, :] = jnp.zeros((extent - filled, latent), BF16)

    span = 256 if edges % 256 == 0 else block
    for start in range(0, edges, span):
        rows = slice(start, start + span)
        senders = dot(hot_ref[rows, :], ext_ref[...]).astype(BF16)
        preact = pre_ref[rows, :] + dot(senders, win_ref[latent : 2 * latent, :])
        gate = 0.5 * jnp.tanh(0.5 * preact) + 0.5
        activated = preact * gate
        slope = gate + activated * (1.0 - gate)
        activated = activated.astype(BF16)
        act_ref[rows, :] = activated
        projected = dot(activated, wout_ref[...])
        centered = projected - row_mean(projected)
        inv_scale = lax.rsqrt(row_mean(centered * centered) + EPSILON)
        message = centered * inv_scale
        message_ref[rows, :] = message
        upstream = up_ref[rows, :]
        grad_project = inv_scale * (upstream - message * row_mean(upstream * message))
        grad_project = grad_project.astype(BF16)
        proj_ref[rows, :] = grad_project
        gpre_ref[rows, :] = (dot_t(grad_project, wout_ref[...]) * slope).astype(BF16)

    sums_ref[...] = dot(hot_turned[...], gpre_ref[...])
    sections = (
        (act_ref, lambda: proj_ref[...]),
        (edge_ref, lambda: gpre_ref[...]),
        (ext_ref, lambda: sums_ref[:extent, :].astype(BF16)),
        (node_ref, lambda: sums_ref[extent:, :].astype(BF16)),
    )
    put_units(0, ways, lax.axis_index("dp") % 2, away_ref, kept_ref, sections)


def rest_kernel(ways, node_ref, edge_ref, ext_ref, gpre_ref, sums_ref, away_ref, kept_ref):
    extent = ext_ref.shape[0]
    sections = (
        (edge_ref, lambda: None),
        (edge_ref, lambda: gpre_ref[...]),
        (ext_ref, lambda: sums_ref[:extent, :].astype(BF16)),
        (node_ref, lambda: sums_ref[extent:, :].astype(BF16)),
    )
    put_units(1, ways, lax.axis_index("dp") % 2, away_ref, kept_ref, sections)


def edge_grad_kernel(
    block,
    arrivals,
    four,
    dst_hbm,
    count_ref,
    after,
    gpre_ref,
    sums_ref,
    cot_ref,
    win_ref,
    edge_ref,
    message_ref,
    out_ref,
    agg_out,
    *refs,
):
    back_sums = refs[:-3]
    dst_ref, agg_ref, sem = refs[-3:]
    copy = load_small(dst_hbm, dst_ref, sem)
    nodes, latent = cot_ref.shape
    tiles = gpre_ref.shape[0] // block
    group = 4 if tiles % 4 == 0 else 1
    places = arrival_places(lax.axis_index("dom"), four, arrivals)
    for place, back_ref in zip(places, back_sums):
        at = pl.multiple_of(nodes + place * block, block)
        back_ref[...] = sums_ref[pl.ds(at, block), :].astype(BF16)
    agg_ref[...] = jnp.zeros_like(agg_ref)
    copy.wait()
    for first in range(0, tiles, group):
        rows = slice(first * block, (first + group) * block)
        upstream = jnp.concatenate(
            [
                rows_of(cot_ref, dst_ref[t], block).astype(F32)
                * jnp.where(t < count_ref[0], 1.0, 0.0)
                for t in range(first, first + group)
            ],
            axis=0,
        )
        out_ref[rows, :] = (dot_t(gpre_ref[rows, :], win_ref[:latent, :]) + upstream).astype(BF16)
        for t in range(first, first + group):
            live = jnp.where(t < count_ref[0], 1.0, 0.0)
            mine = slice(t * block, (t + 1) * block)
            updated = edge_ref[mine, :].astype(F32) + message_ref[mine, :]
            target = pl.ds(pl.multiple_of(dst_ref[t] * block, block), block)
            agg_ref[target, :] += updated * live
    agg_out[...] = agg_ref[...].astype(BF16)


def halve_kernel(bit, came_ref, kept_ref, after, away_ref, left_ref):
    mine = (lax.axis_index("dp") // bit) % 2
    for slot in range(left_ref.shape[0]):
        there, here = 2 * slot + 1 - mine, 2 * slot + mine
        away_ref[slot] = (kept_ref[there] + came_ref[there].astype(F32)).astype(BF16)
        left_ref[slot] = kept_ref[here] + came_ref[here].astype(F32)


def half_rows(rows):
    part = lax.axis_index("dom")
    inner = (part == 1) | (part == 2)
    here = pl.ds(pl.multiple_of(jnp.where(inner, 0, rows), rows), rows)
    there = pl.ds(pl.multiple_of(jnp.where(inner, rows, 0), rows), rows)
    return here, there


def back_block(nodes, block, sums_ref, which):
    place = arrival_places(lax.axis_index("dom"), True, 3)[which]
    return sums_ref[pl.ds(pl.multiple_of(nodes + place * block, block), block), :].astype(BF16)


def over_first_kernel(nodes, block, came_ref, kept_ref, sums_ref, away_ref, left_ref, *back_refs):
    halve_kernel(2, came_ref, kept_ref, None, away_ref, left_ref)
    for which, back_ref in enumerate(back_refs):
        back_ref[...] = back_block(nodes, block, sums_ref, 1 + which)


def beside_first_kernel(nodes, block, came_ref, kept_ref, sums_ref, away_ref, left_ref):
    rows = left_ref.shape[1]
    here, there = half_rows(rows)
    for slot in range(2):
        away_ref[slot * rows : (slot + 1) * rows, :] = (
            kept_ref[slot, there, :] + came_ref[slot, there, :].astype(F32)
        ).astype(BF16)
        left_ref[slot] = kept_ref[slot, here, :] + came_ref[slot, here, :].astype(F32)
    away_ref[2 * rows :, :] = back_block(nodes, block, sums_ref, 0)


def beside_second_kernel(came_ref, kept_ref, *refs):
    away_ref, left_ref = refs[-2:]
    here, there = half_rows(left_ref.shape[0])
    away_ref[...] = (kept_ref[0, there, :] + came_ref[0, there, :].astype(F32)).astype(BF16)
    left_ref[...] = kept_ref[0, here, :] + came_ref[0, here, :].astype(F32)


def over_second_kernel(came_ref, kept_ref, *refs):
    away_ref, left_ref = refs[-2:]
    mine = lax.axis_index("dp") // 2
    rows = left_ref.shape[0]

    def came(slot):
        spot = pl.ds(pl.multiple_of(slot * rows, rows), rows)
        return came_ref[spot, :].astype(F32)

    away_ref[...] = (kept_ref[1 - mine] + came(1 - mine)).astype(BF16)
    left_ref[...] = kept_ref[mine] + came(mine)


def add_kernel(left_ref, came_ref, *refs):
    out_ref = refs[-1]
    out_ref[...] = (left_ref[...] + came_ref[...].astype(F32)).astype(BF16)


def node_grad_kernel(arrivals, four, boundary_hbm, after, sums_ref, win_ref, *refs):
    returned = refs[:arrivals]
    out_ref, total_ref, boundary_ref, sem = refs[arrivals:]
    nodes, latent = out_ref.shape
    extent = sums_ref.shape[0] - nodes
    block = returned[-1].shape[0]
    copy = load_small(boundary_hbm, boundary_ref, sem)
    total_ref[...] = sums_ref[:nodes, :]
    copy.wait()
    for which, place in enumerate(boundary_places(boundary_ref, lax.axis_index("dom"), four)):
        spot = pl.ds(pl.multiple_of(place * block, block), block)
        total_ref[spot, :] += returned[which][-block:, :].astype(F32)

    def wide_dot(value, weight):
        high = value.astype(BF16)
        low = (value - high.astype(F32)).astype(BF16)
        return dot_t(high, weight) + dot_t(low, weight)

    out_ref[...] = (
        wide_dot(total_ref[...], win_ref[latent : 2 * latent, :])
        + wide_dot(sums_ref[extent:, :], win_ref[2 * latent :, :])
    ).astype(BF16)


def last_kernel(after, own_a, other_a, own_b, other_b, in_ref, out_ref):
    unit = out_ref.shape[0]
    part = lax.axis_index("dom")
    inner = (part == 1) | (part == 2)

    def write(low_a, high_a, low_b, high_b):
        out_ref[...] = low_a[...].astype(F32)
        in_ref[:unit, :] = high_a[...].astype(F32)
        in_ref[unit : 2 * unit, :] = low_b[...].astype(F32)
        in_ref[2 * unit :, :] = high_b[...].astype(F32)

    @pl.when(inner)
    def _():
        write(own_a, other_a, own_b, other_b)

    @pl.when(jnp.logical_not(inner))
    def _():
        write(other_a, own_a, other_b, own_b)


def swap(array, axis, partner):
    devices = lax.axis_size(axis)
    return lax.ppermute(array, axis, [(i, partner(i)) for i in range(devices)])


def from_behind(array, axis, by):
    devices = lax.axis_size(axis)
    pairs = [(i, i + by) for i in range(devices) if 0 <= i + by < devices]
    return lax.ppermute(array, axis, pairs)


def partners_of_four(which):
    return ((1, 0, 3, 2), (0, 2, 1, 3), (2, 3, 0, 1))[which]


def exchange_of_four(first, second, third):
    third = swap(third, "dom", lambda i: partners_of_four(2)[i])
    second = swap(second, "dom", lambda i: partners_of_four(1)[i])
    first = swap(first, "dom", lambda i: partners_of_four(0)[i])
    return [first, second, third]


def halve(bit, came, kept, after):
    slots, rows, latent = kept.shape
    return pl.pallas_call(
        functools.partial(halve_kernel, bit),
        out_shape=(
            pltpu.VMEM((slots // 2, rows, latent), BF16),
            pltpu.VMEM((slots // 2, rows, latent), F32),
        ),
        in_specs=[VMEM] * 3,
        out_specs=(VMEM,) * 2,
        compiler_params=pltpu.CompilerParams(vmem_limit_bytes=4 * 1024 * 1024),
        cost_estimate=pl.CostEstimate(flops=0, bytes_accessed=500_000, transcendentals=0),
        name="halve",
    )(in_vmem(came), in_vmem(kept), in_vmem(after))


def sum_over_dp(away, kept, after):
    devices = lax.axis_size("dp")
    bit = 1
    while True:
        came = swap(away, "dp", lambda i, bit=bit: i ^ bit)
        bit *= 2
        if bit >= devices:
            return came, kept, away
        away, kept = halve(bit, came, kept, after)


def small_call(kernel, name, out_shape, *operands, after=()):
    many = isinstance(out_shape, tuple)
    return pl.pallas_call(
        kernel,
        out_shape=out_shape,
        in_specs=[VMEM] * len(operands) + [HBM] * len(after),
        out_specs=(VMEM,) * len(out_shape) if many else VMEM,
        compiler_params=pltpu.CompilerParams(vmem_limit_bytes=4 * 1024 * 1024),
        cost_estimate=pl.CostEstimate(flops=0, bytes_accessed=500_000, transcendentals=0),
        name=name,
    )(*[in_vmem(array) for array in operands], *[in_hbm(array) for array in after])


def sum_of_four(kept):
    return (kept.astype(F32) + swap(kept, "dom", lambda i: 3 - i).astype(F32)).astype(BF16)


def with_other_half(kept):
    return kept, swap(kept, "dom", lambda i: i ^ 1)


def sum_over_dom(rows):
    piece = lax.psum_scatter(rows, "dom", scatter_dimension=0, tiled=True)
    return lax.all_gather(piece, "dom", axis=0, tiled=True)


def in_vmem(array):
    return pltpu.with_memory_space_constraint(array, pltpu.VMEM)


def in_hbm(array):
    return pltpu.with_memory_space_constraint(array, pltpu.HBM)


def body(
    node_latents,
    edge_latents,
    agg_cotangent,
    weight_in,
    weight_out,
    boundary,
    tile_src,
    tile_dst,
    edge_slot,
    tile_count,
):
    tiles, block = edge_slot.shape
    edges, latent = edge_latents.shape[1:]
    nodes = node_latents.shape[1]
    parts = lax.axis_size("dom")
    ways = lax.axis_size("dp")
    four = parts == 4 and ways == 4
    arrivals = 3 if four else 4
    boundary = in_hbm(boundary)
    tile_dst = in_hbm(tile_dst)
    node_rows = in_hbm(node_latents[0])
    block_shape = pltpu.VMEM((block, latent), BF16)
    small = pltpu.CompilerParams(vmem_limit_bytes=8 * 1024 * 1024)

    sent = pl.pallas_call(
        functools.partial(pick_kernel, four, block),
        out_shape=(block_shape,) * arrivals,
        in_specs=[HBM] * 2,
        out_specs=(VMEM,) * arrivals,
        scratch_shapes=[
            pltpu.SMEM(boundary.shape, jnp.int32),
            pltpu.SemaphoreType.DMA,
            pltpu.SemaphoreType.DMA((arrivals,)),
        ],
        compiler_params=small,
        cost_estimate=pl.CostEstimate(flops=0, bytes_accessed=400_000, transcendentals=0),
        name="pick_blocks",
    )(boundary, node_rows)
    if four:
        came = exchange_of_four(*sent)
    else:
        came = [from_behind(sent[which], "dom", OFFSET_LIST[which]) for which in range(4)]
    unit = latent // ways
    half = ways // 2
    extent = -(-(nodes + arrivals * block) // 128) * 128

    node_v, edge_v, cot_v, win_v, wout_v, pre, up, hot, turned = pl.pallas_call(
        functools.partial(prep_kernel, parts, arrivals),
        out_shape=(
            pltpu.VMEM((nodes, latent), BF16),
            pltpu.VMEM((edges, latent), BF16),
            pltpu.VMEM((nodes, latent), BF16),
            pltpu.VMEM(weight_in.shape, BF16),
            pltpu.VMEM(weight_out.shape, BF16),
            pltpu.VMEM((edges, latent), F32),
            pltpu.VMEM((edges, latent), F32),
            pltpu.VMEM((edges, extent), BF16),
            pltpu.VMEM((extent + nodes, edges), BF16),
        ),
        in_specs=[SMEM] + [HBM] * 8,
        out_specs=(VMEM,) * 9,
        scratch_shapes=[
            pltpu.SMEM((tiles,), jnp.int32),
            pltpu.SMEM((tiles,), jnp.int32),
            pltpu.VMEM((tiles, block), jnp.int32),
            pltpu.VMEM((nodes, latent), F32),
            pltpu.VMEM((nodes, latent), F32),
            pltpu.SemaphoreType.DMA((10,)),
        ],
        compiler_params=small,
        cost_estimate=pl.CostEstimate(
            flops=2 * edges * latent * latent, bytes_accessed=8_000_000, transcendentals=0
        ),
        name="prepare",
    )(
        tile_count,
        in_hbm(tile_src),
        tile_dst,
        in_hbm(edge_slot),
        node_rows,
        in_hbm(edge_latents[0]),
        in_hbm(agg_cotangent[0]),
        in_hbm(weight_in),
        in_hbm(weight_out),
    )
    sent_shape = pltpu.VMEM((half, 2 * unit, latent), BF16)
    kept_shape = pltpu.VMEM((half, 2 * unit, latent), F32)
    grad_pre, message, sums, ext, away_a, kept_a = pl.pallas_call(
        functools.partial(edge_kernel, ways, arrivals, four, block),
        out_shape=(
            pltpu.VMEM((edges, latent), BF16),
            pltpu.VMEM((edges, latent), F32),
            pltpu.VMEM((extent + nodes, latent), F32),
            pltpu.VMEM((extent, latent), BF16),
            sent_shape,
            kept_shape,
        ),
        in_specs=[VMEM] * (8 + arrivals),
        out_specs=(VMEM,) * 6,
        scratch_shapes=[
            pltpu.VMEM((edges, latent), BF16),
            pltpu.VMEM((edges, latent), BF16),
        ],
        compiler_params=pltpu.CompilerParams(vmem_limit_bytes=16 * 1024 * 1024),
        cost_estimate=pl.CostEstimate(
            flops=12 * edges * latent * latent,
            bytes_accessed=12_000_000,
            transcendentals=edges * latent,
        ),
        name="edge_block",
    )(
        *[
            in_vmem(array)
            for array in (*came, node_v, edge_v, win_v, wout_v, pre, up, hot, turned)
        ],
    )
    away_b, kept_b = pl.pallas_call(
        functools.partial(rest_kernel, ways),
        out_shape=(sent_shape, kept_shape),
        in_specs=[VMEM] * 5,
        out_specs=(VMEM,) * 2,
        compiler_params=small,
        cost_estimate=pl.CostEstimate(
            flops=2 * edges * latent * latent, bytes_accessed=4_000_000, transcendentals=0
        ),
        name="rest_weights",
    )(*[in_vmem(array) for array in (node_v, edge_v, ext, grad_pre, sums)])
    if four:
        rows = 2 * unit
        piece, wide = pltpu.VMEM((unit, latent), BF16), pltpu.VMEM((unit, latent), F32)
        came_a = swap(away_a, "dp", lambda i: i ^ 1)
        away_a, kept_a, near, far = small_call(
            functools.partial(over_first_kernel, nodes, block),
            "over_first",
            (
                pltpu.VMEM((1, rows, latent), BF16),
                pltpu.VMEM((1, rows, latent), F32),
                block_shape,
                block_shape,
            ),
            came_a,
            kept_a,
            sums,
        )
        came_a = swap(away_a, "dp", lambda i: i ^ 2)
        came_b = swap(away_b, "dp", lambda i: i ^ 1)
        away_b, kept_b = small_call(
            functools.partial(beside_first_kernel, nodes, block),
            "beside_first",
            (pltpu.VMEM((rows + block, latent), BF16), pltpu.VMEM((2, unit, latent), F32)),
            came_b,
            kept_b,
            sums,
        )
        beside = swap(away_b, "dom", lambda i: i ^ 1)
        far = swap(far, "dom", lambda i: partners_of_four(2)[i])
        near = swap(near, "dom", lambda i: partners_of_four(1)[i])
        away_a, kept_a = small_call(
            beside_second_kernel, "beside_second", (piece, wide), came_a, kept_a, near, far
        )
        came_a = swap(away_a, "dom", lambda i: i ^ 1)
        away_b, kept_b = small_call(
            over_second_kernel, "over_second", (piece, wide), beside, kept_b
        )
        came_b = swap(away_b, "dp", lambda i: i ^ 2)
        pair_a = small_call(add_kernel, "add_terms", piece, kept_a, came_a)
        returned = [beside, near, far]
        late, backs = pair_a, 0
    else:
        came_a, kept_a, late = sum_over_dp(away_a, kept_a, cot_v)
        came_b, kept_b, _ = sum_over_dp(away_b, kept_b, cot_v)
        backs = arrivals
    edge_grad, agg, *back_sums = pl.pallas_call(
        functools.partial(edge_grad_kernel, block, arrivals, four),
        out_shape=(
            jax.ShapeDtypeStruct((edges, latent), BF16),
            jax.ShapeDtypeStruct((nodes, latent), BF16),
        )
        + (block_shape,) * backs,
        in_specs=[HBM, SMEM] + [VMEM] * 7,
        out_specs=(VMEM,) * (2 + backs),
        scratch_shapes=[
            pltpu.SMEM((tiles,), jnp.int32),
            pltpu.VMEM((nodes, latent), F32),
            pltpu.SemaphoreType.DMA,
        ],
        compiler_params=small,
        cost_estimate=pl.CostEstimate(
            flops=2 * edges * latent * latent, bytes_accessed=3_000_000, transcendentals=0
        ),
        name="edge_grads",
    )(
        tile_dst,
        tile_count,
        *[in_vmem(array) for array in (late, grad_pre, sums, cot_v, win_v, edge_v, message)],
    )
    if four:
        pair_b = small_call(add_kernel, "add_terms", piece, kept_b, came_b, after=(edge_grad,))
        later = pair_b
    else:
        later = late
        returned = [
            from_behind(back_sums[which], "dom", -OFFSET_LIST[which]) for which in range(4)
        ]
    node_out = pl.pallas_call(
        functools.partial(node_grad_kernel, arrivals, four),
        out_shape=jax.ShapeDtypeStruct((nodes, latent), BF16),
        in_specs=[HBM] + [VMEM] * (3 + arrivals),
        out_specs=VMEM,
        scratch_shapes=[
            pltpu.VMEM((nodes, latent), F32),
            pltpu.SMEM(boundary.shape, jnp.int32),
            pltpu.SemaphoreType.DMA,
        ],
        compiler_params=small,
        cost_estimate=pl.CostEstimate(
            flops=8 * nodes * latent * latent, bytes_accessed=2_000_000, transcendentals=0
        ),
        name="node_grads",
    )(boundary, *[in_vmem(array) for array in (later, sums, win_v, *returned)])
    if four:
        w_in_grad, w_out_grad = pl.pallas_call(
            last_kernel,
            out_shape=(
                jax.ShapeDtypeStruct((3 * unit, latent), F32),
                jax.ShapeDtypeStruct((unit, latent), F32),
            ),
            in_specs=[HBM] + [VMEM] * 4,
            out_specs=(VMEM,) * 2,
            compiler_params=small,
            cost_estimate=pl.CostEstimate(flops=0, bytes_accessed=1_500_000, transcendentals=0),
            name="widen",
        )(in_hbm(node_out), *with_other_half(sum_of_four(pair_a)), *with_other_half(sum_of_four(pair_b)))
    else:
        sum_a = sum_over_dom(kept_a[0] + came_a[0].astype(F32))
        sum_b = sum_over_dom(kept_b[0] + came_b[0].astype(F32))
        w_in_grad = jnp.concatenate([sum_a[unit:], sum_b], axis=0)
        w_out_grad = sum_a[:unit]
    return (agg[None], edge_grad[None], node_out[None], w_in_grad, w_out_grad)


def solution(mesh):
    in_specs = (
        P(("group", "dp"), "dom", None),
        P(("group", "dp"), "dom", None),
        P(("group", "dp"), "dom", None),
        P(),
        P(),
        P(("group", "dom"), None),
        P(("group", "dom")),
        P(("group", "dom")),
        P(("group", "dom"), None),
        P(("group", "dom")),
    )
    out_specs = (
        P(("group", "dp"), "dom", None),
        P(("group", "dp"), "dom", None),
        P(("group", "dp"), "dom", None),
        P(("group", "dp"), None),
        P(("group", "dp"), None),
    )
    return jax.shard_map(body, mesh=mesh, in_specs=in_specs, out_specs=out_specs, check_vma=False)
```

```python
import functools

import jax
import jax.numpy as jnp
from jax import lax
from jax.experimental import pallas as pl
from jax.experimental.pallas import tpu as pltpu
from jax.sharding import PartitionSpec as P

OFFSET_LIST = (1, -1, 2, -2)
EPSILON = 1e-05
VMEM = pl.BlockSpec(memory_space=pltpu.VMEM)
HBM = pl.BlockSpec(memory_space=pltpu.HBM)
SMEM = pl.BlockSpec(memory_space=pltpu.SMEM)
ANY = pl.BlockSpec(memory_space=pl.ANY)
F32 = jnp.float32
BF16 = jnp.bfloat16


def dot(left, right):
    return jnp.dot(left, right, preferred_element_type=F32)


def dot_t(left, right):
    return lax.dot_general(left, right, (((1,), (1,)), ((), ())), preferred_element_type=F32)


def t_dot(left, right):
    return lax.dot_general(left, right, (((0,), (0,)), ((), ())), preferred_element_type=F32)


def row_mean(array):
    return jnp.sum(array, axis=1, keepdims=True) * (1.0 / array.shape[1])


def rows_of(ref, block, size):
    return ref[pl.ds(pl.multiple_of(block * size, size), size), :]


def load_small(source, target, sem):
    copy = pltpu.make_async_copy(source, target, sem)
    copy.start()
    return copy


def boundary_places(boundary_ref, part, four):
    taken = [boundary_ref[0, which] for which in range(4)]
    if not four:
        return taken
    even = part % 2 == 0
    return [
        jnp.where(even, taken[0], taken[1]),
        jnp.where(even, taken[1], taken[0]),
        jnp.where(part < 2, taken[2], taken[3]),
    ]


def arrival_places(part, four, arrivals):
    if not four:
        return list(range(arrivals))
    even = part % 2 == 0
    return [jnp.where(even, 1, 0), jnp.where(even, 0, 1), 2]


def pick_kernel(four, block, boundary_hbm, node_hbm, *refs):
    count = 3 if four else 4
    outs = refs[:count]
    boundary_ref, node_ref, sems = refs[count:]
    small = load_small(boundary_hbm, boundary_ref, sems.at[0])
    large = load_small(node_hbm, node_ref, sems.at[1])
    small.wait()
    places = boundary_places(boundary_ref, lax.axis_index("dom"), four)
    large.wait()
    for place, out in zip(places, outs):
        out[...] = rows_of(node_ref, place, block)


def prep_kernel(
    parts,
    arrivals,
    count_ref,
    src_hbm,
    dst_hbm,
    slot_hbm,
    node_hbm,
    edge_hbm,
    cot_hbm,
    win_hbm,
    wout_hbm,
    node_ref,
    edge_ref,
    cot_ref,
    win_ref,
    wout_ref,
    pre_ref,
    up_ref,
    hot_ref,
    hot_turned,
    src_ref,
    dst_ref,
    slot_ref,
    recv_ref,
    mid_ref,
    sems,
):
    tiles, block = slot_ref.shape
    nodes, latent = node_ref.shape
    owned = nodes // block
    extent = hot_ref.shape[1]
    pairs = (
        (src_hbm, src_ref),
        (dst_hbm, dst_ref),
        (slot_hbm, slot_ref),
        (node_hbm, node_ref),
        (win_hbm.at[2 * latent :, :], win_ref.at[2 * latent :, :]),
        (win_hbm.at[:latent, :], win_ref.at[:latent, :]),
        (edge_hbm, edge_ref),
        (cot_hbm, cot_ref),
        (win_hbm.at[latent : 2 * latent, :], win_ref.at[latent : 2 * latent, :]),
        (wout_hbm, wout_ref),
    )
    copies = [load_small(*pair, sems.at[number]) for number, pair in enumerate(pairs)]
    part = lax.axis_index("dom")
    for copy in copies[:3]:
        copy.wait()
    index = lax.broadcasted_iota(jnp.int32, (extent, 2 * block), 0)
    lane = lax.broadcasted_iota(jnp.int32, (1, 2 * block), 1)
    first = lane < block
    within = jnp.where(first, lane, lane - block)
    node_index = lax.broadcasted_iota(jnp.int32, (nodes, 2 * block), 0)
    for tile in range(0, tiles, 2):
        wanted = []
        for member in (tile, tile + 1):
            source = src_ref[member]
            which = source - owned
            reach = jnp.where(which >= 2, 2, 1)
            partner = part - jnp.where(which % 2 == 1, -reach, reach)
            exists = (source < owned) | ((partner >= 0) & (partner < parts))
            place = jnp.minimum(source, owned + arrivals - 1)
            wanted.append(jnp.where(exists, place * block, -2 * extent))
        slots = jnp.concatenate(
            [slot_ref[tile : tile + 1, :], slot_ref[tile + 1 : tile + 2, :]], axis=1
        )
        row = slots + jnp.where(first, wanted[0], wanted[1])
        hot = jnp.where(index == row, 1.0, 0.0)
        at = slice(tile * block, (tile + 2) * block)
        hot_turned[:extent, at] = hot.astype(BF16)
        target = within + jnp.where(first, dst_ref[tile] * block, dst_ref[tile + 1] * block)
        hot_turned[extent:, at] = jnp.where(node_index == target, 1.0, 0.0).astype(BF16)
        hot_ref[at, :] = hot.T.astype(BF16)
    copies[3].wait()
    copies[4].wait()
    recv_ref[...] = dot(node_ref[...], win_ref[2 * latent :, :])
    copies[5].wait()
    copies[6].wait()
    group = 4 if tiles % 4 == 0 else 2
    for tile in range(0, tiles, group):
        rows = slice(tile * block, (tile + group) * block)
        received = jnp.concatenate(
            [rows_of(recv_ref, dst_ref[t], block) for t in range(tile, tile + group)], axis=0
        )
        pre_ref[rows, :] = dot(edge_ref[rows, :], win_ref[:latent, :]) + received
    copies[7].wait()
    cot = cot_ref[...].astype(F32)
    mid_ref[...] = cot - row_mean(cot)
    for tile in range(tiles):
        live = jnp.where(tile < count_ref[0], 1.0, 0.0)
        up_ref[tile * block : (tile + 1) * block, :] = rows_of(mid_ref, dst_ref[tile], block) * live
    copies[8].wait()
    copies[9].wait()


def put_units(chunk, ways, bit, away, kept, sections):
    latent = sections[0][0].shape[1]
    unit = latent // ways
    step = 128

    def wanted(number, start):
        if number == 0:
            return [(start + at) // unit for at in range(0, step, unit)] if chunk == 0 else []
        found = []
        for at in range(0, step, unit):
            spot = ((number - 1) * latent + start + at) // unit
            if (1 + spot % 3) // 2 == chunk:
                found.append(spot)
        return found

    for number, (left, right) in enumerate(sections):
        value_right = right()
        start = 0
        while start < latent:
            size = step
            if start + 2 * step <= latent and wanted(number, start + step):
                size = 2 * step
            if wanted(number, start):
                value = t_dot(left[:, start : start + size], value_right)
                for at in range(0, size, unit):
                    if number == 0:
                        owner, spot = (start + at) // unit, 0
                    else:
                        place = ((number - 1) * latent + start + at) // unit
                        owner, spot = place // 3, 1 + place % 3
                    if spot // 2 != chunk:
                        continue
                    part = value[at : at + unit]
                    where = slice((spot % 2) * unit, (spot % 2 + 1) * unit)

                    @pl.when(bit == owner % 2)
                    def _(owner=owner, where=where, part=part):
                        kept[owner // 2, where, :] = part

                    @pl.when(bit != owner % 2)
                    def _(owner=owner, where=where, part=part):
                        away[owner // 2, where, :] = part.astype(BF16)

                start += size
            else:
                start += step


def edge_kernel(ways, arrivals, four, block, *refs):
    arrived = refs[:arrivals][::-1]
    (
        node_ref,
        edge_ref,
        win_ref,
        wout_ref,
        pre_ref,
        up_ref,
        hot_ref,
        hot_turned,
        gpre_ref,
        message_ref,
        sums_ref,
        ext_ref,
        away_ref,
        kept_ref,
        act_ref,
        proj_ref,
    ) = refs[arrivals:]
    nodes, latent = node_ref.shape
    edges = edge_ref.shape[0]
    extent = ext_ref.shape[0]
    places = arrival_places(lax.axis_index("dom"), four, arrivals)

    ext_ref[:nodes, :] = node_ref[...]
    for which in range(arrivals):
        at = pl.multiple_of(nodes + places[which] * block, block)
        ext_ref[pl.ds(at, block), :] = arrived[which][...]
    filled = nodes + arrivals * block
    if filled < extent:
        ext_ref[filled:, :] = jnp.zeros((extent - filled, latent), BF16)

    span = 256 if edges % 256 == 0 else block
    for start in range(0, edges, span):
        rows = slice(start, start + span)
        senders = dot(hot_ref[rows, :], ext_ref[...]).astype(BF16)
        preact = pre_ref[rows, :] + dot(senders, win_ref[latent : 2 * latent, :])
        gate = 0.5 * jnp.tanh(0.5 * preact) + 0.5
        activated = preact * gate
        slope = gate + activated * (1.0 - gate)
        activated = activated.astype(BF16)
        act_ref[rows, :] = activated
        projected = dot(activated, wout_ref[...])
        centered = projected - row_mean(projected)
        inv_scale = lax.rsqrt(row_mean(centered * centered) + EPSILON)
        message = centered * inv_scale
        message_ref[rows, :] = message
        upstream = up_ref[rows, :]
        grad_project = inv_scale * (upstream - message * row_mean(upstream * message))
        grad_project = grad_project.astype(BF16)
        proj_ref[rows, :] = grad_project
        gpre_ref[rows, :] = (dot_t(grad_project, wout_ref[...]) * slope).astype(BF16)

    sums_ref[...] = dot(hot_turned[...], gpre_ref[...])
    sections = (
        (act_ref, lambda: proj_ref[...]),
        (edge_ref, lambda: gpre_ref[...]),
        (ext_ref, lambda: sums_ref[:extent, :].astype(BF16)),
        (node_ref, lambda: sums_ref[extent:, :].astype(BF16)),
    )
    put_units(0, ways, lax.axis_index("dp") % 2, away_ref, kept_ref, sections)


def rest_kernel(ways, node_ref, edge_ref, ext_ref, gpre_ref, sums_ref, away_ref, kept_ref):
    extent = ext_ref.shape[0]
    sections = (
        (edge_ref, lambda: None),
        (edge_ref, lambda: gpre_ref[...]),
        (ext_ref, lambda: sums_ref[:extent, :].astype(BF16)),
        (node_ref, lambda: sums_ref[extent:, :].astype(BF16)),
    )
    put_units(1, ways, lax.axis_index("dp") % 2, away_ref, kept_ref, sections)


def edge_grad_kernel(
    block,
    arrivals,
    four,
    dst_hbm,
    count_ref,
    after,
    gpre_ref,
    sums_ref,
    cot_ref,
    win_ref,
    edge_ref,
    message_ref,
    out_ref,
    agg_out,
    *refs,
):
    back_sums = refs[:-3]
    dst_ref, agg_ref, sem = refs[-3:]
    copy = load_small(dst_hbm, dst_ref, sem)
    nodes, latent = cot_ref.shape
    tiles = gpre_ref.shape[0] // block
    group = 4 if tiles % 4 == 0 else 1
    places = arrival_places(lax.axis_index("dom"), four, arrivals)
    for place, back_ref in zip(places, back_sums):
        at = pl.multiple_of(nodes + place * block, block)
        back_ref[...] = sums_ref[pl.ds(at, block), :].astype(BF16)
    agg_ref[...] = jnp.zeros_like(agg_ref)
    copy.wait()
    for first in range(0, tiles, group):
        rows = slice(first * block, (first + group) * block)
        upstream = jnp.concatenate(
            [
                rows_of(cot_ref, dst_ref[t], block).astype(F32)
                * jnp.where(t < count_ref[0], 1.0, 0.0)
                for t in range(first, first + group)
            ],
            axis=0,
        )
        out_ref[rows, :] = (dot_t(gpre_ref[rows, :], win_ref[:latent, :]) + upstream).astype(BF16)
        for t in range(first, first + group):
            live = jnp.where(t < count_ref[0], 1.0, 0.0)
            mine = slice(t * block, (t + 1) * block)
            updated = edge_ref[mine, :].astype(F32) + message_ref[mine, :]
            target = pl.ds(pl.multiple_of(dst_ref[t] * block, block), block)
            agg_ref[target, :] += updated * live
    agg_out[...] = agg_ref[...].astype(BF16)


def halve_kernel(bit, came_ref, kept_ref, after, away_ref, left_ref):
    mine = (lax.axis_index("dp") // bit) % 2
    for slot in range(left_ref.shape[0]):
        there, here = 2 * slot + 1 - mine, 2 * slot + mine
        away_ref[slot] = (kept_ref[there] + came_ref[there].astype(F32)).astype(BF16)
        left_ref[slot] = kept_ref[here] + came_ref[here].astype(F32)


def half_rows(rows):
    part = lax.axis_index("dom")
    inner = (part == 1) | (part == 2)
    here = pl.ds(pl.multiple_of(jnp.where(inner, 0, rows), rows), rows)
    there = pl.ds(pl.multiple_of(jnp.where(inner, rows, 0), rows), rows)
    return here, there


def back_block(nodes, block, sums_ref, which):
    place = arrival_places(lax.axis_index("dom"), True, 3)[which]
    return sums_ref[pl.ds(pl.multiple_of(nodes + place * block, block), block), :].astype(BF16)


def beside_first_kernel(nodes, block, came_ref, kept_ref, sums_ref, away_ref, left_ref):
    rows = left_ref.shape[1]
    here, there = half_rows(rows)
    for slot in range(2):
        away_ref[slot * rows : (slot + 1) * rows, :] = (
            kept_ref[slot, there, :] + came_ref[slot, there, :].astype(F32)
        ).astype(BF16)
        left_ref[slot] = kept_ref[slot, here, :] + came_ref[slot, here, :].astype(F32)
    away_ref[2 * rows :, :] = back_block(nodes, block, sums_ref, 0)


def beside_second_kernel(came_ref, kept_ref, *refs):
    away_ref, left_ref = refs[-2:]
    here, there = half_rows(left_ref.shape[0])
    away_ref[...] = (kept_ref[0, there, :] + came_ref[0, there, :].astype(F32)).astype(BF16)
    left_ref[...] = kept_ref[0, here, :] + came_ref[0, here, :].astype(F32)


def over_second_kernel(
    nodes, block, came_ref, kept_ref, sums_ref, away_ref, left_ref, near_ref, far_ref
):
    mine = lax.axis_index("dp") // 2
    rows = left_ref.shape[0]

    def came(slot):
        spot = pl.ds(pl.multiple_of(slot * rows, rows), rows)
        return came_ref[spot, :].astype(F32)

    away_ref[...] = (kept_ref[1 - mine] + came(1 - mine)).astype(BF16)
    left_ref[...] = kept_ref[mine] + came(mine)
    near_ref[...] = back_block(nodes, block, sums_ref, 1)
    far_ref[...] = back_block(nodes, block, sums_ref, 2)


def add_kernel(left_a, came_a, left_b, came_b, *refs):
    out_ref = refs[-1]
    rows = left_a.shape[0]
    out_ref[:rows, :] = (left_a[...] + came_a[...].astype(F32)).astype(BF16)
    out_ref[rows:, :] = (left_b[...] + came_b[...].astype(F32)).astype(BF16)


def node_grad_kernel(arrivals, four, boundary_hbm, after, sums_ref, win_ref, *refs):
    returned = refs[:arrivals]
    out_ref, total_ref, boundary_ref, sem = refs[arrivals:]
    nodes, latent = out_ref.shape
    extent = sums_ref.shape[0] - nodes
    block = returned[-1].shape[0]
    copy = load_small(boundary_hbm, boundary_ref, sem)
    total_ref[...] = sums_ref[:nodes, :]
    copy.wait()
    for which, place in enumerate(boundary_places(boundary_ref, lax.axis_index("dom"), four)):
        spot = pl.ds(pl.multiple_of(place * block, block), block)
        total_ref[spot, :] += returned[which][-block:, :].astype(F32)

    def wide_dot(value, weight):
        high = value.astype(BF16)
        low = (value - high.astype(F32)).astype(BF16)
        return dot_t(high, weight) + dot_t(low, weight)

    out_ref[...] = (
        wide_dot(total_ref[...], win_ref[latent : 2 * latent, :])
        + wide_dot(sums_ref[extent:, :], win_ref[2 * latent :, :])
    ).astype(BF16)


def last_kernel(node_out, edge_grad, own_ref, other_ref, in_ref, out_ref):
    unit = out_ref.shape[0]
    part = lax.axis_index("dom")
    inner = (part == 1) | (part == 2)

    def write(low, high):
        out_ref[...] = low[:unit, :].astype(F32)
        in_ref[:unit, :] = high[:unit, :].astype(F32)
        in_ref[unit : 2 * unit, :] = low[unit:, :].astype(F32)
        in_ref[2 * unit :, :] = high[unit:, :].astype(F32)

    @pl.when(inner)
    def _():
        write(own_ref, other_ref)

    @pl.when(jnp.logical_not(inner))
    def _():
        write(other_ref, own_ref)


def swap(array, axis, partner):
    devices = lax.axis_size(axis)
    return lax.ppermute(array, axis, [(i, partner(i)) for i in range(devices)])


def from_behind(array, axis, by):
    devices = lax.axis_size(axis)
    pairs = [(i, i + by) for i in range(devices) if 0 <= i + by < devices]
    return lax.ppermute(array, axis, pairs)


def partners_of_four(which):
    return ((1, 0, 3, 2), (0, 2, 1, 3), (2, 3, 0, 1))[which]


def exchange_of_four(first, second, third):
    third = swap(third, "dom", lambda i: partners_of_four(2)[i])
    second = swap(second, "dom", lambda i: partners_of_four(1)[i])
    first = swap(first, "dom", lambda i: partners_of_four(0)[i])
    return [first, second, third]


def halve(bit, came, kept, after):
    slots, rows, latent = kept.shape
    return pl.pallas_call(
        functools.partial(halve_kernel, bit),
        out_shape=(
            pltpu.VMEM((slots // 2, rows, latent), BF16),
            pltpu.VMEM((slots // 2, rows, latent), F32),
        ),
        in_specs=[VMEM] * 3,
        out_specs=(VMEM,) * 2,
        compiler_params=pltpu.CompilerParams(vmem_limit_bytes=4 * 1024 * 1024),
        cost_estimate=pl.CostEstimate(flops=0, bytes_accessed=500_000, transcendentals=0),
        name="halve",
    )(in_vmem(came), in_vmem(kept), in_vmem(after))


def sum_over_dp(away, kept, after):
    devices = lax.axis_size("dp")
    bit = 1
    while True:
        came = swap(away, "dp", lambda i, bit=bit: i ^ bit)
        bit *= 2
        if bit >= devices:
            return came, kept, away
        away, kept = halve(bit, came, kept, after)


def small_call(kernel, name, out_shape, *operands, after=()):
    many = isinstance(out_shape, tuple)
    return pl.pallas_call(
        kernel,
        out_shape=out_shape,
        in_specs=[VMEM] * len(operands) + [HBM] * len(after),
        out_specs=(VMEM,) * len(out_shape) if many else VMEM,
        compiler_params=pltpu.CompilerParams(vmem_limit_bytes=4 * 1024 * 1024),
        cost_estimate=pl.CostEstimate(flops=0, bytes_accessed=500_000, transcendentals=0),
        name=name,
    )(*[in_vmem(array) for array in operands], *[in_hbm(array) for array in after])


def sum_of_four(kept):
    return (kept.astype(F32) + swap(kept, "dom", lambda i: 3 - i).astype(F32)).astype(BF16)


def with_other_half(kept):
    return kept, swap(kept, "dom", lambda i: i ^ 1)


def sum_over_dom(rows):
    piece = lax.psum_scatter(rows, "dom", scatter_dimension=0, tiled=True)
    return lax.all_gather(piece, "dom", axis=0, tiled=True)


def in_vmem(array):
    return pltpu.with_memory_space_constraint(array, pltpu.VMEM)


def in_hbm(array):
    return pltpu.with_memory_space_constraint(array, pltpu.HBM)


def body(
    node_latents,
    edge_latents,
    agg_cotangent,
    weight_in,
    weight_out,
    boundary,
    tile_src,
    tile_dst,
    edge_slot,
    tile_count,
):
    tiles, block = edge_slot.shape
    edges, latent = edge_latents.shape[1:]
    nodes = node_latents.shape[1]
    parts = lax.axis_size("dom")
    ways = lax.axis_size("dp")
    four = parts == 4 and ways == 4
    arrivals = 3 if four else 4
    boundary = in_hbm(boundary)
    tile_dst = in_hbm(tile_dst)
    node_rows = in_hbm(node_latents[0])
    block_shape = pltpu.VMEM((block, latent), BF16)
    small = pltpu.CompilerParams(vmem_limit_bytes=8 * 1024 * 1024)

    sent = pl.pallas_call(
        functools.partial(pick_kernel, four, block),
        out_shape=(block_shape,) * arrivals,
        in_specs=[HBM] * 2,
        out_specs=(VMEM,) * arrivals,
        scratch_shapes=[
            pltpu.SMEM(boundary.shape, jnp.int32),
            pltpu.VMEM((nodes, latent), BF16),
            pltpu.SemaphoreType.DMA((2,)),
        ],
        compiler_params=small,
        cost_estimate=pl.CostEstimate(flops=0, bytes_accessed=400_000, transcendentals=0),
        name="pick_blocks",
    )(boundary, node_rows)
    if four:
        came = exchange_of_four(*sent)
    else:
        came = [from_behind(sent[which], "dom", OFFSET_LIST[which]) for which in range(4)]
    unit = latent // ways
    half = ways // 2
    extent = -(-(nodes + arrivals * block) // 128) * 128

    node_v, edge_v, cot_v, win_v, wout_v, pre, up, hot, turned = pl.pallas_call(
        functools.partial(prep_kernel, parts, arrivals),
        out_shape=(
            pltpu.VMEM((nodes, latent), BF16),
            pltpu.VMEM((edges, latent), BF16),
            pltpu.VMEM((nodes, latent), BF16),
            pltpu.VMEM(weight_in.shape, BF16),
            pltpu.VMEM(weight_out.shape, BF16),
            pltpu.VMEM((edges, latent), F32),
            pltpu.VMEM((edges, latent), F32),
            pltpu.VMEM((edges, extent), BF16),
            pltpu.VMEM((extent + nodes, edges), BF16),
        ),
        in_specs=[SMEM] + [HBM] * 8,
        out_specs=(VMEM,) * 9,
        scratch_shapes=[
            pltpu.SMEM((tiles,), jnp.int32),
            pltpu.SMEM((tiles,), jnp.int32),
            pltpu.VMEM((tiles, block), jnp.int32),
            pltpu.VMEM((nodes, latent), F32),
            pltpu.VMEM((nodes, latent), F32),
            pltpu.SemaphoreType.DMA((10,)),
        ],
        compiler_params=small,
        cost_estimate=pl.CostEstimate(
            flops=2 * edges * latent * latent, bytes_accessed=8_000_000, transcendentals=0
        ),
        name="prepare",
    )(
        tile_count,
        in_hbm(tile_src),
        tile_dst,
        in_hbm(edge_slot),
        node_rows,
        in_hbm(edge_latents[0]),
        in_hbm(agg_cotangent[0]),
        in_hbm(weight_in),
        in_hbm(weight_out),
    )
    sent_shape = pltpu.VMEM((half, 2 * unit, latent), BF16)
    kept_shape = pltpu.VMEM((half, 2 * unit, latent), F32)
    grad_pre, message, sums, ext, away_a, kept_a = pl.pallas_call(
        functools.partial(edge_kernel, ways, arrivals, four, block),
        out_shape=(
            pltpu.VMEM((edges, latent), BF16),
            pltpu.VMEM((edges, latent), F32),
            pltpu.VMEM((extent + nodes, latent), F32),
            pltpu.VMEM((extent, latent), BF16),
            sent_shape,
            kept_shape,
        ),
        in_specs=[VMEM] * (8 + arrivals),
        out_specs=(VMEM,) * 6,
        scratch_shapes=[
            pltpu.VMEM((edges, latent), BF16),
            pltpu.VMEM((edges, latent), BF16),
        ],
        compiler_params=pltpu.CompilerParams(vmem_limit_bytes=16 * 1024 * 1024),
        cost_estimate=pl.CostEstimate(
            flops=12 * edges * latent * latent,
            bytes_accessed=12_000_000,
            transcendentals=edges * latent,
        ),
        name="edge_block",
    )(
        *[
            in_vmem(array)
            for array in (*came[::-1], node_v, edge_v, win_v, wout_v, pre, up, hot, turned)
        ],
    )
    away_b, kept_b = pl.pallas_call(
        functools.partial(rest_kernel, ways),
        out_shape=(sent_shape, kept_shape),
        in_specs=[VMEM] * 5,
        out_specs=(VMEM,) * 2,
        compiler_params=small,
        cost_estimate=pl.CostEstimate(
            flops=2 * edges * latent * latent, bytes_accessed=4_000_000, transcendentals=0
        ),
        name="rest_weights",
    )(*[in_vmem(array) for array in (node_v, edge_v, ext, grad_pre, sums)])
    if four:
        rows = 2 * unit
        piece, wide = pltpu.VMEM((unit, latent), BF16), pltpu.VMEM((unit, latent), F32)
        came_a = swap(away_a, "dp", lambda i: i ^ 1)
        away_a, kept_a = halve(2, came_a, kept_a, cot_v)
        came_a = swap(away_a, "dp", lambda i: i ^ 2)
        came_b = swap(away_b, "dp", lambda i: i ^ 1)
        away_b, kept_b = small_call(
            functools.partial(beside_first_kernel, nodes, block),
            "beside_first",
            (pltpu.VMEM((rows + block, latent), BF16), pltpu.VMEM((2, unit, latent), F32)),
            came_b,
            kept_b,
            sums,
        )
        beside = swap(away_b, "dom", lambda i: i ^ 1)
        away_a, kept_a = small_call(
            beside_second_kernel, "beside_second", (piece, wide), came_a, kept_a
        )
        came_a = swap(away_a, "dom", lambda i: i ^ 1)
        away_b, kept_b, near, far = small_call(
            functools.partial(over_second_kernel, nodes, block),
            "over_second",
            (piece, wide, block_shape, block_shape),
            beside,
            kept_b,
            sums,
        )
        came_b = swap(away_b, "dp", lambda i: i ^ 2)
        far = swap(far, "dom", lambda i: partners_of_four(2)[i])
        near = swap(near, "dom", lambda i: partners_of_four(1)[i])
        pair = small_call(
            add_kernel,
            "add_terms",
            pltpu.VMEM((rows, latent), BF16),
            kept_a,
            came_a,
            kept_b,
            came_b,
            near,
            far,
        )
        returned = [beside, near, far]
        late, backs = pair, 0
    else:
        came_a, kept_a, late = sum_over_dp(away_a, kept_a, cot_v)
        came_b, kept_b, _ = sum_over_dp(away_b, kept_b, cot_v)
        backs = arrivals
    edge_grad, agg, *back_sums = pl.pallas_call(
        functools.partial(edge_grad_kernel, block, arrivals, four),
        out_shape=(
            jax.ShapeDtypeStruct((edges, latent), BF16),
            jax.ShapeDtypeStruct((nodes, latent), BF16),
        )
        + (block_shape,) * backs,
        in_specs=[HBM, SMEM] + [VMEM] * 7,
        out_specs=(VMEM,) * (2 + backs),
        scratch_shapes=[
            pltpu.SMEM((tiles,), jnp.int32),
            pltpu.VMEM((nodes, latent), F32),
            pltpu.SemaphoreType.DMA,
        ],
        compiler_params=small,
        cost_estimate=pl.CostEstimate(
            flops=2 * edges * latent * latent, bytes_accessed=3_000_000, transcendentals=0
        ),
        name="edge_grads",
    )(
        tile_dst,
        tile_count,
        *[in_vmem(array) for array in (late, grad_pre, sums, cot_v, win_v, edge_v, message)],
    )
    if not four:
        returned = [
            from_behind(back_sums[which], "dom", -OFFSET_LIST[which]) for which in range(4)
        ]
    node_out = pl.pallas_call(
        functools.partial(node_grad_kernel, arrivals, four),
        out_shape=jax.ShapeDtypeStruct((nodes, latent), BF16),
        in_specs=[HBM] + [VMEM] * (3 + arrivals),
        out_specs=VMEM,
        scratch_shapes=[
            pltpu.VMEM((nodes, latent), F32),
            pltpu.SMEM(boundary.shape, jnp.int32),
            pltpu.SemaphoreType.DMA,
        ],
        compiler_params=small,
        cost_estimate=pl.CostEstimate(
            flops=8 * nodes * latent * latent, bytes_accessed=2_000_000, transcendentals=0
        ),
        name="node_grads",
    )(boundary, *[in_vmem(array) for array in (late, sums, win_v, *returned)])
    if four:
        w_in_grad, w_out_grad = pl.pallas_call(
            last_kernel,
            out_shape=(
                jax.ShapeDtypeStruct((3 * unit, latent), F32),
                jax.ShapeDtypeStruct((unit, latent), F32),
            ),
            in_specs=[HBM] * 2 + [VMEM] * 2,
            out_specs=(VMEM,) * 2,
            compiler_params=small,
            cost_estimate=pl.CostEstimate(flops=0, bytes_accessed=1_500_000, transcendentals=0),
            name="widen",
        )(in_hbm(node_out), in_hbm(edge_grad), *with_other_half(sum_of_four(pair)))
    else:
        sum_a = sum_over_dom(kept_a[0] + came_a[0].astype(F32))
        sum_b = sum_over_dom(kept_b[0] + came_b[0].astype(F32))
        w_in_grad = jnp.concatenate([sum_a[unit:], sum_b], axis=0)
        w_out_grad = sum_a[:unit]
    return (agg[None], edge_grad[None], node_out[None], w_in_grad, w_out_grad)


def solution(mesh):
    in_specs = (
        P(("group", "dp"), "dom", None),
        P(("group", "dp"), "dom", None),
        P(("group", "dp"), "dom", None),
        P(),
        P(),
        P(("group", "dom"), None),
        P(("group", "dom")),
        P(("group", "dom")),
        P(("group", "dom"), None),
        P(("group", "dom")),
    )
    out_specs = (
        P(("group", "dp"), "dom", None),
        P(("group", "dp"), "dom", None),
        P(("group", "dp"), "dom", None),
        P(("group", "dp"), None),
        P(("group", "dp"), None),
    )
    return jax.shard_map(body, mesh=mesh, in_specs=in_specs, out_specs=out_specs, check_vma=False)
```

```python
import functools

import jax
import jax.numpy as jnp
from jax import lax
from jax.experimental import pallas as pl
from jax.experimental.pallas import tpu as pltpu
from jax.sharding import PartitionSpec as P

OFFSET_LIST = (1, -1, 2, -2)
EPSILON = 1e-05
VMEM = pl.BlockSpec(memory_space=pltpu.VMEM)
HBM = pl.BlockSpec(memory_space=pltpu.HBM)
SMEM = pl.BlockSpec(memory_space=pltpu.SMEM)
ANY = pl.BlockSpec(memory_space=pl.ANY)
F32 = jnp.float32
BF16 = jnp.bfloat16


def dot(left, right):
    return jnp.dot(left, right, preferred_element_type=F32)


def dot_t(left, right):
    return lax.dot_general(left, right, (((1,), (1,)), ((), ())), preferred_element_type=F32)


def t_dot(left, right):
    return lax.dot_general(left, right, (((0,), (0,)), ((), ())), preferred_element_type=F32)


def row_mean(array):
    return jnp.sum(array, axis=1, keepdims=True) * (1.0 / array.shape[1])


def rows_of(ref, block, size):
    return ref[pl.ds(pl.multiple_of(block * size, size), size), :]


def load_small(source, target, sem):
    copy = pltpu.make_async_copy(source, target, sem)
    copy.start()
    return copy


def boundary_places(boundary_ref, part, four):
    taken = [boundary_ref[0, which] for which in range(4)]
    if not four:
        return taken
    even = part % 2 == 0
    return [
        jnp.where(even, taken[0], taken[1]),
        jnp.where(even, taken[1], taken[0]),
        jnp.where(part < 2, taken[2], taken[3]),
    ]


def arrival_places(part, four, arrivals):
    if not four:
        return list(range(arrivals))
    even = part % 2 == 0
    return [jnp.where(even, 1, 0), jnp.where(even, 0, 1), 2]


def pick_kernel(four, block, boundary_hbm, node_hbm, *refs):
    count = 3 if four else 4
    outs = refs[:count]
    boundary_ref, node_ref, sems = refs[count:]
    small = load_small(boundary_hbm, boundary_ref, sems.at[0])
    large = load_small(node_hbm, node_ref, sems.at[1])
    small.wait()
    places = boundary_places(boundary_ref, lax.axis_index("dom"), four)
    large.wait()
    for place, out in zip(places, outs):
        out[...] = rows_of(node_ref, place, block)


def prep_kernel(
    parts,
    arrivals,
    count_ref,
    src_hbm,
    dst_hbm,
    slot_hbm,
    node_hbm,
    edge_hbm,
    cot_hbm,
    win_hbm,
    wout_hbm,
    node_ref,
    edge_ref,
    cot_ref,
    win_ref,
    wout_ref,
    pre_ref,
    up_ref,
    hot_ref,
    hot_turned,
    src_ref,
    dst_ref,
    slot_ref,
    recv_ref,
    mid_ref,
    sems,
):
    tiles, block = slot_ref.shape
    nodes, latent = node_ref.shape
    owned = nodes // block
    extent = hot_ref.shape[1]
    pairs = (
        (src_hbm, src_ref),
        (dst_hbm, dst_ref),
        (slot_hbm, slot_ref),
        (node_hbm, node_ref),
        (win_hbm.at[2 * latent :, :], win_ref.at[2 * latent :, :]),
        (win_hbm.at[:latent, :], win_ref.at[:latent, :]),
        (edge_hbm, edge_ref),
        (cot_hbm, cot_ref),
        (win_hbm.at[latent : 2 * latent, :], win_ref.at[latent : 2 * latent, :]),
        (wout_hbm, wout_ref),
    )
    copies = [load_small(*pair, sems.at[number]) for number, pair in enumerate(pairs)]
    part = lax.axis_index("dom")
    for copy in copies[:3]:
        copy.wait()
    index = lax.broadcasted_iota(jnp.int32, (extent, 2 * block), 0)
    lane = lax.broadcasted_iota(jnp.int32, (1, 2 * block), 1)
    first = lane < block
    within = jnp.where(first, lane, lane - block)
    node_index = lax.broadcasted_iota(jnp.int32, (nodes, 2 * block), 0)
    for tile in range(0, tiles, 2):
        wanted = []
        for member in (tile, tile + 1):
            source = src_ref[member]
            which = source - owned
            reach = jnp.where(which >= 2, 2, 1)
            partner = part - jnp.where(which % 2 == 1, -reach, reach)
            exists = (source < owned) | ((partner >= 0) & (partner < parts))
            place = jnp.minimum(source, owned + arrivals - 1)
            wanted.append(jnp.where(exists, place * block, -2 * extent))
        slots = jnp.concatenate(
            [slot_ref[tile : tile + 1, :], slot_ref[tile + 1 : tile + 2, :]], axis=1
        )
        row = slots + jnp.where(first, wanted[0], wanted[1])
        hot = jnp.where(index == row, 1.0, 0.0)
        at = slice(tile * block, (tile + 2) * block)
        hot_turned[:extent, at] = hot.astype(BF16)
        target = within + jnp.where(first, dst_ref[tile] * block, dst_ref[tile + 1] * block)
        hot_turned[extent:, at] = jnp.where(node_index == target, 1.0, 0.0).astype(BF16)
        hot_ref[at, :] = hot.T.astype(BF16)
    copies[3].wait()
    copies[4].wait()
    recv_ref[...] = dot(node_ref[...], win_ref[2 * latent :, :])
    copies[5].wait()
    copies[6].wait()
    group = 4 if tiles % 4 == 0 else 2
    for tile in range(0, tiles, group):
        rows = slice(tile * block, (tile + group) * block)
        received = jnp.concatenate(
            [rows_of(recv_ref, dst_ref[t], block) for t in range(tile, tile + group)], axis=0
        )
        pre_ref[rows, :] = dot(edge_ref[rows, :], win_ref[:latent, :]) + received
    copies[7].wait()
    cot = cot_ref[...].astype(F32)
    mid_ref[...] = cot - row_mean(cot)
    for tile in range(tiles):
        live = jnp.where(tile < count_ref[0], 1.0, 0.0)
        up_ref[tile * block : (tile + 1) * block, :] = rows_of(mid_ref, dst_ref[tile], block) * live
    copies[8].wait()
    copies[9].wait()


def put_units(ways, bit, targets, sections):
    latent = sections[0][0].shape[1]
    unit = latent // ways
    step = 256
    for number, (left, right) in enumerate(sections):
        value_right = right()
        for start in range(0, latent, step):
            value = t_dot(left[:, start : start + step], value_right)
            for at in range(0, step, unit):
                owner, spot = (start + at) // unit, 0
                if number > 0:
                    place = ((number - 1) * latent + start + at) // unit
                    owner, spot = place // 3, 1 + place % 3
                away, kept = targets[spot // 2]
                part = value[at : at + unit]
                where = slice((spot % 2) * unit, (spot % 2 + 1) * unit)

                @pl.when(bit == owner % 2)
                def _(kept=kept, owner=owner, where=where, part=part):
                    kept[owner // 2, where, :] = part

                @pl.when(bit != owner % 2)
                def _(away=away, owner=owner, where=where, part=part):
                    away[owner // 2, where, :] = part.astype(BF16)


def edge_kernel(ways, arrivals, four, block, *refs):
    arrived = refs[:arrivals][::-1]
    (
        node_ref,
        edge_ref,
        win_ref,
        wout_ref,
        pre_ref,
        up_ref,
        hot_ref,
        hot_turned,
        gpre_ref,
        message_ref,
        sums_ref,
        away_a,
        kept_a,
        away_b,
        kept_b,
        *back_refs,
        ext_ref,
        act_ref,
        proj_ref,
    ) = refs[arrivals:]
    nodes, latent = node_ref.shape
    edges = edge_ref.shape[0]
    extent = ext_ref.shape[0]
    places = arrival_places(lax.axis_index("dom"), four, arrivals)

    ext_ref[:nodes, :] = node_ref[...]
    for which in range(arrivals):
        at = pl.multiple_of(nodes + places[which] * block, block)
        ext_ref[pl.ds(at, block), :] = arrived[which][...]
    filled = nodes + arrivals * block
    if filled < extent:
        ext_ref[filled:, :] = jnp.zeros((extent - filled, latent), BF16)

    span = 256 if edges % 256 == 0 else block
    for start in range(0, edges, span):
        rows = slice(start, start + span)
        senders = dot(hot_ref[rows, :], ext_ref[...]).astype(BF16)
        preact = pre_ref[rows, :] + dot(senders, win_ref[latent : 2 * latent, :])
        gate = 0.5 * jnp.tanh(0.5 * preact) + 0.5
        activated = preact * gate
        slope = gate + activated * (1.0 - gate)
        activated = activated.astype(BF16)
        act_ref[rows, :] = activated
        projected = dot(activated, wout_ref[...])
        centered = projected - row_mean(projected)
        inv_scale = lax.rsqrt(row_mean(centered * centered) + EPSILON)
        message = centered * inv_scale
        message_ref[rows, :] = message
        upstream = up_ref[rows, :]
        grad_project = inv_scale * (upstream - message * row_mean(upstream * message))
        grad_project = grad_project.astype(BF16)
        proj_ref[rows, :] = grad_project
        gpre_ref[rows, :] = (dot_t(grad_project, wout_ref[...]) * slope).astype(BF16)

    sums_ref[...] = dot(hot_turned[...], gpre_ref[...])
    for which, back_ref in enumerate(back_refs):
        back_ref[...] = back_block(nodes, block, sums_ref, 1 + which)
    sections = (
        (act_ref, lambda: proj_ref[...]),
        (edge_ref, lambda: gpre_ref[...]),
        (ext_ref, lambda: sums_ref[:extent, :].astype(BF16)),
        (node_ref, lambda: sums_ref[extent:, :].astype(BF16)),
    )
    targets = ((away_a, kept_a), (away_b, kept_b))
    put_units(ways, lax.axis_index("dp") % 2, targets, sections)


def edge_grad_kernel(
    block,
    arrivals,
    four,
    dst_hbm,
    count_ref,
    after,
    gpre_ref,
    sums_ref,
    cot_ref,
    win_ref,
    edge_ref,
    message_ref,
    out_ref,
    agg_out,
    *refs,
):
    back_sums = refs[:-3]
    dst_ref, agg_ref, sem = refs[-3:]
    copy = load_small(dst_hbm, dst_ref, sem)
    nodes, latent = cot_ref.shape
    tiles = gpre_ref.shape[0] // block
    group = 4 if tiles % 4 == 0 else 1
    places = arrival_places(lax.axis_index("dom"), four, arrivals)
    for place, back_ref in zip(places, back_sums):
        at = pl.multiple_of(nodes + place * block, block)
        back_ref[...] = sums_ref[pl.ds(at, block), :].astype(BF16)
    agg_ref[...] = jnp.zeros_like(agg_ref)
    copy.wait()
    for first in range(0, tiles, group):
        rows = slice(first * block, (first + group) * block)
        upstream = jnp.concatenate(
            [
                rows_of(cot_ref, dst_ref[t], block).astype(F32)
                * jnp.where(t < count_ref[0], 1.0, 0.0)
                for t in range(first, first + group)
            ],
            axis=0,
        )
        out_ref[rows, :] = (dot_t(gpre_ref[rows, :], win_ref[:latent, :]) + upstream).astype(BF16)
        for t in range(first, first + group):
            live = jnp.where(t < count_ref[0], 1.0, 0.0)
            mine = slice(t * block, (t + 1) * block)
            updated = edge_ref[mine, :].astype(F32) + message_ref[mine, :]
            target = pl.ds(pl.multiple_of(dst_ref[t] * block, block), block)
            agg_ref[target, :] += updated * live
    agg_out[...] = agg_ref[...].astype(BF16)


def halve_kernel(bit, came_ref, kept_ref, after, away_ref, left_ref):
    mine = (lax.axis_index("dp") // bit) % 2
    for slot in range(left_ref.shape[0]):
        there, here = 2 * slot + 1 - mine, 2 * slot + mine
        away_ref[slot] = (kept_ref[there] + came_ref[there].astype(F32)).astype(BF16)
        left_ref[slot] = kept_ref[here] + came_ref[here].astype(F32)


def half_rows(rows):
    part = lax.axis_index("dom")
    inner = (part == 1) | (part == 2)
    here = pl.ds(pl.multiple_of(jnp.where(inner, 0, rows), rows), rows)
    there = pl.ds(pl.multiple_of(jnp.where(inner, rows, 0), rows), rows)
    return here, there


def back_block(nodes, block, sums_ref, which):
    place = arrival_places(lax.axis_index("dom"), True, 3)[which]
    return sums_ref[pl.ds(pl.multiple_of(nodes + place * block, block), block), :].astype(BF16)


def beside_first_kernel(nodes, block, came_ref, kept_ref, sums_ref, away_ref, left_ref):
    rows = left_ref.shape[1]
    here, there = half_rows(rows)
    for slot in range(2):
        away_ref[slot * rows : (slot + 1) * rows, :] = (
            kept_ref[slot, there, :] + came_ref[slot, there, :].astype(F32)
        ).astype(BF16)
        left_ref[slot] = kept_ref[slot, here, :] + came_ref[slot, here, :].astype(F32)
    away_ref[2 * rows :, :] = back_block(nodes, block, sums_ref, 0)


def beside_second_kernel(came_ref, kept_ref, *refs):
    away_ref, left_ref = refs[-2:]
    here, there = half_rows(left_ref.shape[0])
    away_ref[...] = (kept_ref[0, there, :] + came_ref[0, there, :].astype(F32)).astype(BF16)
    left_ref[...] = kept_ref[0, here, :] + came_ref[0, here, :].astype(F32)


def over_second_kernel(came_ref, kept_ref, *refs):
    away_ref, left_ref = refs[-2:]
    mine = lax.axis_index("dp") // 2
    rows = left_ref.shape[0]

    def came(slot):
        spot = pl.ds(pl.multiple_of(slot * rows, rows), rows)
        return came_ref[spot, :].astype(F32)

    away_ref[...] = (kept_ref[1 - mine] + came(1 - mine)).astype(BF16)
    left_ref[...] = kept_ref[mine] + came(mine)


def add_kernel(left_a, came_a, left_b, came_b, *refs):
    out_ref = refs[-1]
    rows = left_a.shape[0]
    out_ref[:rows, :] = (left_a[...] + came_a[...].astype(F32)).astype(BF16)
    out_ref[rows:, :] = (left_b[...] + came_b[...].astype(F32)).astype(BF16)


def node_grad_kernel(arrivals, four, boundary_hbm, after, sums_ref, win_ref, *refs):
    returned = refs[:arrivals]
    out_ref, total_ref, boundary_ref, sem = refs[arrivals:]
    nodes, latent = out_ref.shape
    extent = sums_ref.shape[0] - nodes
    block = returned[-1].shape[0]
    copy = load_small(boundary_hbm, boundary_ref, sem)
    total_ref[...] = sums_ref[:nodes, :]
    copy.wait()
    for which, place in enumerate(boundary_places(boundary_ref, lax.axis_index("dom"), four)):
        spot = pl.ds(pl.multiple_of(place * block, block), block)
        total_ref[spot, :] += returned[which][-block:, :].astype(F32)

    def wide_dot(value, weight):
        high = value.astype(BF16)
        low = (value - high.astype(F32)).astype(BF16)
        return dot_t(high, weight) + dot_t(low, weight)

    out_ref[...] = (
        wide_dot(total_ref[...], win_ref[latent : 2 * latent, :])
        + wide_dot(sums_ref[extent:, :], win_ref[2 * latent :, :])
    ).astype(BF16)


def last_kernel(node_out, edge_grad, own_ref, other_ref, in_ref, out_ref):
    unit = out_ref.shape[0]
    part = lax.axis_index("dom")
    inner = (part == 1) | (part == 2)

    def write(low, high):
        out_ref[...] = low[:unit, :].astype(F32)
        in_ref[:unit, :] = high[:unit, :].astype(F32)
        in_ref[unit : 2 * unit, :] = low[unit:, :].astype(F32)
        in_ref[2 * unit :, :] = high[unit:, :].astype(F32)

    @pl.when(inner)
    def _():
        write(own_ref, other_ref)

    @pl.when(jnp.logical_not(inner))
    def _():
        write(other_ref, own_ref)


def swap(array, axis, partner):
    devices = lax.axis_size(axis)
    return lax.ppermute(array, axis, [(i, partner(i)) for i in range(devices)])


def from_behind(array, axis, by):
    devices = lax.axis_size(axis)
    pairs = [(i, i + by) for i in range(devices) if 0 <= i + by < devices]
    return lax.ppermute(array, axis, pairs)


def partners_of_four(which):
    return ((1, 0, 3, 2), (0, 2, 1, 3), (2, 3, 0, 1))[which]


def exchange_of_four(first, second, third):
    third = swap(third, "dom", lambda i: partners_of_four(2)[i])
    second = swap(second, "dom", lambda i: partners_of_four(1)[i])
    first = swap(first, "dom", lambda i: partners_of_four(0)[i])
    return [first, second, third]


def halve(bit, came, kept, after):
    slots, rows, latent = kept.shape
    return pl.pallas_call(
        functools.partial(halve_kernel, bit),
        out_shape=(
            pltpu.VMEM((slots // 2, rows, latent), BF16),
            pltpu.VMEM((slots // 2, rows, latent), F32),
        ),
        in_specs=[VMEM] * 3,
        out_specs=(VMEM,) * 2,
        compiler_params=pltpu.CompilerParams(vmem_limit_bytes=4 * 1024 * 1024),
        cost_estimate=pl.CostEstimate(flops=0, bytes_accessed=500_000, transcendentals=0),
        name="halve",
    )(in_vmem(came), in_vmem(kept), in_vmem(after))


def sum_over_dp(away, kept, after):
    devices = lax.axis_size("dp")
    bit = 1
    while True:
        came = swap(away, "dp", lambda i, bit=bit: i ^ bit)
        bit *= 2
        if bit >= devices:
            return came, kept, away
        away, kept = halve(bit, came, kept, after)


def small_call(kernel, name, out_shape, *operands, after=()):
    many = isinstance(out_shape, tuple)
    return pl.pallas_call(
        kernel,
        out_shape=out_shape,
        in_specs=[VMEM] * len(operands) + [HBM] * len(after),
        out_specs=(VMEM,) * len(out_shape) if many else VMEM,
        compiler_params=pltpu.CompilerParams(vmem_limit_bytes=4 * 1024 * 1024),
        cost_estimate=pl.CostEstimate(flops=0, bytes_accessed=500_000, transcendentals=0),
        name=name,
    )(*[in_vmem(array) for array in operands], *[in_hbm(array) for array in after])


def sum_of_four(kept):
    return (kept.astype(F32) + swap(kept, "dom", lambda i: 3 - i).astype(F32)).astype(BF16)


def with_other_half(kept):
    return kept, swap(kept, "dom", lambda i: i ^ 1)


def sum_over_dom(rows):
    piece = lax.psum_scatter(rows, "dom", scatter_dimension=0, tiled=True)
    return lax.all_gather(piece, "dom", axis=0, tiled=True)


def in_vmem(array):
    return pltpu.with_memory_space_constraint(array, pltpu.VMEM)


def in_hbm(array):
    return pltpu.with_memory_space_constraint(array, pltpu.HBM)


def body(
    node_latents,
    edge_latents,
    agg_cotangent,
    weight_in,
    weight_out,
    boundary,
    tile_src,
    tile_dst,
    edge_slot,
    tile_count,
):
    tiles, block = edge_slot.shape
    edges, latent = edge_latents.shape[1:]
    nodes = node_latents.shape[1]
    parts = lax.axis_size("dom")
    ways = lax.axis_size("dp")
    four = parts == 4 and ways == 4
    arrivals = 3 if four else 4
    boundary = in_hbm(boundary)
    tile_dst = in_hbm(tile_dst)
    node_rows = in_hbm(node_latents[0])
    block_shape = pltpu.VMEM((block, latent), BF16)
    small = pltpu.CompilerParams(vmem_limit_bytes=8 * 1024 * 1024)

    sent = pl.pallas_call(
        functools.partial(pick_kernel, four, block),
        out_shape=(block_shape,) * arrivals,
        in_specs=[HBM] * 2,
        out_specs=(VMEM,) * arrivals,
        scratch_shapes=[
            pltpu.SMEM(boundary.shape, jnp.int32),
            pltpu.VMEM((nodes, latent), BF16),
            pltpu.SemaphoreType.DMA((2,)),
        ],
        compiler_params=small,
        cost_estimate=pl.CostEstimate(flops=0, bytes_accessed=400_000, transcendentals=0),
        name="pick_blocks",
    )(boundary, node_rows)
    if four:
        came = exchange_of_four(*sent)
    else:
        came = [from_behind(sent[which], "dom", OFFSET_LIST[which]) for which in range(4)]
    unit = latent // ways
    half = ways // 2
    extent = -(-(nodes + arrivals * block) // 128) * 128

    node_v, edge_v, cot_v, win_v, wout_v, pre, up, hot, turned = pl.pallas_call(
        functools.partial(prep_kernel, parts, arrivals),
        out_shape=(
            pltpu.VMEM((nodes, latent), BF16),
            pltpu.VMEM((edges, latent), BF16),
            pltpu.VMEM((nodes, latent), BF16),
            pltpu.VMEM(weight_in.shape, BF16),
            pltpu.VMEM(weight_out.shape, BF16),
            pltpu.VMEM((edges, latent), F32),
            pltpu.VMEM((edges, latent), F32),
            pltpu.VMEM((edges, extent), BF16),
            pltpu.VMEM((extent + nodes, edges), BF16),
        ),
        in_specs=[SMEM] + [HBM] * 8,
        out_specs=(VMEM,) * 9,
        scratch_shapes=[
            pltpu.SMEM((tiles,), jnp.int32),
            pltpu.SMEM((tiles,), jnp.int32),
            pltpu.VMEM((tiles, block), jnp.int32),
            pltpu.VMEM((nodes, latent), F32),
            pltpu.VMEM((nodes, latent), F32),
            pltpu.SemaphoreType.DMA((10,)),
        ],
        compiler_params=small,
        cost_estimate=pl.CostEstimate(
            flops=2 * edges * latent * latent, bytes_accessed=8_000_000, transcendentals=0
        ),
        name="prepare",
    )(
        tile_count,
        in_hbm(tile_src),
        tile_dst,
        in_hbm(edge_slot),
        node_rows,
        in_hbm(edge_latents[0]),
        in_hbm(agg_cotangent[0]),
        in_hbm(weight_in),
        in_hbm(weight_out),
    )
    sent_shape = pltpu.VMEM((half, 2 * unit, latent), BF16)
    kept_shape = pltpu.VMEM((half, 2 * unit, latent), F32)
    grad_pre, message, sums, away_a, kept_a, away_b, kept_b, *outer = pl.pallas_call(
        functools.partial(edge_kernel, ways, arrivals, four, block),
        out_shape=(
            pltpu.VMEM((edges, latent), BF16),
            pltpu.VMEM((edges, latent), F32),
            pltpu.VMEM((extent + nodes, latent), F32),
            sent_shape,
            kept_shape,
            sent_shape,
            kept_shape,
            *[block_shape] * (2 if four else 0),
        ),
        in_specs=[VMEM] * (8 + arrivals),
        out_specs=(VMEM,) * (9 if four else 7),
        scratch_shapes=[
            pltpu.VMEM((extent, latent), BF16),
            pltpu.VMEM((edges, latent), BF16),
            pltpu.VMEM((edges, latent), BF16),
        ],
        compiler_params=pltpu.CompilerParams(vmem_limit_bytes=16 * 1024 * 1024),
        cost_estimate=pl.CostEstimate(
            flops=12 * edges * latent * latent,
            bytes_accessed=12_000_000,
            transcendentals=edges * latent,
        ),
        name="edge_block",
    )(
        *[
            in_vmem(array)
            for array in (*came[::-1], node_v, edge_v, win_v, wout_v, pre, up, hot, turned)
        ],
    )
    if four:
        rows = 2 * unit
        piece, wide = pltpu.VMEM((unit, latent), BF16), pltpu.VMEM((unit, latent), F32)
        came_a = swap(away_a, "dp", lambda i: i ^ 1)
        away_a, kept_a = halve(2, came_a, kept_a, cot_v)
        came_a = swap(away_a, "dp", lambda i: i ^ 2)
        came_b = swap(away_b, "dp", lambda i: i ^ 1)
        away_b, kept_b = small_call(
            functools.partial(beside_first_kernel, nodes, block),
            "beside_first",
            (pltpu.VMEM((rows + block, latent), BF16), pltpu.VMEM((2, unit, latent), F32)),
            came_b,
            kept_b,
            sums,
        )
        beside = swap(away_b, "dom", lambda i: i ^ 1)
        far = swap(outer[1], "dom", lambda i: partners_of_four(2)[i])
        near = swap(outer[0], "dom", lambda i: partners_of_four(1)[i])
        away_a, kept_a = small_call(
            beside_second_kernel, "beside_second", (piece, wide), came_a, kept_a, far, near
        )
        came_a = swap(away_a, "dom", lambda i: i ^ 1)
        away_b, kept_b = small_call(
            over_second_kernel, "over_second", (piece, wide), beside, kept_b
        )
        came_b = swap(away_b, "dp", lambda i: i ^ 2)
        pair = small_call(
            add_kernel,
            "add_terms",
            pltpu.VMEM((rows, latent), BF16),
            kept_a,
            came_a,
            kept_b,
            came_b,
        )
        returned = [beside, near, far]
        late, backs = pair, 0
    else:
        came_a, kept_a, late = sum_over_dp(away_a, kept_a, cot_v)
        came_b, kept_b, _ = sum_over_dp(away_b, kept_b, cot_v)
        backs = arrivals
    edge_grad, agg, *back_sums = pl.pallas_call(
        functools.partial(edge_grad_kernel, block, arrivals, four),
        out_shape=(
            jax.ShapeDtypeStruct((edges, latent), BF16),
            jax.ShapeDtypeStruct((nodes, latent), BF16),
        )
        + (block_shape,) * backs,
        in_specs=[HBM, SMEM] + [VMEM] * 7,
        out_specs=(VMEM,) * (2 + backs),
        scratch_shapes=[
            pltpu.SMEM((tiles,), jnp.int32),
            pltpu.VMEM((nodes, latent), F32),
            pltpu.SemaphoreType.DMA,
        ],
        compiler_params=small,
        cost_estimate=pl.CostEstimate(
            flops=2 * edges * latent * latent, bytes_accessed=3_000_000, transcendentals=0
        ),
        name="edge_grads",
    )(
        tile_dst,
        tile_count,
        *[in_vmem(array) for array in (late, grad_pre, sums, cot_v, win_v, edge_v, message)],
    )
    if not four:
        returned = [
            from_behind(back_sums[which], "dom", -OFFSET_LIST[which]) for which in range(4)
        ]
    node_out = pl.pallas_call(
        functools.partial(node_grad_kernel, arrivals, four),
        out_shape=jax.ShapeDtypeStruct((nodes, latent), BF16),
        in_specs=[HBM] + [VMEM] * (3 + arrivals),
        out_specs=VMEM,
        scratch_shapes=[
            pltpu.VMEM((nodes, latent), F32),
            pltpu.SMEM(boundary.shape, jnp.int32),
            pltpu.SemaphoreType.DMA,
        ],
        compiler_params=small,
        cost_estimate=pl.CostEstimate(
            flops=8 * nodes * latent * latent, bytes_accessed=2_000_000, transcendentals=0
        ),
        name="node_grads",
    )(boundary, *[in_vmem(array) for array in (late, sums, win_v, *returned)])
    if four:
        w_in_grad, w_out_grad = pl.pallas_call(
            last_kernel,
            out_shape=(
                jax.ShapeDtypeStruct((3 * unit, latent), F32),
                jax.ShapeDtypeStruct((unit, latent), F32),
            ),
            in_specs=[HBM] * 2 + [VMEM] * 2,
            out_specs=(VMEM,) * 2,
            compiler_params=small,
            cost_estimate=pl.CostEstimate(flops=0, bytes_accessed=1_500_000, transcendentals=0),
            name="widen",
        )(in_hbm(node_out), in_hbm(edge_grad), *with_other_half(sum_of_four(pair)))
    else:
        sum_a = sum_over_dom(kept_a[0] + came_a[0].astype(F32))
        sum_b = sum_over_dom(kept_b[0] + came_b[0].astype(F32))
        w_in_grad = jnp.concatenate([sum_a[unit:], sum_b], axis=0)
        w_out_grad = sum_a[:unit]
    return (agg[None], edge_grad[None], node_out[None], w_in_grad, w_out_grad)


def solution(mesh):
    in_specs = (
        P(("group", "dp"), "dom", None),
        P(("group", "dp"), "dom", None),
        P(("group", "dp"), "dom", None),
        P(),
        P(),
        P(("group", "dom"), None),
        P(("group", "dom")),
        P(("group", "dom")),
        P(("group", "dom"), None),
        P(("group", "dom")),
    )
    out_specs = (
        P(("group", "dp"), "dom", None),
        P(("group", "dp"), "dom", None),
        P(("group", "dp"), "dom", None),
        P(("group", "dp"), None),
        P(("group", "dp"), None),
    )
    return jax.shard_map(body, mesh=mesh, in_specs=in_specs, out_specs=out_specs, check_vma=False)
```

```python
import functools

import jax
import jax.numpy as jnp
from jax import lax
from jax.experimental import pallas as pl
from jax.experimental.pallas import tpu as pltpu
from jax.sharding import PartitionSpec as P

OFFSET_LIST = (1, -1, 2, -2)
EPSILON = 1e-05
VMEM = pl.BlockSpec(memory_space=pltpu.VMEM)
HBM = pl.BlockSpec(memory_space=pltpu.HBM)
SMEM = pl.BlockSpec(memory_space=pltpu.SMEM)
ANY = pl.BlockSpec(memory_space=pl.ANY)
F32 = jnp.float32
BF16 = jnp.bfloat16


def dot(left, right):
    return jnp.dot(left, right, preferred_element_type=F32)


def dot_t(left, right):
    return lax.dot_general(left, right, (((1,), (1,)), ((), ())), preferred_element_type=F32)


def t_dot(left, right):
    return lax.dot_general(left, right, (((0,), (0,)), ((), ())), preferred_element_type=F32)


def row_mean(array):
    return jnp.sum(array, axis=1, keepdims=True) * (1.0 / array.shape[1])


def rows_of(ref, block, size):
    return ref[pl.ds(pl.multiple_of(block * size, size), size), :]


def load_small(source, target, sem):
    copy = pltpu.make_async_copy(source, target, sem)
    copy.start()
    return copy


def boundary_places(boundary_ref, part, four):
    taken = [boundary_ref[0, which] for which in range(4)]
    if not four:
        return taken
    even = part % 2 == 0
    return [
        jnp.where(even, taken[0], taken[1]),
        jnp.where(even, taken[1], taken[0]),
        jnp.where(part < 2, taken[2], taken[3]),
    ]


def arrival_places(part, four, arrivals):
    if not four:
        return list(range(arrivals))
    even = part % 2 == 0
    return [jnp.where(even, 1, 0), jnp.where(even, 0, 1), 2]


def pick_kernel(four, block, boundary_hbm, node_hbm, *refs):
    count = 3 if four else 4
    outs = refs[:count]
    boundary_ref, node_ref, sems = refs[count:]
    small = load_small(boundary_hbm, boundary_ref, sems.at[0])
    large = load_small(node_hbm, node_ref, sems.at[1])
    small.wait()
    places = boundary_places(boundary_ref, lax.axis_index("dom"), four)
    large.wait()
    for place, out in zip(places, outs):
        out[...] = rows_of(node_ref, place, block)


def prep_kernel(
    parts,
    arrivals,
    count_ref,
    src_hbm,
    dst_hbm,
    slot_hbm,
    node_hbm,
    edge_hbm,
    cot_hbm,
    win_hbm,
    wout_hbm,
    node_ref,
    edge_ref,
    cot_ref,
    win_ref,
    wout_ref,
    pre_ref,
    up_ref,
    hot_ref,
    hot_turned,
    src_ref,
    dst_ref,
    slot_ref,
    recv_ref,
    mid_ref,
    sems,
):
    tiles, block = slot_ref.shape
    nodes, latent = node_ref.shape
    owned = nodes // block
    extent = hot_ref.shape[1]
    pairs = (
        (src_hbm, src_ref),
        (dst_hbm, dst_ref),
        (slot_hbm, slot_ref),
        (node_hbm, node_ref),
        (win_hbm.at[2 * latent :, :], win_ref.at[2 * latent :, :]),
        (win_hbm.at[:latent, :], win_ref.at[:latent, :]),
        (edge_hbm, edge_ref),
        (cot_hbm, cot_ref),
        (win_hbm.at[latent : 2 * latent, :], win_ref.at[latent : 2 * latent, :]),
        (wout_hbm, wout_ref),
    )
    copies = [load_small(*pair, sems.at[number]) for number, pair in enumerate(pairs)]
    part = lax.axis_index("dom")
    for copy in copies[:3]:
        copy.wait()
    index = lax.broadcasted_iota(jnp.int32, (extent, 2 * block), 0)
    lane = lax.broadcasted_iota(jnp.int32, (1, 2 * block), 1)
    first = lane < block
    within = jnp.where(first, lane, lane - block)
    node_index = lax.broadcasted_iota(jnp.int32, (nodes, 2 * block), 0)
    for tile in range(0, tiles, 2):
        wanted = []
        for member in (tile, tile + 1):
            source = src_ref[member]
            which = source - owned
            reach = jnp.where(which >= 2, 2, 1)
            partner = part - jnp.where(which % 2 == 1, -reach, reach)
            exists = (source < owned) | ((partner >= 0) & (partner < parts))
            place = jnp.minimum(source, owned + arrivals - 1)
            wanted.append(jnp.where(exists, place * block, -2 * extent))
        slots = jnp.concatenate(
            [slot_ref[tile : tile + 1, :], slot_ref[tile + 1 : tile + 2, :]], axis=1
        )
        row = slots + jnp.where(first, wanted[0], wanted[1])
        hot = jnp.where(index == row, 1.0, 0.0)
        at = slice(tile * block, (tile + 2) * block)
        hot_turned[:extent, at] = hot.astype(BF16)
        target = within + jnp.where(first, dst_ref[tile] * block, dst_ref[tile + 1] * block)
        hot_turned[extent:, at] = jnp.where(node_index == target, 1.0, 0.0).astype(BF16)
        hot_ref[at, :] = hot.T.astype(BF16)
    copies[3].wait()
    copies[4].wait()
    recv_ref[...] = dot(node_ref[...], win_ref[2 * latent :, :])
    copies[5].wait()
    copies[6].wait()
    group = 4 if tiles % 4 == 0 else 2
    for tile in range(0, tiles, group):
        rows = slice(tile * block, (tile + group) * block)
        received = jnp.concatenate(
            [rows_of(recv_ref, dst_ref[t], block) for t in range(tile, tile + group)], axis=0
        )
        pre_ref[rows, :] = dot(edge_ref[rows, :], win_ref[:latent, :]) + received
    copies[7].wait()
    cot = cot_ref[...].astype(F32)
    mid_ref[...] = cot - row_mean(cot)
    for tile in range(tiles):
        live = jnp.where(tile < count_ref[0], 1.0, 0.0)
        up_ref[tile * block : (tile + 1) * block, :] = rows_of(mid_ref, dst_ref[tile], block) * live
    copies[8].wait()
    copies[9].wait()


def put_units(ways, bit, targets, sections):
    latent = sections[0][0].shape[1]
    unit = latent // ways
    step = 256
    for number, (left, right) in enumerate(sections):
        value_right = right()
        for start in range(0, latent, step):
            value = t_dot(left[:, start : start + step], value_right)
            for at in range(0, step, unit):
                owner, spot = (start + at) // unit, 0
                if number > 0:
                    place = ((number - 1) * latent + start + at) // unit
                    owner, spot = place // 3, 1 + place % 3
                away, kept = targets[spot // 2]
                part = value[at : at + unit]
                where = slice((spot % 2) * unit, (spot % 2 + 1) * unit)

                @pl.when(bit == owner % 2)
                def _(kept=kept, owner=owner, where=where, part=part):
                    kept[owner // 2, where, :] = part

                @pl.when(bit != owner % 2)
                def _(away=away, owner=owner, where=where, part=part):
                    away[owner // 2, where, :] = part.astype(BF16)


def arrival_order(arrivals):
    return (2, 0, 1) if arrivals == 3 else tuple(range(arrivals))


def edge_kernel(ways, arrivals, four, block, *refs):
    arrived = [refs[which] for which in arrival_order(arrivals)]
    (
        node_ref,
        edge_ref,
        win_ref,
        wout_ref,
        pre_ref,
        up_ref,
        hot_ref,
        hot_turned,
        gpre_ref,
        message_ref,
        sums_ref,
        away_a,
        kept_a,
        away_b,
        kept_b,
        *back_refs,
        ext_ref,
        act_ref,
        proj_ref,
    ) = refs[arrivals:]
    nodes, latent = node_ref.shape
    edges = edge_ref.shape[0]
    extent = ext_ref.shape[0]
    places = arrival_places(lax.axis_index("dom"), four, arrivals)

    ext_ref[:nodes, :] = node_ref[...]
    for which in range(arrivals):
        at = pl.multiple_of(nodes + places[which] * block, block)
        ext_ref[pl.ds(at, block), :] = arrived[which][...]
    filled = nodes + arrivals * block
    if filled < extent:
        ext_ref[filled:, :] = jnp.zeros((extent - filled, latent), BF16)

    span = 384 if edges % 384 == 0 else block
    for start in range(0, edges, span):
        rows = slice(start, start + span)
        senders = dot(hot_ref[rows, :], ext_ref[...]).astype(BF16)
        preact = pre_ref[rows, :] + dot(senders, win_ref[latent : 2 * latent, :])
        gate = 0.5 * jnp.tanh(0.5 * preact) + 0.5
        activated = preact * gate
        slope = gate + activated * (1.0 - gate)
        activated = activated.astype(BF16)
        act_ref[rows, :] = activated
        projected = dot(activated, wout_ref[...])
        centered = projected - row_mean(projected)
        inv_scale = lax.rsqrt(row_mean(centered * centered) + EPSILON)
        message = centered * inv_scale
        message_ref[rows, :] = message
        upstream = up_ref[rows, :]
        grad_project = inv_scale * (upstream - message * row_mean(upstream * message))
        grad_project = grad_project.astype(BF16)
        proj_ref[rows, :] = grad_project
        gpre_ref[rows, :] = (dot_t(grad_project, wout_ref[...]) * slope).astype(BF16)

    sums_ref[...] = dot(hot_turned[...], gpre_ref[...])
    for which, back_ref in enumerate(back_refs):
        back_ref[...] = back_block(nodes, block, sums_ref, 1 + which)
    sections = (
        (act_ref, lambda: proj_ref[...]),
        (edge_ref, lambda: gpre_ref[...]),
        (ext_ref, lambda: sums_ref[:extent, :].astype(BF16)),
        (node_ref, lambda: sums_ref[extent:, :].astype(BF16)),
    )
    targets = ((away_a, kept_a), (away_b, kept_b))
    put_units(ways, lax.axis_index("dp") % 2, targets, sections)


def edge_grad_kernel(
    block,
    arrivals,
    four,
    dst_hbm,
    count_ref,
    after,
    gpre_ref,
    sums_ref,
    cot_ref,
    win_ref,
    edge_ref,
    message_ref,
    out_ref,
    agg_out,
    *refs,
):
    back_sums = refs[:-3]
    dst_ref, agg_ref, sem = refs[-3:]
    copy = load_small(dst_hbm, dst_ref, sem)
    nodes, latent = cot_ref.shape
    tiles = gpre_ref.shape[0] // block
    group = 4 if tiles % 4 == 0 else 1
    places = arrival_places(lax.axis_index("dom"), four, arrivals)
    for place, back_ref in zip(places, back_sums):
        at = pl.multiple_of(nodes + place * block, block)
        back_ref[...] = sums_ref[pl.ds(at, block), :].astype(BF16)
    agg_ref[...] = jnp.zeros_like(agg_ref)
    copy.wait()
    for first in range(0, tiles, group):
        rows = slice(first * block, (first + group) * block)
        upstream = jnp.concatenate(
            [
                rows_of(cot_ref, dst_ref[t], block).astype(F32)
                * jnp.where(t < count_ref[0], 1.0, 0.0)
                for t in range(first, first + group)
            ],
            axis=0,
        )
        out_ref[rows, :] = (dot_t(gpre_ref[rows, :], win_ref[:latent, :]) + upstream).astype(BF16)
        for t in range(first, first + group):
            live = jnp.where(t < count_ref[0], 1.0, 0.0)
            mine = slice(t * block, (t + 1) * block)
            updated = edge_ref[mine, :].astype(F32) + message_ref[mine, :]
            target = pl.ds(pl.multiple_of(dst_ref[t] * block, block), block)
            agg_ref[target, :] += updated * live
    agg_out[...] = agg_ref[...].astype(BF16)


def halve_kernel(bit, came_ref, kept_ref, after, away_ref, left_ref):
    mine = (lax.axis_index("dp") // bit) % 2
    for slot in range(left_ref.shape[0]):
        there, here = 2 * slot + 1 - mine, 2 * slot + mine
        away_ref[slot] = (kept_ref[there] + came_ref[there].astype(F32)).astype(BF16)
        left_ref[slot] = kept_ref[here] + came_ref[here].astype(F32)


def half_rows(rows):
    part = lax.axis_index("dom")
    inner = (part == 1) | (part == 2)
    here = pl.ds(pl.multiple_of(jnp.where(inner, 0, rows), rows), rows)
    there = pl.ds(pl.multiple_of(jnp.where(inner, rows, 0), rows), rows)
    return here, there


def back_block(nodes, block, sums_ref, which):
    place = arrival_places(lax.axis_index("dom"), True, 3)[which]
    return sums_ref[pl.ds(pl.multiple_of(nodes + place * block, block), block), :].astype(BF16)


def beside_first_kernel(came_ref, kept_ref, away_ref, left_ref):
    rows = left_ref.shape[1]
    here, there = half_rows(rows)
    for slot in range(2):
        away_ref[slot * rows : (slot + 1) * rows, :] = (
            kept_ref[slot, there, :] + came_ref[slot, there, :].astype(F32)
        ).astype(BF16)
        left_ref[slot] = kept_ref[slot, here, :] + came_ref[slot, here, :].astype(F32)


def beside_second_kernel(nodes, block, came_ref, kept_ref, sums_ref, *refs):
    away_ref, left_ref = refs[-2:]
    rows = left_ref.shape[0]
    here, there = half_rows(rows)
    away_ref[:rows, :] = (kept_ref[0, there, :] + came_ref[0, there, :].astype(F32)).astype(BF16)
    away_ref[rows:, :] = back_block(nodes, block, sums_ref, 0)
    left_ref[...] = kept_ref[0, here, :] + came_ref[0, here, :].astype(F32)


def over_second_kernel(came_ref, kept_ref, *refs):
    away_ref, left_ref = refs[-2:]
    mine = lax.axis_index("dp") // 2
    rows = left_ref.shape[0]

    def came(slot):
        spot = pl.ds(pl.multiple_of(slot * rows, rows), rows)
        return came_ref[spot, :].astype(F32)

    away_ref[...] = (kept_ref[1 - mine] + came(1 - mine)).astype(BF16)
    left_ref[...] = kept_ref[mine] + came(mine)


def add_kernel(left_a, came_a, left_b, came_b, *refs):
    out_ref = refs[-1]
    rows = left_a.shape[0]
    out_ref[:rows, :] = (left_a[...] + came_a[:rows, :].astype(F32)).astype(BF16)
    out_ref[rows:, :] = (left_b[...] + came_b[...].astype(F32)).astype(BF16)


def node_grad_kernel(arrivals, four, boundary_hbm, after, sums_ref, win_ref, *refs):
    returned = refs[:arrivals]
    out_ref, total_ref, boundary_ref, sem = refs[arrivals:]
    nodes, latent = out_ref.shape
    extent = sums_ref.shape[0] - nodes
    block = returned[-1].shape[0]
    copy = load_small(boundary_hbm, boundary_ref, sem)
    total_ref[...] = sums_ref[:nodes, :]
    copy.wait()
    for which, place in enumerate(boundary_places(boundary_ref, lax.axis_index("dom"), four)):
        spot = pl.ds(pl.multiple_of(place * block, block), block)
        total_ref[spot, :] += returned[which][-block:, :].astype(F32)

    def wide_dot(value, weight):
        high = value.astype(BF16)
        low = (value - high.astype(F32)).astype(BF16)
        return dot_t(high, weight) + dot_t(low, weight)

    out_ref[...] = (
        wide_dot(total_ref[...], win_ref[latent : 2 * latent, :])
        + wide_dot(sums_ref[extent:, :], win_ref[2 * latent :, :])
    ).astype(BF16)


def last_kernel(node_out, edge_grad, own_ref, other_ref, in_ref, out_ref):
    unit = out_ref.shape[0]
    part = lax.axis_index("dom")
    inner = (part == 1) | (part == 2)

    def write(low, high):
        out_ref[...] = low[:unit, :].astype(F32)
        in_ref[:unit, :] = high[:unit, :].astype(F32)
        in_ref[unit : 2 * unit, :] = low[unit:, :].astype(F32)
        in_ref[2 * unit :, :] = high[unit:, :].astype(F32)

    @pl.when(inner)
    def _():
        write(own_ref, other_ref)

    @pl.when(jnp.logical_not(inner))
    def _():
        write(other_ref, own_ref)


def swap(array, axis, partner):
    devices = lax.axis_size(axis)
    return lax.ppermute(array, axis, [(i, partner(i)) for i in range(devices)])


def from_behind(array, axis, by):
    devices = lax.axis_size(axis)
    pairs = [(i, i + by) for i in range(devices) if 0 <= i + by < devices]
    return lax.ppermute(array, axis, pairs)


def partners_of_four(which):
    return ((1, 0, 3, 2), (0, 2, 1, 3), (2, 3, 0, 1))[which]


def exchange_of_four(first, second, third):
    third = swap(third, "dom", lambda i: partners_of_four(2)[i])
    second = swap(second, "dom", lambda i: partners_of_four(1)[i])
    first = swap(first, "dom", lambda i: partners_of_four(0)[i])
    return [first, second, third]


def halve(bit, came, kept, after):
    slots, rows, latent = kept.shape
    return pl.pallas_call(
        functools.partial(halve_kernel, bit),
        out_shape=(
            pltpu.VMEM((slots // 2, rows, latent), BF16),
            pltpu.VMEM((slots // 2, rows, latent), F32),
        ),
        in_specs=[VMEM] * 3,
        out_specs=(VMEM,) * 2,
        compiler_params=pltpu.CompilerParams(vmem_limit_bytes=4 * 1024 * 1024),
        cost_estimate=pl.CostEstimate(flops=0, bytes_accessed=500_000, transcendentals=0),
        name="halve",
    )(in_vmem(came), in_vmem(kept), in_vmem(after))


def sum_over_dp(away, kept, after):
    devices = lax.axis_size("dp")
    bit = 1
    while True:
        came = swap(away, "dp", lambda i, bit=bit: i ^ bit)
        bit *= 2
        if bit >= devices:
            return came, kept, away
        away, kept = halve(bit, came, kept, after)


def small_call(kernel, name, out_shape, *operands, after=()):
    many = isinstance(out_shape, tuple)
    return pl.pallas_call(
        kernel,
        out_shape=out_shape,
        in_specs=[VMEM] * len(operands) + [HBM] * len(after),
        out_specs=(VMEM,) * len(out_shape) if many else VMEM,
        compiler_params=pltpu.CompilerParams(vmem_limit_bytes=4 * 1024 * 1024),
        cost_estimate=pl.CostEstimate(flops=0, bytes_accessed=500_000, transcendentals=0),
        name=name,
    )(*[in_vmem(array) for array in operands], *[in_hbm(array) for array in after])


def sum_of_four(kept):
    return (kept.astype(F32) + swap(kept, "dom", lambda i: 3 - i).astype(F32)).astype(BF16)


def with_other_half(kept):
    return kept, swap(kept, "dom", lambda i: i ^ 1)


def sum_over_dom(rows):
    piece = lax.psum_scatter(rows, "dom", scatter_dimension=0, tiled=True)
    return lax.all_gather(piece, "dom", axis=0, tiled=True)


def in_vmem(array):
    return pltpu.with_memory_space_constraint(array, pltpu.VMEM)


def in_hbm(array):
    return pltpu.with_memory_space_constraint(array, pltpu.HBM)


def body(
    node_latents,
    edge_latents,
    agg_cotangent,
    weight_in,
    weight_out,
    boundary,
    tile_src,
    tile_dst,
    edge_slot,
    tile_count,
):
    tiles, block = edge_slot.shape
    edges, latent = edge_latents.shape[1:]
    nodes = node_latents.shape[1]
    parts = lax.axis_size("dom")
    ways = lax.axis_size("dp")
    four = parts == 4 and ways == 4
    arrivals = 3 if four else 4
    boundary = in_hbm(boundary)
    tile_dst = in_hbm(tile_dst)
    node_rows = in_hbm(node_latents[0])
    block_shape = pltpu.VMEM((block, latent), BF16)
    small = pltpu.CompilerParams(vmem_limit_bytes=8 * 1024 * 1024)

    sent = pl.pallas_call(
        functools.partial(pick_kernel, four, block),
        out_shape=(block_shape,) * arrivals,
        in_specs=[HBM] * 2,
        out_specs=(VMEM,) * arrivals,
        scratch_shapes=[
            pltpu.SMEM(boundary.shape, jnp.int32),
            pltpu.VMEM((nodes, latent), BF16),
            pltpu.SemaphoreType.DMA((2,)),
        ],
        compiler_params=small,
        cost_estimate=pl.CostEstimate(flops=0, bytes_accessed=400_000, transcendentals=0),
        name="pick_blocks",
    )(boundary, node_rows)
    if four:
        came = exchange_of_four(*sent)
    else:
        came = [from_behind(sent[which], "dom", OFFSET_LIST[which]) for which in range(4)]
    unit = latent // ways
    half = ways // 2
    extent = -(-(nodes + arrivals * block) // 128) * 128

    node_v, edge_v, cot_v, win_v, wout_v, pre, up, hot, turned = pl.pallas_call(
        functools.partial(prep_kernel, parts, arrivals),
        out_shape=(
            pltpu.VMEM((nodes, latent), BF16),
            pltpu.VMEM((edges, latent), BF16),
            pltpu.VMEM((nodes, latent), BF16),
            pltpu.VMEM(weight_in.shape, BF16),
            pltpu.VMEM(weight_out.shape, BF16),
            pltpu.VMEM((edges, latent), F32),
            pltpu.VMEM((edges, latent), F32),
            pltpu.VMEM((edges, extent), BF16),
            pltpu.VMEM((extent + nodes, edges), BF16),
        ),
        in_specs=[SMEM] + [HBM] * 8,
        out_specs=(VMEM,) * 9,
        scratch_shapes=[
            pltpu.SMEM((tiles,), jnp.int32),
            pltpu.SMEM((tiles,), jnp.int32),
            pltpu.VMEM((tiles, block), jnp.int32),
            pltpu.VMEM((nodes, latent), F32),
            pltpu.VMEM((nodes, latent), F32),
            pltpu.SemaphoreType.DMA((10,)),
        ],
        compiler_params=small,
        cost_estimate=pl.CostEstimate(
            flops=2 * edges * latent * latent, bytes_accessed=8_000_000, transcendentals=0
        ),
        name="prepare",
    )(
        tile_count,
        in_hbm(tile_src),
        tile_dst,
        in_hbm(edge_slot),
        node_rows,
        in_hbm(edge_latents[0]),
        in_hbm(agg_cotangent[0]),
        in_hbm(weight_in),
        in_hbm(weight_out),
    )
    sent_shape = pltpu.VMEM((half, 2 * unit, latent), BF16)
    kept_shape = pltpu.VMEM((half, 2 * unit, latent), F32)
    ordered = [None] * arrivals
    for array, which in zip(came, arrival_order(arrivals)):
        ordered[which] = array
    grad_pre, message, sums, away_a, kept_a, away_b, kept_b, *outer = pl.pallas_call(
        functools.partial(edge_kernel, ways, arrivals, four, block),
        out_shape=(
            pltpu.VMEM((edges, latent), BF16),
            pltpu.VMEM((edges, latent), F32),
            pltpu.VMEM((extent + nodes, latent), F32),
            sent_shape,
            kept_shape,
            sent_shape,
            kept_shape,
            *[block_shape] * (2 if four else 0),
        ),
        in_specs=[VMEM] * (8 + arrivals),
        out_specs=(VMEM,) * (9 if four else 7),
        scratch_shapes=[
            pltpu.VMEM((extent, latent), BF16),
            pltpu.VMEM((edges, latent), BF16),
            pltpu.VMEM((edges, latent), BF16),
        ],
        compiler_params=pltpu.CompilerParams(vmem_limit_bytes=16 * 1024 * 1024),
        cost_estimate=pl.CostEstimate(
            flops=12 * edges * latent * latent,
            bytes_accessed=12_000_000,
            transcendentals=edges * latent,
        ),
        name="edge_block",
    )(
        *[
            in_vmem(array)
            for array in (*ordered, node_v, edge_v, win_v, wout_v, pre, up, hot, turned)
        ],
    )
    if four:
        rows = 2 * unit
        piece, wide = pltpu.VMEM((unit, latent), BF16), pltpu.VMEM((unit, latent), F32)
        came_a = swap(away_a, "dp", lambda i: i ^ 1)
        away_a, kept_a = halve(2, came_a, kept_a, cot_v)
        came_a = swap(away_a, "dp", lambda i: i ^ 2)
        came_b = swap(away_b, "dp", lambda i: i ^ 1)
        away_b, kept_b = small_call(
            beside_first_kernel,
            "beside_first",
            (pltpu.VMEM((rows, latent), BF16), pltpu.VMEM((2, unit, latent), F32)),
            came_b,
            kept_b,
        )
        beside = swap(away_b, "dom", lambda i: i ^ 1)
        far = swap(outer[1], "dom", lambda i: partners_of_four(2)[i])
        near = swap(outer[0], "dom", lambda i: partners_of_four(1)[i])
        away_a, kept_a = small_call(
            functools.partial(beside_second_kernel, nodes, block),
            "beside_second",
            (pltpu.VMEM((unit + block, latent), BF16), wide),
            came_a,
            kept_a,
            sums,
            far,
            near,
        )
        came_a = swap(away_a, "dom", lambda i: i ^ 1)
        away_b, kept_b = small_call(
            over_second_kernel, "over_second", (piece, wide), beside, kept_b
        )
        came_b = swap(away_b, "dp", lambda i: i ^ 2)
        pair = small_call(
            add_kernel,
            "add_terms",
            pltpu.VMEM((rows, latent), BF16),
            kept_a,
            came_a,
            kept_b,
            came_b,
        )
        returned = [came_a, near, far]
        late, backs = pair, 0
    else:
        came_a, kept_a, late = sum_over_dp(away_a, kept_a, cot_v)
        came_b, kept_b, _ = sum_over_dp(away_b, kept_b, cot_v)
        backs = arrivals
    edge_grad, agg, *back_sums = pl.pallas_call(
        functools.partial(edge_grad_kernel, block, arrivals, four),
        out_shape=(
            jax.ShapeDtypeStruct((edges, latent), BF16),
            jax.ShapeDtypeStruct((nodes, latent), BF16),
        )
        + (block_shape,) * backs,
        in_specs=[HBM, SMEM] + [VMEM] * 7,
        out_specs=(VMEM,) * (2 + backs),
        scratch_shapes=[
            pltpu.SMEM((tiles,), jnp.int32),
            pltpu.VMEM((nodes, latent), F32),
            pltpu.SemaphoreType.DMA,
        ],
        compiler_params=small,
        cost_estimate=pl.CostEstimate(
            flops=2 * edges * latent * latent, bytes_accessed=3_000_000, transcendentals=0
        ),
        name="edge_grads",
    )(
        tile_dst,
        tile_count,
        *[in_vmem(array) for array in (late, grad_pre, sums, cot_v, win_v, edge_v, message)],
    )
    if not four:
        returned = [
            from_behind(back_sums[which], "dom", -OFFSET_LIST[which]) for which in range(4)
        ]
    node_out = pl.pallas_call(
        functools.partial(node_grad_kernel, arrivals, four),
        out_shape=jax.ShapeDtypeStruct((nodes, latent), BF16),
        in_specs=[HBM] + [VMEM] * (3 + arrivals),
        out_specs=VMEM,
        scratch_shapes=[
            pltpu.VMEM((nodes, latent), F32),
            pltpu.SMEM(boundary.shape, jnp.int32),
            pltpu.SemaphoreType.DMA,
        ],
        compiler_params=small,
        cost_estimate=pl.CostEstimate(
            flops=8 * nodes * latent * latent, bytes_accessed=2_000_000, transcendentals=0
        ),
        name="node_grads",
    )(boundary, *[in_vmem(array) for array in (late, sums, win_v, *returned)])
    if four:
        w_in_grad, w_out_grad = pl.pallas_call(
            last_kernel,
            out_shape=(
                jax.ShapeDtypeStruct((3 * unit, latent), F32),
                jax.ShapeDtypeStruct((unit, latent), F32),
            ),
            in_specs=[HBM] * 2 + [VMEM] * 2,
            out_specs=(VMEM,) * 2,
            compiler_params=small,
            cost_estimate=pl.CostEstimate(flops=0, bytes_accessed=1_500_000, transcendentals=0),
            name="widen",
        )(in_hbm(node_out), in_hbm(edge_grad), *with_other_half(sum_of_four(pair)))
    else:
        sum_a = sum_over_dom(kept_a[0] + came_a[0].astype(F32))
        sum_b = sum_over_dom(kept_b[0] + came_b[0].astype(F32))
        w_in_grad = jnp.concatenate([sum_a[unit:], sum_b], axis=0)
        w_out_grad = sum_a[:unit]
    return (agg[None], edge_grad[None], node_out[None], w_in_grad, w_out_grad)


def solution(mesh):
    in_specs = (
        P(("group", "dp"), "dom", None),
        P(("group", "dp"), "dom", None),
        P(("group", "dp"), "dom", None),
        P(),
        P(),
        P(("group", "dom"), None),
        P(("group", "dom")),
        P(("group", "dom")),
        P(("group", "dom"), None),
        P(("group", "dom")),
    )
    out_specs = (
        P(("group", "dp"), "dom", None),
        P(("group", "dp"), "dom", None),
        P(("group", "dp"), "dom", None),
        P(("group", "dp"), None),
        P(("group", "dp"), None),
    )
    return jax.shard_map(body, mesh=mesh, in_specs=in_specs, out_specs=out_specs, check_vma=False)
```

```python
import functools

import jax
import jax.numpy as jnp
from jax import lax
from jax.experimental import pallas as pl
from jax.experimental.pallas import tpu as pltpu
from jax.sharding import PartitionSpec as P

OFFSET_LIST = (1, -1, 2, -2)
EPSILON = 1e-05
VMEM = pl.BlockSpec(memory_space=pltpu.VMEM)
HBM = pl.BlockSpec(memory_space=pltpu.HBM)
SMEM = pl.BlockSpec(memory_space=pltpu.SMEM)
ANY = pl.BlockSpec(memory_space=pl.ANY)
F32 = jnp.float32
BF16 = jnp.bfloat16


def dot(left, right):
    return jnp.dot(left, right, preferred_element_type=F32)


def dot_t(left, right):
    return lax.dot_general(left, right, (((1,), (1,)), ((), ())), preferred_element_type=F32)


def t_dot(left, right):
    return lax.dot_general(left, right, (((0,), (0,)), ((), ())), preferred_element_type=F32)


def row_mean(array):
    return jnp.sum(array, axis=1, keepdims=True) * (1.0 / array.shape[1])


def rows_of(ref, block, size):
    return ref[pl.ds(pl.multiple_of(block * size, size), size), :]


def load_small(source, target, sem):
    copy = pltpu.make_async_copy(source, target, sem)
    copy.start()
    return copy


def boundary_places(boundary_ref, part, four):
    taken = [boundary_ref[0, which] for which in range(4)]
    if not four:
        return taken
    even = part % 2 == 0
    return [
        jnp.where(even, taken[0], taken[1]),
        jnp.where(even, taken[1], taken[0]),
        jnp.where(part < 2, taken[2], taken[3]),
    ]


def arrival_places(part, four, arrivals):
    if not four:
        return list(range(arrivals))
    even = part % 2 == 0
    return [jnp.where(even, 1, 0), jnp.where(even, 0, 1), 2]


def pick_kernel(four, block, boundary_hbm, node_hbm, *refs):
    count = 3 if four else 4
    outs = refs[:count]
    boundary_ref, node_ref, sems = refs[count:]
    small = load_small(boundary_hbm, boundary_ref, sems.at[0])
    large = load_small(node_hbm, node_ref, sems.at[1])
    small.wait()
    places = boundary_places(boundary_ref, lax.axis_index("dom"), four)
    large.wait()
    for place, out in zip(places, outs):
        out[...] = rows_of(node_ref, place, block)


def prep_kernel(
    parts,
    arrivals,
    count_ref,
    src_hbm,
    dst_hbm,
    slot_hbm,
    node_hbm,
    edge_hbm,
    cot_hbm,
    win_hbm,
    wout_hbm,
    node_ref,
    edge_ref,
    cot_ref,
    win_ref,
    wout_ref,
    pre_ref,
    up_ref,
    hot_ref,
    hot_turned,
    src_ref,
    dst_ref,
    slot_ref,
    recv_ref,
    mid_ref,
    sems,
):
    tiles, block = slot_ref.shape
    nodes, latent = node_ref.shape
    owned = nodes // block
    extent = hot_ref.shape[1]
    pairs = (
        (src_hbm, src_ref),
        (dst_hbm, dst_ref),
        (slot_hbm, slot_ref),
        (node_hbm, node_ref),
        (win_hbm.at[2 * latent :, :], win_ref.at[2 * latent :, :]),
        (win_hbm.at[:latent, :], win_ref.at[:latent, :]),
        (edge_hbm, edge_ref),
        (cot_hbm, cot_ref),
        (win_hbm.at[latent : 2 * latent, :], win_ref.at[latent : 2 * latent, :]),
        (wout_hbm, wout_ref),
    )
    copies = [load_small(*pair, sems.at[number]) for number, pair in enumerate(pairs)]
    part = lax.axis_index("dom")
    for copy in copies[:3]:
        copy.wait()
    index = lax.broadcasted_iota(jnp.int32, (extent, 2 * block), 0)
    lane = lax.broadcasted_iota(jnp.int32, (1, 2 * block), 1)
    first = lane < block
    within = jnp.where(first, lane, lane - block)
    node_index = lax.broadcasted_iota(jnp.int32, (nodes, 2 * block), 0)
    for tile in range(0, tiles, 2):
        wanted = []
        for member in (tile, tile + 1):
            source = src_ref[member]
            which = source - owned
            reach = jnp.where(which >= 2, 2, 1)
            partner = part - jnp.where(which % 2 == 1, -reach, reach)
            exists = (source < owned) | ((partner >= 0) & (partner < parts))
            place = jnp.minimum(source, owned + arrivals - 1)
            wanted.append(jnp.where(exists, place * block, -2 * extent))
        slots = jnp.concatenate(
            [slot_ref[tile : tile + 1, :], slot_ref[tile + 1 : tile + 2, :]], axis=1
        )
        row = slots + jnp.where(first, wanted[0], wanted[1])
        hot = jnp.where(index == row, 1.0, 0.0)
        at = slice(tile * block, (tile + 2) * block)
        hot_turned[:extent, at] = hot.astype(BF16)
        target = within + jnp.where(first, dst_ref[tile] * block, dst_ref[tile + 1] * block)
        hot_turned[extent:, at] = jnp.where(node_index == target, 1.0, 0.0).astype(BF16)
        hot_ref[at, :] = hot.T.astype(BF16)
    copies[3].wait()
    copies[4].wait()
    recv_ref[...] = dot(node_ref[...], win_ref[2 * latent :, :])
    copies[5].wait()
    copies[6].wait()
    group = 4 if tiles % 4 == 0 else 2
    for tile in range(0, tiles, group):
        rows = slice(tile * block, (tile + group) * block)
        received = jnp.concatenate(
            [rows_of(recv_ref, dst_ref[t], block) for t in range(tile, tile + group)], axis=0
        )
        pre_ref[rows, :] = dot(edge_ref[rows, :], win_ref[:latent, :]) + received
    copies[7].wait()
    cot = cot_ref[...].astype(F32)
    mid_ref[...] = cot - row_mean(cot)
    for tile in range(tiles):
        live = jnp.where(tile < count_ref[0], 1.0, 0.0)
        up_ref[tile * block : (tile + 1) * block, :] = rows_of(mid_ref, dst_ref[tile], block) * live
    copies[8].wait()
    copies[9].wait()


def put_units(ways, bit, targets, sections):
    latent = sections[0][0].shape[1]
    unit = latent // ways
    step = 256
    for number, (left, right) in enumerate(sections):
        value_right = right()
        for start in range(0, latent, step):
            value = t_dot(left[:, start : start + step], value_right)
            for at in range(0, step, unit):
                owner, spot = (start + at) // unit, 0
                if number > 0:
                    place = ((number - 1) * latent + start + at) // unit
                    owner, spot = place // 3, 1 + place % 3
                away, kept = targets[spot // 2]
                part = value[at : at + unit]
                where = slice((spot % 2) * unit, (spot % 2 + 1) * unit)

                @pl.when(bit == owner % 2)
                def _(kept=kept, owner=owner, where=where, part=part):
                    kept[owner // 2, where, :] = part

                @pl.when(bit != owner % 2)
                def _(away=away, owner=owner, where=where, part=part):
                    away[owner // 2, where, :] = part.astype(BF16)


def arrival_order(arrivals):
    return (2, 0, 1) if arrivals == 3 else tuple(range(arrivals))


def edge_kernel(ways, arrivals, four, block, *refs):
    arrived = [refs[which] for which in arrival_order(arrivals)]
    (
        node_ref,
        edge_ref,
        win_ref,
        wout_ref,
        pre_ref,
        up_ref,
        hot_ref,
        hot_turned,
        gpre_ref,
        message_ref,
        sums_ref,
        away_a,
        kept_a,
        away_b,
        kept_b,
        *back_refs,
        ext_ref,
        act_ref,
        proj_ref,
    ) = refs[arrivals:]
    nodes, latent = node_ref.shape
    edges = edge_ref.shape[0]
    extent = ext_ref.shape[0]
    places = arrival_places(lax.axis_index("dom"), four, arrivals)

    ext_ref[:nodes, :] = node_ref[...]
    for which in range(arrivals):
        at = pl.multiple_of(nodes + places[which] * block, block)
        ext_ref[pl.ds(at, block), :] = arrived[which][...]
    filled = nodes + arrivals * block
    if filled < extent:
        ext_ref[filled:, :] = jnp.zeros((extent - filled, latent), BF16)

    span = edges
    for start in range(0, edges, span):
        rows = slice(start, start + span)
        senders = dot(hot_ref[rows, :], ext_ref[...]).astype(BF16)
        preact = pre_ref[rows, :] + dot(senders, win_ref[latent : 2 * latent, :])
        gate = 0.5 * jnp.tanh(0.5 * preact) + 0.5
        activated = preact * gate
        slope = gate + activated * (1.0 - gate)
        activated = activated.astype(BF16)
        act_ref[rows, :] = activated
        projected = dot(activated, wout_ref[...])
        centered = projected - row_mean(projected)
        inv_scale = lax.rsqrt(row_mean(centered * centered) + EPSILON)
        message = centered * inv_scale
        message_ref[rows, :] = message
        upstream = up_ref[rows, :]
        grad_project = inv_scale * (upstream - message * row_mean(upstream * message))
        grad_project = grad_project.astype(BF16)
        proj_ref[rows, :] = grad_project
        gpre_ref[rows, :] = (dot_t(grad_project, wout_ref[...]) * slope).astype(BF16)

    sums_ref[...] = dot(hot_turned[...], gpre_ref[...])
    for which, back_ref in enumerate(back_refs):
        back_ref[...] = back_block(nodes, block, sums_ref, 1 + which)
    sections = (
        (act_ref, lambda: proj_ref[...]),
        (edge_ref, lambda: gpre_ref[...]),
        (ext_ref, lambda: sums_ref[:extent, :].astype(BF16)),
        (node_ref, lambda: sums_ref[extent:, :].astype(BF16)),
    )
    targets = ((away_a, kept_a), (away_b, kept_b))
    put_units(ways, lax.axis_index("dp") % 2, targets, sections)


def edge_grad_kernel(
    block,
    arrivals,
    four,
    dst_hbm,
    count_ref,
    after,
    gpre_ref,
    sums_ref,
    cot_ref,
    win_ref,
    edge_ref,
    message_ref,
    out_ref,
    agg_out,
    *refs,
):
    back_sums = refs[:-3]
    dst_ref, agg_ref, sem = refs[-3:]
    copy = load_small(dst_hbm, dst_ref, sem)
    nodes, latent = cot_ref.shape
    tiles = gpre_ref.shape[0] // block
    group = 4 if tiles % 4 == 0 else 1
    places = arrival_places(lax.axis_index("dom"), four, arrivals)
    for place, back_ref in zip(places, back_sums):
        at = pl.multiple_of(nodes + place * block, block)
        back_ref[...] = sums_ref[pl.ds(at, block), :].astype(BF16)
    agg_ref[...] = jnp.zeros_like(agg_ref)
    copy.wait()
    for first in range(0, tiles, group):
        rows = slice(first * block, (first + group) * block)
        upstream = jnp.concatenate(
            [
                rows_of(cot_ref, dst_ref[t], block).astype(F32)
                * jnp.where(t < count_ref[0], 1.0, 0.0)
                for t in range(first, first + group)
            ],
            axis=0,
        )
        out_ref[rows, :] = (dot_t(gpre_ref[rows, :], win_ref[:latent, :]) + upstream).astype(BF16)
        for t in range(first, first + group):
            live = jnp.where(t < count_ref[0], 1.0, 0.0)
            mine = slice(t * block, (t + 1) * block)
            updated = edge_ref[mine, :].astype(F32) + message_ref[mine, :]
            target = pl.ds(pl.multiple_of(dst_ref[t] * block, block), block)
            agg_ref[target, :] += updated * live
    agg_out[...] = agg_ref[...].astype(BF16)


def halve_kernel(bit, came_ref, kept_ref, after, away_ref, left_ref):
    mine = (lax.axis_index("dp") // bit) % 2
    for slot in range(left_ref.shape[0]):
        there, here = 2 * slot + 1 - mine, 2 * slot + mine
        away_ref[slot] = (kept_ref[there] + came_ref[there].astype(F32)).astype(BF16)
        left_ref[slot] = kept_ref[here] + came_ref[here].astype(F32)


def half_rows(rows):
    part = lax.axis_index("dom")
    inner = (part == 1) | (part == 2)
    here = pl.ds(pl.multiple_of(jnp.where(inner, 0, rows), rows), rows)
    there = pl.ds(pl.multiple_of(jnp.where(inner, rows, 0), rows), rows)
    return here, there


def back_block(nodes, block, sums_ref, which):
    place = arrival_places(lax.axis_index("dom"), True, 3)[which]
    return sums_ref[pl.ds(pl.multiple_of(nodes + place * block, block), block), :].astype(BF16)


def beside_first_kernel(came_ref, kept_ref, away_ref, left_ref):
    rows = left_ref.shape[1]
    here, there = half_rows(rows)
    for slot in range(2):
        away_ref[slot * rows : (slot + 1) * rows, :] = (
            kept_ref[slot, there, :] + came_ref[slot, there, :].astype(F32)
        ).astype(BF16)
        left_ref[slot] = kept_ref[slot, here, :] + came_ref[slot, here, :].astype(F32)


def beside_second_kernel(nodes, block, came_ref, kept_ref, sums_ref, *refs):
    away_ref, left_ref = refs[-2:]
    rows = left_ref.shape[0]
    here, there = half_rows(rows)
    away_ref[:rows, :] = (kept_ref[0, there, :] + came_ref[0, there, :].astype(F32)).astype(BF16)
    away_ref[rows:, :] = back_block(nodes, block, sums_ref, 0)
    left_ref[...] = kept_ref[0, here, :] + came_ref[0, here, :].astype(F32)


def over_second_kernel(came_ref, kept_ref, *refs):
    away_ref, left_ref = refs[-2:]
    mine = lax.axis_index("dp") // 2
    rows = left_ref.shape[0]

    def came(slot):
        spot = pl.ds(pl.multiple_of(slot * rows, rows), rows)
        return came_ref[spot, :].astype(F32)

    away_ref[...] = (kept_ref[1 - mine] + came(1 - mine)).astype(BF16)
    left_ref[...] = kept_ref[mine] + came(mine)


def add_kernel(left_a, came_a, left_b, came_b, *refs):
    out_ref = refs[-1]
    rows = left_a.shape[0]
    out_ref[:rows, :] = (left_a[...] + came_a[:rows, :].astype(F32)).astype(BF16)
    out_ref[rows:, :] = (left_b[...] + came_b[...].astype(F32)).astype(BF16)


def node_grad_kernel(arrivals, four, boundary_hbm, after, sums_ref, win_ref, *refs):
    returned = refs[:arrivals]
    out_ref, total_ref, boundary_ref, sem = refs[arrivals:]
    nodes, latent = out_ref.shape
    extent = sums_ref.shape[0] - nodes
    block = returned[-1].shape[0]
    copy = load_small(boundary_hbm, boundary_ref, sem)
    total_ref[...] = sums_ref[:nodes, :]
    copy.wait()
    for which, place in enumerate(boundary_places(boundary_ref, lax.axis_index("dom"), four)):
        spot = pl.ds(pl.multiple_of(place * block, block), block)
        total_ref[spot, :] += returned[which][-block:, :].astype(F32)

    def wide_dot(value, weight):
        high = value.astype(BF16)
        low = (value - high.astype(F32)).astype(BF16)
        return dot_t(high, weight) + dot_t(low, weight)

    out_ref[...] = (
        wide_dot(total_ref[...], win_ref[latent : 2 * latent, :])
        + wide_dot(sums_ref[extent:, :], win_ref[2 * latent :, :])
    ).astype(BF16)


def last_kernel(node_out, edge_grad, own_ref, other_ref, in_ref, out_ref):
    unit = out_ref.shape[0]
    part = lax.axis_index("dom")
    inner = (part == 1) | (part == 2)

    def write(low, high):
        out_ref[...] = low[:unit, :].astype(F32)
        in_ref[:unit, :] = high[:unit, :].astype(F32)
        in_ref[unit : 2 * unit, :] = low[unit:, :].astype(F32)
        in_ref[2 * unit :, :] = high[unit:, :].astype(F32)

    @pl.when(inner)
    def _():
        write(own_ref, other_ref)

    @pl.when(jnp.logical_not(inner))
    def _():
        write(other_ref, own_ref)


def swap(array, axis, partner):
    devices = lax.axis_size(axis)
    return lax.ppermute(array, axis, [(i, partner(i)) for i in range(devices)])


def from_behind(array, axis, by):
    devices = lax.axis_size(axis)
    pairs = [(i, i + by) for i in range(devices) if 0 <= i + by < devices]
    return lax.ppermute(array, axis, pairs)


def partners_of_four(which):
    return ((1, 0, 3, 2), (0, 2, 1, 3), (2, 3, 0, 1))[which]


def exchange_of_four(first, second, third):
    third = swap(third, "dom", lambda i: partners_of_four(2)[i])
    second = swap(second, "dom", lambda i: partners_of_four(1)[i])
    first = swap(first, "dom", lambda i: partners_of_four(0)[i])
    return [first, second, third]


def halve(bit, came, kept, after):
    slots, rows, latent = kept.shape
    return pl.pallas_call(
        functools.partial(halve_kernel, bit),
        out_shape=(
            pltpu.VMEM((slots // 2, rows, latent), BF16),
            pltpu.VMEM((slots // 2, rows, latent), F32),
        ),
        in_specs=[VMEM] * 3,
        out_specs=(VMEM,) * 2,
        compiler_params=pltpu.CompilerParams(vmem_limit_bytes=4 * 1024 * 1024),
        cost_estimate=pl.CostEstimate(flops=0, bytes_accessed=500_000, transcendentals=0),
        name="halve",
    )(in_vmem(came), in_vmem(kept), in_vmem(after))


def sum_over_dp(away, kept, after):
    devices = lax.axis_size("dp")
    bit = 1
    while True:
        came = swap(away, "dp", lambda i, bit=bit: i ^ bit)
        bit *= 2
        if bit >= devices:
            return came, kept, away
        away, kept = halve(bit, came, kept, after)


def small_call(kernel, name, out_shape, *operands, after=()):
    many = isinstance(out_shape, tuple)
    return pl.pallas_call(
        kernel,
        out_shape=out_shape,
        in_specs=[VMEM] * len(operands) + [HBM] * len(after),
        out_specs=(VMEM,) * len(out_shape) if many else VMEM,
        compiler_params=pltpu.CompilerParams(vmem_limit_bytes=4 * 1024 * 1024),
        cost_estimate=pl.CostEstimate(flops=0, bytes_accessed=500_000, transcendentals=0),
        name=name,
    )(*[in_vmem(array) for array in operands], *[in_hbm(array) for array in after])


def sum_of_four(kept):
    return (kept.astype(F32) + swap(kept, "dom", lambda i: 3 - i).astype(F32)).astype(BF16)


def with_other_half(kept):
    return kept, swap(kept, "dom", lambda i: i ^ 1)


def sum_over_dom(rows):
    piece = lax.psum_scatter(rows, "dom", scatter_dimension=0, tiled=True)
    return lax.all_gather(piece, "dom", axis=0, tiled=True)


def in_vmem(array):
    return pltpu.with_memory_space_constraint(array, pltpu.VMEM)


def in_hbm(array):
    return pltpu.with_memory_space_constraint(array, pltpu.HBM)


def body(
    node_latents,
    edge_latents,
    agg_cotangent,
    weight_in,
    weight_out,
    boundary,
    tile_src,
    tile_dst,
    edge_slot,
    tile_count,
):
    tiles, block = edge_slot.shape
    edges, latent = edge_latents.shape[1:]
    nodes = node_latents.shape[1]
    parts = lax.axis_size("dom")
    ways = lax.axis_size("dp")
    four = parts == 4 and ways == 4
    arrivals = 3 if four else 4
    boundary = in_hbm(boundary)
    tile_dst = in_hbm(tile_dst)
    node_rows = in_hbm(node_latents[0])
    block_shape = pltpu.VMEM((block, latent), BF16)
    small = pltpu.CompilerParams(vmem_limit_bytes=8 * 1024 * 1024)

    sent = pl.pallas_call(
        functools.partial(pick_kernel, four, block),
        out_shape=(block_shape,) * arrivals,
        in_specs=[HBM] * 2,
        out_specs=(VMEM,) * arrivals,
        scratch_shapes=[
            pltpu.SMEM(boundary.shape, jnp.int32),
            pltpu.VMEM((nodes, latent), BF16),
            pltpu.SemaphoreType.DMA((2,)),
        ],
        compiler_params=small,
        cost_estimate=pl.CostEstimate(flops=0, bytes_accessed=400_000, transcendentals=0),
        name="pick_blocks",
    )(boundary, node_rows)
    if four:
        came = exchange_of_four(*sent)
    else:
        came = [from_behind(sent[which], "dom", OFFSET_LIST[which]) for which in range(4)]
    unit = latent // ways
    half = ways // 2
    extent = -(-(nodes + arrivals * block) // 128) * 128

    node_v, edge_v, cot_v, win_v, wout_v, pre, up, hot, turned = pl.pallas_call(
        functools.partial(prep_kernel, parts, arrivals),
        out_shape=(
            pltpu.VMEM((nodes, latent), BF16),
            pltpu.VMEM((edges, latent), BF16),
            pltpu.VMEM((nodes, latent), BF16),
            pltpu.VMEM(weight_in.shape, BF16),
            pltpu.VMEM(weight_out.shape, BF16),
            pltpu.VMEM((edges, latent), F32),
            pltpu.VMEM((edges, latent), F32),
            pltpu.VMEM((edges, extent), BF16),
            pltpu.VMEM((extent + nodes, edges), BF16),
        ),
        in_specs=[SMEM] + [HBM] * 8,
        out_specs=(VMEM,) * 9,
        scratch_shapes=[
            pltpu.SMEM((tiles,), jnp.int32),
            pltpu.SMEM((tiles,), jnp.int32),
            pltpu.VMEM((tiles, block), jnp.int32),
            pltpu.VMEM((nodes, latent), F32),
            pltpu.VMEM((nodes, latent), F32),
            pltpu.SemaphoreType.DMA((10,)),
        ],
        compiler_params=small,
        cost_estimate=pl.CostEstimate(
            flops=2 * edges * latent * latent, bytes_accessed=8_000_000, transcendentals=0
        ),
        name="prepare",
    )(
        tile_count,
        in_hbm(tile_src),
        tile_dst,
        in_hbm(edge_slot),
        node_rows,
        in_hbm(edge_latents[0]),
        in_hbm(agg_cotangent[0]),
        in_hbm(weight_in),
        in_hbm(weight_out),
    )
    sent_shape = pltpu.VMEM((half, 2 * unit, latent), BF16)
    kept_shape = pltpu.VMEM((half, 2 * unit, latent), F32)
    ordered = [None] * arrivals
    for array, which in zip(came, arrival_order(arrivals)):
        ordered[which] = array
    grad_pre, message, sums, away_a, kept_a, away_b, kept_b, *outer = pl.pallas_call(
        functools.partial(edge_kernel, ways, arrivals, four, block),
        out_shape=(
            pltpu.VMEM((edges, latent), BF16),
            pltpu.VMEM((edges, latent), F32),
            pltpu.VMEM((extent + nodes, latent), F32),
            sent_shape,
            kept_shape,
            sent_shape,
            kept_shape,
            *[block_shape] * (2 if four else 0),
        ),
        in_specs=[VMEM] * (8 + arrivals),
        out_specs=(VMEM,) * (9 if four else 7),
        scratch_shapes=[
            pltpu.VMEM((extent, latent), BF16),
            pltpu.VMEM((edges, latent), BF16),
            pltpu.VMEM((edges, latent), BF16),
        ],
        compiler_params=pltpu.CompilerParams(vmem_limit_bytes=16 * 1024 * 1024),
        cost_estimate=pl.CostEstimate(
            flops=12 * edges * latent * latent,
            bytes_accessed=12_000_000,
            transcendentals=edges * latent,
        ),
        name="edge_block",
    )(
        *[
            in_vmem(array)
            for array in (*ordered, node_v, edge_v, win_v, wout_v, pre, up, hot, turned)
        ],
    )
    if four:
        rows = 2 * unit
        piece, wide = pltpu.VMEM((unit, latent), BF16), pltpu.VMEM((unit, latent), F32)
        came_a = swap(away_a, "dp", lambda i: i ^ 1)
        away_a, kept_a = halve(2, came_a, kept_a, cot_v)
        came_a = swap(away_a, "dp", lambda i: i ^ 2)
        came_b = swap(away_b, "dp", lambda i: i ^ 1)
        away_b, kept_b = small_call(
            beside_first_kernel,
            "beside_first",
            (pltpu.VMEM((rows, latent), BF16), pltpu.VMEM((2, unit, latent), F32)),
            came_b,
            kept_b,
        )
        beside = swap(away_b, "dom", lambda i: i ^ 1)
        far = swap(outer[1], "dom", lambda i: partners_of_four(2)[i])
        near = swap(outer[0], "dom", lambda i: partners_of_four(1)[i])
        away_a, kept_a = small_call(
            functools.partial(beside_second_kernel, nodes, block),
            "beside_second",
            (pltpu.VMEM((unit + block, latent), BF16), wide),
            came_a,
            kept_a,
            sums,
            far,
        )
        came_a = swap(away_a, "dom", lambda i: i ^ 1)
        away_b, kept_b = small_call(
            over_second_kernel, "over_second", (piece, wide), beside, kept_b
        )
        came_b = swap(away_b, "dp", lambda i: i ^ 2)
        pair = small_call(
            add_kernel,
            "add_terms",
            pltpu.VMEM((rows, latent), BF16),
            kept_a,
            came_a,
            kept_b,
            came_b,
            near,
        )
        returned = [came_a, near, far]
        late, backs = pair, 0
    else:
        came_a, kept_a, late = sum_over_dp(away_a, kept_a, cot_v)
        came_b, kept_b, _ = sum_over_dp(away_b, kept_b, cot_v)
        backs = arrivals
    edge_grad, agg, *back_sums = pl.pallas_call(
        functools.partial(edge_grad_kernel, block, arrivals, four),
        out_shape=(
            jax.ShapeDtypeStruct((edges, latent), BF16),
            jax.ShapeDtypeStruct((nodes, latent), BF16),
        )
        + (block_shape,) * backs,
        in_specs=[HBM, SMEM] + [VMEM] * 7,
        out_specs=(VMEM,) * (2 + backs),
        scratch_shapes=[
            pltpu.SMEM((tiles,), jnp.int32),
            pltpu.VMEM((nodes, latent), F32),
            pltpu.SemaphoreType.DMA,
        ],
        compiler_params=small,
        cost_estimate=pl.CostEstimate(
            flops=2 * edges * latent * latent, bytes_accessed=3_000_000, transcendentals=0
        ),
        name="edge_grads",
    )(
        tile_dst,
        tile_count,
        *[in_vmem(array) for array in (late, grad_pre, sums, cot_v, win_v, edge_v, message)],
    )
    if not four:
        returned = [
            from_behind(back_sums[which], "dom", -OFFSET_LIST[which]) for which in range(4)
        ]
    node_out = pl.pallas_call(
        functools.partial(node_grad_kernel, arrivals, four),
        out_shape=jax.ShapeDtypeStruct((nodes, latent), BF16),
        in_specs=[HBM] + [VMEM] * (3 + arrivals),
        out_specs=VMEM,
        scratch_shapes=[
            pltpu.VMEM((nodes, latent), F32),
            pltpu.SMEM(boundary.shape, jnp.int32),
            pltpu.SemaphoreType.DMA,
        ],
        compiler_params=small,
        cost_estimate=pl.CostEstimate(
            flops=8 * nodes * latent * latent, bytes_accessed=2_000_000, transcendentals=0
        ),
        name="node_grads",
    )(boundary, *[in_vmem(array) for array in (late, sums, win_v, *returned)])
    if four:
        w_in_grad, w_out_grad = pl.pallas_call(
            last_kernel,
            out_shape=(
                jax.ShapeDtypeStruct((3 * unit, latent), F32),
                jax.ShapeDtypeStruct((unit, latent), F32),
            ),
            in_specs=[HBM] * 2 + [VMEM] * 2,
            out_specs=(VMEM,) * 2,
            compiler_params=small,
            cost_estimate=pl.CostEstimate(flops=0, bytes_accessed=1_500_000, transcendentals=0),
            name="widen",
        )(in_hbm(node_out), in_hbm(edge_grad), *with_other_half(sum_of_four(pair)))
    else:
        sum_a = sum_over_dom(kept_a[0] + came_a[0].astype(F32))
        sum_b = sum_over_dom(kept_b[0] + came_b[0].astype(F32))
        w_in_grad = jnp.concatenate([sum_a[unit:], sum_b], axis=0)
        w_out_grad = sum_a[:unit]
    return (agg[None], edge_grad[None], node_out[None], w_in_grad, w_out_grad)


def solution(mesh):
    in_specs = (
        P(("group", "dp"), "dom", None),
        P(("group", "dp"), "dom", None),
        P(("group", "dp"), "dom", None),
        P(),
        P(),
        P(("group", "dom"), None),
        P(("group", "dom")),
        P(("group", "dom")),
        P(("group", "dom"), None),
        P(("group", "dom")),
    )
    out_specs = (
        P(("group", "dp"), "dom", None),
        P(("group", "dp"), "dom", None),
        P(("group", "dp"), "dom", None),
        P(("group", "dp"), None),
        P(("group", "dp"), None),
    )
    return jax.shard_map(body, mesh=mesh, in_specs=in_specs, out_specs=out_specs, check_vma=False)
```

```python
import functools

import jax
import jax.numpy as jnp
from jax import lax
from jax.experimental import pallas as pl
from jax.experimental.pallas import tpu as pltpu
from jax.sharding import PartitionSpec as P

OFFSET_LIST = (1, -1, 2, -2)
EPSILON = 1e-05
VMEM = pl.BlockSpec(memory_space=pltpu.VMEM)
HBM = pl.BlockSpec(memory_space=pltpu.HBM)
SMEM = pl.BlockSpec(memory_space=pltpu.SMEM)
ANY = pl.BlockSpec(memory_space=pl.ANY)
F32 = jnp.float32
BF16 = jnp.bfloat16


def dot(left, right):
    return jnp.dot(left, right, preferred_element_type=F32)


def dot_t(left, right):
    return lax.dot_general(left, right, (((1,), (1,)), ((), ())), preferred_element_type=F32)


def t_dot(left, right):
    return lax.dot_general(left, right, (((0,), (0,)), ((), ())), preferred_element_type=F32)


def row_mean(array):
    return jnp.sum(array, axis=1, keepdims=True) * (1.0 / array.shape[1])


def rows_of(ref, block, size):
    return ref[pl.ds(pl.multiple_of(block * size, size), size), :]


def load_small(source, target, sem):
    copy = pltpu.make_async_copy(source, target, sem)
    copy.start()
    return copy


def boundary_places(boundary_ref, part, four):
    taken = [boundary_ref[0, which] for which in range(4)]
    if not four:
        return taken
    even = part % 2 == 0
    return [
        jnp.where(even, taken[0], taken[1]),
        jnp.where(even, taken[1], taken[0]),
        jnp.where(part < 2, taken[2], taken[3]),
    ]


def arrival_places(part, four, arrivals):
    if not four:
        return list(range(arrivals))
    even = part % 2 == 0
    return [jnp.where(even, 1, 0), jnp.where(even, 0, 1), 2]


def pick_kernel(four, block, boundary_hbm, node_hbm, *refs):
    count = 3 if four else 4
    outs = refs[:count]
    boundary_ref, node_ref, sems = refs[count:]
    small = load_small(boundary_hbm, boundary_ref, sems.at[0])
    large = load_small(node_hbm, node_ref, sems.at[1])
    small.wait()
    places = boundary_places(boundary_ref, lax.axis_index("dom"), four)
    large.wait()
    for place, out in zip(places, outs):
        out[...] = rows_of(node_ref, place, block)


def prep_kernel(
    parts,
    arrivals,
    count_ref,
    src_hbm,
    dst_hbm,
    slot_hbm,
    node_hbm,
    edge_hbm,
    cot_hbm,
    win_hbm,
    wout_hbm,
    node_ref,
    edge_ref,
    cot_ref,
    win_ref,
    wout_ref,
    pre_ref,
    up_ref,
    hot_ref,
    hot_turned,
    src_ref,
    dst_ref,
    slot_ref,
    recv_ref,
    mid_ref,
    sems,
):
    tiles, block = slot_ref.shape
    nodes, latent = node_ref.shape
    owned = nodes // block
    extent = hot_ref.shape[1]
    pairs = (
        (src_hbm, src_ref),
        (dst_hbm, dst_ref),
        (slot_hbm, slot_ref),
        (node_hbm, node_ref),
        (win_hbm.at[2 * latent :, :], win_ref.at[2 * latent :, :]),
        (win_hbm.at[:latent, :], win_ref.at[:latent, :]),
        (edge_hbm, edge_ref),
        (cot_hbm, cot_ref),
        (win_hbm.at[latent : 2 * latent, :], win_ref.at[latent : 2 * latent, :]),
        (wout_hbm, wout_ref),
    )
    copies = [load_small(*pair, sems.at[number]) for number, pair in enumerate(pairs)]
    part = lax.axis_index("dom")
    for copy in copies[:3]:
        copy.wait()
    index = lax.broadcasted_iota(jnp.int32, (extent, 2 * block), 0)
    lane = lax.broadcasted_iota(jnp.int32, (1, 2 * block), 1)
    first = lane < block
    within = jnp.where(first, lane, lane - block)
    node_index = lax.broadcasted_iota(jnp.int32, (nodes, 2 * block), 0)
    for tile in range(0, tiles, 2):
        wanted = []
        for member in (tile, tile + 1):
            source = src_ref[member]
            which = source - owned
            reach = jnp.where(which >= 2, 2, 1)
            partner = part - jnp.where(which % 2 == 1, -reach, reach)
            exists = (source < owned) | ((partner >= 0) & (partner < parts))
            place = jnp.minimum(source, owned + arrivals - 1)
            wanted.append(jnp.where(exists, place * block, -2 * extent))
        slots = jnp.concatenate(
            [slot_ref[tile : tile + 1, :], slot_ref[tile + 1 : tile + 2, :]], axis=1
        )
        row = slots + jnp.where(first, wanted[0], wanted[1])
        hot = jnp.where(index == row, 1.0, 0.0)
        at = slice(tile * block, (tile + 2) * block)
        hot_turned[:extent, at] = hot.astype(BF16)
        target = within + jnp.where(first, dst_ref[tile] * block, dst_ref[tile + 1] * block)
        hot_turned[extent:, at] = jnp.where(node_index == target, 1.0, 0.0).astype(BF16)
        hot_ref[at, :] = hot.T.astype(BF16)
    copies[3].wait()
    copies[4].wait()
    recv_ref[...] = dot(node_ref[...], win_ref[2 * latent :, :])
    copies[5].wait()
    copies[6].wait()
    group = 4 if tiles % 4 == 0 else 2
    for tile in range(0, tiles, group):
        rows = slice(tile * block, (tile + group) * block)
        received = jnp.concatenate(
            [rows_of(recv_ref, dst_ref[t], block) for t in range(tile, tile + group)], axis=0
        )
        pre_ref[rows, :] = dot(edge_ref[rows, :], win_ref[:latent, :]) + received
    copies[7].wait()
    cot = cot_ref[...].astype(F32)
    mid_ref[...] = cot - row_mean(cot)
    for tile in range(tiles):
        live = jnp.where(tile < count_ref[0], 1.0, 0.0)
        up_ref[tile * block : (tile + 1) * block, :] = rows_of(mid_ref, dst_ref[tile], block) * live
    copies[8].wait()
    copies[9].wait()


def put_units(ways, bit, targets, sections):
    latent = sections[0][0].shape[1]
    unit = latent // ways
    step = 256
    for number, (left, right) in enumerate(sections):
        value_right = right()
        for start in range(0, latent, step):
            value = t_dot(left[:, start : start + step], value_right)
            for at in range(0, step, unit):
                owner, spot = (start + at) // unit, 0
                if number > 0:
                    place = ((number - 1) * latent + start + at) // unit
                    owner, spot = place // 3, 1 + place % 3
                away, kept = targets[spot // 2]
                part = value[at : at + unit]
                where = slice((spot % 2) * unit, (spot % 2 + 1) * unit)

                @pl.when(bit == owner % 2)
                def _(kept=kept, owner=owner, where=where, part=part):
                    kept[owner // 2, where, :] = part

                @pl.when(bit != owner % 2)
                def _(away=away, owner=owner, where=where, part=part):
                    away[owner // 2, where, :] = part.astype(BF16)


def arrival_order(arrivals):
    return (2, 0, 1) if arrivals == 3 else tuple(range(arrivals))


def edge_kernel(ways, arrivals, four, block, *refs):
    arrived = [refs[which] for which in arrival_order(arrivals)]
    (
        node_ref,
        edge_ref,
        win_ref,
        wout_ref,
        pre_ref,
        up_ref,
        hot_ref,
        hot_turned,
        gpre_ref,
        message_ref,
        sums_ref,
        away_a,
        kept_a,
        away_b,
        kept_b,
        *back_refs,
        ext_ref,
        act_ref,
        proj_ref,
    ) = refs[arrivals:]
    nodes, latent = node_ref.shape
    edges = edge_ref.shape[0]
    extent = ext_ref.shape[0]
    places = arrival_places(lax.axis_index("dom"), four, arrivals)

    ext_ref[:nodes, :] = node_ref[...]
    for which in range(arrivals):
        at = pl.multiple_of(nodes + places[which] * block, block)
        ext_ref[pl.ds(at, block), :] = arrived[which][...]
    filled = nodes + arrivals * block
    if filled < extent:
        ext_ref[filled:, :] = jnp.zeros((extent - filled, latent), BF16)

    span = edges
    for start in range(0, edges, span):
        rows = slice(start, start + span)
        senders = dot(hot_ref[rows, :], ext_ref[...]).astype(BF16)
        preact = pre_ref[rows, :] + dot(senders, win_ref[latent : 2 * latent, :])
        gate = 0.5 * jnp.tanh(0.5 * preact) + 0.5
        activated = preact * gate
        slope = gate + activated * (1.0 - gate)
        activated = activated.astype(BF16)
        act_ref[rows, :] = activated
        projected = dot(activated, wout_ref[...])
        centered = projected - row_mean(projected)
        inv_scale = lax.rsqrt(row_mean(centered * centered) + EPSILON)
        message = centered * inv_scale
        message_ref[rows, :] = message
        upstream = up_ref[rows, :]
        grad_project = inv_scale * (upstream - message * row_mean(upstream * message))
        grad_project = grad_project.astype(BF16)
        proj_ref[rows, :] = grad_project
        gpre_ref[rows, :] = (dot_t(grad_project, wout_ref[...]) * slope).astype(BF16)

    sums_ref[...] = dot(hot_turned[...], gpre_ref[...])
    for which, back_ref in enumerate(back_refs):
        back_ref[...] = back_block(nodes, block, sums_ref, 1 + which)
    sections = (
        (act_ref, lambda: proj_ref[...]),
        (edge_ref, lambda: gpre_ref[...]),
        (ext_ref, lambda: sums_ref[:extent, :].astype(BF16)),
        (node_ref, lambda: sums_ref[extent:, :].astype(BF16)),
    )
    targets = ((away_a, kept_a), (away_b, kept_b))
    put_units(ways, lax.axis_index("dp") % 2, targets, sections)


def edge_grad_kernel(
    block,
    arrivals,
    four,
    dst_hbm,
    count_ref,
    after,
    gpre_ref,
    sums_ref,
    cot_ref,
    win_ref,
    edge_ref,
    message_ref,
    out_ref,
    agg_out,
    *refs,
):
    back_sums = refs[:-3]
    dst_ref, agg_ref, sem = refs[-3:]
    copy = load_small(dst_hbm, dst_ref, sem)
    nodes, latent = cot_ref.shape
    tiles = gpre_ref.shape[0] // block
    group = 4 if tiles % 4 == 0 else 1
    places = arrival_places(lax.axis_index("dom"), four, arrivals)
    for place, back_ref in zip(places, back_sums):
        at = pl.multiple_of(nodes + place * block, block)
        back_ref[...] = sums_ref[pl.ds(at, block), :].astype(BF16)
    agg_ref[...] = jnp.zeros_like(agg_ref)
    copy.wait()
    for first in range(0, tiles, group):
        rows = slice(first * block, (first + group) * block)
        upstream = jnp.concatenate(
            [
                rows_of(cot_ref, dst_ref[t], block).astype(F32)
                * jnp.where(t < count_ref[0], 1.0, 0.0)
                for t in range(first, first + group)
            ],
            axis=0,
        )
        out_ref[rows, :] = (dot_t(gpre_ref[rows, :], win_ref[:latent, :]) + upstream).astype(BF16)
        for t in range(first, first + group):
            live = jnp.where(t < count_ref[0], 1.0, 0.0)
            mine = slice(t * block, (t + 1) * block)
            updated = edge_ref[mine, :].astype(F32) + message_ref[mine, :]
            target = pl.ds(pl.multiple_of(dst_ref[t] * block, block), block)
            agg_ref[target, :] += updated * live
    agg_out[...] = agg_ref[...].astype(BF16)


def halve_kernel(bit, came_ref, kept_ref, after, away_ref, left_ref):
    mine = (lax.axis_index("dp") // bit) % 2
    for slot in range(left_ref.shape[0]):
        there, here = 2 * slot + 1 - mine, 2 * slot + mine
        away_ref[slot] = (kept_ref[there] + came_ref[there].astype(F32)).astype(BF16)
        left_ref[slot] = kept_ref[here] + came_ref[here].astype(F32)


def half_rows(rows):
    part = lax.axis_index("dom")
    inner = (part == 1) | (part == 2)
    here = pl.ds(pl.multiple_of(jnp.where(inner, 0, rows), rows), rows)
    there = pl.ds(pl.multiple_of(jnp.where(inner, rows, 0), rows), rows)
    return here, there


def back_block(nodes, block, sums_ref, which):
    place = arrival_places(lax.axis_index("dom"), True, 3)[which]
    return sums_ref[pl.ds(pl.multiple_of(nodes + place * block, block), block), :].astype(BF16)


def beside_first_kernel(came_ref, kept_ref, away_ref, left_ref):
    rows = left_ref.shape[1]
    here, there = half_rows(rows)
    for slot in range(2):
        away_ref[slot * rows : (slot + 1) * rows, :] = (
            kept_ref[slot, there, :] + came_ref[slot, there, :].astype(F32)
        ).astype(BF16)
        left_ref[slot] = kept_ref[slot, here, :] + came_ref[slot, here, :].astype(F32)


def beside_second_kernel(nodes, block, came_ref, kept_ref, sums_ref, *refs):
    away_ref, left_ref = refs[-2:]
    rows = left_ref.shape[0]
    here, there = half_rows(rows)
    away_ref[:rows, :] = (kept_ref[0, there, :] + came_ref[0, there, :].astype(F32)).astype(BF16)
    away_ref[rows:, :] = back_block(nodes, block, sums_ref, 0)
    left_ref[...] = kept_ref[0, here, :] + came_ref[0, here, :].astype(F32)


def over_second_kernel(came_ref, kept_ref, *refs):
    away_ref, left_ref = refs[-2:]
    mine = lax.axis_index("dp") // 2
    rows = left_ref.shape[0]

    def came(slot):
        spot = pl.ds(pl.multiple_of(slot * rows, rows), rows)
        return came_ref[spot, :].astype(F32)

    away_ref[...] = (kept_ref[1 - mine] + came(1 - mine)).astype(BF16)
    left_ref[...] = kept_ref[mine] + came(mine)


def add_kernel(left_a, came_a, left_b, came_b, *refs):
    out_ref = refs[-1]
    rows = left_a.shape[0]
    out_ref[:rows, :] = (left_a[...] + came_a[:rows, :].astype(F32)).astype(BF16)
    out_ref[rows:, :] = (left_b[...] + came_b[...].astype(F32)).astype(BF16)


def node_grad_kernel(arrivals, four, boundary_hbm, after, sums_ref, win_ref, *refs):
    returned = refs[:arrivals]
    out_ref, total_ref, boundary_ref, sem = refs[arrivals:]
    nodes, latent = out_ref.shape
    extent = sums_ref.shape[0] - nodes
    block = returned[-1].shape[0]
    copy = load_small(boundary_hbm, boundary_ref, sem)
    total_ref[...] = sums_ref[:nodes, :]
    copy.wait()
    for which, place in enumerate(boundary_places(boundary_ref, lax.axis_index("dom"), four)):
        spot = pl.ds(pl.multiple_of(place * block, block), block)
        total_ref[spot, :] += returned[which][-block:, :].astype(F32)

    def wide_dot(value, weight):
        high = value.astype(BF16)
        low = (value - high.astype(F32)).astype(BF16)
        return dot_t(high, weight) + dot_t(low, weight)

    out_ref[...] = (
        wide_dot(total_ref[...], win_ref[latent : 2 * latent, :])
        + wide_dot(sums_ref[extent:, :], win_ref[2 * latent :, :])
    ).astype(BF16)


def last_kernel(node_out, edge_grad, own_ref, other_ref, in_ref, out_ref):
    unit = out_ref.shape[0]
    part = lax.axis_index("dom")
    inner = (part == 1) | (part == 2)

    def write(low, high):
        out_ref[...] = low[:unit, :].astype(F32)
        in_ref[:unit, :] = high[:unit, :].astype(F32)
        in_ref[unit : 2 * unit, :] = low[unit:, :].astype(F32)
        in_ref[2 * unit :, :] = high[unit:, :].astype(F32)

    @pl.when(inner)
    def _():
        write(own_ref, other_ref)

    @pl.when(jnp.logical_not(inner))
    def _():
        write(other_ref, own_ref)


def swap(array, axis, partner):
    devices = lax.axis_size(axis)
    return lax.ppermute(array, axis, [(i, partner(i)) for i in range(devices)])


def from_behind(array, axis, by):
    devices = lax.axis_size(axis)
    pairs = [(i, i + by) for i in range(devices) if 0 <= i + by < devices]
    return lax.ppermute(array, axis, pairs)


def partners_of_four(which):
    return ((1, 0, 3, 2), (0, 2, 1, 3), (2, 3, 0, 1))[which]


def exchange_of_four(first, second, third):
    third = swap(third, "dom", lambda i: partners_of_four(2)[i])
    second = swap(second, "dom", lambda i: partners_of_four(1)[i])
    first = swap(first, "dom", lambda i: partners_of_four(0)[i])
    return [first, second, third]


def halve(bit, came, kept, after):
    slots, rows, latent = kept.shape
    return pl.pallas_call(
        functools.partial(halve_kernel, bit),
        out_shape=(
            pltpu.VMEM((slots // 2, rows, latent), BF16),
            pltpu.VMEM((slots // 2, rows, latent), F32),
        ),
        in_specs=[VMEM] * 3,
        out_specs=(VMEM,) * 2,
        compiler_params=pltpu.CompilerParams(vmem_limit_bytes=4 * 1024 * 1024),
        cost_estimate=pl.CostEstimate(flops=0, bytes_accessed=500_000, transcendentals=0),
        name="halve",
    )(in_vmem(came), in_vmem(kept), in_vmem(after))


def sum_over_dp(away, kept, after):
    devices = lax.axis_size("dp")
    bit = 1
    while True:
        came = swap(away, "dp", lambda i, bit=bit: i ^ bit)
        bit *= 2
        if bit >= devices:
            return came, kept, away
        away, kept = halve(bit, came, kept, after)


def small_call(kernel, name, out_shape, *operands, after=()):
    many = isinstance(out_shape, tuple)
    return pl.pallas_call(
        kernel,
        out_shape=out_shape,
        in_specs=[VMEM] * len(operands) + [HBM] * len(after),
        out_specs=(VMEM,) * len(out_shape) if many else VMEM,
        compiler_params=pltpu.CompilerParams(vmem_limit_bytes=4 * 1024 * 1024),
        cost_estimate=pl.CostEstimate(flops=0, bytes_accessed=500_000, transcendentals=0),
        name=name,
    )(*[in_vmem(array) for array in operands], *[in_hbm(array) for array in after])


def sum_of_four(kept):
    return (kept.astype(F32) + swap(kept, "dom", lambda i: 3 - i).astype(F32)).astype(BF16)


def with_other_half(kept):
    return kept, swap(kept, "dom", lambda i: i ^ 1)


def sum_over_dom(rows):
    piece = lax.psum_scatter(rows, "dom", scatter_dimension=0, tiled=True)
    return lax.all_gather(piece, "dom", axis=0, tiled=True)


def in_vmem(array):
    return pltpu.with_memory_space_constraint(array, pltpu.VMEM)


def in_hbm(array):
    return pltpu.with_memory_space_constraint(array, pltpu.HBM)


def body(
    node_latents,
    edge_latents,
    agg_cotangent,
    weight_in,
    weight_out,
    boundary,
    tile_src,
    tile_dst,
    edge_slot,
    tile_count,
):
    tiles, block = edge_slot.shape
    edges, latent = edge_latents.shape[1:]
    nodes = node_latents.shape[1]
    parts = lax.axis_size("dom")
    ways = lax.axis_size("dp")
    four = parts == 4 and ways == 4
    arrivals = 3 if four else 4
    boundary = in_hbm(boundary)
    tile_dst = in_hbm(tile_dst)
    node_rows = in_hbm(node_latents[0])
    block_shape = pltpu.VMEM((block, latent), BF16)
    small = pltpu.CompilerParams(vmem_limit_bytes=8 * 1024 * 1024)

    sent = pl.pallas_call(
        functools.partial(pick_kernel, four, block),
        out_shape=(block_shape,) * arrivals,
        in_specs=[HBM] * 2,
        out_specs=(VMEM,) * arrivals,
        scratch_shapes=[
            pltpu.SMEM(boundary.shape, jnp.int32),
            pltpu.VMEM((nodes, latent), BF16),
            pltpu.SemaphoreType.DMA((2,)),
        ],
        compiler_params=small,
        cost_estimate=pl.CostEstimate(flops=0, bytes_accessed=400_000, transcendentals=0),
        name="pick_blocks",
    )(boundary, node_rows)
    if four:
        came = exchange_of_four(*sent)
    else:
        came = [from_behind(sent[which], "dom", OFFSET_LIST[which]) for which in range(4)]
    unit = latent // ways
    half = ways // 2
    extent = -(-(nodes + arrivals * block) // 128) * 128

    node_v, edge_v, cot_v, win_v, wout_v, pre, up, hot, turned = pl.pallas_call(
        functools.partial(prep_kernel, parts, arrivals),
        out_shape=(
            pltpu.VMEM((nodes, latent), BF16),
            pltpu.VMEM((edges, latent), BF16),
            pltpu.VMEM((nodes, latent), BF16),
            pltpu.VMEM(weight_in.shape, BF16),
            pltpu.VMEM(weight_out.shape, BF16),
            pltpu.VMEM((edges, latent), F32),
            pltpu.VMEM((edges, latent), F32),
            pltpu.VMEM((edges, extent), BF16),
            pltpu.VMEM((extent + nodes, edges), BF16),
        ),
        in_specs=[SMEM] + [HBM] * 8,
        out_specs=(VMEM,) * 9,
        scratch_shapes=[
            pltpu.SMEM((tiles,), jnp.int32),
            pltpu.SMEM((tiles,), jnp.int32),
            pltpu.VMEM((tiles, block), jnp.int32),
            pltpu.VMEM((nodes, latent), F32),
            pltpu.VMEM((nodes, latent), F32),
            pltpu.SemaphoreType.DMA((10,)),
        ],
        compiler_params=small,
        cost_estimate=pl.CostEstimate(
            flops=2 * edges * latent * latent, bytes_accessed=8_000_000, transcendentals=0
        ),
        name="prepare",
    )(
        tile_count,
        in_hbm(tile_src),
        tile_dst,
        in_hbm(edge_slot),
        node_rows,
        in_hbm(edge_latents[0]),
        in_hbm(agg_cotangent[0]),
        in_hbm(weight_in),
        in_hbm(weight_out),
    )
    sent_shape = pltpu.VMEM((half, 2 * unit, latent), BF16)
    kept_shape = pltpu.VMEM((half, 2 * unit, latent), F32)
    ordered = [None] * arrivals
    for array, which in zip(came, arrival_order(arrivals)):
        ordered[which] = array
    grad_pre, message, sums, away_a, kept_a, away_b, kept_b, *outer = pl.pallas_call(
        functools.partial(edge_kernel, ways, arrivals, four, block),
        out_shape=(
            pltpu.VMEM((edges, latent), BF16),
            pltpu.VMEM((edges, latent), F32),
            pltpu.VMEM((extent + nodes, latent), F32),
            sent_shape,
            kept_shape,
            sent_shape,
            kept_shape,
            *[block_shape] * (2 if four else 0),
        ),
        in_specs=[VMEM] * (8 + arrivals),
        out_specs=(VMEM,) * (9 if four else 7),
        scratch_shapes=[
            pltpu.VMEM((extent, latent), BF16),
            pltpu.VMEM((edges, latent), BF16),
            pltpu.VMEM((edges, latent), BF16),
        ],
        compiler_params=pltpu.CompilerParams(vmem_limit_bytes=16 * 1024 * 1024),
        cost_estimate=pl.CostEstimate(
            flops=12 * edges * latent * latent,
            bytes_accessed=12_000_000,
            transcendentals=edges * latent,
        ),
        name="edge_block",
    )(
        *[
            in_vmem(array)
            for array in (*ordered, node_v, edge_v, win_v, wout_v, pre, up, hot, turned)
        ],
    )
    if four:
        rows = 2 * unit
        piece, wide = pltpu.VMEM((unit, latent), BF16), pltpu.VMEM((unit, latent), F32)
        came_a = swap(away_a, "dp", lambda i: i ^ 1)
        away_a, kept_a = halve(2, came_a, kept_a, cot_v)
        came_a = swap(away_a, "dp", lambda i: i ^ 2)
        came_b = swap(away_b, "dp", lambda i: i ^ 1)
        away_b, kept_b = small_call(
            beside_first_kernel,
            "beside_first",
            (pltpu.VMEM((rows, latent), BF16), pltpu.VMEM((2, unit, latent), F32)),
            came_b,
            kept_b,
        )
        beside = swap(away_b, "dom", lambda i: i ^ 1)
        far = swap(outer[1], "dom", lambda i: partners_of_four(2)[i])
        near = swap(outer[0], "dom", lambda i: partners_of_four(1)[i])
        away_a, kept_a = small_call(
            functools.partial(beside_second_kernel, nodes, block),
            "beside_second",
            (pltpu.VMEM((unit + block, latent), BF16), wide),
            came_a,
            kept_a,
            sums,
            far,
            near,
        )
        came_a = swap(away_a, "dom", lambda i: i ^ 1)
        away_b, kept_b = small_call(
            over_second_kernel, "over_second", (piece, wide), beside, kept_b
        )
        came_b = swap(away_b, "dp", lambda i: i ^ 2)
        pair = small_call(
            add_kernel,
            "add_terms",
            pltpu.VMEM((rows, latent), BF16),
            kept_a,
            came_a,
            kept_b,
            came_b,
        )
        returned = [came_a, near, far]
        late, backs = pair, 0
    else:
        came_a, kept_a, late = sum_over_dp(away_a, kept_a, cot_v)
        came_b, kept_b, _ = sum_over_dp(away_b, kept_b, cot_v)
        backs = arrivals
    edge_grad, agg, *back_sums = pl.pallas_call(
        functools.partial(edge_grad_kernel, block, arrivals, four),
        out_shape=(
            jax.ShapeDtypeStruct((edges, latent), BF16),
            jax.ShapeDtypeStruct((nodes, latent), BF16),
        )
        + (block_shape,) * backs,
        in_specs=[HBM, SMEM] + [VMEM] * 7,
        out_specs=(VMEM,) * (2 + backs),
        scratch_shapes=[
            pltpu.SMEM((tiles,), jnp.int32),
            pltpu.VMEM((nodes, latent), F32),
            pltpu.SemaphoreType.DMA,
        ],
        compiler_params=small,
        cost_estimate=pl.CostEstimate(
            flops=2 * edges * latent * latent, bytes_accessed=3_000_000, transcendentals=0
        ),
        name="edge_grads",
    )(
        tile_dst,
        tile_count,
        *[in_vmem(array) for array in (late, grad_pre, sums, cot_v, win_v, edge_v, message)],
    )
    if not four:
        returned = [
            from_behind(back_sums[which], "dom", -OFFSET_LIST[which]) for which in range(4)
        ]
    node_out = pl.pallas_call(
        functools.partial(node_grad_kernel, arrivals, four),
        out_shape=jax.ShapeDtypeStruct((nodes, latent), BF16),
        in_specs=[HBM] + [VMEM] * (3 + arrivals),
        out_specs=VMEM,
        scratch_shapes=[
            pltpu.VMEM((nodes, latent), F32),
            pltpu.SMEM(boundary.shape, jnp.int32),
            pltpu.SemaphoreType.DMA,
        ],
        compiler_params=small,
        cost_estimate=pl.CostEstimate(
            flops=8 * nodes * latent * latent, bytes_accessed=2_000_000, transcendentals=0
        ),
        name="node_grads",
    )(boundary, *[in_vmem(array) for array in (late, sums, win_v, *returned)])
    if four:
        w_in_grad, w_out_grad = pl.pallas_call(
            last_kernel,
            out_shape=(
                jax.ShapeDtypeStruct((3 * unit, latent), F32),
                jax.ShapeDtypeStruct((unit, latent), F32),
            ),
            in_specs=[HBM] * 2 + [VMEM] * 2,
            out_specs=(VMEM,) * 2,
            compiler_params=small,
            cost_estimate=pl.CostEstimate(flops=0, bytes_accessed=1_500_000, transcendentals=0),
            name="widen",
        )(in_hbm(node_out), in_hbm(edge_grad), *with_other_half(sum_of_four(pair)))
    else:
        sum_a = sum_over_dom(kept_a[0] + came_a[0].astype(F32))
        sum_b = sum_over_dom(kept_b[0] + came_b[0].astype(F32))
        w_in_grad = jnp.concatenate([sum_a[unit:], sum_b], axis=0)
        w_out_grad = sum_a[:unit]
    return (agg[None], edge_grad[None], node_out[None], w_in_grad, w_out_grad)


def solution(mesh):
    in_specs = (
        P(("group", "dp"), "dom", None),
        P(("group", "dp"), "dom", None),
        P(("group", "dp"), "dom", None),
        P(),
        P(),
        P(("group", "dom"), None),
        P(("group", "dom")),
        P(("group", "dom")),
        P(("group", "dom"), None),
        P(("group", "dom")),
    )
    out_specs = (
        P(("group", "dp"), "dom", None),
        P(("group", "dp"), "dom", None),
        P(("group", "dp"), "dom", None),
        P(("group", "dp"), None),
        P(("group", "dp"), None),
    )
    return jax.shard_map(body, mesh=mesh, in_specs=in_specs, out_specs=out_specs, check_vma=False)
```

```python
import functools

import jax
import jax.numpy as jnp
from jax import lax
from jax.experimental import pallas as pl
from jax.experimental.pallas import tpu as pltpu
from jax.sharding import PartitionSpec as P

OFFSET_LIST = (1, -1, 2, -2)
EPSILON = 1e-05
VMEM = pl.BlockSpec(memory_space=pltpu.VMEM)
HBM = pl.BlockSpec(memory_space=pltpu.HBM)
SMEM = pl.BlockSpec(memory_space=pltpu.SMEM)
ANY = pl.BlockSpec(memory_space=pl.ANY)
F32 = jnp.float32
BF16 = jnp.bfloat16


def dot(left, right):
    return jnp.dot(left, right, preferred_element_type=F32)


def dot_t(left, right):
    return lax.dot_general(left, right, (((1,), (1,)), ((), ())), preferred_element_type=F32)


def t_dot(left, right):
    return lax.dot_general(left, right, (((0,), (0,)), ((), ())), preferred_element_type=F32)


def row_mean(array):
    return jnp.sum(array, axis=1, keepdims=True) * (1.0 / array.shape[1])


def rows_of(ref, block, size):
    return ref[pl.ds(pl.multiple_of(block * size, size), size), :]


def load_small(source, target, sem):
    copy = pltpu.make_async_copy(source, target, sem)
    copy.start()
    return copy


def boundary_places(boundary_ref, part, four):
    taken = [boundary_ref[0, which] for which in range(4)]
    if not four:
        return taken
    even = part % 2 == 0
    return [
        jnp.where(even, taken[0], taken[1]),
        jnp.where(even, taken[1], taken[0]),
        jnp.where(part < 2, taken[2], taken[3]),
    ]


def arrival_places(part, four, arrivals):
    if not four:
        return list(range(arrivals))
    even = part % 2 == 0
    return [jnp.where(even, 1, 0), jnp.where(even, 0, 1), 2]


def pick_kernel(four, block, boundary_hbm, node_hbm, *refs):
    count = 3 if four else 4
    outs = refs[:count]
    boundary_ref, node_ref, sems = refs[count:]
    small = load_small(boundary_hbm, boundary_ref, sems.at[0])
    large = load_small(node_hbm, node_ref, sems.at[1])
    small.wait()
    places = boundary_places(boundary_ref, lax.axis_index("dom"), four)
    large.wait()
    for place, out in zip(places, outs):
        out[...] = rows_of(node_ref, place, block)


def prep_kernel(
    parts,
    arrivals,
    count_ref,
    src_hbm,
    dst_hbm,
    slot_hbm,
    node_hbm,
    edge_hbm,
    cot_hbm,
    win_hbm,
    wout_hbm,
    node_ref,
    edge_ref,
    cot_ref,
    win_ref,
    wout_ref,
    pre_ref,
    up_ref,
    hot_ref,
    hot_turned,
    edge_turned,
    src_ref,
    dst_ref,
    slot_ref,
    recv_ref,
    mid_ref,
    sems,
):
    tiles, block = slot_ref.shape
    nodes, latent = node_ref.shape
    owned = nodes // block
    extent = hot_ref.shape[1]
    pairs = (
        (src_hbm, src_ref),
        (dst_hbm, dst_ref),
        (slot_hbm, slot_ref),
        (node_hbm, node_ref),
        (win_hbm.at[2 * latent :, :], win_ref.at[2 * latent :, :]),
        (win_hbm.at[:latent, :], win_ref.at[:latent, :]),
        (edge_hbm, edge_ref),
        (cot_hbm, cot_ref),
        (win_hbm.at[latent : 2 * latent, :], win_ref.at[latent : 2 * latent, :]),
        (wout_hbm, wout_ref),
    )
    copies = [load_small(*pair, sems.at[number]) for number, pair in enumerate(pairs)]
    part = lax.axis_index("dom")
    for copy in copies[:3]:
        copy.wait()
    index = lax.broadcasted_iota(jnp.int32, (extent, 2 * block), 0)
    lane = lax.broadcasted_iota(jnp.int32, (1, 2 * block), 1)
    first = lane < block
    within = jnp.where(first, lane, lane - block)
    node_index = lax.broadcasted_iota(jnp.int32, (nodes, 2 * block), 0)
    for tile in range(0, tiles, 2):
        wanted = []
        for member in (tile, tile + 1):
            source = src_ref[member]
            which = source - owned
            reach = jnp.where(which >= 2, 2, 1)
            partner = part - jnp.where(which % 2 == 1, -reach, reach)
            exists = (source < owned) | ((partner >= 0) & (partner < parts))
            place = jnp.minimum(source, owned + arrivals - 1)
            wanted.append(jnp.where(exists, place * block, -2 * extent))
        slots = jnp.concatenate(
            [slot_ref[tile : tile + 1, :], slot_ref[tile + 1 : tile + 2, :]], axis=1
        )
        row = slots + jnp.where(first, wanted[0], wanted[1])
        hot = jnp.where(index == row, 1.0, 0.0)
        at = slice(tile * block, (tile + 2) * block)
        hot_turned[:extent, at] = hot.astype(BF16)
        target = within + jnp.where(first, dst_ref[tile] * block, dst_ref[tile + 1] * block)
        hot_turned[extent:, at] = jnp.where(node_index == target, 1.0, 0.0).astype(BF16)
        hot_ref[at, :] = hot.T.astype(BF16)
    copies[3].wait()
    copies[4].wait()
    recv_ref[...] = dot(node_ref[...], win_ref[2 * latent :, :])
    copies[5].wait()
    copies[6].wait()
    group = 4 if tiles % 4 == 0 else 2
    for tile in range(0, tiles, group):
        rows = slice(tile * block, (tile + group) * block)
        received = jnp.concatenate(
            [rows_of(recv_ref, dst_ref[t], block) for t in range(tile, tile + group)], axis=0
        )
        pre_ref[rows, :] = dot(edge_ref[rows, :], win_ref[:latent, :]) + received
    copies[7].wait()
    cot = cot_ref[...].astype(F32)
    mid_ref[...] = cot - row_mean(cot)
    for tile in range(tiles):
        live = jnp.where(tile < count_ref[0], 1.0, 0.0)
        up_ref[tile * block : (tile + 1) * block, :] = rows_of(mid_ref, dst_ref[tile], block) * live
    edge_turned[...] = edge_ref[...].T
    copies[8].wait()
    copies[9].wait()


def put_units(ways, bit, targets, sections):
    latent = sections[0][0].shape[1]
    unit = latent // ways
    step = 256
    for number, (left, right, turned) in enumerate(sections):
        value_right = right()
        for start in range(0, latent, step):
            if turned:
                value = dot(left[start : start + step, :], value_right)
            else:
                value = t_dot(left[:, start : start + step], value_right)
            for at in range(0, step, unit):
                owner, spot = (start + at) // unit, 0
                if number > 0:
                    place = ((number - 1) * latent + start + at) // unit
                    owner, spot = place // 3, 1 + place % 3
                away, kept = targets[spot // 2]
                part = value[at : at + unit]
                where = slice((spot % 2) * unit, (spot % 2 + 1) * unit)

                @pl.when(bit == owner % 2)
                def _(kept=kept, owner=owner, where=where, part=part):
                    kept[owner // 2, where, :] = part

                @pl.when(bit != owner % 2)
                def _(away=away, owner=owner, where=where, part=part):
                    away[owner // 2, where, :] = part.astype(BF16)


def arrival_order(arrivals):
    return (2, 0, 1) if arrivals == 3 else tuple(range(arrivals))


def edge_kernel(ways, arrivals, four, block, *refs):
    arrived = [refs[which] for which in arrival_order(arrivals)]
    (
        node_ref,
        edge_ref,
        win_ref,
        wout_ref,
        pre_ref,
        up_ref,
        hot_ref,
        hot_turned,
        edge_turned,
        gpre_ref,
        message_ref,
        sums_ref,
        away_a,
        kept_a,
        away_b,
        kept_b,
        *back_refs,
        ext_ref,
        act_ref,
        proj_ref,
    ) = refs[arrivals:]
    nodes, latent = node_ref.shape
    edges = edge_ref.shape[0]
    extent = ext_ref.shape[0]
    places = arrival_places(lax.axis_index("dom"), four, arrivals)

    ext_ref[:nodes, :] = node_ref[...]
    for which in range(arrivals):
        at = pl.multiple_of(nodes + places[which] * block, block)
        ext_ref[pl.ds(at, block), :] = arrived[which][...]
    filled = nodes + arrivals * block
    if filled < extent:
        ext_ref[filled:, :] = jnp.zeros((extent - filled, latent), BF16)

    span = edges
    for start in range(0, edges, span):
        rows = slice(start, start + span)
        senders = dot(hot_ref[rows, :], ext_ref[...]).astype(BF16)
        preact = pre_ref[rows, :] + dot(senders, win_ref[latent : 2 * latent, :])
        gate = 0.5 * jnp.tanh(0.5 * preact) + 0.5
        activated = preact * gate
        slope = gate + activated * (1.0 - gate)
        activated = activated.astype(BF16)
        act_ref[rows, :] = activated
        projected = dot(activated, wout_ref[...])
        centered = projected - row_mean(projected)
        inv_scale = lax.rsqrt(row_mean(centered * centered) + EPSILON)
        message = centered * inv_scale
        message_ref[rows, :] = message
        upstream = up_ref[rows, :]
        grad_project = inv_scale * (upstream - message * row_mean(upstream * message))
        grad_project = grad_project.astype(BF16)
        proj_ref[rows, :] = grad_project
        gpre_ref[rows, :] = (dot_t(grad_project, wout_ref[...]) * slope).astype(BF16)

    sums_ref[...] = dot(hot_turned[...], gpre_ref[...])
    for which, back_ref in enumerate(back_refs):
        back_ref[...] = back_block(nodes, block, sums_ref, 1 + which)
    sections = (
        (act_ref, lambda: proj_ref[...], False),
        (edge_turned, lambda: gpre_ref[...], True),
        (ext_ref, lambda: sums_ref[:extent, :].astype(BF16), False),
        (node_ref, lambda: sums_ref[extent:, :].astype(BF16), False),
    )
    targets = ((away_a, kept_a), (away_b, kept_b))
    put_units(ways, lax.axis_index("dp") % 2, targets, sections)


def edge_grad_kernel(
    block,
    arrivals,
    four,
    dst_hbm,
    count_ref,
    after,
    gpre_ref,
    sums_ref,
    cot_ref,
    win_ref,
    edge_ref,
    message_ref,
    out_ref,
    agg_out,
    *refs,
):
    back_sums = refs[:-3]
    dst_ref, agg_ref, sem = refs[-3:]
    copy = load_small(dst_hbm, dst_ref, sem)
    nodes, latent = cot_ref.shape
    tiles = gpre_ref.shape[0] // block
    group = 4 if tiles % 4 == 0 else 1
    places = arrival_places(lax.axis_index("dom"), four, arrivals)
    for place, back_ref in zip(places, back_sums):
        at = pl.multiple_of(nodes + place * block, block)
        back_ref[...] = sums_ref[pl.ds(at, block), :].astype(BF16)
    agg_ref[...] = jnp.zeros_like(agg_ref)
    copy.wait()
    for first in range(0, tiles, group):
        rows = slice(first * block, (first + group) * block)
        upstream = jnp.concatenate(
            [
                rows_of(cot_ref, dst_ref[t], block).astype(F32)
                * jnp.where(t < count_ref[0], 1.0, 0.0)
                for t in range(first, first + group)
            ],
            axis=0,
        )
        out_ref[rows, :] = (dot_t(gpre_ref[rows, :], win_ref[:latent, :]) + upstream).astype(BF16)
        for t in range(first, first + group):
            live = jnp.where(t < count_ref[0], 1.0, 0.0)
            mine = slice(t * block, (t + 1) * block)
            updated = edge_ref[mine, :].astype(F32) + message_ref[mine, :]
            target = pl.ds(pl.multiple_of(dst_ref[t] * block, block), block)
            agg_ref[target, :] += updated * live
    agg_out[...] = agg_ref[...].astype(BF16)


def halve_kernel(bit, came_ref, kept_ref, after, away_ref, left_ref):
    mine = (lax.axis_index("dp") // bit) % 2
    for slot in range(left_ref.shape[0]):
        there, here = 2 * slot + 1 - mine, 2 * slot + mine
        away_ref[slot] = (kept_ref[there] + came_ref[there].astype(F32)).astype(BF16)
        left_ref[slot] = kept_ref[here] + came_ref[here].astype(F32)


def half_rows(rows):
    part = lax.axis_index("dom")
    inner = (part == 1) | (part == 2)
    here = pl.ds(pl.multiple_of(jnp.where(inner, 0, rows), rows), rows)
    there = pl.ds(pl.multiple_of(jnp.where(inner, rows, 0), rows), rows)
    return here, there


def back_block(nodes, block, sums_ref, which):
    place = arrival_places(lax.axis_index("dom"), True, 3)[which]
    return sums_ref[pl.ds(pl.multiple_of(nodes + place * block, block), block), :].astype(BF16)


def beside_first_kernel(came_ref, kept_ref, away_ref, left_ref):
    rows = left_ref.shape[1]
    here, there = half_rows(rows)
    for slot in range(2):
        away_ref[slot * rows : (slot + 1) * rows, :] = (
            kept_ref[slot, there, :] + came_ref[slot, there, :].astype(F32)
        ).astype(BF16)
        left_ref[slot] = kept_ref[slot, here, :] + came_ref[slot, here, :].astype(F32)


def beside_second_kernel(nodes, block, came_ref, kept_ref, sums_ref, *refs):
    away_ref, left_ref = refs[-2:]
    rows = left_ref.shape[0]
    here, there = half_rows(rows)
    away_ref[:rows, :] = (kept_ref[0, there, :] + came_ref[0, there, :].astype(F32)).astype(BF16)
    away_ref[rows:, :] = back_block(nodes, block, sums_ref, 0)
    left_ref[...] = kept_ref[0, here, :] + came_ref[0, here, :].astype(F32)


def over_second_kernel(came_ref, kept_ref, *refs):
    away_ref, left_ref = refs[-2:]
    mine = lax.axis_index("dp") // 2
    rows = left_ref.shape[0]

    def came(slot):
        spot = pl.ds(pl.multiple_of(slot * rows, rows), rows)
        return came_ref[spot, :].astype(F32)

    away_ref[...] = (kept_ref[1 - mine] + came(1 - mine)).astype(BF16)
    left_ref[...] = kept_ref[mine] + came(mine)


def add_kernel(left_a, came_a, left_b, came_b, *refs):
    out_ref = refs[-1]
    rows = left_a.shape[0]
    out_ref[:rows, :] = (left_a[...] + came_a[:rows, :].astype(F32)).astype(BF16)
    out_ref[rows:, :] = (left_b[...] + came_b[...].astype(F32)).astype(BF16)


def node_grad_kernel(arrivals, four, boundary_hbm, after, sums_ref, win_ref, *refs):
    returned = refs[:arrivals]
    out_ref, total_ref, boundary_ref, sem = refs[arrivals:]
    nodes, latent = out_ref.shape
    extent = sums_ref.shape[0] - nodes
    block = returned[-1].shape[0]
    copy = load_small(boundary_hbm, boundary_ref, sem)
    total_ref[...] = sums_ref[:nodes, :]
    copy.wait()
    for which, place in enumerate(boundary_places(boundary_ref, lax.axis_index("dom"), four)):
        spot = pl.ds(pl.multiple_of(place * block, block), block)
        total_ref[spot, :] += returned[which][-block:, :].astype(F32)

    def wide_dot(value, weight):
        high = value.astype(BF16)
        low = (value - high.astype(F32)).astype(BF16)
        return dot_t(high, weight) + dot_t(low, weight)

    out_ref[...] = (
        wide_dot(total_ref[...], win_ref[latent : 2 * latent, :])
        + wide_dot(sums_ref[extent:, :], win_ref[2 * latent :, :])
    ).astype(BF16)


def last_kernel(node_out, edge_grad, own_ref, other_ref, in_ref, out_ref):
    unit = out_ref.shape[0]
    part = lax.axis_index("dom")
    inner = (part == 1) | (part == 2)

    def write(low, high):
        out_ref[...] = low[:unit, :].astype(F32)
        in_ref[:unit, :] = high[:unit, :].astype(F32)
        in_ref[unit : 2 * unit, :] = low[unit:, :].astype(F32)
        in_ref[2 * unit :, :] = high[unit:, :].astype(F32)

    @pl.when(inner)
    def _():
        write(own_ref, other_ref)

    @pl.when(jnp.logical_not(inner))
    def _():
        write(other_ref, own_ref)


def swap(array, axis, partner):
    devices = lax.axis_size(axis)
    return lax.ppermute(array, axis, [(i, partner(i)) for i in range(devices)])


def from_behind(array, axis, by):
    devices = lax.axis_size(axis)
    pairs = [(i, i + by) for i in range(devices) if 0 <= i + by < devices]
    return lax.ppermute(array, axis, pairs)


def partners_of_four(which):
    return ((1, 0, 3, 2), (0, 2, 1, 3), (2, 3, 0, 1))[which]


def exchange_of_four(first, second, third):
    third = swap(third, "dom", lambda i: partners_of_four(2)[i])
    second = swap(second, "dom", lambda i: partners_of_four(1)[i])
    first = swap(first, "dom", lambda i: partners_of_four(0)[i])
    return [first, second, third]


def halve(bit, came, kept, after):
    slots, rows, latent = kept.shape
    return pl.pallas_call(
        functools.partial(halve_kernel, bit),
        out_shape=(
            pltpu.VMEM((slots // 2, rows, latent), BF16),
            pltpu.VMEM((slots // 2, rows, latent), F32),
        ),
        in_specs=[VMEM] * 3,
        out_specs=(VMEM,) * 2,
        compiler_params=pltpu.CompilerParams(vmem_limit_bytes=4 * 1024 * 1024),
        cost_estimate=pl.CostEstimate(flops=0, bytes_accessed=500_000, transcendentals=0),
        name="halve",
    )(in_vmem(came), in_vmem(kept), in_vmem(after))


def sum_over_dp(away, kept, after):
    devices = lax.axis_size("dp")
    bit = 1
    while True:
        came = swap(away, "dp", lambda i, bit=bit: i ^ bit)
        bit *= 2
        if bit >= devices:
            return came, kept, away
        away, kept = halve(bit, came, kept, after)


def small_call(kernel, name, out_shape, *operands, after=()):
    many = isinstance(out_shape, tuple)
    return pl.pallas_call(
        kernel,
        out_shape=out_shape,
        in_specs=[VMEM] * len(operands) + [HBM] * len(after),
        out_specs=(VMEM,) * len(out_shape) if many else VMEM,
        compiler_params=pltpu.CompilerParams(vmem_limit_bytes=4 * 1024 * 1024),
        cost_estimate=pl.CostEstimate(flops=0, bytes_accessed=500_000, transcendentals=0),
        name=name,
    )(*[in_vmem(array) for array in operands], *[in_hbm(array) for array in after])


def sum_of_four(kept):
    return (kept.astype(F32) + swap(kept, "dom", lambda i: 3 - i).astype(F32)).astype(BF16)


def with_other_half(kept):
    return kept, swap(kept, "dom", lambda i: i ^ 1)


def sum_over_dom(rows):
    piece = lax.psum_scatter(rows, "dom", scatter_dimension=0, tiled=True)
    return lax.all_gather(piece, "dom", axis=0, tiled=True)


def in_vmem(array):
    return pltpu.with_memory_space_constraint(array, pltpu.VMEM)


def in_hbm(array):
    return pltpu.with_memory_space_constraint(array, pltpu.HBM)


def body(
    node_latents,
    edge_latents,
    agg_cotangent,
    weight_in,
    weight_out,
    boundary,
    tile_src,
    tile_dst,
    edge_slot,
    tile_count,
):
    tiles, block = edge_slot.shape
    edges, latent = edge_latents.shape[1:]
    nodes = node_latents.shape[1]
    parts = lax.axis_size("dom")
    ways = lax.axis_size("dp")
    four = parts == 4 and ways == 4
    arrivals = 3 if four else 4
    boundary = in_hbm(boundary)
    tile_dst = in_hbm(tile_dst)
    node_rows = in_hbm(node_latents[0])
    block_shape = pltpu.VMEM((block, latent), BF16)
    small = pltpu.CompilerParams(vmem_limit_bytes=8 * 1024 * 1024)

    sent = pl.pallas_call(
        functools.partial(pick_kernel, four, block),
        out_shape=(block_shape,) * arrivals,
        in_specs=[HBM] * 2,
        out_specs=(VMEM,) * arrivals,
        scratch_shapes=[
            pltpu.SMEM(boundary.shape, jnp.int32),
            pltpu.VMEM((nodes, latent), BF16),
            pltpu.SemaphoreType.DMA((2,)),
        ],
        compiler_params=small,
        cost_estimate=pl.CostEstimate(flops=0, bytes_accessed=400_000, transcendentals=0),
        name="pick_blocks",
    )(boundary, node_rows)
    if four:
        came = exchange_of_four(*sent)
    else:
        came = [from_behind(sent[which], "dom", OFFSET_LIST[which]) for which in range(4)]
    unit = latent // ways
    half = ways // 2
    extent = -(-(nodes + arrivals * block) // 128) * 128

    node_v, edge_v, cot_v, win_v, wout_v, pre, up, hot, turned, edge_t = pl.pallas_call(
        functools.partial(prep_kernel, parts, arrivals),
        out_shape=(
            pltpu.VMEM((nodes, latent), BF16),
            pltpu.VMEM((edges, latent), BF16),
            pltpu.VMEM((nodes, latent), BF16),
            pltpu.VMEM(weight_in.shape, BF16),
            pltpu.VMEM(weight_out.shape, BF16),
            pltpu.VMEM((edges, latent), F32),
            pltpu.VMEM((edges, latent), F32),
            pltpu.VMEM((edges, extent), BF16),
            pltpu.VMEM((extent + nodes, edges), BF16),
            pltpu.VMEM((latent, edges), BF16),
        ),
        in_specs=[SMEM] + [HBM] * 8,
        out_specs=(VMEM,) * 10,
        scratch_shapes=[
            pltpu.SMEM((tiles,), jnp.int32),
            pltpu.SMEM((tiles,), jnp.int32),
            pltpu.VMEM((tiles, block), jnp.int32),
            pltpu.VMEM((nodes, latent), F32),
            pltpu.VMEM((nodes, latent), F32),
            pltpu.SemaphoreType.DMA((10,)),
        ],
        compiler_params=small,
        cost_estimate=pl.CostEstimate(
            flops=2 * edges * latent * latent, bytes_accessed=8_000_000, transcendentals=0
        ),
        name="prepare",
    )(
        tile_count,
        in_hbm(tile_src),
        tile_dst,
        in_hbm(edge_slot),
        node_rows,
        in_hbm(edge_latents[0]),
        in_hbm(agg_cotangent[0]),
        in_hbm(weight_in),
        in_hbm(weight_out),
    )
    sent_shape = pltpu.VMEM((half, 2 * unit, latent), BF16)
    kept_shape = pltpu.VMEM((half, 2 * unit, latent), F32)
    ordered = [None] * arrivals
    for array, which in zip(came, arrival_order(arrivals)):
        ordered[which] = array
    grad_pre, message, sums, away_a, kept_a, away_b, kept_b, *outer = pl.pallas_call(
        functools.partial(edge_kernel, ways, arrivals, four, block),
        out_shape=(
            pltpu.VMEM((edges, latent), BF16),
            pltpu.VMEM((edges, latent), F32),
            pltpu.VMEM((extent + nodes, latent), F32),
            sent_shape,
            kept_shape,
            sent_shape,
            kept_shape,
            *[block_shape] * (2 if four else 0),
        ),
        in_specs=[VMEM] * (9 + arrivals),
        out_specs=(VMEM,) * (9 if four else 7),
        scratch_shapes=[
            pltpu.VMEM((extent, latent), BF16),
            pltpu.VMEM((edges, latent), BF16),
            pltpu.VMEM((edges, latent), BF16),
        ],
        compiler_params=pltpu.CompilerParams(vmem_limit_bytes=16 * 1024 * 1024),
        cost_estimate=pl.CostEstimate(
            flops=12 * edges * latent * latent,
            bytes_accessed=12_000_000,
            transcendentals=edges * latent,
        ),
        name="edge_block",
    )(
        *[
            in_vmem(array)
            for array in (*ordered, node_v, edge_v, win_v, wout_v, pre, up, hot, turned, edge_t)
        ],
    )
    if four:
        rows = 2 * unit
        piece, wide = pltpu.VMEM((unit, latent), BF16), pltpu.VMEM((unit, latent), F32)
        came_a = swap(away_a, "dp", lambda i: i ^ 1)
        away_a, kept_a = halve(2, came_a, kept_a, cot_v)
        came_a = swap(away_a, "dp", lambda i: i ^ 2)
        came_b = swap(away_b, "dp", lambda i: i ^ 1)
        away_b, kept_b = small_call(
            beside_first_kernel,
            "beside_first",
            (pltpu.VMEM((rows, latent), BF16), pltpu.VMEM((2, unit, latent), F32)),
            came_b,
            kept_b,
        )
        beside = swap(away_b, "dom", lambda i: i ^ 1)
        far = swap(outer[1], "dom", lambda i: partners_of_four(2)[i])
        near = swap(outer[0], "dom", lambda i: partners_of_four(1)[i])
        away_a, kept_a = small_call(
            functools.partial(beside_second_kernel, nodes, block),
            "beside_second",
            (pltpu.VMEM((unit + block, latent), BF16), wide),
            came_a,
            kept_a,
            sums,
            far,
            near,
        )
        came_a = swap(away_a, "dom", lambda i: i ^ 1)
        away_b, kept_b = small_call(
            over_second_kernel, "over_second", (piece, wide), beside, kept_b
        )
        came_b = swap(away_b, "dp", lambda i: i ^ 2)
        pair = small_call(
            add_kernel,
            "add_terms",
            pltpu.VMEM((rows, latent), BF16),
            kept_a,
            came_a,
            kept_b,
            came_b,
        )
        returned = [came_a, near, far]
        late, backs = pair, 0
    else:
        came_a, kept_a, late = sum_over_dp(away_a, kept_a, cot_v)
        came_b, kept_b, _ = sum_over_dp(away_b, kept_b, cot_v)
        backs = arrivals
    edge_grad, agg, *back_sums = pl.pallas_call(
        functools.partial(edge_grad_kernel, block, arrivals, four),
        out_shape=(
            jax.ShapeDtypeStruct((edges, latent), BF16),
            jax.ShapeDtypeStruct((nodes, latent), BF16),
        )
        + (block_shape,) * backs,
        in_specs=[HBM, SMEM] + [VMEM] * 7,
        out_specs=(VMEM,) * (2 + backs),
        scratch_shapes=[
            pltpu.SMEM((tiles,), jnp.int32),
            pltpu.VMEM((nodes, latent), F32),
            pltpu.SemaphoreType.DMA,
        ],
        compiler_params=small,
        cost_estimate=pl.CostEstimate(
            flops=2 * edges * latent * latent, bytes_accessed=3_000_000, transcendentals=0
        ),
        name="edge_grads",
    )(
        tile_dst,
        tile_count,
        *[in_vmem(array) for array in (late, grad_pre, sums, cot_v, win_v, edge_v, message)],
    )
    if not four:
        returned = [
            from_behind(back_sums[which], "dom", -OFFSET_LIST[which]) for which in range(4)
        ]
    node_out = pl.pallas_call(
        functools.partial(node_grad_kernel, arrivals, four),
        out_shape=jax.ShapeDtypeStruct((nodes, latent), BF16),
        in_specs=[HBM] + [VMEM] * (3 + arrivals),
        out_specs=VMEM,
        scratch_shapes=[
            pltpu.VMEM((nodes, latent), F32),
            pltpu.SMEM(boundary.shape, jnp.int32),
            pltpu.SemaphoreType.DMA,
        ],
        compiler_params=small,
        cost_estimate=pl.CostEstimate(
            flops=8 * nodes * latent * latent, bytes_accessed=2_000_000, transcendentals=0
        ),
        name="node_grads",
    )(boundary, *[in_vmem(array) for array in (late, sums, win_v, *returned)])
    if four:
        w_in_grad, w_out_grad = pl.pallas_call(
            last_kernel,
            out_shape=(
                jax.ShapeDtypeStruct((3 * unit, latent), F32),
                jax.ShapeDtypeStruct((unit, latent), F32),
            ),
            in_specs=[HBM] * 2 + [VMEM] * 2,
            out_specs=(VMEM,) * 2,
            compiler_params=small,
            cost_estimate=pl.CostEstimate(flops=0, bytes_accessed=1_500_000, transcendentals=0),
            name="widen",
        )(in_hbm(node_out), in_hbm(edge_grad), *with_other_half(sum_of_four(pair)))
    else:
        sum_a = sum_over_dom(kept_a[0] + came_a[0].astype(F32))
        sum_b = sum_over_dom(kept_b[0] + came_b[0].astype(F32))
        w_in_grad = jnp.concatenate([sum_a[unit:], sum_b], axis=0)
        w_out_grad = sum_a[:unit]
    return (agg[None], edge_grad[None], node_out[None], w_in_grad, w_out_grad)


def solution(mesh):
    in_specs = (
        P(("group", "dp"), "dom", None),
        P(("group", "dp"), "dom", None),
        P(("group", "dp"), "dom", None),
        P(),
        P(),
        P(("group", "dom"), None),
        P(("group", "dom")),
        P(("group", "dom")),
        P(("group", "dom"), None),
        P(("group", "dom")),
    )
    out_specs = (
        P(("group", "dp"), "dom", None),
        P(("group", "dp"), "dom", None),
        P(("group", "dp"), "dom", None),
        P(("group", "dp"), None),
        P(("group", "dp"), None),
    )
    return jax.shard_map(body, mesh=mesh, in_specs=in_specs, out_specs=out_specs, check_vma=False)
```
